128 devices in a mesh: rep: 16 (over z, y), ep: 8 (over x, core).
Axes of the slice: x: 4, y: 4, z: 4, core: 2. Of those that a mesh axis runs over, the one named last changes fastest.
Arguments:
- tokens: bfloat16 [32768, 1024], P(('rep', 'ep')), may hold values from -6 to 6
- segments: int32 [16, 2048], P('rep'), may hold values from 0 to 2, as said below
- routes: int32 [32768, 8], P(('rep', 'ep')), may hold values from 0 to 31, all different within a row; in each aligned block of 256 rows (0 to 255, 256 to 511, ...) at most 88 rows name the same one
- w_query: bfloat16 [1024, 1024], P(('rep', 'ep')), may hold values from -0.1875 to 0.1875
- w_key: bfloat16 [1024, 512], P(('rep', 'ep')), may hold values from -0.1875 to 0.1875
- w_value: bfloat16 [1024, 512], P(('rep', 'ep')), may hold values from -0.1875 to 0.1875
- w_out: bfloat16 [1024, 1024], P(('rep', 'ep')), may hold values from -1.5 to 1.5
- w_router: bfloat16 [1024, 32], P(('rep', 'ep')), may hold values from -0.09375 to 0.09375
- gain_attn: bfloat16 [1024], P(('rep', 'ep')), may hold values from 0.25 to 1.75
- gain_query: bfloat16 [1024], P(('rep', 'ep')), may hold values from 0.25 to 1.75
- gain_key: bfloat16 [512], P(('rep', 'ep')), may hold values from 0.25 to 1.75
- gain_ffn: bfloat16 [1024], P(('rep', 'ep')), may hold values from 0.25 to 1.75
- w_gate: bfloat16 [32, 1024, 512], P('ep'), may hold values from -0.1875 to 0.1875
- w_up: bfloat16 [32, 1024, 512], P('ep'), may hold values from -0.1875 to 0.1875
- w_down: bfloat16 [32, 512, 1024], P('ep'), may hold values from -1 to 1
- out_grad: bfloat16 [32768, 1024], P(('rep', 'ep')), may hold values from -6 to 6
Outputs:
- output: bfloat16 [32768, 1024], P(('rep', 'ep'))
- input_grad: float32 [32768, 1024], P(('rep', 'ep'))
- grad_query: float32 [1024, 1024], P(('rep', 'ep'))
- grad_key: float32 [1024, 512], P(('rep', 'ep'))
- grad_value: float32 [1024, 512], P(('rep', 'ep'))
- grad_out: float32 [1024, 1024], P(('rep', 'ep'))
- grad_router: float32 [1024, 32], P(('rep', 'ep'))
- grad_gain_attn: float32 [1024], P(('rep', 'ep'))
- grad_gain_query: float32 [1024], P(('rep', 'ep'))
- grad_gain_key: float32 [512], P(('rep', 'ep'))
- grad_gain_ffn: float32 [1024], P(('rep', 'ep'))
- grad_gate: float32 [32, 1024, 512], P('ep', 'rep')
- grad_up: float32 [32, 1024, 512], P('ep', 'rep')
- grad_down: float32 [32, 512, 1024], P('ep', 'rep')
The draws below stay inside these ranges and needn't reach their ends.
Inputs may be any that keep to these rules, and one draw needn't show every extreme that they name: `routes`: each row names 8 different experts. In the rows of one device no expert is named more than 88 times, and that count is reached in every draw. `segments`: along each sequence the numbers never fall.
All inputs are finite; a program needn't handle non-finite values.
Results may differ from the reference program's by a relative error of at most 0.03.
Values may be sent and summed in bfloat16 or wider, within the bound.
A program may use at most 192 MiB of HBM per device.

```python
import math
import jax
import jax.numpy as jnp
import numpy as np
from jax import lax

D = 1024
HEADS = 16
KV_HEADS = 8
HEAD_DIM = 64
FF = 512
TOP = 8
WINDOW = 1024
LENGTH = 2048
TOK_DEV = 256
SEQS = 16
TOKENS = 32768
KV = 512
EXPERTS = 32
CAP = 88
N_EP = 8


def draw_segments(key, part):
    key = jax.random.fold_in(key, 7)
    first_key, last_key = jax.random.split(key)
    opening = jax.random.randint(first_key, (SEQS, 1), 1, TOK_DEV)
    closing = jax.random.randint(last_key, (SEQS, 1), LENGTH - TOK_DEV + 1, LENGTH)
    places = jnp.arange(LENGTH, dtype=jnp.int32)[None, :]
    return (places >= opening).astype(jnp.int32) + (places >= closing).astype(jnp.int32)


def levels(rng, shape, cuts, smallest, high):
    level, own = 1.0, jax.random.fold_in(rng, 6)
    for dim, blocks in cuts:
        draws = jnp.exp(jax.random.uniform(jax.random.fold_in(own, dim), (blocks,), jnp.float32, smallest / len(cuts), high / len(cuts)))
        level = level * jnp.repeat(draws, shape[dim] // blocks).reshape([-1 if axis == dim else 1 for axis in range(len(shape))])
    return level


def deal_out(stream_key, own, number, rows, amount, top, most, lean):
    order = jax.random.permutation(stream_key, amount)
    crowded, common = portions_of(amount, rows * top, most, lean, True), portions_of(amount, rows * top, most, lean, False)
    places = jnp.arange(amount)

    def named(lengths, rotation):
        used = int((lengths > 0).sum())
        fixed = max(1, used // 4)
        passed = fixed + (places - fixed + rotation * (used - fixed)) % max(1, amount - fixed)
        return jnp.zeros((amount,), jnp.int32).at[order[jnp.where(places < fixed, places, passed)]].set(jnp.asarray(lengths, jnp.int32))

    lengths = jnp.where(number % 4 == 0, named(crowded, number // 4), named(common, number - number // 4 - 1))
    mixed = jax.random.permutation(jax.random.fold_in(own, 3), amount)
    donor, taker = mixed[0:amount // 2 * 2:2], mixed[1:amount // 2 * 2:2]
    slack = jnp.minimum(lengths[donor] - 1, most - lengths[taker]) // 2
    slack = jnp.where((donor == order[0]) | (taker == order[0]) | (lengths[taker] == 0), 0, jnp.maximum(slack, 0))
    passed = jax.random.randint(jax.random.fold_in(own, 4), (amount // 2,), 0, 1 << 20) % (slack + 1)
    lengths = lengths.at[donor].add(-passed).at[taker].add(passed)
    items = jnp.searchsorted(jnp.cumsum(lengths), jnp.arange(rows * top), side="right").astype(jnp.int32)
    grid = items.reshape(top, rows).T
    grid = grid[jax.random.permutation(jax.random.fold_in(own, 1), rows)]
    rotation = jax.random.randint(jax.random.fold_in(own, 2), (rows, 1), 0, top)
    return jnp.take_along_axis(grid, (jnp.arange(top)[None, :] + rotation) % top, axis=1)


def portions_of(amount, total, bound, lean, full):
    weights = [(1 << 20) // math.isqrt(grade ** lean) + 1 for grade in range(1, amount + 1)]
    largest = bound if full else min(bound, max(-(-total // amount), total * weights[0] // sum(weights)))
    least = 1 if total - largest >= amount - 1 else 0
    counts, spare = [largest] + [least] * (amount - 1), total - largest - least * (amount - 1)
    while spare > 0:
        movable = [i for i in range(1, amount) if counts[i] < largest] or [i for i in range(1, amount) if counts[i] < bound]
        pool, left = sum([weights[i] for i in movable]), spare
        for i in movable:
            extra = min(bound - counts[i], max(1, left * weights[i] // pool), spare)
            counts[i] = counts[i] + extra
            spare = spare - extra
    return np.array(counts)


def bell_draw(own_key, extent, scale, reach, shards=(), kind=jnp.bfloat16):
    gain = levels(own_key, extent, shards, -0.22, 0.18) if shards else 1.0
    values = jax.random.normal(own_key, extent, jnp.float32) * scale * gain
    return jnp.minimum(jnp.maximum(values, -reach), reach).astype(kind)


def setup_inputs(seed: int = 0) -> dict:
    seeds = jax.random.split(jax.random.key(seed), 17)
    tokens = bell_draw(seeds[0], (TOKENS, D), 1.0, 6.0, ((0, 128),))
    segments = draw_segments(jax.random.fold_in(seeds[16], 71), 0)
    routes_keys = jax.random.split(jax.random.fold_in(seeds[2], 1), TOKENS // TOK_DEV)
    routes_turns = jax.random.permutation(jax.random.fold_in(seeds[2], 3), TOKENS // TOK_DEV)
    routes = jax.vmap(lambda own, number: deal_out(jax.random.fold_in(seeds[2], 2), own, number, TOK_DEV, EXPERTS, TOP, CAP, 2))(routes_keys, routes_turns).reshape((TOKENS, TOP))
    w_query = bell_draw(seeds[3], (D, D), D ** -0.5, 0.1875, ((0, 128),))
    w_key = bell_draw(seeds[4], (D, KV), D ** -0.5, 0.1875, ((0, 128),))
    w_value = bell_draw(seeds[5], (D, KV), D ** -0.5, 0.1875, ((0, 128),))
    w_out = bell_draw(seeds[6], (D, D), (D // 64) ** -0.5, 1.5, ((0, 128),))
    w_router = bell_draw(seeds[7], (D, EXPERTS), (4 * D) ** -0.5, 0.09375, ((0, 128),))
    gain_attn = jnp.clip(1.0 + 0.15 * jax.random.normal(seeds[8], (D,), jnp.float32), 0.25, 1.75).astype(jnp.bfloat16)
    gain_query = jnp.clip(1.0 + 0.15 * jax.random.normal(seeds[9], (D,), jnp.float32), 0.25, 1.75).astype(jnp.bfloat16)
    gain_key = jnp.clip(1.0 + 0.15 * jax.random.normal(seeds[10], (KV,), jnp.float32), 0.25, 1.75).astype(jnp.bfloat16)
    gain_ffn = jnp.clip(1.0 + 0.15 * jax.random.normal(seeds[11], (D,), jnp.float32), 0.25, 1.75).astype(jnp.bfloat16)
    w_gate = bell_draw(seeds[12], (EXPERTS, D, FF), D ** -0.5, 0.1875, ((0, 8),))
    w_up = bell_draw(seeds[13], (EXPERTS, D, FF), D ** -0.5, 0.1875, ((0, 8),))
    w_down = bell_draw(seeds[14], (EXPERTS, FF, D), (FF // 16) ** -0.5, 1.0, ((0, 8),))
    out_grad = bell_draw(seeds[15], (TOKENS, D), 1.0, 6.0, ((0, 128),))
    return dict(tokens=tokens, segments=segments, routes=routes, w_query=w_query, w_key=w_key, w_value=w_value, w_out=w_out, w_router=w_router, gain_attn=gain_attn, gain_query=gain_query, gain_key=gain_key, gain_ffn=gain_ffn, w_gate=w_gate, w_up=w_up, w_down=w_down, out_grad=out_grad)


@jax.custom_vjp
def low(v):
    return lax.optimization_barrier(v.astype(jnp.bfloat16)).astype(jnp.float32)

@jax.custom_vjp
def low_back(v):
    return v

def low_keep(v):
    return (low(v), None)

def low_pass(kept, grad):
    return (grad,)

def back_keep(v):
    return (v, None)

def back_low(kept, grad):
    return (low(grad),)
low.defvjp(low_keep, low_pass)
low_back.defvjp(back_keep, back_low)
EPSILON = 1e-06
ROPE_BASE = 10000.0
MASKED = -1e+30
PRECISE = lax.Precision.HIGHEST

def rms_norm(values, norm_gain):
    return values * lax.rsqrt(lax.optimization_barrier(jnp.mean(values * values, axis=-1, keepdims=True)) + EPSILON) * norm_gain

def rotate(values, places):
    halfway = HEAD_DIM // 2
    frequency = ROPE_BASE ** (-(jnp.arange(halfway, dtype=jnp.float32) * 2.0 / HEAD_DIM))
    angles = places.astype(jnp.float32)[:, None] * frequency[None, :]
    cosine = jnp.cos(angles)[:, None, :]
    sine_part = jnp.sin(angles)[:, None, :]
    former = values[..., :halfway]
    latter = values[..., halfway:]
    return jnp.concatenate([former * cosine - latter * sine_part, latter * cosine + former * sine_part], axis=-1)

def attend_rows(start, queries, keys, values, segment_row):
    length = queries.shape[0]
    block_rows = math.gcd(length, 512)
    block_queries = lax.dynamic_slice_in_dim(queries, start, block_rows, 0)
    row_places = start + jnp.arange(block_rows, dtype=jnp.int32)
    col_places = jnp.arange(length, dtype=jnp.int32)
    row_segments = lax.dynamic_slice_in_dim(segment_row, start, block_rows, 0)
    distance = row_places[:, None] - col_places[None, :]
    allowed = (distance >= 0) & (distance < WINDOW) & (row_segments[:, None] == segment_row[None, :])
    grouped = block_queries.reshape(block_rows, KV_HEADS, HEADS // KV_HEADS, HEAD_DIM)
    scores = jnp.einsum('tgrd,kgd->grtk', grouped, keys, precision=PRECISE) * HEAD_DIM ** (-0.5)
    scores = jnp.where(allowed, low_back(scores), MASKED)
    score_peak = lax.optimization_barrier(jnp.max(scores, axis=-1, keepdims=True))
    raised = jnp.exp(scores - score_peak)
    attn_probs = low(raised / lax.optimization_barrier(jnp.sum(raised, axis=-1, keepdims=True)))
    mixed = jnp.einsum('grtk,kgd->tgrd', attn_probs, values, precision=PRECISE)
    return mixed.reshape(block_rows, HEADS * HEAD_DIM)

def layer(inputs, segment_row, route_rows, weights):
    w_query, w_key, w_value, w_out, w_router, gain_attn, gain_query, gain_key, gain_ffn, w_gate, w_up, w_down = weights
    length = inputs.shape[0]
    places = jnp.arange(length, dtype=jnp.int32)
    normed = low(rms_norm(inputs, gain_attn))
    query_lin = low_back(jnp.dot(normed, w_query, precision=PRECISE))
    key_lin = low_back(jnp.dot(normed, w_key, precision=PRECISE))
    value_rows = low_back(low(jnp.dot(normed, w_value, precision=PRECISE)))
    query_rot = low_back(low(rotate(rms_norm(query_lin, gain_query).reshape(length, HEADS, HEAD_DIM), places)))
    key_rot = low_back(low(rotate(rms_norm(key_lin, gain_key).reshape(length, KV_HEADS, HEAD_DIM), places)))
    value_heads = value_rows.reshape(length, KV_HEADS, HEAD_DIM)
    block_rows = math.gcd(length, 512)
    starts = jnp.arange(length // block_rows, dtype=jnp.int32) * block_rows
    attend = jax.checkpoint(lambda start: attend_rows(start, query_rot, key_rot, value_heads, segment_row))
    attended = lax.map(attend, starts).reshape(length, HEADS * HEAD_DIM)
    attended = low_back(low(attended))
    hidden = inputs + low_back(jnp.dot(attended, w_out, precision=PRECISE))
    moe_in = low(rms_norm(hidden, gain_ffn))
    logits = low_back(jnp.dot(moe_in, w_router, precision=PRECISE))
    chosen = jnp.take_along_axis(logits, route_rows, axis=1)
    lifted = jnp.exp(chosen - lax.optimization_barrier(jnp.max(chosen, axis=1, keepdims=True)))
    gate_weights = lifted / lax.optimization_barrier(jnp.sum(lifted, axis=1, keepdims=True))
    flat_routes = route_rows.reshape(-1)
    one_hot = (flat_routes[:, None] == jnp.arange(EXPERTS, dtype=jnp.int32)[None, :]).astype(jnp.int32)
    slot_rank = lax.optimization_barrier(jnp.sum((jnp.cumsum(one_hot, axis=0) - 1) * one_hot, axis=1))
    room_size = N_EP * CAP
    slot_index = (flat_routes * room_size + slot_rank).astype(jnp.int32)
    pair_rows = low_back(jnp.repeat(moe_in, TOP, axis=0))
    buffer = jnp.zeros((EXPERTS * room_size, D), pair_rows.dtype).at[slot_index].set(pair_rows)
    buffer = buffer.reshape(EXPERTS, room_size, D)
    gate_pre = low_back(jnp.einsum('esd,edf->esf', buffer, w_gate, precision=PRECISE))
    up_pre = low_back(jnp.einsum('esd,edf->esf', buffer, w_up, precision=PRECISE))
    activated = low(gate_pre * jax.nn.sigmoid(gate_pre) * up_pre)
    produced = low_back(low(jnp.einsum('esf,efd->esd', activated, w_down, precision=PRECISE)))
    picked = produced.reshape(EXPERTS * room_size, D)[slot_index].reshape(length, TOP, D)
    return hidden + jnp.einsum('tk,tkd->td', gate_weights, picked, precision=PRECISE)

def reference(tokens, segments, routes, w_query, w_key, w_value, w_out, w_router, gain_attn, gain_query, gain_key, gain_ffn, w_gate, w_up, w_down, out_grad):
    weights = tuple((weight_array.astype(jnp.float32) for weight_array in (w_query, w_key, w_value, w_out, w_router, gain_attn, gain_query, gain_key, gain_ffn, w_gate, w_up, w_down)))
    inputs = tokens.astype(jnp.float32).reshape(SEQS, LENGTH, D)
    cotangents = out_grad.astype(jnp.float32).reshape(SEQS, LENGTH, D)
    route_seqs = routes.reshape(SEQS, LENGTH, TOP)

    def one_sequence(totals, sequence_item):
        sequence, segment_row, route_rows, cotangent = sequence_item
        result, pullback = jax.vjp(lambda values, params: layer(values, segment_row, route_rows, params), sequence, weights)
        grad_values, grad_params = pullback(cotangent)
        totals = jax.tree.map(lambda former_sum, addend: former_sum + addend, totals, grad_params)
        return (totals, (result.astype(jnp.bfloat16), grad_values))
    start_totals = jax.tree.map(jnp.zeros_like, weights)
    totals, (outputs, input_grads) = lax.scan(one_sequence, start_totals, (inputs, segments, route_seqs, cotangents))
    return (outputs.reshape(TOKENS, D), input_grads.reshape(TOKENS, D), totals[0], totals[1], totals[2], totals[3], totals[4], totals[5], totals[6], totals[7], totals[8], totals[9], totals[10], totals[11])
```

```python
import functools

import jax
import jax.numpy as jnp
import numpy as np
from jax import lax
from jax.experimental import pallas as pl
from jax.experimental.pallas import tpu as pltpu
from jax.sharding import PartitionSpec as P

BF = jnp.bfloat16
F32 = jnp.float32
MESH = pl.DeviceIdType.MESH
ANY = pl.BlockSpec(memory_space=pl.ANY)
VM = pl.BlockSpec(memory_space=pltpu.VMEM)
DMA = pltpu.SemaphoreType.DMA
MIB = 1 << 20

HEADS = 16
KV_HEADS = 8
HEAD_DIM = 64
TOP = 8
WINDOW = 1024
EPSILON = 1e-06
ROPE_BASE = 10000.0
MASKED = -1e30
EP = 8
REP = 16
TOK = 256
LENGTH = 2048
D = 1024
KV = 512
FF = 512
EXPERTS = 32
LOCAL = 4
CAP = 96
NT = (((1,), (1,)), ((), ()))
TN = (((0,), (0,)), ((), ()))
HIGH = lax.Precision.HIGHEST


def dot(a, b):
    return jnp.dot(a, b, preferred_element_type=F32)


def dot_nt(a, b, precision=None):
    return lax.dot_general(a, b, NT, preferred_element_type=F32, precision=precision)


def dot_tn(a, b):
    return lax.dot_general(a, b, TN, preferred_element_type=F32)


def iota(shape, dim):
    return lax.broadcasted_iota(jnp.int32, shape, dim)


def ep_device(x, c):
    return {"ep": x * 2 + c}


def greet(devices):
    barrier = pltpu.get_barrier_semaphore()
    for device in devices:
        pl.semaphore_signal(barrier, inc=1, device_id=device, device_id_type=MESH)
    pl.semaphore_wait(barrier, len(devices))


def remote(src, dst, sems, i, device):
    return pltpu.make_async_remote_copy(
        src_ref=src,
        dst_ref=dst,
        send_sem=sems[0].at[i],
        recv_sem=sems[1].at[i],
        device_id=device,
        device_id_type=MESH,
    )


def place():
    e = lax.axis_index("ep")
    return e, e // 2, e % 2


def ep_others(e):
    return [(e + k) % EP for k in range(1, EP)]


def rep_others(r):
    return [(r + k) % REP for k in range(1, REP)]


class RingGather:
    SEMS = 10

    def __init__(self, x_ref, o_ref, sems, lsem):
        e, x, c = place()
        self.n = n = x_ref.shape[0]
        h = n // 2
        self.o_ref = o_ref
        right, left = ep_device((x + 1) % 4, c), ep_device((x + 3) % 4, c)
        peer = ep_device(x, 1 - c)
        b_left, b_right, b_opp = (((x + 3) % 4) * 2 + c, ((x + 1) % 4) * 2 + c, ((x + 2) % 4) * 2 + c)

        def rows(b, off=0, size=n):
            return o_ref.at[pl.ds(pl.multiple_of(b * n + off, 16), size)]

        low, high = x_ref.at[pl.ds(0, h)], x_ref.at[pl.ds(h, h)]
        self.first = [
            remote(low, rows(e, 0, h), sems, 0, right),
            remote(high, rows(e, h, h), sems, 2, left),
            remote(high, rows(e, h, h), sems, 1, right),
            remote(low, rows(e, 0, h), sems, 3, left),
            remote(x_ref, rows(e), sems, 4, peer),
        ]
        self.fwd_right = remote(rows(b_left, 0, h), rows(b_left, 0, h), sems, 5, right)
        self.fwd_left = remote(rows(b_right, h, h), rows(b_right, h, h), sems, 6, left)
        self.to_peer = [
            remote(rows(b_left), rows(b_left), sems, 7, peer),
            remote(rows(b_right), rows(b_right), sems, 8, peer),
            remote(rows(b_opp), rows(b_opp), sems, 9, peer),
        ]
        self.own = pltpu.make_async_copy(x_ref, rows(e), lsem)

    def start(self):
        for copy in self.first:
            copy.start()
        self.own.start()

    def forward(self):
        self.first[0].wait_recv()
        self.fwd_right.start()
        self.first[1].wait_recv()
        self.fwd_left.start()
        self.first[2].wait_recv()
        self.to_peer[0].start()
        self.first[3].wait_recv()
        self.to_peer[1].start()

    def finish(self):
        self.fwd_right.wait_recv()
        self.fwd_left.wait_recv()
        self.to_peer[2].start()
        self.first[4].wait_recv()
        for copy in self.to_peer:
            copy.wait_recv()
        self.own.wait()
        for copy in self.first + [self.fwd_right, self.fwd_left] + self.to_peer:
            copy.wait_send()


class RingReduce:
    SEMS = 10
    STEP = 64

    def __init__(self, p_ref, n, pc, snd, rcv, hop, sems, lsems):
        e, x, c = place()
        self.n, self.h = n, n // 2
        h = n // 2
        self.pc, self.snd, self.rcv, self.hop = pc, snd, rcv, hop
        right, left = ep_device((x + 1) % 4, c), ep_device((x + 3) % 4, c)
        peer = ep_device(x, 1 - c)

        def rows(b):
            return p_ref.at[pl.ds(pl.multiple_of(b * n, 16), n)]

        chips = [(x + 2) % 4, (x + 1) % 4, (x + 3) % 4, x]
        self.swap = [remote(rows(b * 2 + 1 - c), pc.at[k], sems, k, peer) for k, b in enumerate(chips)]
        self.load = [
            pltpu.make_async_copy(rows(b * 2 + c), snd.at[k], lsems.at[k]) for k, b in enumerate(chips)
        ]
        low, high = pl.ds(0, h), pl.ds(h, h)
        self.opp = [
            remote(snd.at[0, low], hop.at[low], sems, 4, right),
            remote(snd.at[0, high], hop.at[high], sems, 5, left),
        ]
        self.near = [
            remote(snd.at[1, high], rcv.at[0, high], sems, 6, right),
            remote(snd.at[2, low], rcv.at[1, low], sems, 7, left),
        ]
        self.far = [
            remote(snd.at[1, low], rcv.at[0, low], sems, 8, right),
            remote(snd.at[2, high], rcv.at[1, high], sems, 9, left),
        ]

    def rows_loop(self, low, count, body):
        step = self.STEP

        def loop(i, carry):
            body(pl.ds(pl.multiple_of(low + i * step, 16), step))
            return carry

        lax.fori_loop(0, count // step, loop, 0)

    def merge(self, k):
        def body(s):
            self.snd[k, s] = (self.snd[k, s].astype(F32) + self.pc[k, s].astype(F32)).astype(BF)

        self.load[k].wait()
        self.swap[k].wait_recv()
        self.rows_loop(0, self.n, body)

    def merge_hop(self, k, low):
        def body(s):
            self.snd[k, s] = (self.snd[k, s].astype(F32) + self.hop[s].astype(F32)).astype(BF)

        self.rows_loop(low, self.h, body)

    def start(self):
        for copy in self.swap + self.load:
            copy.start()

    def middle(self):
        self.merge(0)
        for copy in self.opp:
            copy.start()
        self.merge(1)
        self.near[0].start()
        self.merge(2)
        self.near[1].start()
        self.merge(3)
        self.opp[0].wait_recv()
        self.merge_hop(1, 0)
        self.far[0].start()
        self.opp[1].wait_recv()
        self.merge_hop(2, self.h)
        self.far[1].start()

    def finish(self, out_ref):
        for copy in self.near + self.far:
            copy.wait_recv()

        def body(s):
            out_ref[s] = self.snd[3, s].astype(F32) + (
                self.rcv[0, s].astype(F32) + self.rcv[1, s].astype(F32)
            )

        self.rows_loop(0, self.n, body)
        for copy in self.swap + self.opp + self.near + self.far:
            copy.wait_send()


def reduce_scratch(n, w):
    return [
        pltpu.VMEM((4, n, w), BF),
        pltpu.VMEM((4, n, w), BF),
        pltpu.VMEM((2, n, w), BF),
        pltpu.VMEM((n, w), BF),
        DMA((RingReduce.SEMS,)),
        DMA((RingReduce.SEMS,)),
        DMA((4,)),
    ]


def comm_call(kernel, name, collective_id, out_shape, in_specs, out_specs, scratch, limit=48):
    return pl.pallas_call(
        kernel,
        out_shape=out_shape,
        in_specs=in_specs,
        out_specs=out_specs,
        scratch_shapes=scratch,
        compiler_params=pltpu.CompilerParams(
            collective_id=collective_id, has_side_effects=True, vmem_limit_bytes=limit * MIB
        ),
        name=name,
    )


def shape(dims, dtype=F32):
    return jax.ShapeDtypeStruct(dims, dtype)


def gather_first_kernel(
    tok, cot, wsl, wo, x_all, g_all, wg, wog, lsem, s_tok, r_tok, s_cot, r_cot, s_w, r_w, s_o, r_o
):
    r = lax.axis_index("rep")
    e, x, c = place()
    others = ep_others(e)
    copies = rep_others(r)
    greet([{"ep": d} for d in others] + [{"rep": d} for d in copies])
    stage = []
    for k, d in enumerate(others):
        stage.append(remote(wsl.at[d], wg.at[r, e], (s_w, r_w), k, {"ep": d}))
        stage.append(remote(wo, wog.at[r, e], (s_o, r_o), k, {"ep": d}))
    own = [
        pltpu.make_async_copy(wsl.at[e], wg.at[r, e], lsem.at[2]),
        pltpu.make_async_copy(wo, wog.at[r, e], lsem.at[3]),
    ]
    for copy in stage + own:
        copy.start()
    tokens = RingGather(tok, x_all, (s_tok, r_tok), lsem.at[0])
    grads = RingGather(cot, g_all, (s_cot, r_cot), lsem.at[1])
    tokens.start()
    for copy in own:
        copy.wait()
    for copy in stage:
        copy.wait_recv()
    spread = []
    for k, d in enumerate(copies):
        spread.append(remote(wg.at[r], wg.at[r], (s_w, r_w), 7 + k, {"rep": d}))
        spread.append(remote(wog.at[r], wog.at[r], (s_o, r_o), 7 + k, {"rep": d}))
    for copy in spread:
        copy.start()
    tokens.forward()
    grads.start()
    tokens.finish()
    grads.forward()
    grads.finish()
    for copy in spread:
        copy.wait_recv()
    for copy in stage + spread:
        copy.wait_send()


def gather_first(tok, cot, wsl, wo):
    return comm_call(
        gather_first_kernel,
        "gather_first",
        1,
        [
            shape((EP * TOK, D), BF),
            shape((EP * TOK, D), BF),
            shape((REP, EP, 32, 128), BF),
            shape((REP, EP, 64, 128), BF),
        ],
        [ANY] * 4,
        [ANY] * 4,
        [DMA((4,)), DMA((10,)), DMA((10,)), DMA((10,)), DMA((10,)), DMA((22,)), DMA((22,)), DMA((22,)), DMA((22,))],
    )(tok, cot, wsl, wo)


def sum_stats_kernel(x_ref, o_ref, held, ssem, rsem):
    e, _, _ = place()
    others = ep_others(e)
    greet([{"ep": d} for d in others])
    copies = [remote(x_ref, held.at[e], (ssem, rsem), k, {"ep": d}) for k, d in enumerate(others)]
    for copy in copies:
        copy.start()
    held[e] = x_ref[...]
    for copy in copies:
        copy.wait_recv()
    total = held[0]
    for k in range(1, EP):
        total = total + held[k]
    o_ref[...] = total
    for copy in copies:
        copy.wait_send()


def sum_stats(x, name, collective_id):
    return comm_call(
        sum_stats_kernel,
        name,
        collective_id,
        shape(x.shape),
        [VM],
        VM,
        [pltpu.VMEM((EP,) + x.shape, F32), DMA((7,)), DMA((7,))],
    )(x)


def swap_kernel(to_rows, x_ref, o_ref, lsem, ssem, rsem):
    e, _, _ = place()
    others = ep_others(e)
    greet([{"ep": d} for d in others])

    def rows(ref, b):
        return ref.at[pl.ds(pl.multiple_of(b * TOK, 16), TOK)]

    def cols(ref, b):
        return ref.at[:, pl.ds(pl.multiple_of(b * 128, 128), 128)]

    src, dst = (rows, cols) if to_rows else (cols, rows)
    own = pltpu.make_async_copy(src(x_ref, e), dst(o_ref, e), lsem)
    copies = [
        remote(src(x_ref, d), dst(o_ref, e), (ssem, rsem), k, {"ep": d}) for k, d in enumerate(others)
    ]
    for copy in copies:
        copy.start()
    own.start()
    own.wait()
    for copy in copies:
        copy.wait_recv()
    for copy in copies:
        copy.wait_send()


def swap_heads(x, to_rows, name, collective_id):
    out = (TOK, D) if to_rows else (LENGTH, 128)
    return comm_call(
        functools.partial(swap_kernel, to_rows),
        name,
        collective_id,
        shape(out, BF),
        [ANY],
        ANY,
        [DMA(()), DMA((7,)), DMA((7,))],
    )(x)


def gather_rows_kernel(x_ref, t_ref, o_ref, ot_ref, lsem, s_x, r_x, s_t, r_t):
    e, _, _ = place()
    others = ep_others(e)
    greet([{"ep": d} for d in others])
    small = [remote(t_ref, ot_ref.at[e], (s_t, r_t), k, {"ep": d}) for k, d in enumerate(others)]
    own = pltpu.make_async_copy(t_ref, ot_ref.at[e], lsem.at[1])
    for copy in small:
        copy.start()
    own.start()
    ring = RingGather(x_ref, o_ref, (s_x, r_x), lsem.at[0])
    ring.start()
    ring.forward()
    ring.finish()
    own.wait()
    for copy in small:
        copy.wait_recv()
    for copy in small:
        copy.wait_send()


def gather_rows(x, t):
    return comm_call(
        gather_rows_kernel,
        "gather_rows",
        4,
        [shape((EP * TOK, D), BF), shape((EP,) + t.shape)],
        [ANY, ANY],
        [ANY, ANY],
        [DMA((2,)), DMA((10,)), DMA((10,)), DMA((7,)), DMA((7,))],
    )(x, t)


def reduce_rows_kernel(p_ref, t_ref, o_ref, ot_ref, pc, snd, rcv, hop, ssem, rsem, lsems, lsem, s_t, r_t):
    e, _, _ = place()
    others = ep_others(e)
    greet([{"ep": d} for d in others])
    ring = RingReduce(p_ref, TOK, pc, snd, rcv, hop, (ssem, rsem), lsems)
    ring.start()
    small = [remote(t_ref.at[d], ot_ref.at[e], (s_t, r_t), k, {"ep": d}) for k, d in enumerate(others)]
    own = pltpu.make_async_copy(t_ref.at[e], ot_ref.at[e], lsem)
    for copy in small:
        copy.start()
    own.start()
    ring.middle()
    ring.finish(o_ref)
    own.wait()
    for copy in small:
        copy.wait_recv()
    for copy in small:
        copy.wait_send()


def reduce_rows(p, t):
    w = p.shape[1]
    return comm_call(
        reduce_rows_kernel,
        "reduce_rows",
        5,
        [shape((TOK, w)), shape(t.shape)],
        [ANY, ANY],
        [VM, ANY],
        reduce_scratch(TOK, w) + [DMA(()), DMA((7,)), DMA((7,))],
    )(p, t)


WB = D + 128


def reduce_last_kernel(
    gn, wb, dw, o_gn, o_wb, o_dw,
    pc1, snd1, rcv1, hop1, ss1, rs1, ls1,
    pc2, snd2, rcv2, hop2, ss2, rs2, ls2,
    wsum, wheld, dheld, dsum, lsem, s_w, r_w, s_d, r_d, s_e, r_e,
):
    r = lax.axis_index("rep")
    e, _, _ = place()
    others = ep_others(e)
    copies = rep_others(r)
    greet([{"ep": d} for d in others] + [{"rep": d} for d in copies])
    ring_w = RingReduce(wb, 128, pc2, snd2, rcv2, hop2, (ss2, rs2), ls2)
    ring_g = RingReduce(gn, TOK, pc1, snd1, rcv1, hop1, (ss1, rs1), ls1)
    ring_w.start()
    ring_g.start()

    def part(ref, b, n):
        return ref.at[pl.ds(pl.multiple_of(b * n, 8), n)]

    spread_d = [remote(part(dw, d, 64), dheld.at[r], (s_d, r_d), k, {"rep": d}) for k, d in enumerate(copies)]
    own_d = pltpu.make_async_copy(part(dw, r, 64), dheld.at[r], lsem.at[0])
    for copy in spread_d + [own_d]:
        copy.start()
    ring_w.middle()
    ring_g.middle()
    ring_w.finish(wsum)
    spread_w = [remote(part(wsum, d, 8), wheld.at[r], (s_w, r_w), k, {"rep": d}) for k, d in enumerate(copies)]
    own_w = pltpu.make_async_copy(part(wsum, r, 8), wheld.at[r], lsem.at[1])
    for copy in spread_w + [own_w]:
        copy.start()
    own_d.wait()
    for copy in spread_d:
        copy.wait_recv()
    total = dheld[0]
    for k in range(1, REP):
        total = total + dheld[k]
    dsum[...] = total
    spread_e = [remote(part(dsum, d, 8), o_dw.at[e], (s_e, r_e), k, {"ep": d}) for k, d in enumerate(others)]
    own_e = pltpu.make_async_copy(part(dsum, e, 8), o_dw.at[e], lsem.at[2])
    for copy in spread_e + [own_e]:
        copy.start()
    ring_g.finish(o_gn)
    own_w.wait()
    for copy in spread_w:
        copy.wait_recv()
    total = wheld[0]
    for k in range(1, REP):
        total = total + wheld[k]
    o_wb[...] = total
    own_e.wait()
    for copy in spread_e:
        copy.wait_recv()
    for copy in spread_d + spread_w + spread_e:
        copy.wait_send()


def reduce_last(gn, wb, dw):
    return comm_call(
        reduce_last_kernel,
        "reduce_last",
        6,
        [shape((TOK, D)), shape((8, WB)), shape((EP, 8, 256))],
        [ANY] * 3,
        [VM, VM, ANY],
        reduce_scratch(TOK, D)
        + reduce_scratch(128, WB)
        + [
            pltpu.VMEM((128, WB), F32),
            pltpu.VMEM((REP, 8, WB), F32),
            pltpu.VMEM((REP, 64, 256), F32),
            pltpu.VMEM((64, 256), F32),
            DMA((3,)),
            DMA((15,)),
            DMA((15,)),
            DMA((15,)),
            DMA((15,)),
            DMA((7,)),
            DMA((7,)),
        ],
    )(gn, wb, dw)


def column(row):
    return jnp.transpose(jnp.broadcast_to(row, (128, row.shape[1])))


def lane_row(values):
    return dot_nt(jnp.ones((8, 128), F32), values, precision=HIGH)[0:1]


def project_kernel(x_ref, w_ref, gain_ref, o_ref, st_ref):
    i = pl.program_id(0)
    x = x_ref[...].astype(F32)
    r = lax.rsqrt(jnp.mean(x * x, axis=1, keepdims=True) + EPSILON)
    normed = (x * r * gain_ref[...]).astype(BF)
    lin = dot(normed, w_ref[...])
    o_ref[...] = lin
    keys = iota((TOK, 128), 1) < HEAD_DIM
    sq = lin * lin
    st_ref[pl.ds(2 * i, 1)] = lane_row(sq[:, :128])
    st_ref[pl.ds(2 * i + 1, 1)] = lane_row(jnp.where(keys, sq[:, 128:], 0.0))


def project(x_all, w, gain):
    return pl.pallas_call(
        project_kernel,
        grid=(EP,),
        out_shape=[shape((LENGTH, 256)), shape((2 * EP, 256))],
        in_specs=[
            pl.BlockSpec((TOK, D), lambda i: (i, 0)),
            pl.BlockSpec((D, 256), lambda i: (0, 0)),
            pl.BlockSpec((1, D), lambda i: (0, 0)),
        ],
        out_specs=[pl.BlockSpec((TOK, 256), lambda i: (i, 0)), pl.BlockSpec((16, 256), lambda i: (0, 0))],
        compiler_params=pltpu.CompilerParams(vmem_limit_bytes=32 * MIB),
        name="project",
    )(x_all, w, gain)


def turn_tables():
    half = HEAD_DIM // 2
    freq = np.float32(ROPE_BASE) ** (-(np.arange(half, dtype=np.float32) * np.float32(2.0) / np.float32(HEAD_DIM)))
    angles = np.arange(LENGTH, dtype=np.float32)[:, None] * freq.astype(np.float32)[None, :]
    c, s = np.cos(angles), np.sin(angles)
    cosine = np.concatenate([c, c, c, c], axis=1)
    sine = np.concatenate([-s, s, -s, s], axis=1)
    return cosine.astype(np.float32), sine.astype(np.float32)


def turn(u, cosine, sine):
    early = iota(u.shape, 1) % HEAD_DIM < HEAD_DIM // 2
    partner = jnp.where(early, pltpu.roll(u, 96, 1), pltpu.roll(u, 32, 1))
    return u * cosine + partner * sine


def block_rows(b):
    return pl.ds(pl.multiple_of(b * TOK, TOK), TOK)


def key_start(i):
    return jnp.maximum(i - WINDOW // TOK, 0)


def stack_heads(values):
    first = iota(values.shape, 1) < HEAD_DIM
    return jnp.concatenate([jnp.where(first, values, 0.0), jnp.where(first, 0.0, values)], axis=0)


def merge_heads(values):
    first = iota((TOK, 128), 1) < HEAD_DIM
    return jnp.where(first, values[:TOK], values[TOK:])


def attend_kernel(
    lin, st, lo, cos_ref, sin_ref, gain, q_o, k_o, v_o, a_o, lse_o, s_scr, q2_scr, lo_scr, m_scr, l_scr, acc
):
    first = iota((TOK, 128), 1) < HEAD_DIM

    def prepare(b, carry):
        rows = block_rows(b)
        cq = column(lax.rsqrt(st[pl.ds(2 * b, 1)] * (1.0 / D) + EPSILON))
        ck = column(lax.rsqrt(st[pl.ds(2 * b + 1, 1)] * (1.0 / KV) + EPSILON))
        cosine, sine = cos_ref[rows], sin_ref[rows]
        q_o[rows] = turn(lin[rows, :128] * cq * gain[:, :128], cosine, sine).astype(BF)
        kv = lin[rows, 128:]
        kv = jnp.where(first, turn(kv * ck * gain[:, 128:], cosine, sine), kv)
        other = pltpu.roll(kv, HEAD_DIM, 1)
        k_o[rows] = jnp.where(first, kv, other).astype(BF)
        v_o[rows] = jnp.where(first, other, kv).astype(BF)
        return carry

    lax.fori_loop(0, EP, prepare, 0)

    def queries(i, carry):
        rows = block_rows(i)
        q2_scr[...] = stack_heads(q_o[rows].astype(F32) * HEAD_DIM ** (-0.5)).astype(BF)
        lo_col = column(lo[pl.ds(i, 1)])
        lo_scr[...] = jnp.concatenate([lo_col, lo_col], axis=0)
        m_scr[...] = jnp.full((2 * TOK, 128), MASKED, F32)
        l_scr[...] = jnp.zeros((2 * TOK, 128), F32)
        acc[...] = jnp.zeros((2 * TOK, 128), F32)
        j0 = key_start(i)

        def score(j, inner):
            s = dot_nt(q2_scr[...], k_o[block_rows(j)])
            key = (iota((2 * TOK, TOK), 1) + j * TOK).astype(F32)
            query = (iota((2 * TOK, TOK), 0) % TOK + i * TOK).astype(F32)
            s = jnp.where((key >= lo_scr[:, :1]) & (key <= query), s, MASKED)
            s_scr[j - j0] = s
            m_scr[...] = jnp.maximum(m_scr[...], jnp.maximum(s[:, :128], s[:, 128:]))
            return inner

        lax.fori_loop(j0, i + 1, score, 0)
        m = jnp.max(m_scr[...], axis=1, keepdims=True)
        m_scr[...] = jnp.broadcast_to(m, (2 * TOK, 128))

        def weigh(j, inner):
            p = jnp.exp(s_scr[j - j0] - m_scr[:, :1])
            l_scr[...] += p[:, :128] + p[:, 128:]
            acc[...] += dot(p.astype(BF), v_o[block_rows(j)])
            return inner

        lax.fori_loop(j0, i + 1, weigh, 0)
        total = jnp.sum(l_scr[...], axis=1, keepdims=True)
        a_o[rows] = merge_heads(acc[...] / total).astype(BF)
        lse = jnp.broadcast_to(m_scr[:, :1] + jnp.log(total), (2 * TOK, 128))
        lse_o[i] = jnp.transpose(lse)[:8]
        return carry

    lax.fori_loop(0, EP, queries, 0)


def attend(lin, st, lo, cosine, sine, gain):
    return pl.pallas_call(
        attend_kernel,
        out_shape=[shape((LENGTH, 128), BF)] * 4 + [shape((EP, 8, 2 * TOK))],
        in_specs=[VM] * 6,
        out_specs=[VM] * 5,
        scratch_shapes=[
            pltpu.VMEM((5, 2 * TOK, TOK), F32),
            pltpu.VMEM((2 * TOK, 128), BF),
            pltpu.VMEM((2 * TOK, 128), F32),
            pltpu.VMEM((2 * TOK, 128), F32),
            pltpu.VMEM((2 * TOK, 128), F32),
            pltpu.VMEM((2 * TOK, 128), F32),
        ],
        compiler_params=pltpu.CompilerParams(vmem_limit_bytes=48 * MIB),
        name="attend",
    )(lin, st, lo, cosine, sine, gain)


def attend_back_kernel(
    q_i, k_i, v_i, a_i, lse, lo, go, lin, st, cos_ref, sin_ref, gain, u_o, st_o, q2_scr, do2_scr, row_scr, dq, dk, dv
):
    first = iota((TOK, 128), 1) < HEAD_DIM
    dk[...] = jnp.zeros((LENGTH, 128), F32)
    dv[...] = jnp.zeros((LENGTH, 128), F32)

    def queries(i, carry):
        rows = block_rows(i)
        q2_scr[...] = stack_heads(q_i[rows].astype(F32) * HEAD_DIM ** (-0.5)).astype(BF)
        grad = stack_heads(go[rows].astype(F32))
        do2_scr[...] = grad.astype(BF)
        out = a_i[rows].astype(F32)
        row_scr[0:1] = lane_row(grad * jnp.concatenate([out, out], axis=0))
        row_scr[1:2] = lse[i][0:1]
        row_scr[2:3] = jnp.concatenate([lo[pl.ds(i, 1)]] * 2, axis=1)
        dq[...] = jnp.zeros((128, 2 * TOK), F32)

        def keys(j, inner):
            key_rows = block_rows(j)
            kk = k_i[key_rows]
            key = (iota((TOK, 2 * TOK), 0) + j * TOK).astype(F32)
            query = (iota((TOK, 2 * TOK), 1) % TOK + i * TOK).astype(F32)
            allowed = (key >= row_scr[2:3]) & (key <= query)
            s = dot_nt(kk, q2_scr[...])
            p = jnp.where(allowed, jnp.exp(s - row_scr[1:2]), 0.0)
            dp = dot_nt(v_i[key_rows], do2_scr[...])
            ds = (p * (dp - row_scr[0:1])).astype(BF)
            dv[key_rows] += dot(p.astype(BF), do2_scr[...])
            dk[key_rows] += dot(ds, q2_scr[...])
            dq[...] += dot_tn(kk, ds)
            return inner

        lax.fori_loop(key_start(i), i + 1, keys, 0)
        grad_q = merge_heads(jnp.transpose(dq[...])) * HEAD_DIM ** (-0.5)
        grad_q = turn(grad_q.astype(BF).astype(F32), cos_ref[rows], -sin_ref[rows])
        u_o[rows, :128] = grad_q
        cq = column(lax.rsqrt(st[pl.ds(2 * i, 1)] * (1.0 / D) + EPSILON))
        st_o[pl.ds(2 * i, 1)] = lane_row(grad_q * gain[:, :128] * lin[rows, :128] * cq)
        return carry

    lax.fori_loop(0, EP, queries, 0)

    def close(b, carry):
        rows = block_rows(b)
        grad_k, grad_v = dk[rows], dv[rows]
        grad_k = grad_k + pltpu.roll(grad_k, HEAD_DIM, 1)
        grad_v = grad_v + pltpu.roll(grad_v, HEAD_DIM, 1)
        both = jnp.where(first, grad_k, grad_v).astype(BF).astype(F32)
        both = jnp.where(first, turn(both, cos_ref[rows], -sin_ref[rows]), both)
        u_o[rows, 128:] = both
        ck = column(lax.rsqrt(st[pl.ds(2 * b + 1, 1)] * (1.0 / KV) + EPSILON))
        st_o[pl.ds(2 * b + 1, 1)] = lane_row(
            jnp.where(first, both * gain[:, 128:] * lin[rows, 128:] * ck, 0.0)
        )
        return carry

    lax.fori_loop(0, EP, close, 0)


def attend_back(q, k, v, a, lse, lo, go, lin, st, cosine, sine, gain):
    return pl.pallas_call(
        attend_back_kernel,
        out_shape=[shape((LENGTH, 256)), shape((2 * EP, 256))],
        in_specs=[VM] * 12,
        out_specs=[VM] * 2,
        scratch_shapes=[
            pltpu.VMEM((2 * TOK, 128), BF),
            pltpu.VMEM((2 * TOK, 128), BF),
            pltpu.VMEM((8, 2 * TOK), F32),
            pltpu.VMEM((128, 2 * TOK), F32),
            pltpu.VMEM((LENGTH, 128), F32),
            pltpu.VMEM((LENGTH, 128), F32),
        ],
        compiler_params=pltpu.CompilerParams(vmem_limit_bytes=48 * MIB),
        name="attend_back",
    )(q, k, v, a, lse, lo, go, lin, st, cosine, sine, gain)


def project_back_kernel(x_ref, u_ref, lin_ref, st, st2, gain, attn_gain, w_ref, gn_o, dw_o, ga_o, gqk_o, dwt):
    i = pl.program_id(0)
    first = iota((TOK, 128), 1) < HEAD_DIM

    @pl.when(i == 0)
    def _():
        dwt[...] = jnp.zeros_like(dwt)
        ga_o[...] = jnp.zeros_like(ga_o)
        gqk_o[...] = jnp.zeros_like(gqk_o)

    x = x_ref[...].astype(F32)
    r1 = lax.rsqrt(jnp.mean(x * x, axis=1, keepdims=True) + EPSILON)
    n1 = x * r1
    normed = (n1 * attn_gain[...]).astype(BF)
    u = u_ref[...]
    lin = lin_ref[...]
    cq = column(lax.rsqrt(st[pl.ds(2 * i, 1)] * (1.0 / D) + EPSILON))
    ck = column(lax.rsqrt(st[pl.ds(2 * i + 1, 1)] * (1.0 / KV) + EPSILON))
    mq = column(st2[pl.ds(2 * i, 1)] * (1.0 / D))
    mk = column(st2[pl.ds(2 * i + 1, 1)] * (1.0 / KV))
    nq = lin[:, :128] * cq
    nk = lin[:, 128:] * ck
    gq = cq * (u[:, :128] * gain[:, :128] - nq * mq)
    gk = jnp.where(first, ck * (u[:, 128:] * gain[:, 128:] - nk * mk), u[:, 128:])
    glin = jnp.concatenate([gq, gk], axis=1).astype(BF)
    gqk_o[0:1] += jnp.concatenate(
        [
            jnp.sum(u[:, :128] * nq, axis=0, keepdims=True),
            jnp.sum(u[:, 128:] * nk, axis=0, keepdims=True),
        ],
        axis=1,
    )
    gn = dot_nt(glin, w_ref[...])
    ga_o[0:1] += jnp.sum(gn * n1, axis=0, keepdims=True)
    gn_o[...] = gn.astype(BF)
    dwt[...] += dot_tn(glin, normed)

    @pl.when(i == EP - 1)
    def _():
        dw_o[...] = jnp.transpose(dwt[...])


def project_back(x_all, u, lin, st, st2, gain, attn_gain, w):
    def whole(dims):
        return pl.BlockSpec(dims, lambda i: tuple(0 for _ in dims))

    return pl.pallas_call(
        project_back_kernel,
        grid=(EP,),
        out_shape=[shape((LENGTH, D), BF), shape((D, 256)), shape((8, D)), shape((8, 256))],
        in_specs=[
            pl.BlockSpec((TOK, D), lambda i: (i, 0)),
            pl.BlockSpec((TOK, 256), lambda i: (i, 0)),
            pl.BlockSpec((TOK, 256), lambda i: (i, 0)),
            whole((16, 256)),
            whole((16, 256)),
            whole((1, 256)),
            whole((1, D)),
            whole((D, 256)),
        ],
        out_specs=[pl.BlockSpec((TOK, D), lambda i: (i, 0)), whole((D, 256)), whole((8, D)), whole((8, 256))],
        scratch_shapes=[pltpu.VMEM((256, D), F32)],
        compiler_params=pltpu.CompilerParams(vmem_limit_bytes=48 * MIB),
        name="project_back",
    )(x_all, u, lin, st, st2, gain, attn_gain, w)


ROWS = EP * CAP
HALF = 256


def experts_kernel(
    m_ref, g_ref, slot, gate, slots, wg, wu, wd, p_o, gg_o, dwg_o, dwu_o, dwd_o,
    a_s, c_s, gate_s, gg_s, act_s, gp_s, dgu_s, y_s, z_s,
):
    step = pl.program_id(0)

    def hits(row):
        return iota((CAP, TOK), 0) == row

    @pl.when(step < LOCAL)
    def _():
        def pick(s, carry):
            hit = hits(slot[0, pl.ds(s, 1)])
            chosen = jnp.where(hit, 1.0, 0.0).astype(BF)
            rows = pl.ds(pl.multiple_of(s * CAP, 32), CAP)
            a_s[rows] = dot(chosen, m_ref[block_rows(s)]).astype(BF)
            c_s[rows] = dot(chosen, g_ref[block_rows(s)]).astype(BF)
            weight = jnp.sum(jnp.where(hit, gate[0, pl.ds(s, 1)], 0.0), axis=1, keepdims=True)
            gate_s[rows] = jnp.broadcast_to(weight, (CAP, 128))
            return carry

        lax.fori_loop(0, EP, pick, 0)

        def rows_part(k, carry):
            rows = pl.ds(pl.multiple_of(k * HALF, HALF), HALF)
            a = a_s[rows]
            gate_lin = dot(a, wg[0])
            up_lin = dot(a, wu[0])
            sig = jax.nn.sigmoid(gate_lin)
            silu = gate_lin * sig
            act = (silu * up_lin).astype(BF)
            act_s[rows] = act
            weight = gate_s[rows][:, :1]
            produced = dot(act, wd[0]).astype(BF).astype(F32)
            cot = c_s[rows].astype(F32)
            gg = jnp.sum(produced * cot, axis=1, keepdims=True)
            gg_s[rows] = jnp.broadcast_to(gg, (HALF, 128))
            y_s[step, rows] = (weight * produced).astype(BF)
            grad = (weight * cot).astype(BF)
            gp_s[rows] = grad
            grad_act = dot_nt(grad, wd[0])
            dgate = (grad_act * up_lin * sig * (1.0 + gate_lin * (1.0 - sig))).astype(BF)
            dup = (grad_act * silu).astype(BF)
            dgu_s[rows, :FF] = dgate
            dgu_s[rows, FF:] = dup
            z_s[step, rows] = (dot_nt(dgate, wg[0]) + dot_nt(dup, wu[0])).astype(BF)
            return carry

        lax.fori_loop(0, ROWS // HALF, rows_part, 0)

        def gates_back(s, carry):
            hit = hits(slot[0, pl.ds(s, 1)])
            rows = pl.ds(pl.multiple_of(s * CAP, 32), CAP)
            gg_o[0, pl.ds(s, 1)] = jnp.sum(jnp.where(hit, gg_s[rows][:, :1], 0.0), axis=0, keepdims=True)
            return carry

        lax.fori_loop(0, EP, gates_back, 0)
        dwd_o[0] = dot_tn(act_s[...], gp_s[...]).astype(BF)
        dwg_o[0] = dot_tn(a_s[...], dgu_s[:, :FF]).astype(BF)
        dwu_o[0] = dot_tn(a_s[...], dgu_s[:, FF:]).astype(BF)

    @pl.when(step >= LOCAL)
    def _():
        s = step - LOCAL
        rows = pl.ds(pl.multiple_of(s * CAP, 32), CAP)
        chosen = jnp.concatenate(
            [jnp.where(hits(slots[k, pl.ds(s, 1)]), 1.0, 0.0).astype(BF) for k in range(LOCAL)], axis=0
        )
        y = jnp.concatenate([y_s[k, rows] for k in range(LOCAL)], axis=0)
        p_o[:, :D] = dot_tn(chosen, y).astype(BF)
        z = jnp.concatenate([z_s[k, rows] for k in range(LOCAL)], axis=0)
        p_o[:, D:] = dot_tn(chosen, z).astype(BF)


def experts(m_all, g_all, slot, gate, wg, wu, wd):
    def cur(*rest):
        return lambda i: (jnp.minimum(i, LOCAL - 1),) + rest

    once = pl.Buffered(1)
    return pl.pallas_call(
        experts_kernel,
        grid=(LOCAL + EP,),
        out_shape=[
            shape((LENGTH, 2 * D), BF),
            shape((LOCAL, EP, TOK)),
            shape((LOCAL, D, FF), BF),
            shape((LOCAL, D, FF), BF),
            shape((LOCAL, FF, D), BF),
        ],
        in_specs=[
            pl.BlockSpec((LENGTH, D), lambda i: (0, 0), pipeline_mode=once),
            pl.BlockSpec((LENGTH, D), lambda i: (0, 0), pipeline_mode=once),
            pl.BlockSpec((1, EP, TOK), cur(0, 0)),
            pl.BlockSpec((1, EP, TOK), cur(0, 0)),
            pl.BlockSpec((LOCAL, EP, TOK), lambda i: (0, 0, 0)),
            pl.BlockSpec((1, D, FF), cur(0, 0)),
            pl.BlockSpec((1, D, FF), cur(0, 0)),
            pl.BlockSpec((1, FF, D), cur(0, 0)),
        ],
        out_specs=[
            pl.BlockSpec((TOK, 2 * D), lambda i: (jnp.maximum(i - LOCAL, 0), 0)),
            pl.BlockSpec((1, EP, TOK), cur(0, 0)),
            pl.BlockSpec((1, D, FF), cur(0, 0)),
            pl.BlockSpec((1, D, FF), cur(0, 0)),
            pl.BlockSpec((1, FF, D), cur(0, 0)),
        ],
        scratch_shapes=[
            pltpu.VMEM((ROWS, D), BF),
            pltpu.VMEM((ROWS, D), BF),
            pltpu.VMEM((ROWS, 128), F32),
            pltpu.VMEM((ROWS, 128), F32),
            pltpu.VMEM((ROWS, FF), BF),
            pltpu.VMEM((ROWS, D), BF),
            pltpu.VMEM((ROWS, D), BF),
            pltpu.VMEM((LOCAL, ROWS, D), BF),
            pltpu.VMEM((LOCAL, ROWS, D), BF),
        ],
        compiler_params=pltpu.CompilerParams(vmem_limit_bytes=60 * MIB),
        name="experts",
    )(m_all, g_all, slot, gate, slot, wg, wu, wd)


def hidden_kernel(x_ref, a_ref, w_ref, gain, router, hit, hid_o, m_o, gate_o):
    hidden = x_ref[...].astype(F32) + dot(a_ref[...], w_ref[...])
    hid_o[...] = hidden
    r2 = lax.rsqrt(jnp.mean(hidden * hidden, axis=1, keepdims=True) + EPSILON)
    moe_in = (hidden * r2 * gain[...]).astype(BF)
    m_o[...] = moe_in
    logits = dot_nt(router[...], moe_in)
    chosen = hit[...] >= 0
    logits = jnp.where(chosen, logits, MASKED)
    raised = jnp.where(chosen, jnp.exp(logits - jnp.max(logits, axis=0, keepdims=True)), 0.0)
    gate_o[...] = raised / jnp.sum(raised, axis=0, keepdims=True)


def hidden_call(x, a, w, gain, router, hit):
    return pl.pallas_call(
        hidden_kernel,
        out_shape=[shape((TOK, D)), shape((TOK, D), BF), shape((EXPERTS, TOK))],
        in_specs=[VM] * 6,
        out_specs=[VM] * 3,
        compiler_params=pltpu.CompilerParams(vmem_limit_bytes=32 * MIB),
        name="hidden",
    )(x, a, w, gain, router, hit)


def hidden_back_kernel(
    hid, red, gg, gate, m_ref, cot, gain, router, w_ref, a_ref, out_o, gh_o, ga_o, dwo_o, dr_o, gf_o
):
    hidden = hid[...]
    out_o[...] = (hidden + red[:, :D]).astype(BF)
    weights = gate[...]
    grads = gg[...]
    mean = jnp.sum(weights * grads, axis=0, keepdims=True)
    grad_logits = (weights * (grads - mean)).astype(BF)
    dr_o[...] = dot(grad_logits, m_ref[...])
    grad_moe = red[:, D:] + dot_tn(grad_logits, router[...])
    r2 = lax.rsqrt(jnp.mean(hidden * hidden, axis=1, keepdims=True) + EPSILON)
    n = hidden * r2
    gf_o[...] = jnp.sum(grad_moe * n, axis=0, keepdims=True)
    u = grad_moe * gain[...]
    grad_hidden = cot[...].astype(F32) + r2 * (u - n * jnp.mean(u * n, axis=1, keepdims=True))
    gh_o[...] = grad_hidden
    branch = grad_hidden.astype(BF)
    ga_o[...] = dot_nt(branch, w_ref[...]).astype(BF)
    dwo_o[...] = dot_tn(a_ref[...], branch).astype(BF)


def hidden_back(hid, red, gg, gate, m, cot, gain, router, w, a):
    return pl.pallas_call(
        hidden_back_kernel,
        out_shape=[
            shape((TOK, D), BF),
            shape((TOK, D)),
            shape((TOK, D), BF),
            shape((D, D), BF),
            shape((EXPERTS, D)),
            shape((1, D)),
        ],
        in_specs=[VM] * 10,
        out_specs=[VM] * 6,
        compiler_params=pltpu.CompilerParams(vmem_limit_bytes=48 * MIB),
        name="hidden_back",
    )(hid, red, gg, gate, m, cot, gain, router, w, a)


def body(
    tokens,
    segments,
    routes,
    w_query,
    w_key,
    w_value,
    w_out,
    w_router,
    gain_attn,
    gain_query,
    gain_key,
    gain_ffn,
    w_gate,
    w_up,
    w_down,
    out_grad,
):
    r = lax.axis_index("rep")
    e = lax.axis_index("ep")
    cols = jnp.concatenate(
        [w_query.reshape(8, EP, 128), w_key.reshape(8, EP, 64), w_value.reshape(8, EP, 64)], axis=2
    )
    cols = cols.reshape(8, EP, 2, 128).transpose(1, 2, 0, 3).reshape(EP, 16, 128)
    small = jnp.concatenate([gain_attn, gain_query, gain_key, gain_ffn, w_router.reshape(-1)])
    small = jnp.pad(small, (0, 2048 - small.shape[0])).reshape(1, 16, 128)
    wsl = jnp.concatenate([cols, jnp.broadcast_to(small, (EP, 16, 128))], axis=1)
    wo = w_out.reshape(8, 8, 128).transpose(1, 0, 2).reshape(64, 128)

    expert_ids = jnp.arange(EXPERTS, dtype=jnp.int32)
    routed = jnp.sum((routes[:, :, None] == expert_ids[None, None, :]).astype(BF), axis=1)
    before = (jnp.arange(TOK)[:, None] < jnp.arange(TOK)[None, :]).astype(BF)
    rank = lax.dot_general(routed, before, TN, preferred_element_type=F32)
    slot_own = jnp.where(routed.T > 0, rank, -1.0)

    seg = segments[0]
    positions = jnp.arange(LENGTH, dtype=jnp.int32)
    zeros = jnp.sum((seg == 0).astype(jnp.int32))
    ones = jnp.sum((seg <= 1).astype(jnp.int32))
    opening = jnp.where(seg == 0, 0, jnp.where(seg == 1, zeros, ones))
    lo = jnp.maximum(opening, positions - (WINDOW - 1)).astype(F32).reshape(EP, TOK)
    cosine, sine = turn_tables()

    x_all, g_all, wg_all, wo_all = gather_first(tokens, out_grad, wsl, wo)

    w_cols = wg_all[:, :, :16].reshape(128, 2, 8, 128).transpose(0, 2, 1, 3).reshape(D, 256)
    small_all = wg_all[:, :, 16:].reshape(128, 2048)
    attn_gain = small_all[:, :8].reshape(1, D).astype(F32)
    query_gain = small_all[:, 8:16].reshape(1, D).astype(F32)
    key_gain = small_all[:, 16:20].reshape(1, KV).astype(F32)
    ffn_gain = small_all[:, 20:28].reshape(1, D).astype(F32)
    router = small_all[:, 28:284].reshape(D, EXPERTS).T
    whole_out = wo_all.reshape(128, 8, 8, 128).transpose(0, 2, 1, 3).reshape(D, D)
    qk_gain = jnp.concatenate(
        [
            lax.dynamic_slice_in_dim(query_gain, e * 128, 128, 1),
            lax.dynamic_slice_in_dim(key_gain, e * 64, 64, 1),
            jnp.ones((1, 64), F32),
        ],
        axis=1,
    )

    lin, sums = project(x_all, w_cols, attn_gain)
    st = sum_stats(sums, "sum_stats", 2)
    q, k, v, att, lse = attend(lin, st, lo, cosine, sine, qk_gain)
    attended = swap_heads(att, True, "swap_heads", 3)
    hidden, moe_in, gates = hidden_call(tokens, attended, whole_out, ffn_gain, router, slot_own)
    m_all, tables = gather_rows(moe_in, jnp.concatenate([slot_own, gates], axis=0))
    slot = lax.dynamic_slice_in_dim(tables, e * LOCAL, LOCAL, 1).transpose(1, 0, 2).astype(jnp.int32)
    gate = lax.dynamic_slice_in_dim(tables, EXPERTS + e * LOCAL, LOCAL, 1).transpose(1, 0, 2)
    part, gg, dwg, dwu, dwd = experts(m_all, g_all, slot, gate, w_gate, w_up, w_down)
    expert_sums = [
        lax.psum_scatter(value, "rep", scatter_dimension=1, tiled=True).astype(F32) for value in (dwg, dwu, dwd)
    ]
    gg = jnp.pad(gg.transpose(1, 0, 2), ((0, 0), (0, 4), (0, 0)))
    red, gg = reduce_rows(part, gg)
    gg = gg[:, :LOCAL].reshape(EXPERTS, TOK)
    attended_t = attended.reshape(TOK, REP, EP, 8).transpose(0, 2, 1, 3).reshape(TOK, D)
    output, grad_hidden, grad_att, dwo, drouter, dffn = hidden_back(
        hidden, red, gg, gates, moe_in, out_grad, ffn_gain, router, whole_out, attended_t
    )
    go = swap_heads(grad_att, False, "swap_heads_back", 7)
    u, sums2 = attend_back(q, k, v, att, lse, lo, go, lin, st, cosine, sine, qk_gain)
    st2 = sum_stats(sums2, "sum_stats_back", 8)
    gn, dw, dattn, dqk = project_back(x_all, u, lin, st, st2, qk_gain, attn_gain, w_cols)

    dquery = lax.dynamic_update_slice(jnp.zeros((1, D), F32), dqk[0:1, :128], (0, e * 128))
    dkey = lax.dynamic_update_slice(jnp.zeros((1, KV), F32), dqk[0:1, 128:192], (0, e * 64))
    dkey = jnp.pad(dkey.reshape(128, 4), ((0, 0), (0, 4))).reshape(1, D)
    vectors = jnp.concatenate([drouter, dattn[0:1], dquery, dkey, dffn], axis=0)
    vectors = vectors.reshape(36, REP, EP, 8).transpose(2, 1, 3, 0).reshape(D, 36)
    wb = jnp.concatenate([dwo, jnp.pad(vectors, ((0, 0), (0, 128 - 36))).astype(BF)], axis=1)
    gn_sum, wb_sum, dw_sum = reduce_last(gn, wb, dw)

    x = tokens.astype(F32)
    r1 = lax.rsqrt(jnp.mean(x * x, axis=-1, keepdims=True) + EPSILON)
    n1 = x * r1
    z = gn_sum * attn_gain
    input_grad = grad_hidden + r1 * (z - n1 * jnp.mean(z * n1, axis=-1, keepdims=True))
    dw_rows = dw_sum.transpose(1, 0, 2)
    return (
        output,
        input_grad,
        dw_rows[:, :, :128].reshape(8, D),
        dw_rows[:, :, 128:192].reshape(8, KV),
        dw_rows[:, :, 192:].reshape(8, KV),
        wb_sum[:, :D],
        wb_sum[:, D : D + EXPERTS],
        wb_sum[:, D + 32],
        wb_sum[:, D + 33],
        wb_sum[:4, D + 34],
        wb_sum[:, D + 35],
        expert_sums[0],
        expert_sums[1],
        expert_sums[2],
    )


def solution(mesh):
    both = P(("rep", "ep"), None)
    line = P(("rep", "ep"))
    owner = P("ep", None, None)
    kept = P("ep", "rep", None)
    return jax.shard_map(
        body,
        mesh=mesh,
        in_specs=(both, P("rep", None)) + (both,) * 6 + (line,) * 4 + (owner,) * 3 + (both,),
        out_specs=(both,) * 7 + (line,) * 4 + (kept,) * 3,
        check_vma=False,
    )
```

```python
import functools

import jax
import jax.numpy as jnp
import numpy as np
from jax import lax
from jax.experimental import pallas as pl
from jax.experimental.pallas import tpu as pltpu
from jax.sharding import PartitionSpec as P

BF = jnp.bfloat16
F32 = jnp.float32
MESH = pl.DeviceIdType.MESH
ANY = pl.BlockSpec(memory_space=pl.ANY)
VM = pl.BlockSpec(memory_space=pltpu.VMEM)
DMA = pltpu.SemaphoreType.DMA
MIB = 1 << 20

HEADS = 16
KV_HEADS = 8
HEAD_DIM = 64
TOP = 8
WINDOW = 1024
EPSILON = 1e-06
ROPE_BASE = 10000.0
MASKED = -1e30
EP = 8
REP = 16
TOK = 256
LENGTH = 2048
D = 1024
KV = 512
FF = 512
EXPERTS = 32
LOCAL = 4
CAP = 96
NT = (((1,), (1,)), ((), ()))
TN = (((0,), (0,)), ((), ()))
HIGH = lax.Precision.HIGHEST


def dot(a, b):
    return jnp.dot(a, b, preferred_element_type=F32)


def dot_nt(a, b, precision=None):
    return lax.dot_general(a, b, NT, preferred_element_type=F32, precision=precision)


def dot_tn(a, b):
    return lax.dot_general(a, b, TN, preferred_element_type=F32)


def iota(shape, dim):
    return lax.broadcasted_iota(jnp.int32, shape, dim)


def ep_device(x, c):
    return {"ep": x * 2 + c}


def greet(devices):
    barrier = pltpu.get_barrier_semaphore()
    for device in devices:
        pl.semaphore_signal(barrier, inc=1, device_id=device, device_id_type=MESH)
    pl.semaphore_wait(barrier, len(devices))


def remote(src, dst, sems, i, device):
    return pltpu.make_async_remote_copy(
        src_ref=src,
        dst_ref=dst,
        send_sem=sems[0].at[i],
        recv_sem=sems[1].at[i],
        device_id=device,
        device_id_type=MESH,
    )


def place():
    e = lax.axis_index("ep")
    return e, e // 2, e % 2


def ep_others(e):
    return [(e + k) % EP for k in range(1, EP)]


def rep_others(r):
    return [(r + k) % REP for k in range(1, REP)]


class RingGather:
    SEMS = 10

    def __init__(self, x_ref, o_ref, sems, lsem):
        e, x, c = place()
        self.n = n = x_ref.shape[0]
        h = n // 2
        self.o_ref = o_ref
        right, left = ep_device((x + 1) % 4, c), ep_device((x + 3) % 4, c)
        peer = ep_device(x, 1 - c)
        b_left, b_right, b_opp = (((x + 3) % 4) * 2 + c, ((x + 1) % 4) * 2 + c, ((x + 2) % 4) * 2 + c)

        def rows(b, off=0, size=n):
            return o_ref.at[pl.ds(pl.multiple_of(b * n + off, 16), size)]

        low, high = x_ref.at[pl.ds(0, h)], x_ref.at[pl.ds(h, h)]
        self.first = [
            remote(low, rows(e, 0, h), sems, 0, right),
            remote(high, rows(e, h, h), sems, 2, left),
            remote(high, rows(e, h, h), sems, 1, right),
            remote(low, rows(e, 0, h), sems, 3, left),
            remote(x_ref, rows(e), sems, 4, peer),
        ]
        self.fwd_right = remote(rows(b_left, 0, h), rows(b_left, 0, h), sems, 5, right)
        self.fwd_left = remote(rows(b_right, h, h), rows(b_right, h, h), sems, 6, left)
        self.to_peer = [
            remote(rows(b_left), rows(b_left), sems, 7, peer),
            remote(rows(b_right), rows(b_right), sems, 8, peer),
            remote(rows(b_opp), rows(b_opp), sems, 9, peer),
        ]
        self.own = pltpu.make_async_copy(x_ref, rows(e), lsem)

    def start(self):
        for copy in self.first:
            copy.start()
        self.own.start()

    def forward(self):
        self.first[0].wait_recv()
        self.fwd_right.start()
        self.first[1].wait_recv()
        self.fwd_left.start()
        self.first[2].wait_recv()
        self.to_peer[0].start()
        self.first[3].wait_recv()
        self.to_peer[1].start()

    def finish(self):
        self.fwd_right.wait_recv()
        self.fwd_left.wait_recv()
        self.to_peer[2].start()
        self.first[4].wait_recv()
        for copy in self.to_peer:
            copy.wait_recv()
        self.own.wait()
        for copy in self.first + [self.fwd_right, self.fwd_left] + self.to_peer:
            copy.wait_send()


class RingReduce:
    SEMS = 10
    STEP = 64

    def __init__(self, p_ref, n, pc, snd, rcv, hop, sems, lsems):
        e, x, c = place()
        self.n, self.h = n, n // 2
        h = n // 2
        self.pc, self.snd, self.rcv, self.hop = pc, snd, rcv, hop
        right, left = ep_device((x + 1) % 4, c), ep_device((x + 3) % 4, c)
        peer = ep_device(x, 1 - c)

        def rows(b):
            return p_ref.at[pl.ds(pl.multiple_of(b * n, 16), n)]

        chips = [(x + 2) % 4, (x + 1) % 4, (x + 3) % 4, x]
        self.swap = [remote(rows(b * 2 + 1 - c), pc.at[k], sems, k, peer) for k, b in enumerate(chips)]
        self.load = [
            pltpu.make_async_copy(rows(b * 2 + c), snd.at[k], lsems.at[k]) for k, b in enumerate(chips)
        ]
        low, high = pl.ds(0, h), pl.ds(h, h)
        self.opp = [
            remote(snd.at[0, low], hop.at[low], sems, 4, right),
            remote(snd.at[0, high], hop.at[high], sems, 5, left),
        ]
        self.near = [
            remote(snd.at[1, high], rcv.at[0, high], sems, 6, right),
            remote(snd.at[2, low], rcv.at[1, low], sems, 7, left),
        ]
        self.far = [
            remote(snd.at[1, low], rcv.at[0, low], sems, 8, right),
            remote(snd.at[2, high], rcv.at[1, high], sems, 9, left),
        ]

    def rows_loop(self, low, count, body):
        step = self.STEP

        def loop(i, carry):
            body(pl.ds(pl.multiple_of(low + i * step, 16), step))
            return carry

        lax.fori_loop(0, count // step, loop, 0)

    def merge(self, k):
        def body(s):
            self.snd[k, s] = (self.snd[k, s].astype(F32) + self.pc[k, s].astype(F32)).astype(BF)

        self.load[k].wait()
        self.swap[k].wait_recv()
        self.rows_loop(0, self.n, body)

    def merge_hop(self, k, low):
        def body(s):
            self.snd[k, s] = (self.snd[k, s].astype(F32) + self.hop[s].astype(F32)).astype(BF)

        self.rows_loop(low, self.h, body)

    def start(self):
        for copy in self.swap + self.load:
            copy.start()

    def middle(self):
        self.merge(0)
        for copy in self.opp:
            copy.start()
        self.merge(1)
        self.near[0].start()
        self.merge(2)
        self.near[1].start()
        self.merge(3)
        self.opp[0].wait_recv()
        self.merge_hop(1, 0)
        self.far[0].start()
        self.opp[1].wait_recv()
        self.merge_hop(2, self.h)
        self.far[1].start()

    def finish(self, out_ref):
        for copy in self.near + self.far:
            copy.wait_recv()

        def body(s):
            out_ref[s] = self.snd[3, s].astype(F32) + (
                self.rcv[0, s].astype(F32) + self.rcv[1, s].astype(F32)
            )

        self.rows_loop(0, self.n, body)
        for copy in self.swap + self.opp + self.near + self.far:
            copy.wait_send()


def reduce_scratch(n, w):
    return [
        pltpu.VMEM((4, n, w), BF),
        pltpu.VMEM((4, n, w), BF),
        pltpu.VMEM((2, n, w), BF),
        pltpu.VMEM((n, w), BF),
        DMA((RingReduce.SEMS,)),
        DMA((RingReduce.SEMS,)),
        DMA((4,)),
    ]


def comm_call(kernel, name, collective_id, out_shape, in_specs, out_specs, scratch, limit=48):
    return pl.pallas_call(
        kernel,
        out_shape=out_shape,
        in_specs=in_specs,
        out_specs=out_specs,
        scratch_shapes=scratch,
        compiler_params=pltpu.CompilerParams(
            collective_id=collective_id, has_side_effects=True, vmem_limit_bytes=limit * MIB
        ),
        name=name,
    )


def shape(dims, dtype=F32):
    return jax.ShapeDtypeStruct(dims, dtype)


def gather_first_kernel(
    tok, cot, wsl, wo, x_all, g_all, wg, wog, lsem, s_tok, r_tok, s_cot, r_cot, s_w, r_w, s_o, r_o
):
    r = lax.axis_index("rep")
    e, x, c = place()
    others = ep_others(e)
    copies = rep_others(r)
    greet([{"ep": d} for d in others] + [{"rep": d} for d in copies])
    stage = []
    for k, d in enumerate(others):
        stage.append(remote(wsl.at[d], wg.at[r, e], (s_w, r_w), k, {"ep": d}))
        stage.append(remote(wo, wog.at[r, e], (s_o, r_o), k, {"ep": d}))
    own = [
        pltpu.make_async_copy(wsl.at[e], wg.at[r, e], lsem.at[2]),
        pltpu.make_async_copy(wo, wog.at[r, e], lsem.at[3]),
    ]
    for copy in stage + own:
        copy.start()
    tokens = RingGather(tok, x_all, (s_tok, r_tok), lsem.at[0])
    grads = RingGather(cot, g_all, (s_cot, r_cot), lsem.at[1])
    tokens.start()
    for copy in own:
        copy.wait()
    for copy in stage:
        copy.wait_recv()
    spread = []
    for k, d in enumerate(copies):
        spread.append(remote(wg.at[r], wg.at[r], (s_w, r_w), 7 + k, {"rep": d}))
        spread.append(remote(wog.at[r], wog.at[r], (s_o, r_o), 7 + k, {"rep": d}))
    for copy in spread:
        copy.start()
    tokens.forward()
    grads.start()
    tokens.finish()
    grads.forward()
    grads.finish()
    for copy in spread:
        copy.wait_recv()
    for copy in stage + spread:
        copy.wait_send()


def gather_first(tok, cot, wsl, wo):
    return comm_call(
        gather_first_kernel,
        "gather_first",
        1,
        [
            shape((EP * TOK, D), BF),
            shape((EP * TOK, D), BF),
            shape((REP, EP, 32, 128), BF),
            shape((REP, EP, 64, 128), BF),
        ],
        [ANY] * 4,
        [ANY] * 4,
        [DMA((4,)), DMA((10,)), DMA((10,)), DMA((10,)), DMA((10,)), DMA((22,)), DMA((22,)), DMA((22,)), DMA((22,))],
    )(tok, cot, wsl, wo)


def sum_stats_kernel(x_ref, o_ref, held, ssem, rsem):
    e, _, _ = place()
    others = ep_others(e)
    greet([{"ep": d} for d in others])
    copies = [remote(x_ref, held.at[e], (ssem, rsem), k, {"ep": d}) for k, d in enumerate(others)]
    for copy in copies:
        copy.start()
    held[e] = x_ref[...]
    for copy in copies:
        copy.wait_recv()
    total = held[0]
    for k in range(1, EP):
        total = total + held[k]
    o_ref[...] = total
    for copy in copies:
        copy.wait_send()


def sum_stats(x, name, collective_id):
    return comm_call(
        sum_stats_kernel,
        name,
        collective_id,
        shape(x.shape),
        [VM],
        VM,
        [pltpu.VMEM((EP,) + x.shape, F32), DMA((7,)), DMA((7,))],
    )(x)


def swap_kernel(to_rows, x_ref, o_ref, lsem, ssem, rsem):
    e, _, _ = place()
    others = ep_others(e)
    greet([{"ep": d} for d in others])

    def rows(ref, b):
        return ref.at[pl.ds(pl.multiple_of(b * TOK, 16), TOK)]

    def cols(ref, b):
        return ref.at[:, pl.ds(pl.multiple_of(b * 128, 128), 128)]

    src, dst = (rows, cols) if to_rows else (cols, rows)
    own = pltpu.make_async_copy(src(x_ref, e), dst(o_ref, e), lsem)
    copies = [
        remote(src(x_ref, d), dst(o_ref, e), (ssem, rsem), k, {"ep": d}) for k, d in enumerate(others)
    ]
    for copy in copies:
        copy.start()
    own.start()
    own.wait()
    for copy in copies:
        copy.wait_recv()
    for copy in copies:
        copy.wait_send()


def swap_heads(x, to_rows, name, collective_id):
    out = (TOK, D) if to_rows else (LENGTH, 128)
    return comm_call(
        functools.partial(swap_kernel, to_rows),
        name,
        collective_id,
        shape(out, BF),
        [ANY],
        ANY,
        [DMA(()), DMA((7,)), DMA((7,))],
    )(x)


WB = D + 128


def reduce_last_kernel(
    gn, wb, dw, o_gn, o_wb, o_dw,
    pc1, snd1, rcv1, hop1, ss1, rs1, ls1,
    pc2, snd2, rcv2, hop2, ss2, rs2, ls2,
    wsum, wheld, dheld, dsum, lsem, s_w, r_w, s_d, r_d, s_e, r_e,
):
    r = lax.axis_index("rep")
    e, _, _ = place()
    others = ep_others(e)
    copies = rep_others(r)
    greet([{"ep": d} for d in others] + [{"rep": d} for d in copies])
    ring_w = RingReduce(wb, 128, pc2, snd2, rcv2, hop2, (ss2, rs2), ls2)
    ring_g = RingReduce(gn, TOK, pc1, snd1, rcv1, hop1, (ss1, rs1), ls1)
    ring_w.start()
    ring_g.start()

    def part(ref, b, n):
        return ref.at[pl.ds(pl.multiple_of(b * n, 8), n)]

    spread_d = [remote(part(dw, d, 64), dheld.at[r], (s_d, r_d), k, {"rep": d}) for k, d in enumerate(copies)]
    own_d = pltpu.make_async_copy(part(dw, r, 64), dheld.at[r], lsem.at[0])
    for copy in spread_d + [own_d]:
        copy.start()
    ring_w.middle()
    ring_g.middle()
    ring_w.finish(wsum)
    spread_w = [remote(part(wsum, d, 8), wheld.at[r], (s_w, r_w), k, {"rep": d}) for k, d in enumerate(copies)]
    own_w = pltpu.make_async_copy(part(wsum, r, 8), wheld.at[r], lsem.at[1])
    for copy in spread_w + [own_w]:
        copy.start()
    own_d.wait()
    for copy in spread_d:
        copy.wait_recv()
    total = dheld[0]
    for k in range(1, REP):
        total = total + dheld[k]
    dsum[...] = total
    spread_e = [remote(part(dsum, d, 8), o_dw.at[e], (s_e, r_e), k, {"ep": d}) for k, d in enumerate(others)]
    own_e = pltpu.make_async_copy(part(dsum, e, 8), o_dw.at[e], lsem.at[2])
    for copy in spread_e + [own_e]:
        copy.start()
    ring_g.finish(o_gn)
    own_w.wait()
    for copy in spread_w:
        copy.wait_recv()
    total = wheld[0]
    for k in range(1, REP):
        total = total + wheld[k]
    o_wb[...] = total
    own_e.wait()
    for copy in spread_e:
        copy.wait_recv()
    for copy in spread_d + spread_w + spread_e:
        copy.wait_send()


def reduce_last(gn, wb, dw):
    return comm_call(
        reduce_last_kernel,
        "reduce_last",
        6,
        [shape((TOK, D)), shape((8, WB)), shape((EP, 8, 256))],
        [ANY] * 3,
        [VM, VM, ANY],
        reduce_scratch(TOK, D)
        + reduce_scratch(128, WB)
        + [
            pltpu.VMEM((128, WB), F32),
            pltpu.VMEM((REP, 8, WB), F32),
            pltpu.VMEM((REP, 64, 256), F32),
            pltpu.VMEM((64, 256), F32),
            DMA((3,)),
            DMA((15,)),
            DMA((15,)),
            DMA((15,)),
            DMA((15,)),
            DMA((7,)),
            DMA((7,)),
        ],
    )(gn, wb, dw)


def column(row):
    return jnp.transpose(jnp.broadcast_to(row, (128, row.shape[1])))


def lane_row(values):
    return dot_nt(jnp.ones((8, 128), F32), values, precision=HIGH)[0:1]


def project_kernel(x_ref, w_ref, gain_ref, o_ref, st_ref):
    i = pl.program_id(0)
    x = x_ref[...].astype(F32)
    r = lax.rsqrt(jnp.mean(x * x, axis=1, keepdims=True) + EPSILON)
    normed = (x * r * gain_ref[...]).astype(BF)
    lin = dot(normed, w_ref[...])
    o_ref[...] = lin
    keys = iota((TOK, 128), 1) < HEAD_DIM
    sq = lin * lin
    st_ref[pl.ds(2 * i, 1)] = lane_row(sq[:, :128])
    st_ref[pl.ds(2 * i + 1, 1)] = lane_row(jnp.where(keys, sq[:, 128:], 0.0))


def project(x_all, w, gain):
    return pl.pallas_call(
        project_kernel,
        grid=(EP,),
        out_shape=[shape((LENGTH, 256)), shape((2 * EP, 256))],
        in_specs=[
            pl.BlockSpec((TOK, D), lambda i: (i, 0)),
            pl.BlockSpec((D, 256), lambda i: (0, 0)),
            pl.BlockSpec((1, D), lambda i: (0, 0)),
        ],
        out_specs=[pl.BlockSpec((TOK, 256), lambda i: (i, 0)), pl.BlockSpec((16, 256), lambda i: (0, 0))],
        compiler_params=pltpu.CompilerParams(vmem_limit_bytes=32 * MIB),
        name="project",
    )(x_all, w, gain)


def turn_tables():
    half = HEAD_DIM // 2
    freq = np.float32(ROPE_BASE) ** (-(np.arange(half, dtype=np.float32) * np.float32(2.0) / np.float32(HEAD_DIM)))
    angles = np.arange(LENGTH, dtype=np.float32)[:, None] * freq.astype(np.float32)[None, :]
    c, s = np.cos(angles), np.sin(angles)
    cosine = np.concatenate([c, c, c, c], axis=1)
    sine = np.concatenate([-s, s, -s, s], axis=1)
    return cosine.astype(np.float32), sine.astype(np.float32)


def turn(u, cosine, sine):
    early = iota(u.shape, 1) % HEAD_DIM < HEAD_DIM // 2
    partner = jnp.where(early, pltpu.roll(u, 96, 1), pltpu.roll(u, 32, 1))
    return u * cosine + partner * sine


def block_rows(b):
    return pl.ds(pl.multiple_of(b * TOK, TOK), TOK)


def key_start(i):
    return jnp.maximum(i - WINDOW // TOK, 0)


def stack_heads(values):
    first = iota(values.shape, 1) < HEAD_DIM
    return jnp.concatenate([jnp.where(first, values, 0.0), jnp.where(first, 0.0, values)], axis=0)


def merge_heads(values):
    first = iota((TOK, 128), 1) < HEAD_DIM
    return jnp.where(first, values[:TOK], values[TOK:])


def attend_kernel(
    lin, st, lo, cos_ref, sin_ref, gain, q_o, k_o, v_o, a_o, lse_o, s_scr, q2_scr, lo_scr, m_scr, l_scr, acc
):
    first = iota((TOK, 128), 1) < HEAD_DIM

    def prepare(b, carry):
        rows = block_rows(b)
        cq = column(lax.rsqrt(st[pl.ds(2 * b, 1)] * (1.0 / D) + EPSILON))
        ck = column(lax.rsqrt(st[pl.ds(2 * b + 1, 1)] * (1.0 / KV) + EPSILON))
        cosine, sine = cos_ref[rows], sin_ref[rows]
        q_o[rows] = turn(lin[rows, :128] * cq * gain[:, :128], cosine, sine).astype(BF)
        kv = lin[rows, 128:]
        kv = jnp.where(first, turn(kv * ck * gain[:, 128:], cosine, sine), kv)
        other = pltpu.roll(kv, HEAD_DIM, 1)
        k_o[rows] = jnp.where(first, kv, other).astype(BF)
        v_o[rows] = jnp.where(first, other, kv).astype(BF)
        return carry

    lax.fori_loop(0, EP, prepare, 0)

    def queries(i, carry):
        rows = block_rows(i)
        q2_scr[...] = stack_heads(q_o[rows].astype(F32) * HEAD_DIM ** (-0.5)).astype(BF)
        lo_col = column(lo[pl.ds(i, 1)])
        lo_scr[...] = jnp.concatenate([lo_col, lo_col], axis=0)
        m_scr[...] = jnp.full((2 * TOK, 128), MASKED, F32)
        l_scr[...] = jnp.zeros((2 * TOK, 128), F32)
        acc[...] = jnp.zeros((2 * TOK, 128), F32)
        j0 = key_start(i)

        def score(j, inner):
            s = dot_nt(q2_scr[...], k_o[block_rows(j)])
            key = (iota((2 * TOK, TOK), 1) + j * TOK).astype(F32)
            query = (iota((2 * TOK, TOK), 0) % TOK + i * TOK).astype(F32)
            s = jnp.where((key >= lo_scr[:, :1]) & (key <= query), s, MASKED)
            s_scr[j - j0] = s
            m_scr[...] = jnp.maximum(m_scr[...], jnp.maximum(s[:, :128], s[:, 128:]))
            return inner

        lax.fori_loop(j0, i + 1, score, 0)
        m = jnp.max(m_scr[...], axis=1, keepdims=True)
        m_scr[...] = jnp.broadcast_to(m, (2 * TOK, 128))

        def weigh(j, inner):
            p = jnp.exp(s_scr[j - j0] - m_scr[:, :1])
            l_scr[...] += p[:, :128] + p[:, 128:]
            acc[...] += dot(p.astype(BF), v_o[block_rows(j)])
            return inner

        lax.fori_loop(j0, i + 1, weigh, 0)
        total = jnp.sum(l_scr[...], axis=1, keepdims=True)
        a_o[rows] = merge_heads(acc[...] / total).astype(BF)
        lse = jnp.broadcast_to(m_scr[:, :1] + jnp.log(total), (2 * TOK, 128))
        lse_o[i] = jnp.transpose(lse)[:8]
        return carry

    lax.fori_loop(0, EP, queries, 0)


def attend(lin, st, lo, cosine, sine, gain):
    return pl.pallas_call(
        attend_kernel,
        out_shape=[shape((LENGTH, 128), BF)] * 4 + [shape((EP, 8, 2 * TOK))],
        in_specs=[VM] * 6,
        out_specs=[VM] * 5,
        scratch_shapes=[
            pltpu.VMEM((5, 2 * TOK, TOK), F32),
            pltpu.VMEM((2 * TOK, 128), BF),
            pltpu.VMEM((2 * TOK, 128), F32),
            pltpu.VMEM((2 * TOK, 128), F32),
            pltpu.VMEM((2 * TOK, 128), F32),
            pltpu.VMEM((2 * TOK, 128), F32),
        ],
        compiler_params=pltpu.CompilerParams(vmem_limit_bytes=48 * MIB),
        name="attend",
    )(lin, st, lo, cosine, sine, gain)


def attend_back_kernel(
    q_i, k_i, v_i, a_i, lse, lo, go, lin, st, cos_ref, sin_ref, gain, u_o, st_o, q2_scr, do2_scr, row_scr, dq, dk, dv
):
    first = iota((TOK, 128), 1) < HEAD_DIM
    dk[...] = jnp.zeros((LENGTH, 128), F32)
    dv[...] = jnp.zeros((LENGTH, 128), F32)

    def queries(i, carry):
        rows = block_rows(i)
        q2_scr[...] = stack_heads(q_i[rows].astype(F32) * HEAD_DIM ** (-0.5)).astype(BF)
        grad = stack_heads(go[rows].astype(F32))
        do2_scr[...] = grad.astype(BF)
        out = a_i[rows].astype(F32)
        row_scr[0:1] = lane_row(grad * jnp.concatenate([out, out], axis=0))
        row_scr[1:2] = lse[i][0:1]
        row_scr[2:3] = jnp.concatenate([lo[pl.ds(i, 1)]] * 2, axis=1)
        dq[...] = jnp.zeros((128, 2 * TOK), F32)

        def keys(j, inner):
            key_rows = block_rows(j)
            kk = k_i[key_rows]
            key = (iota((TOK, 2 * TOK), 0) + j * TOK).astype(F32)
            query = (iota((TOK, 2 * TOK), 1) % TOK + i * TOK).astype(F32)
            allowed = (key >= row_scr[2:3]) & (key <= query)
            s = dot_nt(kk, q2_scr[...])
            p = jnp.where(allowed, jnp.exp(s - row_scr[1:2]), 0.0)
            dp = dot_nt(v_i[key_rows], do2_scr[...])
            ds = (p * (dp - row_scr[0:1])).astype(BF)
            dv[key_rows] += dot(p.astype(BF), do2_scr[...])
            dk[key_rows] += dot(ds, q2_scr[...])
            dq[...] += dot_tn(kk, ds)
            return inner

        lax.fori_loop(key_start(i), i + 1, keys, 0)
        grad_q = merge_heads(jnp.transpose(dq[...])) * HEAD_DIM ** (-0.5)
        grad_q = turn(grad_q.astype(BF).astype(F32), cos_ref[rows], -sin_ref[rows])
        u_o[rows, :128] = grad_q
        cq = column(lax.rsqrt(st[pl.ds(2 * i, 1)] * (1.0 / D) + EPSILON))
        st_o[pl.ds(2 * i, 1)] = lane_row(grad_q * gain[:, :128] * lin[rows, :128] * cq)
        return carry

    lax.fori_loop(0, EP, queries, 0)

    def close(b, carry):
        rows = block_rows(b)
        grad_k, grad_v = dk[rows], dv[rows]
        grad_k = grad_k + pltpu.roll(grad_k, HEAD_DIM, 1)
        grad_v = grad_v + pltpu.roll(grad_v, HEAD_DIM, 1)
        both = jnp.where(first, grad_k, grad_v).astype(BF).astype(F32)
        both = jnp.where(first, turn(both, cos_ref[rows], -sin_ref[rows]), both)
        u_o[rows, 128:] = both
        ck = column(lax.rsqrt(st[pl.ds(2 * b + 1, 1)] * (1.0 / KV) + EPSILON))
        st_o[pl.ds(2 * b + 1, 1)] = lane_row(
            jnp.where(first, both * gain[:, 128:] * lin[rows, 128:] * ck, 0.0)
        )
        return carry

    lax.fori_loop(0, EP, close, 0)


def attend_back(q, k, v, a, lse, lo, go, lin, st, cosine, sine, gain):
    return pl.pallas_call(
        attend_back_kernel,
        out_shape=[shape((LENGTH, 256)), shape((2 * EP, 256))],
        in_specs=[VM] * 12,
        out_specs=[VM] * 2,
        scratch_shapes=[
            pltpu.VMEM((2 * TOK, 128), BF),
            pltpu.VMEM((2 * TOK, 128), BF),
            pltpu.VMEM((8, 2 * TOK), F32),
            pltpu.VMEM((128, 2 * TOK), F32),
            pltpu.VMEM((LENGTH, 128), F32),
            pltpu.VMEM((LENGTH, 128), F32),
        ],
        compiler_params=pltpu.CompilerParams(vmem_limit_bytes=48 * MIB),
        name="attend_back",
    )(q, k, v, a, lse, lo, go, lin, st, cosine, sine, gain)


def project_back_kernel(x_ref, u_ref, lin_ref, st, st2, gain, attn_gain, w_ref, gn_o, dw_o, ga_o, gqk_o, dwt):
    i = pl.program_id(0)
    first = iota((TOK, 128), 1) < HEAD_DIM

    @pl.when(i == 0)
    def _():
        dwt[...] = jnp.zeros_like(dwt)
        ga_o[...] = jnp.zeros_like(ga_o)
        gqk_o[...] = jnp.zeros_like(gqk_o)

    x = x_ref[...].astype(F32)
    r1 = lax.rsqrt(jnp.mean(x * x, axis=1, keepdims=True) + EPSILON)
    n1 = x * r1
    normed = (n1 * attn_gain[...]).astype(BF)
    u = u_ref[...]
    lin = lin_ref[...]
    cq = column(lax.rsqrt(st[pl.ds(2 * i, 1)] * (1.0 / D) + EPSILON))
    ck = column(lax.rsqrt(st[pl.ds(2 * i + 1, 1)] * (1.0 / KV) + EPSILON))
    mq = column(st2[pl.ds(2 * i, 1)] * (1.0 / D))
    mk = column(st2[pl.ds(2 * i + 1, 1)] * (1.0 / KV))
    nq = lin[:, :128] * cq
    nk = lin[:, 128:] * ck
    gq = cq * (u[:, :128] * gain[:, :128] - nq * mq)
    gk = jnp.where(first, ck * (u[:, 128:] * gain[:, 128:] - nk * mk), u[:, 128:])
    glin = jnp.concatenate([gq, gk], axis=1).astype(BF)
    gqk_o[0:1] += jnp.concatenate(
        [
            jnp.sum(u[:, :128] * nq, axis=0, keepdims=True),
            jnp.sum(u[:, 128:] * nk, axis=0, keepdims=True),
        ],
        axis=1,
    )
    gn = dot_nt(glin, w_ref[...])
    ga_o[0:1] += jnp.sum(gn * n1, axis=0, keepdims=True)
    gn_o[...] = gn.astype(BF)
    dwt[...] += dot_tn(glin, normed)

    @pl.when(i == EP - 1)
    def _():
        dw_o[...] = jnp.transpose(dwt[...])


def project_back(x_all, u, lin, st, st2, gain, attn_gain, w):
    def whole(dims):
        return pl.BlockSpec(dims, lambda i: tuple(0 for _ in dims))

    return pl.pallas_call(
        project_back_kernel,
        grid=(EP,),
        out_shape=[shape((LENGTH, D), BF), shape((D, 256)), shape((8, D)), shape((8, 256))],
        in_specs=[
            pl.BlockSpec((TOK, D), lambda i: (i, 0)),
            pl.BlockSpec((TOK, 256), lambda i: (i, 0)),
            pl.BlockSpec((TOK, 256), lambda i: (i, 0)),
            whole((16, 256)),
            whole((16, 256)),
            whole((1, 256)),
            whole((1, D)),
            whole((D, 256)),
        ],
        out_specs=[pl.BlockSpec((TOK, D), lambda i: (i, 0)), whole((D, 256)), whole((8, D)), whole((8, 256))],
        scratch_shapes=[pltpu.VMEM((256, D), F32)],
        compiler_params=pltpu.CompilerParams(vmem_limit_bytes=48 * MIB),
        name="project_back",
    )(x_all, u, lin, st, st2, gain, attn_gain, w)


class ChipReduce:
    SEMS = 10
    STEP = 64

    def __init__(self, n, swo, snd, pc, rcv, hop, sems):
        e, x, c = place()
        self.n, self.h = n, n // 2
        h = n // 2
        self.snd, self.pc, self.rcv, self.hop = snd, pc, rcv, hop
        right, left = ep_device((x + 1) % 4, c), ep_device((x + 3) % 4, c)
        peer = ep_device(x, 1 - c)
        self.swap = lambda k: remote(swo.at[k], pc.at[k], sems, k, peer)
        low, high = pl.ds(0, h), pl.ds(h, h)
        self.opp = [
            remote(snd.at[0, low], hop.at[low], sems, 4, right),
            remote(snd.at[0, high], hop.at[high], sems, 5, left),
        ]
        self.near = [
            remote(snd.at[2, high], rcv.at[0, high], sems, 6, right),
            remote(snd.at[1, low], rcv.at[1, low], sems, 7, left),
        ]
        self.far = [
            remote(snd.at[2, low], rcv.at[0, low], sems, 8, right),
            remote(snd.at[1, high], rcv.at[1, high], sems, 9, left),
        ]

    def rows_loop(self, low, count, body):
        step = self.STEP

        def loop(i, carry):
            body(pl.ds(pl.multiple_of(low + i * step, 16), step))
            return carry

        lax.fori_loop(0, count // step, loop, 0)

    def merge(self, k):
        def body(s):
            self.snd[k, s] = (self.snd[k, s].astype(F32) + self.pc[k, s].astype(F32)).astype(BF)

        self.swap(k).wait_recv()
        self.rows_loop(0, self.n, body)

    def merge_hop(self, k, low):
        def body(s):
            self.snd[k, s] = (self.snd[k, s].astype(F32) + self.hop[s].astype(F32)).astype(BF)

        self.rows_loop(low, self.h, body)

    def send_opp(self):
        self.merge(0)
        for copy in self.opp:
            copy.start()

    def send_near(self):
        self.merge(2)
        self.near[0].start()
        self.merge(1)
        self.near[1].start()

    def send_far(self):
        self.opp[0].wait_recv()
        self.merge_hop(2, 0)
        self.far[0].start()
        self.opp[1].wait_recv()
        self.merge_hop(1, self.h)
        self.far[1].start()

    def finish(self, out_ref):
        for copy in self.near + self.far:
            copy.wait_recv()

        def body(s):
            out_ref[s] = self.snd[3, s].astype(F32) + (
                self.rcv[0, s].astype(F32) + self.rcv[1, s].astype(F32)
            )

        self.rows_loop(0, self.n, body)
        for copy in [self.swap(k) for k in range(4)] + self.opp + self.near + self.far:
            copy.wait_send()


ROWS = EP * CAP
HALF = 256
BLOCK = 96


def experts_kernel(
    m_in, t_in, g_in, wg_in, wu_in, wd_in, out_o, gm_o, gg_o, eg_o,
    m_ref, tab, g_ref, wg, wu, wd, a_s, c_s, gl_s, up_s, act_s, dgu_s, y_s, gate_s, gg_s, ggt, eg,
    swo, snd, pc1, rcv1, hop1, pc2, rcv2, hop2,
    s_m, r_m, s_t, r_t, s_1, r_1, s_2, r_2, s_g, r_g, lsem, esem,
):
    e, x, c = place()
    others = ep_others(e)
    greet([{"ep": d} for d in others])
    ring = RingGather(m_in, m_ref, (s_m, r_m), lsem.at[0])
    ring.start()
    tables = [remote(t_in, tab.at[e], (s_t, r_t), k, {"ep": d}) for k, d in enumerate(others)]
    for copy in tables:
        copy.start()
    loads = [
        pltpu.make_async_copy(t_in, tab.at[e], lsem.at[1]),
        pltpu.make_async_copy(wg_in, wg, lsem.at[2]),
        pltpu.make_async_copy(wu_in, wu, lsem.at[3]),
        pltpu.make_async_copy(wd_in, wd, lsem.at[4]),
        pltpu.make_async_copy(g_in, g_ref, lsem.at[5]),
    ]
    for copy in loads:
        copy.start()
    red1 = ChipReduce(TOK, swo, snd, pc1, rcv1, hop1, (s_1, r_1))
    red2 = ChipReduce(TOK, swo, snd, pc2, rcv2, hop2, (s_2, r_2))

    def hits(s, k):
        return iota((CAP, TOK), 0).astype(F32) == tab[s, pl.ds(e * LOCAL + k, 1)]

    def slot_rows(s):
        return pl.ds(pl.multiple_of(s * CAP, 32), CAP)

    def gate_column(s, k, hit):
        row = tab[s, pl.ds(EXPERTS + e * LOCAL + k, 1)]
        return jnp.sum(jnp.where(hit, row, 0.0), axis=1, keepdims=True)

    def one_hot(hit):
        return jnp.where(hit, 1.0, 0.0).astype(BF)

    def combine(s):
        chosen = jnp.concatenate([one_hot(hits(s, k)) for k in range(LOCAL)], axis=0)
        rows = slot_rows(s)
        return dot_tn(chosen, jnp.concatenate([y_s[k, rows] for k in range(LOCAL)], axis=0)).astype(BF)

    def forward(k, carry):
        @pl.when(k == 0)
        def _():
            ring.first[0].wait_recv()
            ring.fwd_right.start()
            ring.first[1].wait_recv()
            ring.fwd_left.start()
            ring.first[4].wait_recv()
            ring.own.wait()
            for copy in tables:
                copy.wait_recv()
            for copy in loads[:4]:
                copy.wait()

        @pl.when(k == 1)
        def _():
            ring.first[3].wait_recv()
            ring.to_peer[1].start()
            ring.first[2].wait_recv()
            ring.to_peer[0].start()
            ring.to_peer[1].wait_recv()

        @pl.when(k == 2)
        def _():
            ring.fwd_right.wait_recv()
            ring.fwd_left.wait_recv()
            ring.to_peer[2].start()
            ring.to_peer[0].wait_recv()

        @pl.when(k == 3)
        def _():
            ring.to_peer[2].wait_recv()

        q = (x + k + k // 2 - 2 * (k // 3)) % 4
        rows = pl.ds(pl.multiple_of(q * 2 * CAP, 64), 2 * CAP)

        def expert(n, inner):
            for core in range(2):
                s = q * 2 + core
                hit = hits(s, n)
                a_s[core * CAP : (core + 1) * CAP] = dot(one_hot(hit), m_ref[block_rows(s)]).astype(BF)
                gate_s[core * CAP : (core + 1) * CAP] = jnp.broadcast_to(gate_column(s, n, hit), (CAP, 128))
            a = a_s[: 2 * CAP]
            gate_lin = dot(a, wg[n])
            up_lin = dot(a, wu[n])
            gl_s[n, rows] = gate_lin.astype(BF)
            up_s[n, rows] = up_lin.astype(BF)
            act = (gate_lin * jax.nn.sigmoid(gate_lin) * up_lin).astype(BF)
            produced = dot(act, wd[n]).astype(BF).astype(F32)
            y_s[n, rows] = (gate_s[: 2 * CAP, :1] * produced).astype(BF)
            return inner

        lax.fori_loop(0, LOCAL, expert, 0)
        slot = 3 - k
        swo[slot] = combine(q * 2 + 1 - c)
        red1.swap(slot).start()
        snd[slot] = combine(q * 2 + c)
        return carry

    lax.fori_loop(0, 4, forward, 0)
    red1.send_opp()
    red1.send_near()
    loads[4].wait()

    def backward(n, carry):
        def pick(s, inner):
            hit = hits(s, n)
            chosen = one_hot(hit)
            rows = slot_rows(s)
            a_s[rows] = dot(chosen, m_ref[block_rows(s)]).astype(BF)
            c_s[rows] = dot(chosen, g_ref[block_rows(s)]).astype(BF)
            gate_s[rows] = jnp.broadcast_to(gate_column(s, n, hit), (CAP, 128))
            return inner

        lax.fori_loop(0, EP, pick, 0)

        def rows_part(k, inner):
            rows = pl.ds(pl.multiple_of(k * HALF, HALF), HALF)
            cot = c_s[rows]
            weight = gate_s[rows][:, :1]
            back = dot_nt(cot, wd[n])
            c_s[rows] = (weight * cot.astype(F32)).astype(BF)
            gate_lin, up_lin = gl_s[n, rows].astype(F32), up_s[n, rows].astype(F32)
            sig = jax.nn.sigmoid(gate_lin)
            silu = gate_lin * sig
            act = silu * up_lin
            act_s[rows] = act.astype(BF)
            gg_s[rows] = jnp.broadcast_to(jnp.sum(act * back, axis=1, keepdims=True), (HALF, 128))
            back = back * weight
            dgate = (back * up_lin * sig * (1.0 + gate_lin * (1.0 - sig))).astype(BF)
            dup = (back * silu).astype(BF)
            dgu_s[rows, :FF] = dgate
            dgu_s[rows, FF:] = dup
            y_s[n, rows] = (dot_nt(dgate, wg[n]) + dot_nt(dup, wu[n])).astype(BF)
            return inner

        lax.fori_loop(0, ROWS // HALF, rows_part, 0)

        def gates_back(s, inner):
            column_ = gg_s[slot_rows(s)][:, :1]
            ggt[s, pl.ds(n, 1)] = jnp.sum(jnp.where(hits(s, n), column_, 0.0), axis=0, keepdims=True)
            return inner

        lax.fori_loop(0, EP, gates_back, 0)

        @pl.when(n == 0)
        def _():
            red1.merge(3)
            red1.send_far()

        @pl.when(n == 2)
        def _():
            red1.finish(out_o)

        @pl.when(n > 0)
        def _():
            pltpu.make_async_copy(eg, eg_o.at[n - 1], esem).wait()

        eg[:, :64, :FF] = dot_tn(a_s[...], dgu_s[:, :FF]).astype(BF).reshape(REP, 64, FF)
        eg[:, :64, FF:] = dot_tn(a_s[...], dgu_s[:, FF:]).astype(BF).reshape(REP, 64, FF)
        eg[:, 64:] = dot_tn(act_s[...], c_s[...]).astype(BF).reshape(REP, 32, D)
        pltpu.make_async_copy(eg, eg_o.at[n], esem).start()
        return carry

    lax.fori_loop(0, LOCAL, backward, 0)
    gates = [remote(ggt.at[d], gg_o.at[e], (s_g, r_g), k, {"ep": d}) for k, d in enumerate(others)]
    own = pltpu.make_async_copy(ggt.at[e], gg_o.at[e], lsem.at[1])
    for copy in gates + [own]:
        copy.start()
    for slot, q in enumerate([(x + 2) % 4, (x + 3) % 4, (x + 1) % 4, x]):
        swo[slot] = combine(q * 2 + 1 - c)
        red2.swap(slot).start()
        snd[slot] = combine(q * 2 + c)
        if slot == 0:
            red2.send_opp()
    red2.send_near()
    red2.merge(3)
    red2.send_far()
    red2.finish(gm_o)
    own.wait()
    pltpu.make_async_copy(eg, eg_o.at[LOCAL - 1], esem).wait()
    for copy in gates:
        copy.wait_recv()
    for copy in ring.first + [ring.fwd_right, ring.fwd_left] + ring.to_peer + tables + gates:
        copy.wait_send()


def experts(m, t, g_all, wg, wu, wd):
    return comm_call(
        experts_kernel,
        "experts",
        4,
        [
            shape((TOK, D)),
            shape((TOK, D)),
            shape((EP, 8, TOK)),
            shape((LOCAL, REP, BLOCK, D), BF),
        ],
        [ANY] * 6,
        [VM, VM, ANY, ANY],
        [
            pltpu.VMEM((LENGTH, D), BF),
            pltpu.VMEM((EP, 2 * EXPERTS, TOK), F32),
            pltpu.VMEM((LENGTH, D), BF),
            pltpu.VMEM((LOCAL, D, FF), BF),
            pltpu.VMEM((LOCAL, D, FF), BF),
            pltpu.VMEM((LOCAL, FF, D), BF),
            pltpu.VMEM((ROWS, D), BF),
            pltpu.VMEM((ROWS, D), BF),
            pltpu.VMEM((LOCAL, ROWS, FF), BF),
            pltpu.VMEM((LOCAL, ROWS, FF), BF),
            pltpu.VMEM((ROWS, FF), BF),
            pltpu.VMEM((ROWS, D), BF),
            pltpu.VMEM((LOCAL, ROWS, D), BF),
            pltpu.VMEM((ROWS, 128), F32),
            pltpu.VMEM((ROWS, 128), F32),
            pltpu.VMEM((EP, 8, TOK), F32),
            pltpu.VMEM((REP, BLOCK, D), BF),
            pltpu.VMEM((4, TOK, D), BF),
            pltpu.VMEM((4, TOK, D), BF),
        ]
        + [pltpu.VMEM((4, TOK, D), BF), pltpu.VMEM((2, TOK, D), BF), pltpu.VMEM((TOK, D), BF)] * 2
        + [DMA((10,))] * 2
        + [DMA((7,))] * 2
        + [DMA((10,))] * 4
        + [DMA((7,))] * 2
        + [DMA((6,)), DMA(())],
        limit=63,
    )(m, t, g_all, wg, wu, wd)


def hidden_kernel(x_ref, a_ref, w_ref, gain, router, hit, hid_o, m_o, gate_o):
    hidden = x_ref[...].astype(F32) + dot(a_ref[...], w_ref[...])
    hid_o[...] = hidden
    r2 = lax.rsqrt(jnp.mean(hidden * hidden, axis=1, keepdims=True) + EPSILON)
    moe_in = (hidden * r2 * gain[...]).astype(BF)
    m_o[...] = moe_in
    logits = dot_nt(router[...], moe_in)
    chosen = hit[...] >= 0
    logits = jnp.where(chosen, logits, MASKED)
    raised = jnp.where(chosen, jnp.exp(logits - jnp.max(logits, axis=0, keepdims=True)), 0.0)
    gate_o[...] = raised / jnp.sum(raised, axis=0, keepdims=True)


def hidden_call(x, a, w, gain, router, hit):
    return pl.pallas_call(
        hidden_kernel,
        out_shape=[shape((TOK, D)), shape((TOK, D), BF), shape((EXPERTS, TOK))],
        in_specs=[VM] * 6,
        out_specs=[VM] * 3,
        compiler_params=pltpu.CompilerParams(vmem_limit_bytes=32 * MIB),
        name="hidden",
    )(x, a, w, gain, router, hit)


def hidden_back_kernel(
    hid, mixed, gmoe, gg, gate, m_ref, cot, gain, router, w_ref, a_ref, out_o, gh_o, ga_o, dwo_o, dr_o, gf_o
):
    hidden = hid[...]
    out_o[...] = (hidden + mixed[...]).astype(BF)
    weights = gate[...]
    grads = gg[...]
    mean = jnp.sum(weights * grads, axis=0, keepdims=True)
    grad_logits = (weights * (grads - mean)).astype(BF)
    dr_o[...] = dot(grad_logits, m_ref[...])
    grad_moe = gmoe[...] + dot_tn(grad_logits, router[...])
    r2 = lax.rsqrt(jnp.mean(hidden * hidden, axis=1, keepdims=True) + EPSILON)
    n = hidden * r2
    gf_o[...] = jnp.sum(grad_moe * n, axis=0, keepdims=True)
    u = grad_moe * gain[...]
    grad_hidden = cot[...].astype(F32) + r2 * (u - n * jnp.mean(u * n, axis=1, keepdims=True))
    gh_o[...] = grad_hidden
    branch = grad_hidden.astype(BF)
    ga_o[...] = dot_nt(branch, w_ref[...]).astype(BF)
    dwo_o[...] = dot_tn(a_ref[...], branch).astype(BF)


def hidden_back(hid, mixed, grad_moe, gg, gate, m, cot, gain, router, w, a):
    return pl.pallas_call(
        hidden_back_kernel,
        out_shape=[
            shape((TOK, D), BF),
            shape((TOK, D)),
            shape((TOK, D), BF),
            shape((D, D), BF),
            shape((EXPERTS, D)),
            shape((1, D)),
        ],
        in_specs=[VM] * 11,
        out_specs=[VM] * 6,
        compiler_params=pltpu.CompilerParams(vmem_limit_bytes=48 * MIB),
        name="hidden_back",
    )(hid, mixed, grad_moe, gg, gate, m, cot, gain, router, w, a)


def body(
    tokens,
    segments,
    routes,
    w_query,
    w_key,
    w_value,
    w_out,
    w_router,
    gain_attn,
    gain_query,
    gain_key,
    gain_ffn,
    w_gate,
    w_up,
    w_down,
    out_grad,
):
    r = lax.axis_index("rep")
    e = lax.axis_index("ep")
    cols = jnp.concatenate(
        [w_query.reshape(8, EP, 128), w_key.reshape(8, EP, 64), w_value.reshape(8, EP, 64)], axis=2
    )
    cols = cols.reshape(8, EP, 2, 128).transpose(1, 2, 0, 3).reshape(EP, 16, 128)
    small = jnp.concatenate([gain_attn, gain_query, gain_key, gain_ffn, w_router.reshape(-1)])
    small = jnp.pad(small, (0, 2048 - small.shape[0])).reshape(1, 16, 128)
    wsl = jnp.concatenate([cols, jnp.broadcast_to(small, (EP, 16, 128))], axis=1)
    wo = w_out.reshape(8, 8, 128).transpose(1, 0, 2).reshape(64, 128)

    expert_ids = jnp.arange(EXPERTS, dtype=jnp.int32)
    routed = jnp.sum((routes[:, :, None] == expert_ids[None, None, :]).astype(BF), axis=1)
    before = (jnp.arange(TOK)[:, None] < jnp.arange(TOK)[None, :]).astype(BF)
    rank = lax.dot_general(routed, before, TN, preferred_element_type=F32)
    slot_own = jnp.where(routed.T > 0, rank, -1.0)

    seg = segments[0]
    positions = jnp.arange(LENGTH, dtype=jnp.int32)
    zeros = jnp.sum((seg == 0).astype(jnp.int32))
    ones = jnp.sum((seg <= 1).astype(jnp.int32))
    opening = jnp.where(seg == 0, 0, jnp.where(seg == 1, zeros, ones))
    lo = jnp.maximum(opening, positions - (WINDOW - 1)).astype(F32).reshape(EP, TOK)
    cosine, sine = turn_tables()

    x_all, g_all, wg_all, wo_all = gather_first(tokens, out_grad, wsl, wo)

    w_cols = wg_all[:, :, :16].reshape(128, 2, 8, 128).transpose(0, 2, 1, 3).reshape(D, 256)
    small_all = wg_all[:, :, 16:].reshape(128, 2048)
    attn_gain = small_all[:, :8].reshape(1, D).astype(F32)
    query_gain = small_all[:, 8:16].reshape(1, D).astype(F32)
    key_gain = small_all[:, 16:20].reshape(1, KV).astype(F32)
    ffn_gain = small_all[:, 20:28].reshape(1, D).astype(F32)
    router = small_all[:, 28:284].reshape(D, EXPERTS).T
    whole_out = wo_all.reshape(128, 8, 8, 128).transpose(0, 2, 1, 3).reshape(D, D)
    qk_gain = jnp.concatenate(
        [
            lax.dynamic_slice_in_dim(query_gain, e * 128, 128, 1),
            lax.dynamic_slice_in_dim(key_gain, e * 64, 64, 1),
            jnp.ones((1, 64), F32),
        ],
        axis=1,
    )

    lin, sums = project(x_all, w_cols, attn_gain)
    st = sum_stats(sums, "sum_stats", 2)
    q, k, v, att, lse = attend(lin, st, lo, cosine, sine, qk_gain)
    attended = swap_heads(att, True, "swap_heads", 3)
    hidden, moe_in, gates = hidden_call(tokens, attended, whole_out, ffn_gain, router, slot_own)
    tables = jnp.concatenate([slot_own, gates], axis=0)
    mixed, grad_moe, gg, grads = experts(moe_in, tables, g_all, w_gate, w_up, w_down)
    grads = grads.reshape(LOCAL, REP * BLOCK, D)
    expert_sums = lax.psum_scatter(grads, "rep", scatter_dimension=1, tiled=True).astype(F32)
    gg = gg[:, :LOCAL].reshape(EXPERTS, TOK)
    attended_t = attended.reshape(TOK, REP, EP, 8).transpose(0, 2, 1, 3).reshape(TOK, D)
    output, grad_hidden, grad_att, dwo, drouter, dffn = hidden_back(
        hidden, mixed, grad_moe, gg, gates, moe_in, out_grad, ffn_gain, router, whole_out, attended_t
    )
    go = swap_heads(grad_att, False, "swap_heads_back", 7)
    u, sums2 = attend_back(q, k, v, att, lse, lo, go, lin, st, cosine, sine, qk_gain)
    st2 = sum_stats(sums2, "sum_stats_back", 8)
    gn, dw, dattn, dqk = project_back(x_all, u, lin, st, st2, qk_gain, attn_gain, w_cols)

    dquery = lax.dynamic_update_slice(jnp.zeros((1, D), F32), dqk[0:1, :128], (0, e * 128))
    dkey = lax.dynamic_update_slice(jnp.zeros((1, KV), F32), dqk[0:1, 128:192], (0, e * 64))
    dkey = jnp.pad(dkey.reshape(128, 4), ((0, 0), (0, 4))).reshape(1, D)
    vectors = jnp.concatenate([drouter, dattn[0:1], dquery, dkey, dffn], axis=0)
    vectors = vectors.reshape(36, REP, EP, 8).transpose(2, 1, 3, 0).reshape(D, 36)
    wb = jnp.concatenate([dwo, jnp.pad(vectors, ((0, 0), (0, 128 - 36))).astype(BF)], axis=1)
    gn_sum, wb_sum, dw_sum = reduce_last(gn, wb, dw)

    x = tokens.astype(F32)
    r1 = lax.rsqrt(jnp.mean(x * x, axis=-1, keepdims=True) + EPSILON)
    n1 = x * r1
    z = gn_sum * attn_gain
    input_grad = grad_hidden + r1 * (z - n1 * jnp.mean(z * n1, axis=-1, keepdims=True))
    dw_rows = dw_sum.transpose(1, 0, 2)
    return (
        output,
        input_grad,
        dw_rows[:, :, :128].reshape(8, D),
        dw_rows[:, :, 128:192].reshape(8, KV),
        dw_rows[:, :, 192:].reshape(8, KV),
        wb_sum[:, :D],
        wb_sum[:, D : D + EXPERTS],
        wb_sum[:, D + 32],
        wb_sum[:, D + 33],
        wb_sum[:4, D + 34],
        wb_sum[:, D + 35],
        expert_sums[:, :64, :FF],
        expert_sums[:, :64, FF:],
        expert_sums[:, 64:],
    )


def solution(mesh):
    both = P(("rep", "ep"), None)
    line = P(("rep", "ep"))
    owner = P("ep", None, None)
    kept = P("ep", "rep", None)
    return jax.shard_map(
        body,
        mesh=mesh,
        in_specs=(both, P("rep", None)) + (both,) * 6 + (line,) * 4 + (owner,) * 3 + (both,),
        out_specs=(both,) * 7 + (line,) * 4 + (kept,) * 3,
        check_vma=False,
    )
```

```python
import functools

import jax
import jax.numpy as jnp
import numpy as np
from jax import lax
from jax.experimental import pallas as pl
from jax.experimental.pallas import tpu as pltpu
from jax.sharding import PartitionSpec as P

BF = jnp.bfloat16
F32 = jnp.float32
MESH = pl.DeviceIdType.MESH
ANY = pl.BlockSpec(memory_space=pl.ANY)
VM = pl.BlockSpec(memory_space=pltpu.VMEM)
DMA = pltpu.SemaphoreType.DMA
MIB = 1 << 20

HEADS = 16
KV_HEADS = 8
HEAD_DIM = 64
TOP = 8
WINDOW = 1024
EPSILON = 1e-06
ROPE_BASE = 10000.0
MASKED = -1e30
EP = 8
REP = 16
TOK = 256
LENGTH = 2048
D = 1024
KV = 512
FF = 512
EXPERTS = 32
LOCAL = 4
CAP = 96
NT = (((1,), (1,)), ((), ()))
TN = (((0,), (0,)), ((), ()))
HIGH = lax.Precision.HIGHEST


def dot(a, b):
    return jnp.dot(a, b, preferred_element_type=F32)


def dot_nt(a, b, precision=None):
    return lax.dot_general(a, b, NT, preferred_element_type=F32, precision=precision)


def dot_tn(a, b):
    return lax.dot_general(a, b, TN, preferred_element_type=F32)


def iota(shape, dim):
    return lax.broadcasted_iota(jnp.int32, shape, dim)


def ep_device(x, c):
    return {"ep": x * 2 + c}


def greet(devices):
    barrier = pltpu.get_barrier_semaphore()
    for device in devices:
        pl.semaphore_signal(barrier, inc=1, device_id=device, device_id_type=MESH)
    pl.semaphore_wait(barrier, len(devices))


def remote(src, dst, sems, i, device):
    return pltpu.make_async_remote_copy(
        src_ref=src,
        dst_ref=dst,
        send_sem=sems[0].at[i],
        recv_sem=sems[1].at[i],
        device_id=device,
        device_id_type=MESH,
    )


def place():
    e = lax.axis_index("ep")
    return e, e // 2, e % 2


def ep_others(e):
    return [(e + k) % EP for k in range(1, EP)]


def rep_others(r):
    return [(r + k) % REP for k in range(1, REP)]


class RingGather:
    SEMS = 10

    def __init__(self, x_ref, o_ref, sems, lsem):
        e, x, c = place()
        self.n = n = x_ref.shape[0]
        h = n // 2
        self.o_ref = o_ref
        right, left = ep_device((x + 1) % 4, c), ep_device((x + 3) % 4, c)
        peer = ep_device(x, 1 - c)
        b_left, b_right, b_opp = (((x + 3) % 4) * 2 + c, ((x + 1) % 4) * 2 + c, ((x + 2) % 4) * 2 + c)

        def rows(b, off=0, size=n):
            return o_ref.at[pl.ds(pl.multiple_of(b * n + off, 16), size)]

        low, high = x_ref.at[pl.ds(0, h)], x_ref.at[pl.ds(h, h)]
        self.first = [
            remote(low, rows(e, 0, h), sems, 0, right),
            remote(high, rows(e, h, h), sems, 2, left),
            remote(high, rows(e, h, h), sems, 1, right),
            remote(low, rows(e, 0, h), sems, 3, left),
            remote(x_ref, rows(e), sems, 4, peer),
        ]
        self.fwd_right = remote(rows(b_left, 0, h), rows(b_left, 0, h), sems, 5, right)
        self.fwd_left = remote(rows(b_right, h, h), rows(b_right, h, h), sems, 6, left)
        self.to_peer = [
            remote(rows(b_left), rows(b_left), sems, 7, peer),
            remote(rows(b_right), rows(b_right), sems, 8, peer),
            remote(rows(b_opp), rows(b_opp), sems, 9, peer),
        ]
        self.own = pltpu.make_async_copy(x_ref, rows(e), lsem)

    def start(self):
        for copy in self.first:
            copy.start()
        self.own.start()

    def forward(self):
        self.first[0].wait_recv()
        self.fwd_right.start()
        self.first[1].wait_recv()
        self.fwd_left.start()
        self.first[2].wait_recv()
        self.to_peer[0].start()
        self.first[3].wait_recv()
        self.to_peer[1].start()

    def finish(self):
        self.fwd_right.wait_recv()
        self.fwd_left.wait_recv()
        self.to_peer[2].start()
        self.first[4].wait_recv()
        for copy in self.to_peer:
            copy.wait_recv()
        self.own.wait()
        for copy in self.first + [self.fwd_right, self.fwd_left] + self.to_peer:
            copy.wait_send()


class RingReduce:
    SEMS = 10
    STEP = 64

    def __init__(self, p_ref, n, pc, snd, rcv, hop, sems, lsems):
        e, x, c = place()
        self.n, self.h = n, n // 2
        h = n // 2
        self.pc, self.snd, self.rcv, self.hop = pc, snd, rcv, hop
        right, left = ep_device((x + 1) % 4, c), ep_device((x + 3) % 4, c)
        peer = ep_device(x, 1 - c)

        def rows(b):
            return p_ref.at[pl.ds(pl.multiple_of(b * n, 16), n)]

        chips = [(x + 2) % 4, (x + 1) % 4, (x + 3) % 4, x]
        self.swap = [remote(rows(b * 2 + 1 - c), pc.at[k], sems, k, peer) for k, b in enumerate(chips)]
        self.load = [
            pltpu.make_async_copy(rows(b * 2 + c), snd.at[k], lsems.at[k]) for k, b in enumerate(chips)
        ]
        low, high = pl.ds(0, h), pl.ds(h, h)
        self.opp = [
            remote(snd.at[0, low], hop.at[low], sems, 4, right),
            remote(snd.at[0, high], hop.at[high], sems, 5, left),
        ]
        self.near = [
            remote(snd.at[1, high], rcv.at[0, high], sems, 6, right),
            remote(snd.at[2, low], rcv.at[1, low], sems, 7, left),
        ]
        self.far = [
            remote(snd.at[1, low], rcv.at[0, low], sems, 8, right),
            remote(snd.at[2, high], rcv.at[1, high], sems, 9, left),
        ]

    def rows_loop(self, low, count, body):
        step = self.STEP

        def loop(i, carry):
            body(pl.ds(pl.multiple_of(low + i * step, 16), step))
            return carry

        lax.fori_loop(0, count // step, loop, 0)

    def merge(self, k):
        def body(s):
            self.snd[k, s] = (self.snd[k, s].astype(F32) + self.pc[k, s].astype(F32)).astype(BF)

        self.load[k].wait()
        self.swap[k].wait_recv()
        self.rows_loop(0, self.n, body)

    def merge_hop(self, k, low):
        def body(s):
            self.snd[k, s] = (self.snd[k, s].astype(F32) + self.hop[s].astype(F32)).astype(BF)

        self.rows_loop(low, self.h, body)

    def start(self):
        for copy in self.swap + self.load:
            copy.start()

    def middle(self):
        self.merge(0)
        for copy in self.opp:
            copy.start()
        self.merge(1)
        self.near[0].start()
        self.merge(2)
        self.near[1].start()
        self.merge(3)
        self.opp[0].wait_recv()
        self.merge_hop(1, 0)
        self.far[0].start()
        self.opp[1].wait_recv()
        self.merge_hop(2, self.h)
        self.far[1].start()

    def finish(self, out_ref):
        for copy in self.near + self.far:
            copy.wait_recv()

        def body(s):
            out_ref[s] = self.snd[3, s].astype(F32) + (
                self.rcv[0, s].astype(F32) + self.rcv[1, s].astype(F32)
            )

        self.rows_loop(0, self.n, body)
        for copy in self.swap + self.opp + self.near + self.far:
            copy.wait_send()


def reduce_scratch(n, w):
    return [
        pltpu.VMEM((4, n, w), BF),
        pltpu.VMEM((4, n, w), BF),
        pltpu.VMEM((2, n, w), BF),
        pltpu.VMEM((n, w), BF),
        DMA((RingReduce.SEMS,)),
        DMA((RingReduce.SEMS,)),
        DMA((4,)),
    ]


def comm_call(kernel, name, collective_id, out_shape, in_specs, out_specs, scratch, limit=48):
    return pl.pallas_call(
        kernel,
        out_shape=out_shape,
        in_specs=in_specs,
        out_specs=out_specs,
        scratch_shapes=scratch,
        compiler_params=pltpu.CompilerParams(
            collective_id=collective_id, has_side_effects=True, vmem_limit_bytes=limit * MIB
        ),
        name=name,
    )


def shape(dims, dtype=F32):
    return jax.ShapeDtypeStruct(dims, dtype)


def sum_stats_kernel(x_ref, o_ref, held, ssem, rsem):
    e, _, _ = place()
    others = ep_others(e)
    greet([{"ep": d} for d in others])
    copies = [remote(x_ref, held.at[e], (ssem, rsem), k, {"ep": d}) for k, d in enumerate(others)]
    for copy in copies:
        copy.start()
    held[e] = x_ref[...]
    for copy in copies:
        copy.wait_recv()
    total = held[0]
    for k in range(1, EP):
        total = total + held[k]
    o_ref[...] = total
    for copy in copies:
        copy.wait_send()


def sum_stats(x, name, collective_id):
    return comm_call(
        sum_stats_kernel,
        name,
        collective_id,
        shape(x.shape),
        [VM],
        VM,
        [pltpu.VMEM((EP,) + x.shape, F32), DMA((7,)), DMA((7,))],
    )(x)


def swap_kernel(to_rows, x_ref, o_ref, lsem, ssem, rsem):
    e, _, _ = place()
    others = ep_others(e)
    greet([{"ep": d} for d in others])

    def rows(ref, b):
        return ref.at[pl.ds(pl.multiple_of(b * TOK, 16), TOK)]

    def cols(ref, b):
        return ref.at[:, pl.ds(pl.multiple_of(b * 128, 128), 128)]

    src, dst = (rows, cols) if to_rows else (cols, rows)
    own = pltpu.make_async_copy(src(x_ref, e), dst(o_ref, e), lsem)
    copies = [
        remote(src(x_ref, d), dst(o_ref, e), (ssem, rsem), k, {"ep": d}) for k, d in enumerate(others)
    ]
    for copy in copies:
        copy.start()
    own.start()
    own.wait()
    for copy in copies:
        copy.wait_recv()
    for copy in copies:
        copy.wait_send()


def swap_heads(x, to_rows, name, collective_id):
    out = (TOK, D) if to_rows else (LENGTH, 128)
    return comm_call(
        functools.partial(swap_kernel, to_rows),
        name,
        collective_id,
        shape(out, BF),
        [ANY],
        ANY,
        [DMA(()), DMA((7,)), DMA((7,))],
    )(x)


WB = D + 128


def reduce_last_kernel(
    gn, wb, dw, o_gn, o_wb, o_dw,
    pc1, snd1, rcv1, hop1, ss1, rs1, ls1,
    pc2, snd2, rcv2, hop2, ss2, rs2, ls2,
    wsum, wheld, dheld, dsum, lsem, s_w, r_w, s_d, r_d, s_e, r_e,
):
    r = lax.axis_index("rep")
    e, _, _ = place()
    others = ep_others(e)
    copies = rep_others(r)
    greet([{"ep": d} for d in others] + [{"rep": d} for d in copies])
    ring_w = RingReduce(wb, 128, pc2, snd2, rcv2, hop2, (ss2, rs2), ls2)
    ring_g = RingReduce(gn, TOK, pc1, snd1, rcv1, hop1, (ss1, rs1), ls1)
    ring_w.start()
    ring_g.start()

    def part(ref, b, n):
        return ref.at[pl.ds(pl.multiple_of(b * n, 8), n)]

    spread_d = [remote(part(dw, d, 64), dheld.at[r], (s_d, r_d), k, {"rep": d}) for k, d in enumerate(copies)]
    own_d = pltpu.make_async_copy(part(dw, r, 64), dheld.at[r], lsem.at[0])
    for copy in spread_d + [own_d]:
        copy.start()
    ring_w.middle()
    ring_g.middle()
    ring_w.finish(wsum)
    spread_w = [remote(part(wsum, d, 8), wheld.at[r], (s_w, r_w), k, {"rep": d}) for k, d in enumerate(copies)]
    own_w = pltpu.make_async_copy(part(wsum, r, 8), wheld.at[r], lsem.at[1])
    for copy in spread_w + [own_w]:
        copy.start()
    own_d.wait()
    for copy in spread_d:
        copy.wait_recv()
    total = dheld[0]
    for k in range(1, REP):
        total = total + dheld[k]
    dsum[...] = total
    spread_e = [remote(part(dsum, d, 8), o_dw.at[e], (s_e, r_e), k, {"ep": d}) for k, d in enumerate(others)]
    own_e = pltpu.make_async_copy(part(dsum, e, 8), o_dw.at[e], lsem.at[2])
    for copy in spread_e + [own_e]:
        copy.start()
    ring_g.finish(o_gn)
    own_w.wait()
    for copy in spread_w:
        copy.wait_recv()
    total = wheld[0]
    for k in range(1, REP):
        total = total + wheld[k]
    o_wb[...] = total
    own_e.wait()
    for copy in spread_e:
        copy.wait_recv()
    for copy in spread_d + spread_w + spread_e:
        copy.wait_send()


def reduce_last(gn, wb, dw):
    return comm_call(
        reduce_last_kernel,
        "reduce_last",
        6,
        [shape((TOK, D)), shape((8, WB)), shape((EP, 8, 256))],
        [ANY] * 3,
        [VM, VM, ANY],
        reduce_scratch(TOK, D)
        + reduce_scratch(128, WB)
        + [
            pltpu.VMEM((128, WB), F32),
            pltpu.VMEM((REP, 8, WB), F32),
            pltpu.VMEM((REP, 64, 256), F32),
            pltpu.VMEM((64, 256), F32),
            DMA((3,)),
            DMA((15,)),
            DMA((15,)),
            DMA((15,)),
            DMA((15,)),
            DMA((7,)),
            DMA((7,)),
        ],
    )(gn, wb, dw)


def column(row):
    return jnp.transpose(jnp.broadcast_to(row, (128, row.shape[1])))


def lane_row(values):
    return dot_nt(jnp.ones((8, 128), F32), values, precision=HIGH)[0:1]


def turn_tables():
    half = HEAD_DIM // 2
    freq = np.float32(ROPE_BASE) ** (-(np.arange(half, dtype=np.float32) * np.float32(2.0) / np.float32(HEAD_DIM)))
    angles = np.arange(LENGTH, dtype=np.float32)[:, None] * freq.astype(np.float32)[None, :]
    c, s = np.cos(angles), np.sin(angles)
    cosine = np.concatenate([c, c, c, c], axis=1)
    sine = np.concatenate([-s, s, -s, s], axis=1)
    return cosine.astype(np.float32), sine.astype(np.float32)


def turn(u, cosine, sine):
    early = iota(u.shape, 1) % HEAD_DIM < HEAD_DIM // 2
    partner = jnp.where(early, pltpu.roll(u, 96, 1), pltpu.roll(u, 32, 1))
    return u * cosine + partner * sine


def block_rows(b):
    return pl.ds(pl.multiple_of(b * TOK, TOK), TOK)


def key_start(i):
    return jnp.maximum(i - WINDOW // TOK, 0)


def stack_heads(values):
    first = iota(values.shape, 1) < HEAD_DIM
    return jnp.concatenate([jnp.where(first, values, 0.0), jnp.where(first, 0.0, values)], axis=0)


def merge_heads(values):
    first = iota((TOK, 128), 1) < HEAD_DIM
    return jnp.where(first, values[:TOK], values[TOK:])


def front_kernel(
    tok, cot, wq, wk, wv, wo_in, small, seg, rts, cos_in, sin_in,
    x_all, g_all, lin, st, lo, q_o, k_o, v_o, a_o, lse_o, hid_o, m_o, tab_o, att_o, gain_a, gain_f, gain, rout_o, whole, wcol,
    x_s, wsl, wos, wg, wog, w32, gains_s, cos_ref, sin_ref, sums, held,
    s_scr, q2_scr, lo_scr, m_scr, l_scr, acc,
    s_tok, r_tok, s_cot, r_cot, s_w, r_w, s_o, r_o, s_st, r_st, s_a, r_a, lsem,
):
    r = lax.axis_index("rep")
    e, x, c = place()
    others = ep_others(e)
    copies = rep_others(r)
    first = iota((TOK, 128), 1) < HEAD_DIM
    greet([{"ep": d} for d in others] + [{"rep": d} for d in copies])

    low_lanes = iota((8, 128), 1) < HEAD_DIM
    for d in range(EP):
        k_t = wk[:, (d // 2) * 128 : (d // 2 + 1) * 128].astype(F32)
        v_t = wv[:, (d // 2) * 128 : (d // 2 + 1) * 128].astype(F32)
        if d % 2:
            k_t = pltpu.roll(k_t, HEAD_DIM, 1)
        else:
            v_t = pltpu.roll(v_t, HEAD_DIM, 1)
        q_t = wq[:, d * 128 : (d + 1) * 128].astype(F32)
        wsl[d, :16] = jnp.concatenate([q_t, jnp.where(low_lanes, k_t, v_t)], axis=0).astype(BF)
        wsl[d, 16:] = small[...]
    wos[...] = jnp.concatenate(
        [wo_in[:, j * 128 : (j + 1) * 128].astype(F32) for j in range(8)], axis=0
    ).astype(BF)
    stage_w = [remote(wsl.at[d], wg.at[r, e], (s_w, r_w), k, {"ep": d}) for k, d in enumerate(others)]
    stage_o = [remote(wos, wog.at[r, e], (s_o, r_o), k, {"ep": d}) for k, d in enumerate(others)]
    spread_w = [remote(wg.at[r], wg.at[r], (s_w, r_w), 7 + k, {"rep": d}) for k, d in enumerate(copies)]
    spread_o = [remote(wog.at[r], wog.at[r], (s_o, r_o), 7 + k, {"rep": d}) for k, d in enumerate(copies)]
    tokens = RingGather(tok, x_s, (s_tok, r_tok), lsem.at[0])
    grads = RingGather(cot, g_all, (s_cot, r_cot), lsem.at[1])
    for copy in stage_w:
        copy.start()
    tokens.start()
    for copy in stage_o:
        copy.start()
    tables = [
        pltpu.make_async_copy(cos_in, cos_ref, lsem.at[2]),
        pltpu.make_async_copy(sin_in, sin_ref, lsem.at[3]),
    ]
    for copy in tables:
        copy.start()
    wg[r, e] = wsl[e]
    wog[r, e] = wos[...]
    for copy in stage_w:
        copy.wait_recv()
    for copy in spread_w:
        copy.start()
    tokens.forward()

    hit = jnp.zeros((EXPERTS, TOK), F32)
    for k in range(TOP):
        hit = jnp.where(iota((EXPERTS, TOK), 0) == rts[k : k + 1], 1.0, hit)
    before = jnp.where(iota((TOK, TOK), 0) < iota((TOK, TOK), 1), 1.0, 0.0).astype(BF)
    tab_o[:EXPERTS] = jnp.where(hit > 0.0, dot(hit.astype(BF), before), -1.0)
    segs = seg[...]
    opening = jnp.zeros((EP, TOK), F32)
    for value in range(2):
        count = jnp.sum(jnp.where(segs == value, 1.0, 0.0), axis=1, keepdims=True)
        opening = opening + jnp.where(segs > value, jnp.sum(count, axis=0, keepdims=True), 0.0)
    places = (iota((EP, TOK), 0) * TOK + iota((EP, TOK), 1)).astype(F32)
    lo[...] = jnp.maximum(opening, places - (WINDOW - 1))

    tokens.fwd_right.wait_recv()
    tokens.fwd_left.wait_recv()
    tokens.to_peer[2].start()
    for copy in spread_w:
        copy.wait_recv()
    for copy in stage_o:
        copy.wait_recv()
    for copy in spread_o:
        copy.start()

    def unpack(b, carry):
        tile = wg[b // EP, b % EP].astype(F32)
        rows = pl.ds(pl.multiple_of(b * 8, 8), 8)
        w32[rows, 0:128] = tile[0:8]
        w32[rows, 128:256] = tile[8:16]
        w32[rows, 256:384] = tile[16:24]
        gains_s[pl.ds(b, 1)] = tile[24:25]
        return carry

    lax.fori_loop(0, 128, unpack, 0)
    wcol[...] = w32[:, :256].astype(BF)
    rout_o[...] = jnp.transpose(w32[:, 256:384])[:EXPERTS].astype(BF)
    packed = gains_s[...].astype(BF)

    def spread_gain(width, group, base, shift):
        lane = base + iota((128, width), 1) % group
        picked = dot(packed, jnp.where(iota((128, width), 0) == lane, 1.0, 0.0).astype(BF))
        mine = iota((128, width), 0) == shift + iota((128, width), 1) // group
        return jnp.sum(jnp.where(mine, picked, 0.0), axis=0, keepdims=True)

    gain_a[...] = spread_gain(D, 8, 0, 0)
    gain_f[...] = spread_gain(D, 8, 20, 0)
    key_part = spread_gain(128, 4, 16, e * 16)
    gain[:, :128] = spread_gain(128, 8, 8, e * 16)
    gain[:, 128:] = jnp.where(iota((1, 128), 1) < HEAD_DIM, key_part, 1.0)

    tokens.first[4].wait_recv()
    tokens.own.wait()
    tokens.to_peer[1].wait_recv()
    tokens.to_peer[0].wait_recv()

    def project(k, carry):
        @pl.when(k == 6)
        def _():
            tokens.to_peer[2].wait_recv()

        g = k // 2
        b = (2 * (x + g + g // 2 - 2 * (g // 3)) + k % 2) % EP
        rows = block_rows(b)
        values = x_s[rows].astype(F32)
        r1 = lax.rsqrt(jnp.mean(values * values, axis=1, keepdims=True) + EPSILON)
        normed = (values * r1 * gain_a[...]).astype(BF)
        out = dot(normed, wcol[...])
        lin[rows] = out
        sq = out * out
        sums[pl.ds(2 * b, 1)] = lane_row(sq[:, :128])
        sums[pl.ds(2 * b + 1, 1)] = lane_row(jnp.where(first, sq[:, 128:], 0.0))
        return carry

    lax.fori_loop(0, EP, project, 0)
    stats = [remote(sums, held.at[e], (s_st, r_st), k, {"ep": d}) for k, d in enumerate(others)]
    for copy in stats:
        copy.start()
    held[e] = sums[...]
    keep = pltpu.make_async_copy(x_s, x_all, lsem.at[4])
    keep.start()
    for copy in tables:
        copy.wait()
    for copy in stats:
        copy.wait_recv()
    total = held[0]
    for k in range(1, EP):
        total = total + held[k]
    st[...] = total
    grads.start()

    def prepare(b, carry):
        rows = block_rows(b)
        cq = column(lax.rsqrt(st[pl.ds(2 * b, 1)] * (1.0 / D) + EPSILON))
        ck = column(lax.rsqrt(st[pl.ds(2 * b + 1, 1)] * (1.0 / KV) + EPSILON))
        cosine, sine = cos_ref[rows], sin_ref[rows]
        q_o[rows] = turn(lin[rows, :128] * cq * gain[:, :128], cosine, sine).astype(BF)
        kv = lin[rows, 128:]
        kv = jnp.where(first, turn(kv * ck * gain[:, 128:], cosine, sine), kv)
        other = pltpu.roll(kv, HEAD_DIM, 1)
        k_o[rows] = jnp.where(first, kv, other).astype(BF)
        v_o[rows] = jnp.where(first, other, kv).astype(BF)
        return carry

    lax.fori_loop(0, EP, prepare, 0)

    def heads(i, source):
        cols = pl.ds(pl.multiple_of(source * 128, 128), 128)
        return pltpu.make_async_remote_copy(
            src_ref=a_o.at[block_rows(i)],
            dst_ref=att_o.at[:, cols],
            send_sem=s_a.at[i],
            recv_sem=r_a.at[source],
            device_id={"ep": i},
            device_id_type=MESH,
        )

    def queries(i, carry):
        rows = block_rows(i)
        q2_scr[...] = stack_heads(q_o[rows].astype(F32) * HEAD_DIM ** (-0.5)).astype(BF)
        lo_col = column(lo[pl.ds(i, 1)])
        lo_scr[...] = jnp.concatenate([lo_col, lo_col], axis=0)
        m_scr[...] = jnp.full((2 * TOK, 128), MASKED, F32)
        l_scr[...] = jnp.zeros((2 * TOK, 128), F32)
        acc[...] = jnp.zeros((2 * TOK, 128), F32)
        j0 = key_start(i)

        def score(j, inner):
            s = dot_nt(q2_scr[...], k_o[block_rows(j)])
            key = (iota((2 * TOK, TOK), 1) + j * TOK).astype(F32)
            query = (iota((2 * TOK, TOK), 0) % TOK + i * TOK).astype(F32)
            s = jnp.where((key >= lo_scr[:, :1]) & (key <= query), s, MASKED)
            s_scr[j - j0] = s
            m_scr[...] = jnp.maximum(m_scr[...], jnp.maximum(s[:, :128], s[:, 128:]))
            return inner

        lax.fori_loop(j0, i + 1, score, 0)
        m = jnp.max(m_scr[...], axis=1, keepdims=True)
        m_scr[...] = jnp.broadcast_to(m, (2 * TOK, 128))

        def weigh(j, inner):
            p = jnp.exp(s_scr[j - j0] - m_scr[:, :1])
            l_scr[...] += p[:, :128] + p[:, 128:]
            acc[...] += dot(p.astype(BF), v_o[block_rows(j)])
            return inner

        lax.fori_loop(j0, i + 1, weigh, 0)
        total = jnp.sum(l_scr[...], axis=1, keepdims=True)
        a_o[rows] = merge_heads(acc[...] / total).astype(BF)
        lse = jnp.broadcast_to(m_scr[:, :1] + jnp.log(total), (2 * TOK, 128))
        lse_o[i] = jnp.transpose(lse)[:8]

        @pl.when(i != e)
        def _():
            heads(i, e).start()

        @pl.when(i == e)
        def _():
            att_o[:, pl.ds(pl.multiple_of(e * 128, 128), 128)] = a_o[rows]

        @pl.when(i == 4)
        def _():
            grads.forward()

        @pl.when(i == 6)
        def _():
            grads.fwd_right.wait_recv()
            grads.fwd_left.wait_recv()
            grads.to_peer[2].start()

        return carry

    lax.fori_loop(0, EP, queries, 0)

    for copy in spread_o:
        copy.wait_recv()

    def unpack_out(b, carry):
        tile = wog[b // EP, b % EP].astype(F32)
        rows = pl.ds(pl.multiple_of(b * 8, 8), 8)
        for j in range(8):
            w32[rows, j * 128 : (j + 1) * 128] = tile[j * 8 : (j + 1) * 8]
        return carry

    lax.fori_loop(0, 128, unpack_out, 0)
    whole[...] = w32[...].astype(BF)
    for d in others:
        heads(d, d).wait_recv()

    hidden = x_s[block_rows(e)].astype(F32) + dot(att_o[...], whole[...])
    hid_o[...] = hidden
    r2 = lax.rsqrt(jnp.mean(hidden * hidden, axis=1, keepdims=True) + EPSILON)
    moe_in = (hidden * r2 * gain_f[...]).astype(BF)
    m_o[...] = moe_in
    logits = dot_nt(rout_o[...], moe_in)
    chosen = hit > 0.0
    logits = jnp.where(chosen, logits, MASKED)
    raised = jnp.where(chosen, jnp.exp(logits - jnp.max(logits, axis=0, keepdims=True)), 0.0)
    tab_o[EXPERTS:] = raised / jnp.sum(raised, axis=0, keepdims=True)

    grads.first[4].wait_recv()
    for copy in grads.to_peer:
        copy.wait_recv()
    grads.own.wait()
    keep.wait()
    for d in others:
        heads(d, d).wait_send()
    for ring in (tokens, grads):
        for copy in ring.first + [ring.fwd_right, ring.fwd_left] + ring.to_peer:
            copy.wait_send()
    for copy in stage_w + stage_o + spread_w + spread_o + stats:
        copy.wait_send()


def front(*args):
    return comm_call(
        front_kernel,
        "front",
        1,
        [
            shape((LENGTH, D), BF),
            shape((LENGTH, D), BF),
            shape((LENGTH, 256)),
            shape((16, 256)),
            shape((EP, TOK)),
            shape((LENGTH, 128), BF),
            shape((LENGTH, 128), BF),
            shape((LENGTH, 128), BF),
            shape((LENGTH, 128), BF),
            shape((EP, 8, 2 * TOK)),
            shape((TOK, D)),
            shape((TOK, D), BF),
            shape((2 * EXPERTS, TOK)),
            shape((TOK, D), BF),
            shape((1, D)),
            shape((1, D)),
            shape((1, 256)),
            shape((EXPERTS, D), BF),
            shape((D, D), BF),
            shape((D, 256), BF),
        ],
        [ANY, ANY] + [VM] * 7 + [ANY, ANY],
        [ANY, ANY] + [VM] * 18,
        [
            pltpu.VMEM((LENGTH, D), BF),
            pltpu.VMEM((EP, 32, 128), BF),
            pltpu.VMEM((64, 128), BF),
            pltpu.VMEM((REP, EP, 32, 128), BF),
            pltpu.VMEM((REP, EP, 64, 128), BF),
            pltpu.VMEM((D, D), F32),
            pltpu.VMEM((128, 128), F32),
            pltpu.VMEM((LENGTH, 128), F32),
            pltpu.VMEM((LENGTH, 128), F32),
            pltpu.VMEM((16, 256), F32),
            pltpu.VMEM((EP, 16, 256), F32),
            pltpu.VMEM((5, 2 * TOK, TOK), F32),
            pltpu.VMEM((2 * TOK, 128), BF),
            pltpu.VMEM((2 * TOK, 128), F32),
            pltpu.VMEM((2 * TOK, 128), F32),
            pltpu.VMEM((2 * TOK, 128), F32),
            pltpu.VMEM((2 * TOK, 128), F32),
        ]
        + [DMA((10,))] * 4
        + [DMA((22,))] * 4
        + [DMA((7,))] * 2
        + [DMA((8,))] * 2
        + [DMA((5,))],
        limit=60,
    )(*args)


def attend_back_kernel(
    q_i, k_i, v_i, a_i, lse, lo, go, lin, st, cos_ref, sin_ref, gain, u_o, st_o, q2_scr, do2_scr, row_scr, dq, dk, dv
):
    first = iota((TOK, 128), 1) < HEAD_DIM
    dk[...] = jnp.zeros((LENGTH, 128), F32)
    dv[...] = jnp.zeros((LENGTH, 128), F32)

    def queries(i, carry):
        rows = block_rows(i)
        q2_scr[...] = stack_heads(q_i[rows].astype(F32) * HEAD_DIM ** (-0.5)).astype(BF)
        grad = stack_heads(go[rows].astype(F32))
        do2_scr[...] = grad.astype(BF)
        out = a_i[rows].astype(F32)
        row_scr[0:1] = lane_row(grad * jnp.concatenate([out, out], axis=0))
        row_scr[1:2] = lse[i][0:1]
        row_scr[2:3] = jnp.concatenate([lo[pl.ds(i, 1)]] * 2, axis=1)
        dq[...] = jnp.zeros((128, 2 * TOK), F32)

        def keys(j, inner):
            key_rows = block_rows(j)
            kk = k_i[key_rows]
            key = (iota((TOK, 2 * TOK), 0) + j * TOK).astype(F32)
            query = (iota((TOK, 2 * TOK), 1) % TOK + i * TOK).astype(F32)
            allowed = (key >= row_scr[2:3]) & (key <= query)
            s = dot_nt(kk, q2_scr[...])
            p = jnp.where(allowed, jnp.exp(s - row_scr[1:2]), 0.0)
            dp = dot_nt(v_i[key_rows], do2_scr[...])
            ds = (p * (dp - row_scr[0:1])).astype(BF)
            dv[key_rows] += dot(p.astype(BF), do2_scr[...])
            dk[key_rows] += dot(ds, q2_scr[...])
            dq[...] += dot_tn(kk, ds)
            return inner

        lax.fori_loop(key_start(i), i + 1, keys, 0)
        grad_q = merge_heads(jnp.transpose(dq[...])) * HEAD_DIM ** (-0.5)
        grad_q = turn(grad_q.astype(BF).astype(F32), cos_ref[rows], -sin_ref[rows])
        u_o[rows, :128] = grad_q
        cq = column(lax.rsqrt(st[pl.ds(2 * i, 1)] * (1.0 / D) + EPSILON))
        st_o[pl.ds(2 * i, 1)] = lane_row(grad_q * gain[:, :128] * lin[rows, :128] * cq)
        return carry

    lax.fori_loop(0, EP, queries, 0)

    def close(b, carry):
        rows = block_rows(b)
        grad_k, grad_v = dk[rows], dv[rows]
        grad_k = grad_k + pltpu.roll(grad_k, HEAD_DIM, 1)
        grad_v = grad_v + pltpu.roll(grad_v, HEAD_DIM, 1)
        both = jnp.where(first, grad_k, grad_v).astype(BF).astype(F32)
        both = jnp.where(first, turn(both, cos_ref[rows], -sin_ref[rows]), both)
        u_o[rows, 128:] = both
        ck = column(lax.rsqrt(st[pl.ds(2 * b + 1, 1)] * (1.0 / KV) + EPSILON))
        st_o[pl.ds(2 * b + 1, 1)] = lane_row(
            jnp.where(first, both * gain[:, 128:] * lin[rows, 128:] * ck, 0.0)
        )
        return carry

    lax.fori_loop(0, EP, close, 0)


def attend_back(q, k, v, a, lse, lo, go, lin, st, cosine, sine, gain):
    return pl.pallas_call(
        attend_back_kernel,
        out_shape=[shape((LENGTH, 256)), shape((2 * EP, 256))],
        in_specs=[VM] * 12,
        out_specs=[VM] * 2,
        scratch_shapes=[
            pltpu.VMEM((2 * TOK, 128), BF),
            pltpu.VMEM((2 * TOK, 128), BF),
            pltpu.VMEM((8, 2 * TOK), F32),
            pltpu.VMEM((128, 2 * TOK), F32),
            pltpu.VMEM((LENGTH, 128), F32),
            pltpu.VMEM((LENGTH, 128), F32),
        ],
        compiler_params=pltpu.CompilerParams(vmem_limit_bytes=48 * MIB),
        name="attend_back",
    )(q, k, v, a, lse, lo, go, lin, st, cosine, sine, gain)


def project_back_kernel(x_ref, u_ref, lin_ref, st, st2, gain, attn_gain, w_ref, gn_o, dw_o, ga_o, gqk_o, dwt):
    i = pl.program_id(0)
    first = iota((TOK, 128), 1) < HEAD_DIM

    @pl.when(i == 0)
    def _():
        dwt[...] = jnp.zeros_like(dwt)
        ga_o[...] = jnp.zeros_like(ga_o)
        gqk_o[...] = jnp.zeros_like(gqk_o)

    x = x_ref[...].astype(F32)
    r1 = lax.rsqrt(jnp.mean(x * x, axis=1, keepdims=True) + EPSILON)
    n1 = x * r1
    normed = (n1 * attn_gain[...]).astype(BF)
    u = u_ref[...]
    lin = lin_ref[...]
    cq = column(lax.rsqrt(st[pl.ds(2 * i, 1)] * (1.0 / D) + EPSILON))
    ck = column(lax.rsqrt(st[pl.ds(2 * i + 1, 1)] * (1.0 / KV) + EPSILON))
    mq = column(st2[pl.ds(2 * i, 1)] * (1.0 / D))
    mk = column(st2[pl.ds(2 * i + 1, 1)] * (1.0 / KV))
    nq = lin[:, :128] * cq
    nk = lin[:, 128:] * ck
    gq = cq * (u[:, :128] * gain[:, :128] - nq * mq)
    gk = jnp.where(first, ck * (u[:, 128:] * gain[:, 128:] - nk * mk), u[:, 128:])
    glin = jnp.concatenate([gq, gk], axis=1).astype(BF)
    gqk_o[0:1] += jnp.concatenate(
        [
            jnp.sum(u[:, :128] * nq, axis=0, keepdims=True),
            jnp.sum(u[:, 128:] * nk, axis=0, keepdims=True),
        ],
        axis=1,
    )
    gn = dot_nt(glin, w_ref[...])
    ga_o[0:1] += jnp.sum(gn * n1, axis=0, keepdims=True)
    gn_o[...] = gn.astype(BF)
    dwt[...] += dot_tn(glin, normed)

    @pl.when(i == EP - 1)
    def _():
        dw_o[...] = jnp.transpose(dwt[...])


def project_back(x_all, u, lin, st, st2, gain, attn_gain, w):
    def whole(dims):
        return pl.BlockSpec(dims, lambda i: tuple(0 for _ in dims))

    return pl.pallas_call(
        project_back_kernel,
        grid=(EP,),
        out_shape=[shape((LENGTH, D), BF), shape((D, 256)), shape((8, D)), shape((8, 256))],
        in_specs=[
            pl.BlockSpec((TOK, D), lambda i: (i, 0)),
            pl.BlockSpec((TOK, 256), lambda i: (i, 0)),
            pl.BlockSpec((TOK, 256), lambda i: (i, 0)),
            whole((16, 256)),
            whole((16, 256)),
            whole((1, 256)),
            whole((1, D)),
            whole((D, 256)),
        ],
        out_specs=[pl.BlockSpec((TOK, D), lambda i: (i, 0)), whole((D, 256)), whole((8, D)), whole((8, 256))],
        scratch_shapes=[pltpu.VMEM((256, D), F32)],
        compiler_params=pltpu.CompilerParams(vmem_limit_bytes=48 * MIB),
        name="project_back",
    )(x_all, u, lin, st, st2, gain, attn_gain, w)


class ChipReduce:
    SEMS = 10
    STEP = 64

    def __init__(self, n, swo, snd, pc, rcv, hop, sems):
        e, x, c = place()
        self.n, self.h = n, n // 2
        h = n // 2
        self.snd, self.pc, self.rcv, self.hop = snd, pc, rcv, hop
        right, left = ep_device((x + 1) % 4, c), ep_device((x + 3) % 4, c)
        peer = ep_device(x, 1 - c)
        self.swap = lambda k: remote(swo.at[k], pc.at[k], sems, k, peer)
        low, high = pl.ds(0, h), pl.ds(h, h)
        self.opp = [
            remote(snd.at[0, low], hop.at[low], sems, 4, right),
            remote(snd.at[0, high], hop.at[high], sems, 5, left),
        ]
        self.near = [
            remote(snd.at[2, high], rcv.at[0, high], sems, 6, right),
            remote(snd.at[1, low], rcv.at[1, low], sems, 7, left),
        ]
        self.far = [
            remote(snd.at[2, low], rcv.at[0, low], sems, 8, right),
            remote(snd.at[1, high], rcv.at[1, high], sems, 9, left),
        ]

    def rows_loop(self, low, count, body):
        step = self.STEP

        def loop(i, carry):
            body(pl.ds(pl.multiple_of(low + i * step, 16), step))
            return carry

        lax.fori_loop(0, count // step, loop, 0)

    def merge(self, k):
        def body(s):
            self.snd[k, s] = (self.snd[k, s].astype(F32) + self.pc[k, s].astype(F32)).astype(BF)

        self.swap(k).wait_recv()
        self.rows_loop(0, self.n, body)

    def merge_hop(self, k, low):
        def body(s):
            self.snd[k, s] = (self.snd[k, s].astype(F32) + self.hop[s].astype(F32)).astype(BF)

        self.rows_loop(low, self.h, body)

    def send_opp(self):
        self.merge(0)
        for copy in self.opp:
            copy.start()

    def send_near(self):
        self.merge(2)
        self.near[0].start()
        self.merge(1)
        self.near[1].start()

    def send_far(self):
        self.opp[0].wait_recv()
        self.merge_hop(2, 0)
        self.far[0].start()
        self.opp[1].wait_recv()
        self.merge_hop(1, self.h)
        self.far[1].start()

    def finish(self, out_ref):
        for copy in self.near + self.far:
            copy.wait_recv()

        def body(s):
            out_ref[s] = self.snd[3, s].astype(F32) + (
                self.rcv[0, s].astype(F32) + self.rcv[1, s].astype(F32)
            )

        self.rows_loop(0, self.n, body)
        for copy in [self.swap(k) for k in range(4)] + self.opp + self.near + self.far:
            copy.wait_send()


ROWS = EP * CAP
HALF = 256
BLOCK = 96


def experts_kernel(
    m_in, t_in, g_in, wg_in, wu_in, wd_in, out_o, gm_o, gg_o, eg_o,
    m_ref, tab, g_ref, wg, wu, wd, a_s, c_s, gl_s, up_s, act_s, dgu_s, y_s, gate_s, gg_s, ggt, eg,
    swo, snd, pc1, rcv1, hop1, pc2, rcv2, hop2,
    s_m, r_m, s_t, r_t, s_1, r_1, s_2, r_2, s_g, r_g, lsem, esem,
):
    e, x, c = place()
    others = ep_others(e)
    greet([{"ep": d} for d in others])
    ring = RingGather(m_in, m_ref, (s_m, r_m), lsem.at[0])
    ring.start()
    tables = [remote(t_in, tab.at[e], (s_t, r_t), k, {"ep": d}) for k, d in enumerate(others)]
    for copy in tables:
        copy.start()
    loads = [
        pltpu.make_async_copy(t_in, tab.at[e], lsem.at[1]),
        pltpu.make_async_copy(wg_in, wg, lsem.at[2]),
        pltpu.make_async_copy(wu_in, wu, lsem.at[3]),
        pltpu.make_async_copy(wd_in, wd, lsem.at[4]),
        pltpu.make_async_copy(g_in, g_ref, lsem.at[5]),
    ]
    for copy in loads:
        copy.start()
    red1 = ChipReduce(TOK, swo, snd, pc1, rcv1, hop1, (s_1, r_1))
    red2 = ChipReduce(TOK, swo, snd, pc2, rcv2, hop2, (s_2, r_2))

    def hits(s, k):
        return iota((CAP, TOK), 0).astype(F32) == tab[s, pl.ds(e * LOCAL + k, 1)]

    def slot_rows(s):
        return pl.ds(pl.multiple_of(s * CAP, 32), CAP)

    def gate_column(s, k, hit):
        row = tab[s, pl.ds(EXPERTS + e * LOCAL + k, 1)]
        return jnp.sum(jnp.where(hit, row, 0.0), axis=1, keepdims=True)

    def one_hot(hit):
        return jnp.where(hit, 1.0, 0.0).astype(BF)

    def combine(s):
        chosen = jnp.concatenate([one_hot(hits(s, k)) for k in range(LOCAL)], axis=0)
        rows = slot_rows(s)
        return dot_tn(chosen, jnp.concatenate([y_s[k, rows] for k in range(LOCAL)], axis=0)).astype(BF)

    def forward(k, carry):
        @pl.when(k == 0)
        def _():
            ring.first[0].wait_recv()
            ring.fwd_right.start()
            ring.first[1].wait_recv()
            ring.fwd_left.start()
            ring.first[4].wait_recv()
            ring.own.wait()
            for copy in tables:
                copy.wait_recv()
            for copy in loads[:4]:
                copy.wait()

        @pl.when(k == 1)
        def _():
            ring.first[3].wait_recv()
            ring.to_peer[1].start()
            ring.first[2].wait_recv()
            ring.to_peer[0].start()
            ring.to_peer[1].wait_recv()

        @pl.when(k == 2)
        def _():
            ring.fwd_right.wait_recv()
            ring.fwd_left.wait_recv()
            ring.to_peer[2].start()
            ring.to_peer[0].wait_recv()

        @pl.when(k == 3)
        def _():
            ring.to_peer[2].wait_recv()

        q = (x + k + k // 2 - 2 * (k // 3)) % 4
        rows = pl.ds(pl.multiple_of(q * 2 * CAP, 64), 2 * CAP)

        def expert(n, inner):
            for core in range(2):
                s = q * 2 + core
                hit = hits(s, n)
                a_s[core * CAP : (core + 1) * CAP] = dot(one_hot(hit), m_ref[block_rows(s)]).astype(BF)
                gate_s[core * CAP : (core + 1) * CAP] = jnp.broadcast_to(gate_column(s, n, hit), (CAP, 128))
            a = a_s[: 2 * CAP]
            gate_lin = dot(a, wg[n])
            up_lin = dot(a, wu[n])
            gl_s[n, rows] = gate_lin.astype(BF)
            up_s[n, rows] = up_lin.astype(BF)
            act = (gate_lin * jax.nn.sigmoid(gate_lin) * up_lin).astype(BF)
            produced = dot(act, wd[n]).astype(BF).astype(F32)
            y_s[n, rows] = (gate_s[: 2 * CAP, :1] * produced).astype(BF)
            return inner

        lax.fori_loop(0, LOCAL, expert, 0)
        slot = 3 - k
        swo[slot] = combine(q * 2 + 1 - c)
        red1.swap(slot).start()
        snd[slot] = combine(q * 2 + c)
        return carry

    lax.fori_loop(0, 4, forward, 0)
    red1.send_opp()
    red1.send_near()
    loads[4].wait()

    def backward(n, carry):
        def pick(s, inner):
            hit = hits(s, n)
            chosen = one_hot(hit)
            rows = slot_rows(s)
            a_s[rows] = dot(chosen, m_ref[block_rows(s)]).astype(BF)
            c_s[rows] = dot(chosen, g_ref[block_rows(s)]).astype(BF)
            gate_s[rows] = jnp.broadcast_to(gate_column(s, n, hit), (CAP, 128))
            return inner

        lax.fori_loop(0, EP, pick, 0)

        def rows_part(k, inner):
            rows = pl.ds(pl.multiple_of(k * HALF, HALF), HALF)
            cot = c_s[rows]
            weight = gate_s[rows][:, :1]
            back = dot_nt(cot, wd[n])
            c_s[rows] = (weight * cot.astype(F32)).astype(BF)
            gate_lin, up_lin = gl_s[n, rows].astype(F32), up_s[n, rows].astype(F32)
            sig = jax.nn.sigmoid(gate_lin)
            silu = gate_lin * sig
            act = silu * up_lin
            act_s[rows] = act.astype(BF)
            gg_s[rows] = jnp.broadcast_to(jnp.sum(act * back, axis=1, keepdims=True), (HALF, 128))
            back = back * weight
            dgate = (back * up_lin * sig * (1.0 + gate_lin * (1.0 - sig))).astype(BF)
            dup = (back * silu).astype(BF)
            dgu_s[rows, :FF] = dgate
            dgu_s[rows, FF:] = dup
            y_s[n, rows] = (dot_nt(dgate, wg[n]) + dot_nt(dup, wu[n])).astype(BF)
            return inner

        lax.fori_loop(0, ROWS // HALF, rows_part, 0)

        def gates_back(s, inner):
            column_ = gg_s[slot_rows(s)][:, :1]
            ggt[s, pl.ds(n, 1)] = jnp.sum(jnp.where(hits(s, n), column_, 0.0), axis=0, keepdims=True)
            return inner

        lax.fori_loop(0, EP, gates_back, 0)

        @pl.when(n == 0)
        def _():
            red1.merge(3)
            red1.send_far()

        @pl.when(n == 2)
        def _():
            red1.finish(out_o)

        @pl.when(n > 0)
        def _():
            pltpu.make_async_copy(eg, eg_o.at[n - 1], esem).wait()

        eg[:, :64, :FF] = dot_tn(a_s[...], dgu_s[:, :FF]).astype(BF).reshape(REP, 64, FF)
        eg[:, :64, FF:] = dot_tn(a_s[...], dgu_s[:, FF:]).astype(BF).reshape(REP, 64, FF)
        eg[:, 64:] = dot_tn(act_s[...], c_s[...]).astype(BF).reshape(REP, 32, D)
        pltpu.make_async_copy(eg, eg_o.at[n], esem).start()
        return carry

    lax.fori_loop(0, LOCAL, backward, 0)
    gates = [remote(ggt.at[d], gg_o.at[e], (s_g, r_g), k, {"ep": d}) for k, d in enumerate(others)]
    own = pltpu.make_async_copy(ggt.at[e], gg_o.at[e], lsem.at[1])
    for copy in gates + [own]:
        copy.start()
    for slot, q in enumerate([(x + 2) % 4, (x + 3) % 4, (x + 1) % 4, x]):
        swo[slot] = combine(q * 2 + 1 - c)
        red2.swap(slot).start()
        snd[slot] = combine(q * 2 + c)
        if slot == 0:
            red2.send_opp()
    red2.send_near()
    red2.merge(3)
    red2.send_far()
    red2.finish(gm_o)
    own.wait()
    pltpu.make_async_copy(eg, eg_o.at[LOCAL - 1], esem).wait()
    for copy in gates:
        copy.wait_recv()
    for copy in ring.first + [ring.fwd_right, ring.fwd_left] + ring.to_peer + tables + gates:
        copy.wait_send()


def experts(m, t, g_all, wg, wu, wd):
    return comm_call(
        experts_kernel,
        "experts",
        4,
        [
            shape((TOK, D)),
            shape((TOK, D)),
            shape((EP, 8, TOK)),
            shape((LOCAL, REP, BLOCK, D), BF),
        ],
        [ANY] * 6,
        [VM, VM, ANY, ANY],
        [
            pltpu.VMEM((LENGTH, D), BF),
            pltpu.VMEM((EP, 2 * EXPERTS, TOK), F32),
            pltpu.VMEM((LENGTH, D), BF),
            pltpu.VMEM((LOCAL, D, FF), BF),
            pltpu.VMEM((LOCAL, D, FF), BF),
            pltpu.VMEM((LOCAL, FF, D), BF),
            pltpu.VMEM((ROWS, D), BF),
            pltpu.VMEM((ROWS, D), BF),
            pltpu.VMEM((LOCAL, ROWS, FF), BF),
            pltpu.VMEM((LOCAL, ROWS, FF), BF),
            pltpu.VMEM((ROWS, FF), BF),
            pltpu.VMEM((ROWS, D), BF),
            pltpu.VMEM((LOCAL, ROWS, D), BF),
            pltpu.VMEM((ROWS, 128), F32),
            pltpu.VMEM((ROWS, 128), F32),
            pltpu.VMEM((EP, 8, TOK), F32),
            pltpu.VMEM((REP, BLOCK, D), BF),
            pltpu.VMEM((4, TOK, D), BF),
            pltpu.VMEM((4, TOK, D), BF),
        ]
        + [pltpu.VMEM((4, TOK, D), BF), pltpu.VMEM((2, TOK, D), BF), pltpu.VMEM((TOK, D), BF)] * 2
        + [DMA((10,))] * 2
        + [DMA((7,))] * 2
        + [DMA((10,))] * 4
        + [DMA((7,))] * 2
        + [DMA((6,)), DMA(())],
        limit=63,
    )(m, t, g_all, wg, wu, wd)


def hidden_back_kernel(
    hid, mixed, gmoe, gg, gate, m_ref, cot, gain, router, w_ref, a_ref, out_o, gh_o, ga_o, dwo_o, dr_o, gf_o
):
    hidden = hid[...]
    out_o[...] = (hidden + mixed[...]).astype(BF)
    weights = gate[...]
    grads = gg[...]
    mean = jnp.sum(weights * grads, axis=0, keepdims=True)
    grad_logits = (weights * (grads - mean)).astype(BF)
    dr_o[...] = dot(grad_logits, m_ref[...])
    grad_moe = gmoe[...] + dot_tn(grad_logits, router[...])
    r2 = lax.rsqrt(jnp.mean(hidden * hidden, axis=1, keepdims=True) + EPSILON)
    n = hidden * r2
    gf_o[...] = jnp.sum(grad_moe * n, axis=0, keepdims=True)
    u = grad_moe * gain[...]
    grad_hidden = cot[...].astype(F32) + r2 * (u - n * jnp.mean(u * n, axis=1, keepdims=True))
    gh_o[...] = grad_hidden
    branch = grad_hidden.astype(BF)
    ga_o[...] = dot_nt(branch, w_ref[...]).astype(BF)
    dwo_o[...] = dot_tn(a_ref[...], branch).astype(BF)


def hidden_back(hid, mixed, grad_moe, gg, gate, m, cot, gain, router, w, a):
    return pl.pallas_call(
        hidden_back_kernel,
        out_shape=[
            shape((TOK, D), BF),
            shape((TOK, D)),
            shape((TOK, D), BF),
            shape((D, D), BF),
            shape((EXPERTS, D)),
            shape((1, D)),
        ],
        in_specs=[VM] * 11,
        out_specs=[VM] * 6,
        compiler_params=pltpu.CompilerParams(vmem_limit_bytes=48 * MIB),
        name="hidden_back",
    )(hid, mixed, grad_moe, gg, gate, m, cot, gain, router, w, a)


def body(
    tokens,
    segments,
    routes,
    w_query,
    w_key,
    w_value,
    w_out,
    w_router,
    gain_attn,
    gain_query,
    gain_key,
    gain_ffn,
    w_gate,
    w_up,
    w_down,
    out_grad,
):
    e = lax.axis_index("ep")
    gains = jnp.concatenate([gain_attn, gain_query, gain_key, gain_ffn]).reshape(1, 28)
    small = jnp.concatenate(
        [jnp.pad(w_router, ((0, 0), (0, 128 - EXPERTS))), jnp.pad(gains, ((0, 7), (0, 100)))], axis=0
    )
    cosine, sine = turn_tables()
    (
        x_all, g_all, lin, st, lo, q, k, v, att, lse, hidden, moe_in, tables, attended,
        attn_gain, ffn_gain, qk_gain, router, whole_out, w_cols,
    ) = front(
        tokens, out_grad, w_query, w_key, w_value, w_out, small, segments.reshape(EP, TOK), routes.T, cosine, sine
    )
    gates = tables[EXPERTS:]
    mixed, grad_moe, gg, grads = experts(moe_in, tables, g_all, w_gate, w_up, w_down)
    grads = grads.reshape(LOCAL, REP * BLOCK, D)
    expert_sums = lax.psum_scatter(grads, "rep", scatter_dimension=1, tiled=True).astype(F32)
    gg = gg[:, :LOCAL].reshape(EXPERTS, TOK)
    attended_t = attended.reshape(TOK, REP, EP, 8).transpose(0, 2, 1, 3).reshape(TOK, D)
    output, grad_hidden, grad_att, dwo, drouter, dffn = hidden_back(
        hidden, mixed, grad_moe, gg, gates, moe_in, out_grad, ffn_gain, router, whole_out, attended_t
    )
    go = swap_heads(grad_att, False, "swap_heads_back", 7)
    u, sums2 = attend_back(q, k, v, att, lse, lo, go, lin, st, cosine, sine, qk_gain)
    st2 = sum_stats(sums2, "sum_stats_back", 8)
    gn, dw, dattn, dqk = project_back(x_all, u, lin, st, st2, qk_gain, attn_gain, w_cols)

    dquery = lax.dynamic_update_slice(jnp.zeros((1, D), F32), dqk[0:1, :128], (0, e * 128))
    dkey = lax.dynamic_update_slice(jnp.zeros((1, KV), F32), dqk[0:1, 128:192], (0, e * 64))
    dkey = jnp.pad(dkey.reshape(128, 4), ((0, 0), (0, 4))).reshape(1, D)
    vectors = jnp.concatenate([drouter, dattn[0:1], dquery, dkey, dffn], axis=0)
    vectors = vectors.reshape(36, REP, EP, 8).transpose(2, 1, 3, 0).reshape(D, 36)
    wb = jnp.concatenate([dwo, jnp.pad(vectors, ((0, 0), (0, 128 - 36))).astype(BF)], axis=1)
    gn_sum, wb_sum, dw_sum = reduce_last(gn, wb, dw)

    x = tokens.astype(F32)
    r1 = lax.rsqrt(jnp.mean(x * x, axis=-1, keepdims=True) + EPSILON)
    n1 = x * r1
    z = gn_sum * attn_gain
    input_grad = grad_hidden + r1 * (z - n1 * jnp.mean(z * n1, axis=-1, keepdims=True))
    dw_rows = dw_sum.transpose(1, 0, 2)
    return (
        output,
        input_grad,
        dw_rows[:, :, :128].reshape(8, D),
        dw_rows[:, :, 128:192].reshape(8, KV),
        dw_rows[:, :, 192:].reshape(8, KV),
        wb_sum[:, :D],
        wb_sum[:, D : D + EXPERTS],
        wb_sum[:, D + 32],
        wb_sum[:, D + 33],
        wb_sum[:4, D + 34],
        wb_sum[:, D + 35],
        expert_sums[:, :64, :FF],
        expert_sums[:, :64, FF:],
        expert_sums[:, 64:],
    )


def solution(mesh):
    both = P(("rep", "ep"), None)
    line = P(("rep", "ep"))
    owner = P("ep", None, None)
    kept = P("ep", "rep", None)
    return jax.shard_map(
        body,
        mesh=mesh,
        in_specs=(both, P("rep", None)) + (both,) * 6 + (line,) * 4 + (owner,) * 3 + (both,),
        out_specs=(both,) * 7 + (line,) * 4 + (kept,) * 3,
        check_vma=False,
    )
```

```python
import functools

import jax
import jax.numpy as jnp
import numpy as np
from jax import lax
from jax.experimental import pallas as pl
from jax.experimental.pallas import tpu as pltpu
from jax.sharding import PartitionSpec as P

BF = jnp.bfloat16
F32 = jnp.float32
MESH = pl.DeviceIdType.MESH
ANY = pl.BlockSpec(memory_space=pl.ANY)
VM = pl.BlockSpec(memory_space=pltpu.VMEM)
DMA = pltpu.SemaphoreType.DMA
MIB = 1 << 20

HEADS = 16
KV_HEADS = 8
HEAD_DIM = 64
TOP = 8
WINDOW = 1024
EPSILON = 1e-06
ROPE_BASE = 10000.0
MASKED = -1e30
EP = 8
REP = 16
TOK = 256
LENGTH = 2048
D = 1024
KV = 512
FF = 512
EXPERTS = 32
LOCAL = 4
CAP = 96
NT = (((1,), (1,)), ((), ()))
TN = (((0,), (0,)), ((), ()))
HIGH = lax.Precision.HIGHEST


def dot(a, b):
    return jnp.dot(a, b, preferred_element_type=F32)


def dot_nt(a, b, precision=None):
    return lax.dot_general(a, b, NT, preferred_element_type=F32, precision=precision)


def dot_tn(a, b):
    return lax.dot_general(a, b, TN, preferred_element_type=F32)


def iota(shape, dim):
    return lax.broadcasted_iota(jnp.int32, shape, dim)


def ep_device(x, c):
    return {"ep": x * 2 + c}


def greet(devices):
    barrier = pltpu.get_barrier_semaphore()
    for device in devices:
        pl.semaphore_signal(barrier, inc=1, device_id=device, device_id_type=MESH)
    pl.semaphore_wait(barrier, len(devices))


def remote(src, dst, sems, i, device):
    return pltpu.make_async_remote_copy(
        src_ref=src,
        dst_ref=dst,
        send_sem=sems[0].at[i],
        recv_sem=sems[1].at[i],
        device_id=device,
        device_id_type=MESH,
    )


def place():
    e = lax.axis_index("ep")
    return e, e // 2, e % 2


def ep_others(e):
    return [(e + k) % EP for k in range(1, EP)]


def rep_others(r):
    return [(r + k) % REP for k in range(1, REP)]


class RingGather:
    SEMS = 10

    def __init__(self, x_ref, o_ref, sems, lsem):
        e, x, c = place()
        self.n = n = x_ref.shape[0]
        h = n // 2
        self.o_ref = o_ref
        right, left = ep_device((x + 1) % 4, c), ep_device((x + 3) % 4, c)
        peer = ep_device(x, 1 - c)
        b_left, b_right, b_opp = (((x + 3) % 4) * 2 + c, ((x + 1) % 4) * 2 + c, ((x + 2) % 4) * 2 + c)

        def rows(b, off=0, size=n):
            return o_ref.at[pl.ds(pl.multiple_of(b * n + off, 16), size)]

        low, high = x_ref.at[pl.ds(0, h)], x_ref.at[pl.ds(h, h)]
        self.first = [
            remote(low, rows(e, 0, h), sems, 0, right),
            remote(high, rows(e, h, h), sems, 2, left),
            remote(high, rows(e, h, h), sems, 1, right),
            remote(low, rows(e, 0, h), sems, 3, left),
            remote(x_ref, rows(e), sems, 4, peer),
        ]
        self.fwd_right = remote(rows(b_left, 0, h), rows(b_left, 0, h), sems, 5, right)
        self.fwd_left = remote(rows(b_right, h, h), rows(b_right, h, h), sems, 6, left)
        self.to_peer = [
            remote(rows(b_left), rows(b_left), sems, 7, peer),
            remote(rows(b_right), rows(b_right), sems, 8, peer),
            remote(rows(b_opp), rows(b_opp), sems, 9, peer),
        ]
        self.own = pltpu.make_async_copy(x_ref, rows(e), lsem)

    def start(self):
        for copy in self.first:
            copy.start()
        self.own.start()

    def forward(self):
        self.first[0].wait_recv()
        self.fwd_right.start()
        self.first[1].wait_recv()
        self.fwd_left.start()
        self.first[2].wait_recv()
        self.to_peer[0].start()
        self.first[3].wait_recv()
        self.to_peer[1].start()

    def finish(self):
        self.fwd_right.wait_recv()
        self.fwd_left.wait_recv()
        self.to_peer[2].start()
        self.first[4].wait_recv()
        for copy in self.to_peer:
            copy.wait_recv()
        self.own.wait()
        for copy in self.first + [self.fwd_right, self.fwd_left] + self.to_peer:
            copy.wait_send()


class RingReduce:
    SEMS = 10
    STEP = 64

    def __init__(self, p_ref, n, pc, snd, rcv, hop, sems, lsems):
        e, x, c = place()
        self.n, self.h = n, n // 2
        h = n // 2
        self.pc, self.snd, self.rcv, self.hop = pc, snd, rcv, hop
        right, left = ep_device((x + 1) % 4, c), ep_device((x + 3) % 4, c)
        peer = ep_device(x, 1 - c)

        def rows(b):
            return p_ref.at[pl.ds(pl.multiple_of(b * n, 16), n)]

        chips = [(x + 2) % 4, (x + 1) % 4, (x + 3) % 4, x]
        self.swap = [remote(rows(b * 2 + 1 - c), pc.at[k], sems, k, peer) for k, b in enumerate(chips)]
        self.load = [
            pltpu.make_async_copy(rows(b * 2 + c), snd.at[k], lsems.at[k]) for k, b in enumerate(chips)
        ]
        low, high = pl.ds(0, h), pl.ds(h, h)
        self.opp = [
            remote(snd.at[0, low], hop.at[low], sems, 4, right),
            remote(snd.at[0, high], hop.at[high], sems, 5, left),
        ]
        self.near = [
            remote(snd.at[1, high], rcv.at[0, high], sems, 6, right),
            remote(snd.at[2, low], rcv.at[1, low], sems, 7, left),
        ]
        self.far = [
            remote(snd.at[1, low], rcv.at[0, low], sems, 8, right),
            remote(snd.at[2, high], rcv.at[1, high], sems, 9, left),
        ]

    def rows_loop(self, low, count, body):
        step = self.STEP

        def loop(i, carry):
            body(pl.ds(pl.multiple_of(low + i * step, 16), step))
            return carry

        lax.fori_loop(0, count // step, loop, 0)

    def merge(self, k):
        def body(s):
            self.snd[k, s] = (self.snd[k, s].astype(F32) + self.pc[k, s].astype(F32)).astype(BF)

        self.load[k].wait()
        self.swap[k].wait_recv()
        self.rows_loop(0, self.n, body)

    def merge_hop(self, k, low):
        def body(s):
            self.snd[k, s] = (self.snd[k, s].astype(F32) + self.hop[s].astype(F32)).astype(BF)

        self.rows_loop(low, self.h, body)

    def start(self):
        for copy in self.swap + self.load:
            copy.start()

    def push_opp(self):
        self.merge(0)
        for copy in self.opp:
            copy.start()

    def push_near(self):
        self.merge(1)
        self.near[0].start()
        self.merge(2)
        self.near[1].start()
        self.merge(3)

    def relay(self):
        self.opp[0].wait_recv()
        self.merge_hop(1, 0)
        self.far[0].start()
        self.opp[1].wait_recv()
        self.merge_hop(2, self.h)
        self.far[1].start()

    def finish(self, out_ref):
        for copy in self.near + self.far:
            copy.wait_recv()

        def body(s):
            out_ref[s] = self.snd[3, s].astype(F32) + (
                self.rcv[0, s].astype(F32) + self.rcv[1, s].astype(F32)
            )

        self.rows_loop(0, self.n, body)
        for copy in self.swap + self.opp + self.near + self.far:
            copy.wait_send()


def comm_call(kernel, name, collective_id, out_shape, in_specs, out_specs, scratch, limit=48):
    return pl.pallas_call(
        kernel,
        out_shape=out_shape,
        in_specs=in_specs,
        out_specs=out_specs,
        scratch_shapes=scratch,
        compiler_params=pltpu.CompilerParams(
            collective_id=collective_id, has_side_effects=True, vmem_limit_bytes=limit * MIB
        ),
        name=name,
    )


def shape(dims, dtype=F32):
    return jax.ShapeDtypeStruct(dims, dtype)


WB = D + 128


def column(row):
    return jnp.transpose(jnp.broadcast_to(row, (128, row.shape[1])))


def lane_row(values):
    return dot_nt(jnp.ones((8, 128), F32), values, precision=HIGH)[0:1]


def turn_tables():
    half = HEAD_DIM // 2
    freq = np.float32(ROPE_BASE) ** (-(np.arange(half, dtype=np.float32) * np.float32(2.0) / np.float32(HEAD_DIM)))
    angles = np.arange(LENGTH, dtype=np.float32)[:, None] * freq.astype(np.float32)[None, :]
    c, s = np.cos(angles), np.sin(angles)
    cosine = np.concatenate([c, c, c, c], axis=1)
    sine = np.concatenate([-s, s, -s, s], axis=1)
    return cosine.astype(np.float32), sine.astype(np.float32)


def turn(u, cosine, sine):
    early = iota(u.shape, 1) % HEAD_DIM < HEAD_DIM // 2
    partner = jnp.where(early, pltpu.roll(u, 96, 1), pltpu.roll(u, 32, 1))
    return u * cosine + partner * sine


def block_rows(b):
    return pl.ds(pl.multiple_of(b * TOK, TOK), TOK)


def key_start(i):
    return jnp.maximum(i - WINDOW // TOK, 0)


def stack_heads(values):
    first = iota(values.shape, 1) < HEAD_DIM
    return jnp.concatenate([jnp.where(first, values, 0.0), jnp.where(first, 0.0, values)], axis=0)


def merge_heads(values):
    first = iota((TOK, 128), 1) < HEAD_DIM
    return jnp.where(first, values[:TOK], values[TOK:])


def front_kernel(
    tok, cot, wq, wk, wv, wo_in, small, seg, rts, cos_in, sin_in,
    x_all, g_all, lin, q_o, k_o, v_o, a_o, lse_o, hid_o, m_o, tab_o, att_o, misc, rout_o, whole, wcol,
    x_s, wsl, wos, wg, wog, w32, gains_s, cos_ref, sin_ref, sums, held,
    s_scr, q2_scr, lo_scr, m_scr, l_scr, acc,
    s_tok, r_tok, s_cot, r_cot, s_w, r_w, s_o, r_o, s_st, r_st, s_a, r_a, lsem,
):
    r = lax.axis_index("rep")
    e, x, c = place()
    others = ep_others(e)
    copies = rep_others(r)
    first = iota((TOK, 128), 1) < HEAD_DIM
    gain_a, gain_f, gain = misc.at[0:1], misc.at[1:2], misc.at[2:3, 0:256]
    lo, st = misc.at[8:16, 0:256], misc.at[16:32, 0:256]
    greet([{"ep": d} for d in others] + [{"rep": d} for d in copies])
    misc[...] = jnp.zeros((32, D), F32)

    low_lanes = iota((8, 128), 1) < HEAD_DIM
    for d in range(EP):
        k_t = wk[:, (d // 2) * 128 : (d // 2 + 1) * 128].astype(F32)
        v_t = wv[:, (d // 2) * 128 : (d // 2 + 1) * 128].astype(F32)
        if d % 2:
            k_t = pltpu.roll(k_t, HEAD_DIM, 1)
        else:
            v_t = pltpu.roll(v_t, HEAD_DIM, 1)
        q_t = wq[:, d * 128 : (d + 1) * 128].astype(F32)
        wsl[d, :16] = jnp.concatenate([q_t, jnp.where(low_lanes, k_t, v_t)], axis=0).astype(BF)
        wsl[d, 16:] = small[...]
    wos[...] = jnp.concatenate(
        [wo_in[:, j * 128 : (j + 1) * 128].astype(F32) for j in range(8)], axis=0
    ).astype(BF)
    stage_w = [remote(wsl.at[d], wg.at[r, e], (s_w, r_w), k, {"ep": d}) for k, d in enumerate(others)]
    stage_o = [remote(wos, wog.at[r, e], (s_o, r_o), k, {"ep": d}) for k, d in enumerate(others)]
    spread_w = [remote(wg.at[r], wg.at[r], (s_w, r_w), 7 + k, {"rep": d}) for k, d in enumerate(copies)]
    spread_o = [remote(wog.at[r], wog.at[r], (s_o, r_o), 7 + k, {"rep": d}) for k, d in enumerate(copies)]
    tokens = RingGather(tok, x_s, (s_tok, r_tok), lsem.at[0])
    grads = RingGather(cot, g_all, (s_cot, r_cot), lsem.at[1])
    for copy in stage_w:
        copy.start()
    tokens.start()
    for copy in stage_o:
        copy.start()
    tables = [
        pltpu.make_async_copy(cos_in, cos_ref, lsem.at[2]),
        pltpu.make_async_copy(sin_in, sin_ref, lsem.at[3]),
    ]
    for copy in tables:
        copy.start()
    wg[r, e] = wsl[e]
    wog[r, e] = wos[...]
    for copy in stage_w:
        copy.wait_recv()
    for copy in spread_w:
        copy.start()
    tokens.forward()

    hit = jnp.zeros((EXPERTS, TOK), F32)
    for k in range(TOP):
        hit = jnp.where(iota((EXPERTS, TOK), 0) == rts[k : k + 1], 1.0, hit)
    before = jnp.where(iota((TOK, TOK), 0) < iota((TOK, TOK), 1), 1.0, 0.0).astype(BF)
    tab_o[:EXPERTS] = jnp.where(hit > 0.0, dot(hit.astype(BF), before), -1.0)
    segs = seg[...]
    opening = jnp.zeros((EP, TOK), F32)
    for value in range(2):
        count = jnp.sum(jnp.where(segs == value, 1.0, 0.0), axis=1, keepdims=True)
        opening = opening + jnp.where(segs > value, jnp.sum(count, axis=0, keepdims=True), 0.0)
    places = (iota((EP, TOK), 0) * TOK + iota((EP, TOK), 1)).astype(F32)
    lo[...] = jnp.maximum(opening, places - (WINDOW - 1))

    tokens.fwd_right.wait_recv()
    tokens.fwd_left.wait_recv()
    tokens.to_peer[2].start()
    for copy in spread_w:
        copy.wait_recv()
    for copy in stage_o:
        copy.wait_recv()
    for copy in spread_o:
        copy.start()

    def unpack(b, carry):
        tile = wg[b // EP, b % EP].astype(F32)
        rows = pl.ds(pl.multiple_of(b * 8, 8), 8)
        w32[rows, 0:128] = tile[0:8]
        w32[rows, 128:256] = tile[8:16]
        w32[rows, 256:384] = tile[16:24]
        gains_s[pl.ds(b, 1)] = tile[24:25]
        return carry

    lax.fori_loop(0, 128, unpack, 0)
    wcol[...] = w32[:, :256].astype(BF)
    rout_o[...] = jnp.transpose(w32[:, 256:384])[:EXPERTS].astype(BF)
    packed = gains_s[...].astype(BF)

    def spread_gain(width, group, base, shift):
        lane = base + iota((128, width), 1) % group
        picked = dot(packed, jnp.where(iota((128, width), 0) == lane, 1.0, 0.0).astype(BF))
        mine = iota((128, width), 0) == shift + iota((128, width), 1) // group
        return jnp.sum(jnp.where(mine, picked, 0.0), axis=0, keepdims=True)

    gain_a[...] = spread_gain(D, 8, 0, 0)
    gain_f[...] = spread_gain(D, 8, 20, 0)
    key_part = spread_gain(128, 4, 16, e * 16)
    gain[:, :128] = spread_gain(128, 8, 8, e * 16)
    gain[:, 128:] = jnp.where(iota((1, 128), 1) < HEAD_DIM, key_part, 1.0)

    tokens.first[4].wait_recv()
    tokens.own.wait()
    tokens.to_peer[1].wait_recv()
    tokens.to_peer[0].wait_recv()

    def project(k, carry):
        @pl.when(k == 6)
        def _():
            tokens.to_peer[2].wait_recv()

        g = k // 2
        b = (2 * (x + g + g // 2 - 2 * (g // 3)) + k % 2) % EP
        rows = block_rows(b)
        values = x_s[rows].astype(F32)
        r1 = lax.rsqrt(jnp.mean(values * values, axis=1, keepdims=True) + EPSILON)
        normed = (values * r1 * gain_a[...]).astype(BF)
        out = dot(normed, wcol[...])
        lin[rows] = out
        sq = out * out
        sums[pl.ds(2 * b, 1)] = lane_row(sq[:, :128])
        sums[pl.ds(2 * b + 1, 1)] = lane_row(jnp.where(first, sq[:, 128:], 0.0))
        return carry

    lax.fori_loop(0, EP, project, 0)
    stats = [remote(sums, held.at[e], (s_st, r_st), k, {"ep": d}) for k, d in enumerate(others)]
    for copy in stats:
        copy.start()
    held[e] = sums[...]
    keep = pltpu.make_async_copy(x_s, x_all, lsem.at[4])
    keep.start()
    for copy in tables:
        copy.wait()
    for copy in stats:
        copy.wait_recv()
    total = held[0]
    for k in range(1, EP):
        total = total + held[k]
    st[...] = total
    grads.start()

    def prepare(b, carry):
        rows = block_rows(b)
        cq = column(lax.rsqrt(st[pl.ds(2 * b, 1)] * (1.0 / D) + EPSILON))
        ck = column(lax.rsqrt(st[pl.ds(2 * b + 1, 1)] * (1.0 / KV) + EPSILON))
        cosine, sine = cos_ref[rows], sin_ref[rows]
        q_o[rows] = turn(lin[rows, :128] * cq * gain[:, :128], cosine, sine).astype(BF)
        kv = lin[rows, 128:]
        kv = jnp.where(first, turn(kv * ck * gain[:, 128:], cosine, sine), kv)
        other = pltpu.roll(kv, HEAD_DIM, 1)
        k_o[rows] = jnp.where(first, kv, other).astype(BF)
        v_o[rows] = jnp.where(first, other, kv).astype(BF)
        return carry

    lax.fori_loop(0, EP, prepare, 0)

    def heads(i, source):
        cols = pl.ds(pl.multiple_of(source * 128, 128), 128)
        return pltpu.make_async_remote_copy(
            src_ref=a_o.at[block_rows(i)],
            dst_ref=att_o.at[:, cols],
            send_sem=s_a.at[i],
            recv_sem=r_a.at[source],
            device_id={"ep": i},
            device_id_type=MESH,
        )

    def queries(i, carry):
        rows = block_rows(i)
        q2_scr[...] = stack_heads(q_o[rows].astype(F32) * HEAD_DIM ** (-0.5)).astype(BF)
        lo_col = column(lo[pl.ds(i, 1)])
        lo_scr[...] = jnp.concatenate([lo_col, lo_col], axis=0)
        m_scr[...] = jnp.full((2 * TOK, 128), MASKED, F32)
        l_scr[...] = jnp.zeros((2 * TOK, 128), F32)
        acc[...] = jnp.zeros((2 * TOK, 128), F32)
        j0 = key_start(i)

        def score(j, inner):
            s = dot_nt(q2_scr[...], k_o[block_rows(j)])
            key = (iota((2 * TOK, TOK), 1) + j * TOK).astype(F32)
            query = (iota((2 * TOK, TOK), 0) % TOK + i * TOK).astype(F32)
            s = jnp.where((key >= lo_scr[:, :1]) & (key <= query), s, MASKED)
            s_scr[j - j0] = s
            m_scr[...] = jnp.maximum(m_scr[...], jnp.maximum(s[:, :128], s[:, 128:]))
            return inner

        lax.fori_loop(j0, i + 1, score, 0)
        m = jnp.max(m_scr[...], axis=1, keepdims=True)
        m_scr[...] = jnp.broadcast_to(m, (2 * TOK, 128))

        def weigh(j, inner):
            p = jnp.exp(s_scr[j - j0] - m_scr[:, :1])
            l_scr[...] += p[:, :128] + p[:, 128:]
            acc[...] += dot(p.astype(BF), v_o[block_rows(j)])
            return inner

        lax.fori_loop(j0, i + 1, weigh, 0)
        total = jnp.sum(l_scr[...], axis=1, keepdims=True)
        a_o[rows] = merge_heads(acc[...] / total).astype(BF)
        lse = jnp.broadcast_to(m_scr[:, :1] + jnp.log(total), (2 * TOK, 128))
        lse_o[i] = jnp.transpose(lse)[:8]

        @pl.when(i != e)
        def _():
            heads(i, e).start()

        @pl.when(i == e)
        def _():
            att_o[:, pl.ds(pl.multiple_of(e * 128, 128), 128)] = a_o[rows]

        @pl.when(i == 4)
        def _():
            grads.forward()

        @pl.when(i == 6)
        def _():
            grads.fwd_right.wait_recv()
            grads.fwd_left.wait_recv()
            grads.to_peer[2].start()

        return carry

    lax.fori_loop(0, EP, queries, 0)

    for copy in spread_o:
        copy.wait_recv()

    def unpack_out(b, carry):
        tile = wog[b // EP, b % EP].astype(F32)
        rows = pl.ds(pl.multiple_of(b * 8, 8), 8)
        for j in range(8):
            w32[rows, j * 128 : (j + 1) * 128] = tile[j * 8 : (j + 1) * 8]
        return carry

    lax.fori_loop(0, 128, unpack_out, 0)
    whole[...] = w32[...].astype(BF)
    for d in others:
        heads(d, d).wait_recv()

    hidden = x_s[block_rows(e)].astype(F32) + dot(att_o[...], whole[...])
    hid_o[...] = hidden
    r2 = lax.rsqrt(jnp.mean(hidden * hidden, axis=1, keepdims=True) + EPSILON)
    moe_in = (hidden * r2 * gain_f[...]).astype(BF)
    m_o[...] = moe_in
    logits = dot_nt(rout_o[...], moe_in)
    chosen = hit > 0.0
    logits = jnp.where(chosen, logits, MASKED)
    raised = jnp.where(chosen, jnp.exp(logits - jnp.max(logits, axis=0, keepdims=True)), 0.0)
    tab_o[EXPERTS:] = raised / jnp.sum(raised, axis=0, keepdims=True)

    grads.first[4].wait_recv()
    for copy in grads.to_peer:
        copy.wait_recv()
    grads.own.wait()
    keep.wait()
    for d in others:
        heads(d, d).wait_send()
    for ring in (tokens, grads):
        for copy in ring.first + [ring.fwd_right, ring.fwd_left] + ring.to_peer:
            copy.wait_send()
    for copy in stage_w + stage_o + spread_w + spread_o + stats:
        copy.wait_send()


def front(*args):
    return comm_call(
        front_kernel,
        "front",
        1,
        [
            shape((LENGTH, D), BF),
            shape((LENGTH, D), BF),
            shape((LENGTH, 256)),
            shape((LENGTH, 128), BF),
            shape((LENGTH, 128), BF),
            shape((LENGTH, 128), BF),
            shape((LENGTH, 128), BF),
            shape((EP, 8, 2 * TOK)),
            shape((TOK, D)),
            shape((TOK, D), BF),
            shape((2 * EXPERTS, TOK)),
            shape((TOK, D), BF),
            shape((32, D)),
            shape((EXPERTS, D), BF),
            shape((D, D), BF),
            shape((D, 256), BF),
        ],
        [ANY, ANY] + [VM] * 7 + [ANY, ANY],
        [ANY, ANY] + [VM] * 14,
        [
            pltpu.VMEM((LENGTH, D), BF),
            pltpu.VMEM((EP, 32, 128), BF),
            pltpu.VMEM((64, 128), BF),
            pltpu.VMEM((REP, EP, 32, 128), BF),
            pltpu.VMEM((REP, EP, 64, 128), BF),
            pltpu.VMEM((D, D), F32),
            pltpu.VMEM((128, 128), F32),
            pltpu.VMEM((LENGTH, 128), F32),
            pltpu.VMEM((LENGTH, 128), F32),
            pltpu.VMEM((16, 256), F32),
            pltpu.VMEM((EP, 16, 256), F32),
            pltpu.VMEM((5, 2 * TOK, TOK), F32),
            pltpu.VMEM((2 * TOK, 128), BF),
            pltpu.VMEM((2 * TOK, 128), F32),
            pltpu.VMEM((2 * TOK, 128), F32),
            pltpu.VMEM((2 * TOK, 128), F32),
            pltpu.VMEM((2 * TOK, 128), F32),
        ]
        + [DMA((10,))] * 4
        + [DMA((22,))] * 4
        + [DMA((7,))] * 2
        + [DMA((8,))] * 2
        + [DMA((5,))],
        limit=60,
    )(*args)


class ChipReduce:
    SEMS = 10
    STEP = 64

    def __init__(self, n, swo, snd, pc, rcv, hop, sems):
        e, x, c = place()
        self.n, self.h = n, n // 2
        h = n // 2
        self.snd, self.pc, self.rcv, self.hop = snd, pc, rcv, hop
        right, left = ep_device((x + 1) % 4, c), ep_device((x + 3) % 4, c)
        peer = ep_device(x, 1 - c)
        self.swap = lambda k: remote(swo.at[k], pc.at[k], sems, k, peer)
        low, high = pl.ds(0, h), pl.ds(h, h)
        self.opp = [
            remote(snd.at[0, low], hop.at[low], sems, 4, right),
            remote(snd.at[0, high], hop.at[high], sems, 5, left),
        ]
        self.near = [
            remote(snd.at[2, high], rcv.at[0, high], sems, 6, right),
            remote(snd.at[1, low], rcv.at[1, low], sems, 7, left),
        ]
        self.far = [
            remote(snd.at[2, low], rcv.at[0, low], sems, 8, right),
            remote(snd.at[1, high], rcv.at[1, high], sems, 9, left),
        ]

    def rows_loop(self, low, count, body):
        step = self.STEP

        def loop(i, carry):
            body(pl.ds(pl.multiple_of(low + i * step, 16), step))
            return carry

        lax.fori_loop(0, count // step, loop, 0)

    def merge(self, k):
        def body(s):
            self.snd[k, s] = (self.snd[k, s].astype(F32) + self.pc[k, s].astype(F32)).astype(BF)

        self.swap(k).wait_recv()
        self.rows_loop(0, self.n, body)

    def merge_hop(self, k, low):
        def body(s):
            self.snd[k, s] = (self.snd[k, s].astype(F32) + self.hop[s].astype(F32)).astype(BF)

        self.rows_loop(low, self.h, body)

    def send_opp(self):
        self.merge(0)
        for copy in self.opp:
            copy.start()

    def send_near(self):
        self.merge(2)
        self.near[0].start()
        self.merge(1)
        self.near[1].start()

    def send_far(self):
        self.opp[0].wait_recv()
        self.merge_hop(2, 0)
        self.far[0].start()
        self.opp[1].wait_recv()
        self.merge_hop(1, self.h)
        self.far[1].start()

    def finish(self, out_ref):
        for copy in self.near + self.far:
            copy.wait_recv()

        def body(s):
            out_ref[s] = self.snd[3, s].astype(F32) + (
                self.rcv[0, s].astype(F32) + self.rcv[1, s].astype(F32)
            )

        self.rows_loop(0, self.n, body)
        for copy in [self.swap(k) for k in range(4)] + self.opp + self.near + self.far:
            copy.wait_send()


ROWS = EP * CAP
HALF = 256
BLOCK = 96


def experts_kernel(
    m_in, t_in, g_in, wg_in, wu_in, wd_in, out_o, gm_o, gg_o, eg_o,
    m_ref, tab, g_ref, wg, wu, wd, a_s, c_s, gl_s, up_s, act_s, dgu_s, y_s, gate_s, gg_s, ggt, eg,
    swo, snd, pc1, rcv1, hop1,
    s_m, r_m, s_t, r_t, s_1, r_1, s_g, r_g, lsem, esem,
):
    e, x, c = place()
    others = ep_others(e)
    greet([{"ep": d} for d in others])
    ring = RingGather(m_in, m_ref, (s_m, r_m), lsem.at[0])
    ring.start()
    tables = [remote(t_in, tab.at[e], (s_t, r_t), k, {"ep": d}) for k, d in enumerate(others)]
    for copy in tables:
        copy.start()
    loads = [
        pltpu.make_async_copy(t_in, tab.at[e], lsem.at[1]),
        pltpu.make_async_copy(wg_in, wg, lsem.at[2]),
        pltpu.make_async_copy(wu_in, wu, lsem.at[3]),
        pltpu.make_async_copy(wd_in, wd, lsem.at[4]),
        pltpu.make_async_copy(g_in, g_ref, lsem.at[5]),
    ]
    for copy in loads:
        copy.start()
    red1 = ChipReduce(TOK, swo, snd, pc1, rcv1, hop1, (s_1, r_1))

    def hits(s, k):
        return iota((CAP, TOK), 0).astype(F32) == tab[s, pl.ds(e * LOCAL + k, 1)]

    def slot_rows(s):
        return pl.ds(pl.multiple_of(s * CAP, 32), CAP)

    def gate_column(s, k, hit):
        row = tab[s, pl.ds(EXPERTS + e * LOCAL + k, 1)]
        return jnp.sum(jnp.where(hit, row, 0.0), axis=1, keepdims=True)

    def one_hot(hit):
        return jnp.where(hit, 1.0, 0.0).astype(BF)

    def combine(s):
        chosen = jnp.concatenate([one_hot(hits(s, k)) for k in range(LOCAL)], axis=0)
        rows = slot_rows(s)
        return dot_tn(chosen, jnp.concatenate([y_s[k, rows] for k in range(LOCAL)], axis=0)).astype(BF)

    def forward(k, carry):
        @pl.when(k == 0)
        def _():
            ring.first[0].wait_recv()
            ring.fwd_right.start()
            ring.first[1].wait_recv()
            ring.fwd_left.start()
            ring.first[4].wait_recv()
            ring.own.wait()
            for copy in tables:
                copy.wait_recv()
            for copy in loads[:4]:
                copy.wait()

        @pl.when(k == 1)
        def _():
            ring.first[3].wait_recv()
            ring.to_peer[1].start()
            ring.first[2].wait_recv()
            ring.to_peer[0].start()
            ring.to_peer[1].wait_recv()

        @pl.when(k == 2)
        def _():
            ring.fwd_right.wait_recv()
            ring.fwd_left.wait_recv()
            ring.to_peer[2].start()
            ring.to_peer[0].wait_recv()

        @pl.when(k == 3)
        def _():
            ring.to_peer[2].wait_recv()

        q = (x + k + k // 2 - 2 * (k // 3)) % 4
        rows = pl.ds(pl.multiple_of(q * 2 * CAP, 64), 2 * CAP)

        def expert(n, inner):
            for core in range(2):
                s = q * 2 + core
                hit = hits(s, n)
                a_s[core * CAP : (core + 1) * CAP] = dot(one_hot(hit), m_ref[block_rows(s)]).astype(BF)
                gate_s[core * CAP : (core + 1) * CAP] = jnp.broadcast_to(gate_column(s, n, hit), (CAP, 128))
            a = a_s[: 2 * CAP]
            gate_lin = dot(a, wg[n])
            up_lin = dot(a, wu[n])
            gl_s[n, rows] = gate_lin.astype(BF)
            up_s[n, rows] = up_lin.astype(BF)
            act = (gate_lin * jax.nn.sigmoid(gate_lin) * up_lin).astype(BF)
            produced = dot(act, wd[n]).astype(BF).astype(F32)
            y_s[n, rows] = (gate_s[: 2 * CAP, :1] * produced).astype(BF)
            return inner

        lax.fori_loop(0, LOCAL, expert, 0)
        slot = 3 - k
        swo[slot] = combine(q * 2 + 1 - c)
        red1.swap(slot).start()
        snd[slot] = combine(q * 2 + c)
        return carry

    lax.fori_loop(0, 4, forward, 0)
    red1.send_opp()
    red1.send_near()
    loads[4].wait()

    def backward(n, carry):
        def pick(s, inner):
            hit = hits(s, n)
            chosen = one_hot(hit)
            rows = slot_rows(s)
            a_s[rows] = dot(chosen, m_ref[block_rows(s)]).astype(BF)
            c_s[rows] = dot(chosen, g_ref[block_rows(s)]).astype(BF)
            gate_s[rows] = jnp.broadcast_to(gate_column(s, n, hit), (CAP, 128))
            return inner

        lax.fori_loop(0, EP, pick, 0)

        def rows_part(k, inner):
            rows = pl.ds(pl.multiple_of(k * HALF, HALF), HALF)
            cot = c_s[rows]
            weight = gate_s[rows][:, :1]
            back = dot_nt(cot, wd[n])
            c_s[rows] = (weight * cot.astype(F32)).astype(BF)
            gate_lin, up_lin = gl_s[n, rows].astype(F32), up_s[n, rows].astype(F32)
            sig = jax.nn.sigmoid(gate_lin)
            silu = gate_lin * sig
            act = silu * up_lin
            act_s[rows] = act.astype(BF)
            gg_s[rows] = jnp.broadcast_to(jnp.sum(act * back, axis=1, keepdims=True), (HALF, 128))
            back = back * weight
            dgate = (back * up_lin * sig * (1.0 + gate_lin * (1.0 - sig))).astype(BF)
            dup = (back * silu).astype(BF)
            dgu_s[rows, :FF] = dgate
            dgu_s[rows, FF:] = dup
            y_s[n, rows] = (dot_nt(dgate, wg[n]) + dot_nt(dup, wu[n])).astype(BF)
            return inner

        lax.fori_loop(0, ROWS // HALF, rows_part, 0)

        def gates_back(s, inner):
            column_ = gg_s[slot_rows(s)][:, :1]
            ggt[s, pl.ds(n, 1)] = jnp.sum(jnp.where(hits(s, n), column_, 0.0), axis=0, keepdims=True)
            return inner

        lax.fori_loop(0, EP, gates_back, 0)

        @pl.when(n == 0)
        def _():
            red1.merge(3)
            red1.send_far()

        @pl.when(n == 2)
        def _():
            red1.finish(out_o)

        @pl.when(n > 0)
        def _():
            pltpu.make_async_copy(eg, eg_o.at[n - 1], esem).wait()

        eg[:, :64, :FF] = dot_tn(a_s[...], dgu_s[:, :FF]).astype(BF).reshape(REP, 64, FF)
        eg[:, :64, FF:] = dot_tn(a_s[...], dgu_s[:, FF:]).astype(BF).reshape(REP, 64, FF)
        eg[:, 64:] = dot_tn(act_s[...], c_s[...]).astype(BF).reshape(REP, 32, D)
        pltpu.make_async_copy(eg, eg_o.at[n], esem).start()
        return carry

    lax.fori_loop(0, LOCAL, backward, 0)
    gates = [remote(ggt.at[d], gg_o.at[e], (s_g, r_g), k, {"ep": d}) for k, d in enumerate(others)]
    own = pltpu.make_async_copy(ggt.at[e], gg_o.at[e], lsem.at[8])
    for copy in gates + [own]:
        copy.start()
    spill = []
    for k, q in enumerate([(x + 2) % 4, (x + 3) % 4, (x + 1) % 4, x]):
        for core, buffer in ((1 - c, swo), (c, snd)):
            buffer[k] = combine(q * 2 + core)
            spill.append(pltpu.make_async_copy(buffer.at[k], gm_o.at[block_rows(q * 2 + core)], lsem.at[len(spill)]))
            spill[-1].start()
    for copy in spill:
        copy.wait()
    own.wait()
    pltpu.make_async_copy(eg, eg_o.at[LOCAL - 1], esem).wait()
    for copy in gates:
        copy.wait_recv()
    for copy in ring.first + [ring.fwd_right, ring.fwd_left] + ring.to_peer + tables + gates:
        copy.wait_send()


def experts(m, t, g_all, wg, wu, wd):
    return comm_call(
        experts_kernel,
        "experts",
        4,
        [
            shape((TOK, D)),
            shape((LENGTH, D), BF),
            shape((EP, 8, TOK)),
            shape((LOCAL, REP, BLOCK, D), BF),
        ],
        [ANY] * 6,
        [VM, ANY, ANY, ANY],
        [
            pltpu.VMEM((LENGTH, D), BF),
            pltpu.VMEM((EP, 2 * EXPERTS, TOK), F32),
            pltpu.VMEM((LENGTH, D), BF),
            pltpu.VMEM((LOCAL, D, FF), BF),
            pltpu.VMEM((LOCAL, D, FF), BF),
            pltpu.VMEM((LOCAL, FF, D), BF),
            pltpu.VMEM((ROWS, D), BF),
            pltpu.VMEM((ROWS, D), BF),
            pltpu.VMEM((LOCAL, ROWS, FF), BF),
            pltpu.VMEM((LOCAL, ROWS, FF), BF),
            pltpu.VMEM((ROWS, FF), BF),
            pltpu.VMEM((ROWS, D), BF),
            pltpu.VMEM((LOCAL, ROWS, D), BF),
            pltpu.VMEM((ROWS, 128), F32),
            pltpu.VMEM((ROWS, 128), F32),
            pltpu.VMEM((EP, 8, TOK), F32),
            pltpu.VMEM((REP, BLOCK, D), BF),
            pltpu.VMEM((4, TOK, D), BF),
            pltpu.VMEM((4, TOK, D), BF),
        ]
        + [pltpu.VMEM((4, TOK, D), BF), pltpu.VMEM((2, TOK, D), BF), pltpu.VMEM((TOK, D), BF)]
        + [DMA((10,))] * 2
        + [DMA((7,))] * 2
        + [DMA((10,))] * 2
        + [DMA((7,))] * 2
        + [DMA((9,)), DMA(())],
        limit=63,
    )(m, t, g_all, wg, wu, wd)


def back_kernel(
    gm_in, mixed_in, gg_in, tab_in, hid_in, m_in, cot_in, att_in, misc_in, rout_in, whole_in, wcol_in, x_in, lin_in,
    q_in, k_in, v_in, a_in, lse_in, cos_in, sin_in,
    out_o, ig_o, wb_o, dw_o, vec_o,
    mixed, gg, tab, hid, m_s, cot, att, misc, rout, whole, wcol, x_s, lin, q_s, k_s, v_s, a_s, lse, cos_ref, sin_ref,
    gm, gh, ga_s, go, q2_s, p_s, do2, row_s, dq, dk, dv, u_s, sums, st2, held, wb, wsum, wheld,
    dwt, dws, dheld, dsum, vec, vheld, vtot, vheld2, swo, snd, pc1, rcv1, hop1, pc2, rcv2, hop2, snd3, pc3, rcv3, hop3,
    s_1, r_1, s_2, r_2, s_3, r_3, s_go, r_go, s_st, r_st, s_w, r_w, s_d, r_d, s_e, r_e, s_v, r_v, s_v2, r_v2, lsem, l_1, l_3,
):
    r = lax.axis_index("rep")
    e, x, c = place()
    others = ep_others(e)
    copies = rep_others(r)
    first = iota((TOK, 128), 1) < HEAD_DIM
    gain_a, gain_f, gain = misc.at[0:1], misc.at[1:2], misc.at[2:3, 0:256]
    lo, st = misc.at[8:16, 0:256], misc.at[16:32, 0:256]
    greet([{"ep": d} for d in others] + [{"rep": d} for d in copies])
    red1 = RingReduce(gm_in, TOK, pc1, snd, rcv1, hop1, (s_1, r_1), l_1)
    red2 = ChipReduce(TOK, swo, snd, pc2, rcv2, hop2, (s_2, r_2))
    red3 = RingReduce(wb, 128, pc3, snd3, rcv3, hop3, (s_3, r_3), l_3)
    red1.start()
    loads = [
        pltpu.make_async_copy(src, dst, lsem.at[k])
        for k, (src, dst) in enumerate(
            [
                (q_in, q_s), (k_in, k_s), (misc_in, misc), (lse_in, lse), (mixed_in, mixed), (gg_in, gg),
                (tab_in, tab), (hid_in, hid), (m_in, m_s), (cot_in, cot), (att_in, att), (rout_in, rout),
                (whole_in, whole), (v_in, v_s), (a_in, a_s), (cos_in, cos_ref), (sin_in, sin_ref),
                (lin_in, lin), (x_in, x_s), (wcol_in, wcol),
            ]
        )
    ]
    for copy in loads:
        copy.start()
    for copy in loads[:4]:
        copy.wait()

    def tile(i, j):
        cut = jnp.minimum(i, 4)
        return cut * (cut + 1) // 2 + 5 * jnp.maximum(i - 4, 0) + j - key_start(i)

    def probabilities(i, carry):
        q2_s[i] = stack_heads(q_s[block_rows(i)].astype(F32) * HEAD_DIM ** (-0.5)).astype(BF)
        row_s[1:2] = lse[i][0:1]
        row_s[2:3] = jnp.concatenate([lo[pl.ds(i, 1)]] * 2, axis=1)

        def keys(j, inner):
            key = (iota((TOK, 2 * TOK), 0) + j * TOK).astype(F32)
            query = (iota((TOK, 2 * TOK), 1) % TOK + i * TOK).astype(F32)
            allowed = (key >= row_s[2:3]) & (key <= query)
            s = dot_nt(k_s[block_rows(j)], q2_s[i])
            p_s[tile(i, j)] = jnp.where(allowed, jnp.exp(s - row_s[1:2]), 0.0).astype(BF)
            return inner

        lax.fori_loop(key_start(i), i + 1, keys, 0)

        @pl.when(i == 1)
        def _():
            red1.push_opp()

        @pl.when(i == 3)
        def _():
            red1.push_near()

        @pl.when(i == 5)
        def _():
            red1.relay()

        return carry

    lax.fori_loop(0, EP, probabilities, 0)
    for copy in loads[4:]:
        copy.wait()
    red1.finish(gm)

    hidden = hid[...]
    weights = tab[EXPERTS:]
    grads = jnp.concatenate([gg[d][:LOCAL] for d in range(EP)], axis=0)
    mean = jnp.sum(weights * grads, axis=0, keepdims=True)
    grad_logits = weights * (grads - mean)
    grad_moe = gm[...] + dot_tn(grad_logits.astype(BF), rout[...])
    r2 = lax.rsqrt(jnp.mean(hidden * hidden, axis=1, keepdims=True) + EPSILON)
    n = hidden * r2
    u = grad_moe * gain_f[...]
    grad_hidden = cot[...].astype(F32) + r2 * (u - n * jnp.mean(u * n, axis=1, keepdims=True))
    gh[...] = grad_hidden
    branch = grad_hidden.astype(BF)
    ga_s[...] = dot_nt(branch, whole[...]).astype(BF)

    def own_cols(ref, b):
        return ref.at[:, pl.ds(pl.multiple_of(b * 128, 128), 128)]

    heads = [
        remote(own_cols(ga_s, d), go.at[block_rows(e)], (s_go, r_go), k, {"ep": d}) for k, d in enumerate(others)
    ]
    for copy in heads:
        copy.start()
    go[block_rows(e)] = own_cols(ga_s, e)[...]
    out_o[...] = (hidden + mixed[...]).astype(BF)
    ffn = jnp.sum(grad_moe * n, axis=0, keepdims=True)
    logit_rows = jnp.transpose(jnp.concatenate([grad_logits, jnp.zeros((96, TOK), F32)], axis=0)).astype(BF)
    router_rows = dot_tn(m_s[...], logit_rows)
    lane = iota((D, 128), 1)
    router_rows = jnp.where(lane == EXPERTS, column(ffn), router_rows).reshape(REP, EP, 8, 128)
    out_rows = dot_tn(att[...], branch).reshape(REP, EP, 8, D)
    for d in range(EP):
        wb[d * 128 : (d + 1) * 128, :D] = out_rows[:, d].reshape(128, D).astype(BF)
        wb[d * 128 : (d + 1) * 128, D:] = router_rows[:, d].reshape(128, 128).astype(BF)
    red3.start()
    dk[...] = jnp.zeros((LENGTH, 128), F32)
    dv[...] = jnp.zeros((LENGTH, 128), F32)
    for copy in heads:
        copy.wait_recv()

    def part(ref, b, size):
        return ref.at[pl.ds(pl.multiple_of(b * size, 8), size)]

    spread_w = [remote(part(wsum, d, 8), wheld.at[r], (s_w, r_w), k, {"rep": d}) for k, d in enumerate(copies)]

    def queries(i, carry):
        rows = block_rows(i)
        grad = stack_heads(go[rows].astype(F32))
        do2[...] = grad.astype(BF)
        out = a_s[rows].astype(F32)
        row_s[0:1] = lane_row(grad * jnp.concatenate([out, out], axis=0))
        dq[...] = jnp.zeros((128, 2 * TOK), F32)

        def keys(j, inner):
            key_rows = block_rows(j)
            p = p_s[tile(i, j)]
            dp = dot_nt(v_s[key_rows], do2[...])
            ds = (p.astype(F32) * (dp - row_s[0:1])).astype(BF)
            dv[key_rows] += dot(p, do2[...])
            dk[key_rows] += dot(ds, q2_s[i])
            dq[...] += dot_tn(k_s[key_rows], ds)
            return inner

        lax.fori_loop(key_start(i), i + 1, keys, 0)
        grad_q = merge_heads(jnp.transpose(dq[...])) * HEAD_DIM ** (-0.5)
        grad_q = turn(grad_q.astype(BF).astype(F32), cos_ref[rows], -sin_ref[rows])
        u_s[rows, :128] = grad_q
        cq = column(lax.rsqrt(st[pl.ds(2 * i, 1)] * (1.0 / D) + EPSILON))
        sums[pl.ds(2 * i, 1)] = lane_row(grad_q * gain[:, :128] * lin[rows, :128] * cq)

        @pl.when(i == 2)
        def _():
            red3.push_opp()
            red3.push_near()

        @pl.when(i == 4)
        def _():
            red3.relay()

        @pl.when(i == 6)
        def _():
            red3.finish(wsum)
            for copy in spread_w:
                copy.start()
            wheld[r] = part(wsum, r, 8)[...]

        return carry

    lax.fori_loop(0, EP, queries, 0)

    def close(b, carry):
        rows = block_rows(b)
        grad_k, grad_v = dk[rows], dv[rows]
        grad_k = grad_k + pltpu.roll(grad_k, HEAD_DIM, 1)
        grad_v = grad_v + pltpu.roll(grad_v, HEAD_DIM, 1)
        both = jnp.where(first, grad_k, grad_v).astype(BF).astype(F32)
        both = jnp.where(first, turn(both, cos_ref[rows], -sin_ref[rows]), both)
        u_s[rows, 128:] = both
        ck = column(lax.rsqrt(st[pl.ds(2 * b + 1, 1)] * (1.0 / KV) + EPSILON))
        sums[pl.ds(2 * b + 1, 1)] = lane_row(jnp.where(first, both * gain[:, 128:] * lin[rows, 128:] * ck, 0.0))
        return carry

    lax.fori_loop(0, EP, close, 0)
    stats = [remote(sums, held.at[e], (s_st, r_st), k, {"ep": d}) for k, d in enumerate(others)]
    for copy in stats:
        copy.start()
    held[e] = sums[...]
    dwt[...] = jnp.zeros((256, D), F32)
    vec[...] = jnp.zeros((8, D), F32)
    for copy in stats:
        copy.wait_recv()
    total = held[0]
    for k in range(1, EP):
        total = total + held[k]
    st2[...] = total

    def project_back(b):
        rows = block_rows(b)
        values = x_s[rows].astype(F32)
        r1 = lax.rsqrt(jnp.mean(values * values, axis=1, keepdims=True) + EPSILON)
        n1 = values * r1
        normed = (n1 * gain_a[...]).astype(BF)
        cq = column(lax.rsqrt(st[pl.ds(2 * b, 1)] * (1.0 / D) + EPSILON))
        ck = column(lax.rsqrt(st[pl.ds(2 * b + 1, 1)] * (1.0 / KV) + EPSILON))
        mq = column(st2[pl.ds(2 * b, 1)] * (1.0 / D))
        mk = column(st2[pl.ds(2 * b + 1, 1)] * (1.0 / KV))
        uq, uk = u_s[rows, :128], u_s[rows, 128:]
        nq = lin[rows, :128] * cq
        nk = lin[rows, 128:] * ck
        gq = cq * (uq * gain[:, :128] - nq * mq)
        gk = jnp.where(first, ck * (uk * gain[:, 128:] - nk * mk), uk)
        glin = jnp.concatenate([gq, gk], axis=1).astype(BF)
        vec[1:2, :128] += jnp.sum(uq * nq, axis=0, keepdims=True)
        vec[2:3, :128] += jnp.sum(uk * nk, axis=0, keepdims=True)
        gn = dot_nt(glin, wcol[...])
        vec[0:1] += jnp.sum(gn * n1, axis=0, keepdims=True)
        dwt[...] += dot_tn(glin, normed)
        return gn.astype(BF)

    def chips(k, carry):
        q = (x + 2 + k - (k // 2) * (2 * k - 1)) % 4
        swo[k] = project_back(q * 2 + 1 - c)
        red2.swap(k).start()
        snd[k] = project_back(q * 2 + c)

        @pl.when(k == 1)
        def _():
            red2.send_opp()

        @pl.when(k == 2)
        def _():
            red2.send_near()

        return carry

    lax.fori_loop(0, 4, chips, 0)
    dws[...] = jnp.transpose(dwt[...])
    spread_d = [remote(part(dws, d, 64), dheld.at[r], (s_d, r_d), k, {"rep": d}) for k, d in enumerate(copies)]
    for copy in spread_d:
        copy.start()
    dheld[r] = part(dws, r, 64)[...]
    gain_q, gain_k = vec[1:2, :128], jnp.where(iota((1, 128), 1) < HEAD_DIM, vec[2:3, :128], 0.0)
    gain_k = jnp.where(e % 2 == 1, pltpu.roll(gain_k, HEAD_DIM, 1), gain_k)
    vec[1:3, :128] = jnp.zeros((2, 128), F32)
    vec[1:2, pl.ds(pl.multiple_of(e * 128, 128), 128)] = gain_q
    vec[2:3, pl.ds(pl.multiple_of(e // 2 * 128, 128), 128)] = gain_k
    spread_v = [remote(vec, vheld.at[e], (s_v, r_v), k, {"ep": d}) for k, d in enumerate(others)]
    for copy in spread_v:
        copy.start()
    vheld[e] = vec[...]
    red2.merge(3)
    for copy in spread_v:
        copy.wait_recv()
    total = vheld[0]
    for k in range(1, EP):
        total = total + vheld[k]
    vtot[...] = total
    spread_v2 = [remote(vtot, vheld2.at[r], (s_v2, r_v2), k, {"rep": d}) for k, d in enumerate(copies)]
    for copy in spread_v2:
        copy.start()
    vheld2[r] = vtot[...]
    red2.send_far()
    for copy in spread_w:
        copy.wait_recv()
    total = wheld[0]
    for k in range(1, REP):
        total = total + wheld[k]
    wb_o[...] = total
    for copy in spread_d:
        copy.wait_recv()
    total = dheld[0]
    for k in range(1, REP):
        total = total + dheld[k]
    dsum[...] = total
    spread_e = [remote(part(dsum, d, 8), dw_o.at[e], (s_e, r_e), k, {"ep": d}) for k, d in enumerate(others)]
    for copy in spread_e:
        copy.start()
    dw_o[e] = part(dsum, e, 8)[...]
    for copy in spread_v2:
        copy.wait_recv()
    total = vheld2[0]
    for k in range(1, REP):
        total = total + vheld2[k]
    start = r * EP + e
    rows_d, lanes_d = iota((D, 128), 0), iota((D, 128), 1)
    eight = jnp.where((rows_d == start * 8 + lanes_d) & (lanes_d < 8), 1.0, 0.0)
    four = jnp.where((rows_d == start * 4 + lanes_d) & (lanes_d < 4), 1.0, 0.0)

    def pick(sel):
        return jnp.dot(total, sel, preferred_element_type=F32, precision=HIGH)

    vec_o[...] = jnp.where(iota((8, 128), 0) == 2, pick(four), pick(eight))
    red2.finish(gm)
    values = x_s[block_rows(e)].astype(F32)
    r1 = lax.rsqrt(jnp.mean(values * values, axis=1, keepdims=True) + EPSILON)
    n1 = values * r1
    z = gm[...] * gain_a[...]
    ig_o[...] = gh[...] + r1 * (z - n1 * jnp.mean(z * n1, axis=1, keepdims=True))
    for copy in spread_e:
        copy.wait_recv()
    for copy in heads + stats + spread_w + spread_d + spread_e + spread_v + spread_v2:
        copy.wait_send()


def back(*args):
    def vm(dims, dtype=F32):
        return pltpu.VMEM(dims, dtype)

    held = [vm(a.shape, a.dtype) for a in args[1:12]] + [vm(args[12].shape, BF)] + [vm(a.shape, a.dtype) for a in args[13:]]
    landing = [vm((4, TOK, D), BF), vm((2, TOK, D), BF), vm((TOK, D), BF)]
    return comm_call(
        back_kernel,
        "back",
        6,
        [shape((TOK, D), BF), shape((TOK, D)), shape((8, WB)), shape((EP, 8, 256)), shape((8, 128))],
        [ANY] * 21,
        [VM] * 5,
        held
        + [
            vm((TOK, D)),
            vm((TOK, D)),
            vm((TOK, D), BF),
            vm((LENGTH, 128), BF),
            vm((EP, 2 * TOK, 128), BF),
            vm((30, TOK, 2 * TOK), BF),
            vm((2 * TOK, 128), BF),
            vm((8, 2 * TOK)),
            vm((128, 2 * TOK)),
            vm((LENGTH, 128)),
            vm((LENGTH, 128)),
            vm((LENGTH, 256)),
            vm((16, 256)),
            vm((16, 256)),
            vm((EP, 16, 256)),
            vm((D, WB), BF),
            vm((128, WB)),
            vm((REP, 8, WB)),
            vm((256, D)),
            vm((D, 256)),
            vm((REP, 64, 256)),
            vm((64, 256)),
            vm((8, D)),
            vm((EP, 8, D)),
            vm((8, D)),
            vm((REP, 8, D)),
            vm((4, TOK, D), BF),
            vm((4, TOK, D), BF),
        ]
        + landing * 2
        + [vm((4, 128, WB), BF), vm((4, 128, WB), BF), vm((2, 128, WB), BF), vm((128, WB), BF)]
        + [DMA((10,))] * 6
        + [DMA((7,))] * 4
        + [DMA((15,))] * 4
        + [DMA((7,))] * 4
        + [DMA((15,))] * 2
        + [DMA((20,)), DMA((4,)), DMA((4,))],
        limit=63,
    )(*args)


def body(
    tokens,
    segments,
    routes,
    w_query,
    w_key,
    w_value,
    w_out,
    w_router,
    gain_attn,
    gain_query,
    gain_key,
    gain_ffn,
    w_gate,
    w_up,
    w_down,
    out_grad,
):
    gains = jnp.concatenate([gain_attn, gain_query, gain_key, gain_ffn]).reshape(1, 28)
    small = jnp.concatenate(
        [jnp.pad(w_router, ((0, 0), (0, 128 - EXPERTS))), jnp.pad(gains, ((0, 7), (0, 100)))], axis=0
    )
    cosine, sine = turn_tables()
    (
        x_all, g_all, lin, q, k, v, att, lse, hidden, moe_in, tables, attended, misc, router, whole_out, w_cols,
    ) = front(
        tokens, out_grad, w_query, w_key, w_value, w_out, small, segments.reshape(EP, TOK), routes.T, cosine, sine
    )
    mixed, grad_rows, gg, grads = experts(moe_in, tables, g_all, w_gate, w_up, w_down)
    grads = grads.reshape(LOCAL, REP * BLOCK, D)
    expert_sums = lax.psum_scatter(grads, "rep", scatter_dimension=1, tiled=True).astype(F32)
    output, input_grad, wb_sum, dw_sum, vec = back(
        grad_rows, mixed, gg, tables, hidden, moe_in, out_grad, attended, misc, router, whole_out, w_cols, x_all, lin,
        q, k, v, att, lse, cosine, sine,
    )
    dw_rows = dw_sum.transpose(1, 0, 2)
    return (
        output,
        input_grad,
        dw_rows[:, :, :128].reshape(8, D),
        dw_rows[:, :, 128:192].reshape(8, KV),
        dw_rows[:, :, 192:].reshape(8, KV),
        wb_sum[:, :D],
        wb_sum[:, D : D + EXPERTS],
        vec[0, :8],
        vec[1, :8],
        vec[2, :4],
        wb_sum[:, D + EXPERTS],
        expert_sums[:, :64, :FF],
        expert_sums[:, :64, FF:],
        expert_sums[:, 64:],
    )


def solution(mesh):
    both = P(("rep", "ep"), None)
    line = P(("rep", "ep"))
    owner = P("ep", None, None)
    kept = P("ep", "rep", None)
    return jax.shard_map(
        body,
        mesh=mesh,
        in_specs=(both, P("rep", None)) + (both,) * 6 + (line,) * 4 + (owner,) * 3 + (both,),
        out_specs=(both,) * 7 + (line,) * 4 + (kept,) * 3,
        check_vma=False,
    )
```

```python
import functools

import jax
import jax.numpy as jnp
import numpy as np
from jax import lax
from jax.experimental import pallas as pl
from jax.experimental.pallas import tpu as pltpu
from jax.sharding import PartitionSpec as P

BF = jnp.bfloat16
F32 = jnp.float32
MESH = pl.DeviceIdType.MESH
ANY = pl.BlockSpec(memory_space=pl.ANY)
VM = pl.BlockSpec(memory_space=pltpu.VMEM)
DMA = pltpu.SemaphoreType.DMA
MIB = 1 << 20

HEADS = 16
KV_HEADS = 8
HEAD_DIM = 64
TOP = 8
WINDOW = 1024
EPSILON = 1e-06
ROPE_BASE = 10000.0
MASKED = -1e30
EP = 8
REP = 16
TOK = 256
LENGTH = 2048
D = 1024
KV = 512
FF = 512
EXPERTS = 32
LOCAL = 4
CAP = 88
NT = (((1,), (1,)), ((), ()))
TN = (((0,), (0,)), ((), ()))
HIGH = lax.Precision.HIGHEST


def dot(a, b):
    return jnp.dot(a, b, preferred_element_type=F32)


def dot_nt(a, b, precision=None):
    return lax.dot_general(a, b, NT, preferred_element_type=F32, precision=precision)


def dot_tn(a, b):
    return lax.dot_general(a, b, TN, preferred_element_type=F32)


def iota(shape, dim):
    return lax.broadcasted_iota(jnp.int32, shape, dim)


def ep_device(x, c):
    return {"ep": x * 2 + c}


def greet(devices):
    barrier = pltpu.get_barrier_semaphore()
    for device in devices:
        pl.semaphore_signal(barrier, inc=1, device_id=device, device_id_type=MESH)
    pl.semaphore_wait(barrier, len(devices))


def remote(src, dst, sems, i, device):
    return pltpu.make_async_remote_copy(
        src_ref=src,
        dst_ref=dst,
        send_sem=sems[0].at[i],
        recv_sem=sems[1].at[i],
        device_id=device,
        device_id_type=MESH,
    )


def place():
    e = lax.axis_index("ep")
    return e, e // 2, e % 2


def ep_others(e):
    return [(e + k) % EP for k in range(1, EP)]


def rep_others(r):
    return [(r + k) % REP for k in range(1, REP)]


class RingGather:
    SEMS = 10

    def __init__(self, x_ref, o_ref, sems, lsem):
        e, x, c = place()
        self.n = n = x_ref.shape[0]
        h = n // 2
        self.o_ref = o_ref
        right, left = ep_device((x + 1) % 4, c), ep_device((x + 3) % 4, c)
        peer = ep_device(x, 1 - c)
        b_left, b_right, b_opp = (((x + 3) % 4) * 2 + c, ((x + 1) % 4) * 2 + c, ((x + 2) % 4) * 2 + c)

        def rows(b, off=0, size=n):
            return o_ref.at[pl.ds(pl.multiple_of(b * n + off, 16), size)]

        low, high = x_ref.at[pl.ds(0, h)], x_ref.at[pl.ds(h, h)]
        self.first = [
            remote(low, rows(e, 0, h), sems, 0, right),
            remote(high, rows(e, h, h), sems, 2, left),
            remote(high, rows(e, h, h), sems, 1, right),
            remote(low, rows(e, 0, h), sems, 3, left),
            remote(x_ref, rows(e), sems, 4, peer),
        ]
        self.fwd_right = remote(rows(b_left, 0, h), rows(b_left, 0, h), sems, 5, right)
        self.fwd_left = remote(rows(b_right, h, h), rows(b_right, h, h), sems, 6, left)
        self.to_peer = [
            remote(rows(b_left), rows(b_left), sems, 7, peer),
            remote(rows(b_right), rows(b_right), sems, 8, peer),
            remote(rows(b_opp), rows(b_opp), sems, 9, peer),
        ]
        self.own = pltpu.make_async_copy(x_ref, rows(e), lsem)

    def start(self):
        for copy in self.first:
            copy.start()
        self.own.start()

    def forward_half(self):
        self.first[0].wait_recv()
        self.fwd_right.start()
        self.first[1].wait_recv()
        self.fwd_left.start()

    def forward_rest(self):
        self.first[2].wait_recv()
        self.to_peer[0].start()
        self.first[3].wait_recv()
        self.to_peer[1].start()

    def finish(self):
        self.fwd_right.wait_recv()
        self.fwd_left.wait_recv()
        self.to_peer[2].start()
        self.first[4].wait_recv()
        for copy in self.to_peer:
            copy.wait_recv()
        self.own.wait()
        for copy in self.first + [self.fwd_right, self.fwd_left] + self.to_peer:
            copy.wait_send()


class RingReduce:
    SEMS = 10
    STEP = 64

    def __init__(self, p_ref, n, pc, snd, rcv, hop, sems, lsems):
        e, x, c = place()
        self.n, self.h = n, n // 2
        h = n // 2
        self.pc, self.snd, self.rcv, self.hop = pc, snd, rcv, hop
        right, left = ep_device((x + 1) % 4, c), ep_device((x + 3) % 4, c)
        peer = ep_device(x, 1 - c)

        def rows(b):
            return p_ref.at[pl.ds(pl.multiple_of(b * n, 16), n)]

        chips = [(x + 2) % 4, (x + 1) % 4, (x + 3) % 4, x]
        self.swap = [remote(rows(b * 2 + 1 - c), pc.at[k], sems, k, peer) for k, b in enumerate(chips)]
        self.load = [
            pltpu.make_async_copy(rows(b * 2 + c), snd.at[k], lsems.at[k]) for k, b in enumerate(chips)
        ]
        low, high = pl.ds(0, h), pl.ds(h, h)
        self.opp = [
            remote(snd.at[0, low], hop.at[low], sems, 4, right),
            remote(snd.at[0, high], hop.at[high], sems, 5, left),
        ]
        self.near = [
            remote(snd.at[1, high], rcv.at[0, high], sems, 6, right),
            remote(snd.at[2, low], rcv.at[1, low], sems, 7, left),
        ]
        self.far = [
            remote(snd.at[1, low], rcv.at[0, low], sems, 8, right),
            remote(snd.at[2, high], rcv.at[1, high], sems, 9, left),
        ]

    def rows_loop(self, low, count, body):
        step = self.STEP

        def loop(i, carry):
            body(pl.ds(pl.multiple_of(low + i * step, 16), step))
            return carry

        lax.fori_loop(0, count // step, loop, 0)

    def merge(self, k):
        def body(s):
            self.snd[k, s] = (self.snd[k, s].astype(F32) + self.pc[k, s].astype(F32)).astype(BF)

        self.load[k].wait()
        self.swap[k].wait_recv()
        self.rows_loop(0, self.n, body)

    def merge_hop(self, k, low):
        def body(s):
            self.snd[k, s] = (self.snd[k, s].astype(F32) + self.hop[s].astype(F32)).astype(BF)

        self.rows_loop(low, self.h, body)

    def start(self):
        for copy in self.swap + self.load:
            copy.start()

    def push_opp(self):
        self.merge(0)
        for copy in self.opp:
            copy.start()

    def push_near(self):
        self.merge(1)
        self.near[0].start()
        self.merge(2)
        self.near[1].start()
        self.merge(3)

    def relay(self):
        self.opp[0].wait_recv()
        self.merge_hop(1, 0)
        self.far[0].start()
        self.opp[1].wait_recv()
        self.merge_hop(2, self.h)
        self.far[1].start()

    def finish(self, out_ref):
        for copy in self.near + self.far:
            copy.wait_recv()

        def body(s):
            out_ref[s] = self.snd[3, s].astype(F32) + (
                self.rcv[0, s].astype(F32) + self.rcv[1, s].astype(F32)
            )

        self.rows_loop(0, self.n, body)
        for copy in self.swap + self.opp + self.near + self.far:
            copy.wait_send()


class AxisReduce:
    def __init__(self, devices, snd, hop, rcv, sems, base):
        right, left = devices
        self.snd, self.hop, self.rcv = snd, hop, rcv
        self.opp = [
            remote(snd.at[0, 0], hop.at[0], sems, base, right),
            remote(snd.at[0, 1], hop.at[1], sems, base + 1, left),
        ]
        self.near = [
            remote(snd.at[2, 1], rcv.at[0, 1], sems, base + 2, right),
            remote(snd.at[1, 0], rcv.at[1, 0], sems, base + 3, left),
        ]
        self.far = [
            remote(snd.at[2, 0], rcv.at[0, 0], sems, base + 4, right),
            remote(snd.at[1, 1], rcv.at[1, 1], sems, base + 5, left),
        ]

    def push(self):
        for copy in self.opp + self.near:
            copy.start()

    def relay(self):
        for k, (slot, half) in enumerate(((2, 0), (1, 1))):
            self.opp[k].wait_recv()
            self.snd[slot, half] = (self.snd[slot, half].astype(F32) + self.hop[half].astype(F32)).astype(BF)
            self.far[k].start()

    def arrive(self):
        for copy in self.near + self.far:
            copy.wait_recv()

    def total(self, *index):
        return self.snd[(3,) + index].astype(F32) + (
            self.rcv[(0,) + index].astype(F32) + self.rcv[(1,) + index].astype(F32)
        )

    def leave(self):
        for copy in self.opp + self.near + self.far:
            copy.wait_send()


class GridReduce:
    def __init__(self, along_z, src, cols, snd, hop, rcv, snd2, hop2, rcv2, sems, lsems):
        r = lax.axis_index("rep")
        z, y = r // 4, r % 4
        along = (lambda k: {"rep": (z + k) % 4 * 4 + y}, lambda k: {"rep": z * 4 + (y + k) % 4})
        one, two = along if along_z else along[::-1]
        here, self.there = (z, y) if along_z else (y, z)
        offsets = (2, 3, 1, 0)
        cut = pl.ds(cols, FF)
        self.load = []
        for k, off in enumerate(offsets):
            b = (here + off) % 4
            block = src.at[:, b, :, :, cut] if along_z else src.at[:, :, b, :, cut]
            self.load.append(pltpu.make_async_copy(block, snd.at[k], lsems.at[k]))
        self.offsets, self.snd2 = offsets, snd2
        self.stage = AxisReduce((one(1), one(3)), snd, hop, rcv, sems, 0)
        self.last = AxisReduce((two(1), two(3)), snd2, hop2, rcv2, sems, 6)

    def push(self):
        for copy in self.load:
            copy.wait()
        self.stage.push()

    def turn(self):
        self.stage.arrive()
        for k, off in enumerate(self.offsets):
            b = (self.there + off) % 4
            for n in range(PAIR):
                self.snd2[k, n] = self.stage.total(n, b).astype(BF)
        self.last.push()

    def finish(self, out_ref, cols):
        self.last.arrive()
        for n in range(PAIR):
            out_ref[n, :, cols : cols + FF] = self.last.total(n).astype(BF)
        self.stage.leave()
        self.last.leave()


def grid_scratch():
    blocks = [(4, PAIR, 4, BLOCK, FF), (PAIR, 4, BLOCK, FF), (2, PAIR, 4, BLOCK, FF)]
    blocks += [(4, PAIR, BLOCK, FF), (PAIR, BLOCK, FF), (2, PAIR, BLOCK, FF)]
    return [pltpu.VMEM(dims, BF) for dims in blocks]


def comm_call(kernel, name, collective_id, out_shape, in_specs, out_specs, scratch, limit=48):
    return pl.pallas_call(
        kernel,
        out_shape=out_shape,
        in_specs=in_specs,
        out_specs=out_specs,
        scratch_shapes=scratch,
        compiler_params=pltpu.CompilerParams(
            collective_id=collective_id, has_side_effects=True, vmem_limit_bytes=limit * MIB
        ),
        name=name,
    )


def shape(dims, dtype=F32):
    return jax.ShapeDtypeStruct(dims, dtype)


WB = D + 128


def column(row):
    return jnp.transpose(jnp.broadcast_to(row, (128, row.shape[1])))


def lane_row(values):
    return dot_nt(jnp.ones((8, 128), F32), values, precision=HIGH)[0:1]


def turn_tables():
    half = HEAD_DIM // 2
    freq = np.float32(ROPE_BASE) ** (-(np.arange(half, dtype=np.float32) * np.float32(2.0) / np.float32(HEAD_DIM)))
    angles = np.arange(LENGTH, dtype=np.float32)[:, None] * freq.astype(np.float32)[None, :]
    c, s = np.cos(angles), np.sin(angles)
    cosine = np.concatenate([c, c, c, c], axis=1)
    sine = np.concatenate([-s, s, -s, s], axis=1)
    return cosine.astype(np.float32), sine.astype(np.float32)


def turn(u, cosine, sine):
    early = iota(u.shape, 1) % HEAD_DIM < HEAD_DIM // 2
    partner = jnp.where(early, pltpu.roll(u, 96, 1), pltpu.roll(u, 32, 1))
    return u * cosine + partner * sine


def block_rows(b):
    return pl.ds(pl.multiple_of(b * TOK, TOK), TOK)


def stack_heads(values):
    first = iota(values.shape, 1) < HEAD_DIM
    return jnp.concatenate([jnp.where(first, values, 0.0), jnp.where(first, 0.0, values)], axis=0)


def merge_heads(values):
    first = iota((TOK, 128), 1) < HEAD_DIM
    return jnp.where(first, values[:TOK], values[TOK:])


def front_kernel(
    tok, cot, wq, wk, wv, wo_in, router_in, ga_in, gq_in, gk_in, gf_in, seg, rts_in, cos_in, sin_in,
    x_all, g_all, lin, q_o, k_o, v_o, a_o, lse_o, hid_o, m_o, tab_o, att_o, misc, rout_o, whole, wcol,
    x_s, cot_s, tiny, tiny_b, smalls, wsl, wos, wg, wog, wog2, w32, gains_s, cos_ref, sin_ref, sums, held,
    s_tok, r_tok, s_cot, r_cot, s_w, r_w, s_o, r_o, s_st, r_st, s_t, r_t, s_a, r_a, lsem,
):
    r = lax.axis_index("rep")
    e, x, c = place()
    others = ep_others(e)
    copies = rep_others(r)
    first = iota((TOK, 128), 1) < HEAD_DIM
    gain_a, gain_f, gain = misc.at[0:1], misc.at[1:2], misc.at[2:3, 0:256]
    lo, st = misc.at[8:16, 0:256], misc.at[16:32, 0:256]
    greet([{"ep": d} for d in others] + [{"rep": d} for d in copies])
    misc[...] = jnp.zeros((32, D), F32)

    tiny[...] = jnp.zeros((16, 128), F32)
    tiny[0:8, 0:EXPERTS] = router_in[...].astype(F32)
    for lane, ref in ((0, ga_in), (8, gq_in), (16, gk_in), (20, gf_in)):
        tiny[8:9, lane : lane + ref.shape[1]] = ref[...].astype(F32)
    tiny_b[...] = tiny[...].astype(BF)
    low_lanes = iota((8, 128), 1) < HEAD_DIM
    for d in range(EP):
        k_t = wk[:, (d // 2) * 128 : (d // 2 + 1) * 128].astype(F32)
        v_t = wv[:, (d // 2) * 128 : (d // 2 + 1) * 128].astype(F32)
        if d % 2:
            k_t = pltpu.roll(k_t, HEAD_DIM, 1)
        else:
            v_t = pltpu.roll(v_t, HEAD_DIM, 1)
        q_t = wq[:, d * 128 : (d + 1) * 128].astype(F32)
        wsl[d] = jnp.concatenate([q_t, jnp.where(low_lanes, k_t, v_t)], axis=0).astype(BF)
    for half in range(2):
        wos[half] = jnp.concatenate(
            [wo_in[:, j * 128 : (j + 1) * 128].astype(F32) for j in range(half * 4, half * 4 + 4)], axis=0
        ).astype(BF)

    def cols_of(b):
        return wg.at[r, pl.ds(pl.multiple_of(b * 16, 16), 16)]

    stage_w = [remote(wsl.at[d], cols_of(e), (s_w, r_w), k, {"ep": d}) for k, d in enumerate(others)]
    stage_t = [remote(tiny_b, smalls.at[e], (s_t, r_t), k, {"ep": d}) for k, d in enumerate(others)]
    stage_o = [remote(wos.at[d % 2], wog.at[r, e], (s_o, r_o), k, {"ep": d}) for k, d in enumerate(others)]
    spread_w = [remote(wg.at[r], wg.at[r], (s_w, r_w), 7 + k, {"rep": d}) for k, d in enumerate(copies)]
    spread_o = [remote(wog.at[r], wog.at[r], (s_o, r_o), 7 + k, {"rep": d}) for k, d in enumerate(copies)]
    other_half = remote(wog, wog2, (s_o, r_o), 22, ep_device(x, 1 - c))
    tokens = RingGather(tok, x_s, (s_tok, r_tok), lsem.at[0])
    grads = RingGather(cot_s, g_all, (s_cot, r_cot), lsem.at[1])
    for copy in stage_w + stage_t:
        copy.start()
    tokens.start()
    for copy in stage_o:
        copy.start()
    tables = [
        pltpu.make_async_copy(cos_in, cos_ref, lsem.at[2]),
        pltpu.make_async_copy(sin_in, sin_ref, lsem.at[3]),
        pltpu.make_async_copy(cot, cot_s, lsem.at[5]),
    ]
    for copy in tables:
        copy.start()
    cols_of(e)[...] = wsl[e]
    smalls[e] = tiny_b[...]
    wog[r, e] = wos[c]
    for copy in stage_w + stage_t:
        copy.wait_recv()
    router_tiles = [
        sum(pltpu.roll(smalls[4 * a + b][:8].astype(F32), 32 * b, 1) if b else smalls[4 * a][:8].astype(F32) for b in range(4))
        for a in range(2)
    ]
    gain_rows = [smalls[d][8:9].astype(F32) for d in range(EP)]
    wg[r, 128:160] = jnp.concatenate(router_tiles + gain_rows + [jnp.zeros((8, 128), F32)], axis=0).astype(BF)
    for copy in spread_w:
        copy.start()
    tokens.forward_half()
    tokens.forward_rest()

    routed = rts_in[...]
    hit = jnp.zeros((EXPERTS, TOK), F32)
    for k in range(TOP):
        hit = jnp.where(iota((EXPERTS, TOK), 0) == routed[k : k + 1], 1.0, hit)
    before = jnp.where(iota((TOK, TOK), 0) < iota((TOK, TOK), 1), 1.0, 0.0).astype(BF)
    tab_o[:EXPERTS] = jnp.where(hit > 0.0, dot(hit.astype(BF), before), -1.0)
    segs = jnp.concatenate([seg[:, b * TOK : (b + 1) * TOK] for b in range(EP)], axis=0)
    opening = jnp.zeros((EP, TOK), F32)
    for value in range(2):
        count = jnp.sum(jnp.where(segs == value, 1.0, 0.0), axis=1, keepdims=True)
        opening = opening + jnp.where(segs > value, jnp.sum(count, axis=0, keepdims=True), 0.0)
    places = (iota((EP, TOK), 0) * TOK + iota((EP, TOK), 1)).astype(F32)
    lo[...] = jnp.maximum(opening, places - (WINDOW - 1))

    for copy in spread_w:
        copy.wait_recv()
    for copy in stage_o:
        copy.wait_recv()
    for copy in spread_o:
        copy.start()

    def unpack(b, carry):
        for d in range(EP):
            tile = wg[b, d * 16 : d * 16 + 16].astype(F32)
            rows = pl.ds(pl.multiple_of(b * 64 + d * 8, 8), 8)
            w32[rows, 0:128] = tile[0:8]
            w32[rows, 128:256] = tile[8:16]
        extra = wg[b, 128:160].astype(F32)
        for d in range(EP):
            tile = extra[d // 4 * 8 : d // 4 * 8 + 8]
            if d % 4:
                tile = pltpu.roll(tile, 128 - 32 * (d % 4), 1)
            w32[pl.ds(pl.multiple_of(b * 64 + d * 8, 8), 8), 256:384] = tile
        gains_s[pl.ds(pl.multiple_of(b * 8, 8), 8)] = extra[16:24]
        return carry

    lax.fori_loop(0, REP, unpack, 0)
    wcol[...] = w32[:, :256].astype(BF)
    rout_o[...] = jnp.transpose(w32[:, 256:384])[:EXPERTS].astype(BF)
    packed = gains_s[...].astype(BF)

    def spread_gain(width, group, base, shift):
        lane = base + iota((128, width), 1) % group
        picked = dot(packed, jnp.where(iota((128, width), 0) == lane, 1.0, 0.0).astype(BF))
        mine = iota((128, width), 0) == shift + iota((128, width), 1) // group
        return jnp.sum(jnp.where(mine, picked, 0.0), axis=0, keepdims=True)

    gain_a[...] = spread_gain(D, 8, 0, 0)
    gain_f[...] = spread_gain(D, 8, 20, 0)
    key_part = spread_gain(128, 4, 16, e * 16)
    gain[:, :128] = spread_gain(128, 8, 8, e * 16)
    gain[:, 128:] = jnp.where(iota((1, 128), 1) < HEAD_DIM, key_part, 1.0)

    tokens.first[4].wait_recv()
    tokens.own.wait()

    def project(k, carry):
        @pl.when(k == 2)
        def _():
            tokens.fwd_right.wait_recv()
            tokens.fwd_left.wait_recv()
            tokens.to_peer[2].start()
            tokens.to_peer[1].wait_recv()

        @pl.when(k == 4)
        def _():
            tokens.to_peer[0].wait_recv()

        @pl.when(k == 6)
        def _():
            tokens.to_peer[2].wait_recv()

        g = k // 2
        b = (2 * (x + g + g // 2 - 2 * (g // 3)) + k % 2) % EP
        rows = block_rows(b)
        values = x_s[rows].astype(F32)
        r1 = lax.rsqrt(jnp.mean(values * values, axis=1, keepdims=True) + EPSILON)
        normed = (values * r1 * gain_a[...]).astype(BF)
        out = dot(normed, wcol[...])
        lin[rows] = out
        sq = out * out
        sums[pl.ds(2 * b, 1)] = lane_row(sq[:, :128])
        sums[pl.ds(2 * b + 1, 1)] = lane_row(jnp.where(first, sq[:, 128:], 0.0))
        return carry

    lax.fori_loop(0, EP, project, 0)
    stats = [remote(sums, held.at[e], (s_st, r_st), k, {"ep": d}) for k, d in enumerate(others)]
    for copy in stats:
        copy.start()
    held[e] = sums[...]
    keep = pltpu.make_async_copy(x_s, x_all, lsem.at[4])
    keep.start()
    for copy in tables:
        copy.wait()
    for copy in stats:
        copy.wait_recv()
    total = held[0]
    for k in range(1, EP):
        total = total + held[k]
    st[...] = total
    grads.start()

    def prepare(b, carry):
        rows = block_rows(b)
        cq = column(lax.rsqrt(st[pl.ds(2 * b, 1)] * (1.0 / D) + EPSILON))
        ck = column(lax.rsqrt(st[pl.ds(2 * b + 1, 1)] * (1.0 / KV) + EPSILON))
        cosine, sine = cos_ref[rows], sin_ref[rows]
        q_o[rows] = turn(lin[rows, :128] * cq * gain[:, :128], cosine, sine).astype(BF)
        kv = lin[rows, 128:]
        kv = jnp.where(first, turn(kv * ck * gain[:, 128:], cosine, sine), kv)
        other = pltpu.roll(kv, HEAD_DIM, 1)
        k_o[rows] = jnp.where(first, kv, other).astype(BF)
        v_o[rows] = jnp.where(first, other, kv).astype(BF)
        return carry

    lax.fori_loop(0, EP, prepare, 0)

    def heads(i, source):
        cols = pl.ds(pl.multiple_of(source * 128, 128), 128)
        return pltpu.make_async_remote_copy(
            src_ref=a_o.at[block_rows(i)],
            dst_ref=att_o.at[:, cols],
            send_sem=s_a.at[i],
            recv_sem=r_a.at[source],
            device_id={"ep": i},
            device_id_type=MESH,
        )

    def attend_block(i, n):
        rows = block_rows(i)
        past = (n - 1) * TOK
        q2 = stack_heads(q_o[rows].astype(F32) * HEAD_DIM ** (-0.5)).astype(BF)
        lo_col = column(lo[pl.ds(i, 1)])[:, :1]
        low = jnp.concatenate([lo_col, lo_col], axis=0)
        own_key = (iota((2 * TOK, TOK), 1) + i * TOK).astype(F32)
        query = (iota((2 * TOK, TOK), 0) % TOK + i * TOK).astype(F32)
        s_own = jnp.where((own_key >= low) & (own_key <= query), dot_nt(q2, k_o[rows]), MASKED)
        m = jnp.max(s_own, axis=1, keepdims=True)
        if past:
            early = pl.ds(pl.multiple_of((i - n + 1) * TOK, TOK), past)
            key = (iota((2 * TOK, past), 1) + (i - n + 1) * TOK).astype(F32)
            s = jnp.where(key >= low, dot_nt(q2, k_o[early]), MASKED)
            m = jnp.maximum(m, jnp.max(s, axis=1, keepdims=True))
        p_own = jnp.exp(s_own - m)
        total = jnp.sum(p_own, axis=1, keepdims=True)
        out = dot(p_own.astype(BF), v_o[rows])
        if past:
            p = jnp.exp(s - m)
            total = total + jnp.sum(p, axis=1, keepdims=True)
            out = out + dot(p.astype(BF), v_o[early])
        a_o[rows] = merge_heads(out / total).astype(BF)
        lse = jnp.broadcast_to(m + jnp.log(total), (2 * TOK, 128))
        lse_o[i] = jnp.transpose(lse)[:8]

        @pl.when(i != e)
        def _():
            heads(i, e).start()

        @pl.when(i == e)
        def _():
            att_o[:, pl.ds(pl.multiple_of(e * 128, 128), 128)] = a_o[rows]

    def later(i, carry):
        attend_block(i, 5)

        @pl.when(i == 5)
        def _():
            grads.forward_rest()

        return carry

    for i in range(4):
        attend_block(i, i + 1)
    grads.forward_half()
    for copy in spread_o:
        copy.wait_recv()
    other_half.start()
    lax.fori_loop(4, EP, later, 0)

    other_half.wait_recv()
    grads.fwd_right.wait_recv()
    grads.fwd_left.wait_recv()
    grads.to_peer[2].start()

    def unpack_out(b, carry):
        rows = pl.ds(pl.multiple_of(b * 8, 8), 8)
        for half, held_half in ((c, wog), (1 - c, wog2)):
            tile = held_half[b // EP, b % EP].astype(F32)
            for j in range(4):
                w32[rows, pl.ds(pl.multiple_of(half * 512 + j * 128, 128), 128)] = tile[j * 8 : (j + 1) * 8]
        return carry

    lax.fori_loop(0, 128, unpack_out, 0)
    whole[...] = w32[...].astype(BF)
    for d in others:
        heads(d, d).wait_recv()

    hidden = x_s[block_rows(e)].astype(F32) + dot(att_o[...], whole[...])
    hid_o[...] = hidden
    r2 = lax.rsqrt(jnp.mean(hidden * hidden, axis=1, keepdims=True) + EPSILON)
    moe_in = (hidden * r2 * gain_f[...]).astype(BF)
    m_o[...] = moe_in
    logits = dot_nt(rout_o[...], moe_in)
    chosen = hit > 0.0
    logits = jnp.where(chosen, logits, MASKED)
    raised = jnp.where(chosen, jnp.exp(logits - jnp.max(logits, axis=0, keepdims=True)), 0.0)
    tab_o[EXPERTS:] = raised / jnp.sum(raised, axis=0, keepdims=True)

    grads.first[4].wait_recv()
    for copy in grads.to_peer:
        copy.wait_recv()
    grads.own.wait()
    keep.wait()
    for d in others:
        heads(d, d).wait_send()
    for ring in (tokens, grads):
        for copy in ring.first + [ring.fwd_right, ring.fwd_left] + ring.to_peer:
            copy.wait_send()
    for copy in stage_w + stage_t + stage_o + spread_w + spread_o + stats + [other_half]:
        copy.wait_send()


def front(*args):
    return comm_call(
        front_kernel,
        "front",
        1,
        [
            shape((LENGTH, D), BF),
            shape((LENGTH, D), BF),
            shape((LENGTH, 256)),
            shape((LENGTH, 128), BF),
            shape((LENGTH, 128), BF),
            shape((LENGTH, 128), BF),
            shape((LENGTH, 128), BF),
            shape((EP, 8, 2 * TOK)),
            shape((TOK, D)),
            shape((TOK, D), BF),
            shape((2 * EXPERTS, TOK)),
            shape((TOK, D), BF),
            shape((32, D)),
            shape((EXPERTS, D), BF),
            shape((D, D), BF),
            shape((D, 256), BF),
        ],
        [ANY, ANY] + [VM] * 11 + [ANY, ANY],
        [ANY, ANY] + [VM] * 14,
        [
            pltpu.VMEM((LENGTH, D), BF),
            pltpu.VMEM((TOK, D), BF),
            pltpu.VMEM((16, 128), F32),
            pltpu.VMEM((16, 128), BF),
            pltpu.VMEM((EP, 16, 128), BF),
            pltpu.VMEM((EP, 16, 128), BF),
            pltpu.VMEM((2, 32, 128), BF),
            pltpu.VMEM((REP, 160, 128), BF),
            pltpu.VMEM((REP, EP, 32, 128), BF),
            pltpu.VMEM((REP, EP, 32, 128), BF),
            pltpu.VMEM((D, D), F32),
            pltpu.VMEM((128, 128), F32),
            pltpu.VMEM((LENGTH, 128), F32),
            pltpu.VMEM((LENGTH, 128), F32),
            pltpu.VMEM((16, 256), F32),
            pltpu.VMEM((EP, 16, 256), F32),
        ]
        + [DMA((10,))] * 4
        + [DMA((23,))] * 4
        + [DMA((7,))] * 4
        + [DMA((8,))] * 2
        + [DMA((6,))],
        limit=60,
    )(*args)


class ChipReduce:
    SEMS = 10
    STEP = 64

    def __init__(self, n, swo, snd, pc, rcv, hop, sems):
        e, x, c = place()
        self.n, self.h = n, n // 2
        h = n // 2
        self.snd, self.pc, self.rcv, self.hop = snd, pc, rcv, hop
        right, left = ep_device((x + 1) % 4, c), ep_device((x + 3) % 4, c)
        peer = ep_device(x, 1 - c)
        self.swap = lambda k: remote(swo.at[k], pc.at[k], sems, k, peer)
        low, high = pl.ds(0, h), pl.ds(h, h)
        self.opp = [
            remote(snd.at[0, low], hop.at[low], sems, 4, right),
            remote(snd.at[0, high], hop.at[high], sems, 5, left),
        ]
        self.near = [
            remote(snd.at[2, high], rcv.at[0, high], sems, 6, right),
            remote(snd.at[1, low], rcv.at[1, low], sems, 7, left),
        ]
        self.far = [
            remote(snd.at[2, low], rcv.at[0, low], sems, 8, right),
            remote(snd.at[1, high], rcv.at[1, high], sems, 9, left),
        ]

    def rows_loop(self, low, count, body):
        step = self.STEP

        def loop(i, carry):
            body(pl.ds(pl.multiple_of(low + i * step, 16), step))
            return carry

        lax.fori_loop(0, count // step, loop, 0)

    def merge(self, k):
        def body(s):
            self.snd[k, s] = (self.snd[k, s].astype(F32) + self.pc[k, s].astype(F32)).astype(BF)

        self.swap(k).wait_recv()
        self.rows_loop(0, self.n, body)

    def merge_hop(self, k, low):
        def body(s):
            self.snd[k, s] = (self.snd[k, s].astype(F32) + self.hop[s].astype(F32)).astype(BF)

        self.rows_loop(low, self.h, body)

    def send_opp(self):
        self.merge(0)
        for copy in self.opp:
            copy.start()

    def send_near(self):
        self.merge(2)
        self.near[0].start()
        self.merge(1)
        self.near[1].start()

    def send_far(self):
        self.opp[0].wait_recv()
        self.merge_hop(2, 0)
        self.far[0].start()
        self.opp[1].wait_recv()
        self.merge_hop(1, self.h)
        self.far[1].start()

    def finish(self, out_ref):
        for copy in self.near + self.far:
            copy.wait_recv()

        def body(s):
            out_ref[s] = self.snd[3, s].astype(F32) + (
                self.rcv[0, s].astype(F32) + self.rcv[1, s].astype(F32)
            )

        self.rows_loop(0, self.n, body)
        for copy in [self.swap(k) for k in range(4)] + self.opp + self.near + self.far:
            copy.wait_send()


PAIR = 2
ROWS = EP * CAP
CHIP = 2 * CAP
BLOCK = 96


def chip_rows(q):
    return pl.ds(pl.multiple_of(q * CHIP, 16), CHIP)


def chip_tokens(q):
    return pl.ds(pl.multiple_of(q * 2 * TOK, 2 * TOK), 2 * TOK)


def expert_hits(tab, e, n, q):
    row = pl.ds(e * LOCAL + n, 1)
    second = tab[2 * q + 1, row]
    slots = jnp.concatenate([tab[2 * q, row], jnp.where(second >= 0.0, second + CAP, -1.0)], axis=1)
    return iota((CHIP, 2 * TOK), 0).astype(F32) == slots


def one_hot(hit):
    return jnp.where(hit, 1.0, 0.0).astype(BF)


def expert_chip(q, e, start, tab, m_ref, g_ref, wgu, wd, a_s, act_s, gp_s, dgu_s, y_s, z_s, ggt):
    hits = [expert_hits(tab, e, start + n, q) for n in range(PAIR)]
    chosen = jnp.concatenate([one_hot(hit) for hit in hits], axis=0)
    rows = chip_rows(q)
    a_both = dot(chosen, m_ref[chip_tokens(q)]).astype(BF)
    c_both = dot(chosen, g_ref[chip_tokens(q)]).astype(BF)
    for n in range(PAIR):
        part = slice(n * CHIP, (n + 1) * CHIP)
        row = pl.ds(EXPERTS + e * LOCAL + start + n, 1)
        gates = jnp.concatenate([tab[2 * q, row], tab[2 * q + 1, row]], axis=1)
        weight = jnp.sum(jnp.where(hits[n], gates, 0.0), axis=1, keepdims=True)
        a, cot = a_both[part], c_both[part]
        lin = dot(a, wgu[n])
        back = dot_nt(cot, wd[n])
        gate_lin, up_lin = lin[:, :FF], lin[:, FF:]
        sig = jax.nn.sigmoid(gate_lin)
        silu = gate_lin * sig
        act = silu * up_lin
        act_low = act.astype(BF)
        produced = dot(act_low, wd[n]).astype(BF).astype(F32)
        gg = jnp.sum(act * back, axis=1, keepdims=True)
        back = back * weight
        dgate = (back * up_lin * sig * (1.0 + gate_lin * (1.0 - sig))).astype(BF)
        dup = (back * silu).astype(BF)
        dgu = jnp.concatenate([dgate, dup], axis=1)
        a_s[n, rows] = a
        act_s[n, rows] = act_low
        gp_s[n, rows] = (weight * cot.astype(F32)).astype(BF)
        dgu_s[n, rows] = dgu
        y_s[n, rows] = (weight * produced).astype(BF)
        z_s[n, rows] = dot_nt(dgu, wgu[n]).astype(BF)
        gg_row = jnp.sum(jnp.where(hits[n], gg, 0.0), axis=0, keepdims=True)
        ggt[2 * q, n : n + 1] = gg_row[:, :TOK]
        ggt[2 * q + 1, n : n + 1] = gg_row[:, TOK:]


def expert_grads(n, a_s, act_s, gp_s, dgu_s, eg):
    eg[n, :, :64] = dot_tn(a_s[n], dgu_s[n]).astype(BF).reshape(REP, 64, D)
    eg[n, :, 64:] = dot_tn(act_s[n], gp_s[n]).astype(BF).reshape(REP, 32, D)


def load_weights(start, wg_in, wu_in, wd_in, wgu, wd, sems):
    some = pl.ds(start, PAIR)
    return [
        pltpu.make_async_copy(wg_in.at[some], wgu.at[:, :, pl.ds(0, FF)], sems.at[0]),
        pltpu.make_async_copy(wu_in.at[some], wgu.at[:, :, pl.ds(FF, FF)], sems.at[1]),
        pltpu.make_async_copy(wd_in.at[some], wd, sems.at[2]),
    ]


def send_gates(ggt, gg_o, e, sems, lsem):
    copies = [remote(ggt.at[d], gg_o.at[e], sems, k, {"ep": d}) for k, d in enumerate(ep_others(e))]
    return copies, pltpu.make_async_copy(ggt.at[e], gg_o.at[e], lsem)


def experts_first_kernel(
    m_in, t_in, g_in, wg_in, wu_in, wd_in, m_o, tab_o, y_o, z_o, gg_o, eg_o,
    m_ref, tab, g_ref, wgu, wd, a_s, act_s, gp_s, dgu_s, y_s, z_s, ggt, eg,
    s_m, r_m, s_t, r_t, s_g, r_g, lsem, wsem, gsem, esem,
):
    e, x, c = place()
    others = ep_others(e)
    greet([{"ep": d} for d in others])
    ring = RingGather(m_in, m_ref, (s_m, r_m), lsem.at[0])
    tables = [remote(t_in, tab.at[e], (s_t, r_t), k, {"ep": d}) for k, d in enumerate(others)]
    for copy in tables:
        copy.start()
    ring.start()
    own = pltpu.make_async_copy(t_in, tab.at[e], lsem.at[1])
    loads = load_weights(0, wg_in, wu_in, wd_in, wgu, wd, wsem)
    cots = [
        pltpu.make_async_copy(g_in.at[chip_tokens(q)], g_ref.at[chip_tokens(q)], gsem.at[k])
        for k, q in enumerate([x, (x + 1) % 4, (x + 3) % 4, (x + 2) % 4])
    ]
    for copy in [own] + loads + cots:
        copy.start()
    ggt[...] = jnp.zeros((EP, 8, TOK), F32)
    kept = pltpu.make_async_copy(m_ref, m_o, lsem.at[2])

    def chips(k, carry):
        @pl.when(k == 0)
        def _():
            ring.first[0].wait_recv()
            ring.fwd_right.start()
            ring.first[1].wait_recv()
            ring.fwd_left.start()
            ring.first[4].wait_recv()
            ring.own.wait()
            own.wait()
            for copy in tables:
                copy.wait_recv()
            for copy in loads:
                copy.wait()
            cots[0].wait()

        @pl.when(k == 1)
        def _():
            ring.first[3].wait_recv()
            ring.to_peer[1].start()
            ring.first[2].wait_recv()
            ring.to_peer[0].start()
            ring.to_peer[1].wait_recv()
            cots[1].wait()

        @pl.when(k == 2)
        def _():
            ring.fwd_right.wait_recv()
            ring.fwd_left.wait_recv()
            ring.to_peer[2].start()
            ring.to_peer[0].wait_recv()
            cots[2].wait()

        @pl.when(k == 3)
        def _():
            ring.to_peer[2].wait_recv()
            cots[3].wait()
            kept.start()

        q = (x + k + k // 2 - 2 * (k // 3)) % 4
        expert_chip(q, e, 0, tab, m_ref, g_ref, wgu, wd, a_s, act_s, gp_s, dgu_s, y_s, z_s, ggt)
        return carry

    lax.fori_loop(0, 4, chips, 0)
    gates, own_gates = send_gates(ggt, gg_o, e, (s_g, r_g), lsem.at[3])
    states = [
        pltpu.make_async_copy(tab, tab_o, lsem.at[4]),
        pltpu.make_async_copy(y_s, y_o, lsem.at[5]),
        pltpu.make_async_copy(z_s, z_o, lsem.at[6]),
    ]
    for copy in gates + [own_gates] + states:
        copy.start()
    for n in range(PAIR):
        expert_grads(n, a_s, act_s, gp_s, dgu_s, eg)
        states.append(pltpu.make_async_copy(eg.at[n], eg_o.at[n], esem.at[n]))
        states[-1].start()
    for copy in states + [kept, own_gates]:
        copy.wait()
    for copy in gates:
        copy.wait_recv()
    for copy in ring.first + [ring.fwd_right, ring.fwd_left] + ring.to_peer + tables + gates:
        copy.wait_send()


def pair_scratch():
    return [
        pltpu.VMEM((LENGTH, D), BF),
        pltpu.VMEM((EP, 2 * EXPERTS, TOK), F32),
        pltpu.VMEM((LENGTH, D), BF),
        pltpu.VMEM((PAIR, D, 2 * FF), BF),
        pltpu.VMEM((PAIR, FF, D), BF),
        pltpu.VMEM((PAIR, ROWS, D), BF),
        pltpu.VMEM((PAIR, ROWS, FF), BF),
        pltpu.VMEM((PAIR, ROWS, D), BF),
        pltpu.VMEM((PAIR, ROWS, D), BF),
        pltpu.VMEM((PAIR, ROWS, D), BF),
        pltpu.VMEM((PAIR, ROWS, D), BF),
        pltpu.VMEM((EP, 8, TOK), F32),
        pltpu.VMEM((PAIR, REP, BLOCK, D), BF),
    ]


def experts_first(m, t, g_all, wg, wu, wd):
    return comm_call(
        experts_first_kernel,
        "experts_first",
        2,
        [
            shape((LENGTH, D), BF),
            shape((EP, 2 * EXPERTS, TOK)),
            shape((PAIR, ROWS, D), BF),
            shape((PAIR, ROWS, D), BF),
            shape((EP, 8, TOK)),
            shape((PAIR, REP, BLOCK, D), BF),
        ],
        [ANY] * 6,
        [ANY] * 6,
        pair_scratch()
        + [DMA((10,))] * 2
        + [DMA((7,))] * 4
        + [DMA((7,)), DMA((3,)), DMA((4,)), DMA((2,))],
        limit=60,
    )(m, t, g_all, wg, wu, wd)


def experts_last_kernel(
    m_in, t_in, y_in, z_in, g_in, wg_in, wu_in, wd_in, gm_o, mix_o, gg_o, eg_o,
    m_ref, tab, g_ref, wgu, wd, a_s, act_s, gp_s, dgu_s, y_s, z_s, ggt, eg,
    y_f, z_f, gm, swo, snd, pc, rcv, hop, mix,
    s_r, r_r, s_g, r_g, lsem, wsem, gsem, msem, esem, osem,
):
    e, x, c = place()
    order = [(x + 2) % 4, (x + 3) % 4, (x + 1) % 4, x]
    loads = [pltpu.make_async_copy(t_in, tab, lsem.at[0])] + load_weights(2, wg_in, wu_in, wd_in, wgu, wd, wsem)
    rows = [
        (
            pltpu.make_async_copy(m_in.at[chip_tokens(q)], m_ref.at[chip_tokens(q)], msem.at[k]),
            pltpu.make_async_copy(g_in.at[chip_tokens(q)], g_ref.at[chip_tokens(q)], gsem.at[k]),
        )
        for k, q in enumerate(order)
    ]
    firsts = [pltpu.make_async_copy(z_in, z_f, lsem.at[1]), pltpu.make_async_copy(y_in, y_f, lsem.at[2])]
    for copy in loads + list(rows[0]) + [firsts[0]] + list(rows[1] + rows[2] + rows[3]) + [firsts[1]]:
        copy.start()
    greet([{"ep": d} for d in ep_others(e)])
    red = ChipReduce(TOK, swo, snd, pc, rcv, hop, (s_r, r_r))
    ggt[...] = jnp.zeros((EP, 8, TOK), F32)

    def combine(q, early, late):
        chosen = jnp.concatenate([one_hot(expert_hits(tab, e, n, q)) for n in range(LOCAL)], axis=0)
        part = chip_rows(q)
        values = [ref[n, part] for ref in (early, late) for n in range(PAIR)]
        return dot_tn(chosen, jnp.concatenate(values, axis=0)).astype(BF)

    for copy in loads:
        copy.wait()

    def chips(k, carry):
        for step in range(4):

            @pl.when(k == step)
            def _(step=step):
                for copy in rows[step]:
                    copy.wait()
                if step == 0:
                    firsts[0].wait()

        q = (x + 2 + k - (k // 2) * (2 * k - 1)) % 4
        expert_chip(q, e, 2, tab, m_ref, g_ref, wgu, wd, a_s, act_s, gp_s, dgu_s, y_s, z_s, ggt)
        mix[...] = combine(q, z_f, z_s)
        swo[k] = mix[pl.ds(pl.multiple_of((1 - c) * TOK, TOK), TOK)]
        red.swap(k).start()
        snd[k] = mix[pl.ds(pl.multiple_of(c * TOK, TOK), TOK)]

        @pl.when(k == 1)
        def _():
            red.send_opp()

        @pl.when(k == 3)
        def _():
            red.send_near()

        return carry

    lax.fori_loop(0, 4, chips, 0)
    gates, own_gates = send_gates(ggt, gg_o, e, (s_g, r_g), lsem.at[3])
    for copy in gates + [own_gates]:
        copy.start()
    states = []

    def grads(n):
        expert_grads(n, a_s, act_s, gp_s, dgu_s, eg)
        states.append(pltpu.make_async_copy(eg.at[n], eg_o.at[n], esem.at[n]))
        states[-1].start()

    grads(0)
    red.merge(3)
    red.send_far()
    grads(1)
    firsts[1].wait()

    def mixture(q, carry):
        @pl.when(q > 0)
        def _():
            pltpu.make_async_copy(mix, mix_o.at[chip_tokens(q)], osem).wait()

        mix[...] = combine(q, y_f, y_s)
        pltpu.make_async_copy(mix, mix_o.at[chip_tokens(q)], osem).start()
        return carry

    lax.fori_loop(0, 4, mixture, 0)
    red.finish(gm)
    last = pltpu.make_async_copy(gm, gm_o, lsem.at[4])
    last.start()
    pltpu.make_async_copy(mix, mix_o.at[chip_tokens(3)], osem).wait()
    for copy in states + [own_gates, last]:
        copy.wait()
    for copy in gates:
        copy.wait_recv()
    for copy in gates:
        copy.wait_send()


def experts_last(m, t, y, z, g_all, wg, wu, wd):
    return comm_call(
        experts_last_kernel,
        "experts_last",
        4,
        [
            shape((TOK, D)),
            shape((LENGTH, D), BF),
            shape((EP, 8, TOK)),
            shape((PAIR, REP, BLOCK, D), BF),
        ],
        [ANY] * 8,
        [ANY] * 4,
        pair_scratch()
        + [
            pltpu.VMEM((PAIR, ROWS, D), BF),
            pltpu.VMEM((PAIR, ROWS, D), BF),
            pltpu.VMEM((TOK, D), F32),
            pltpu.VMEM((4, TOK, D), BF),
            pltpu.VMEM((4, TOK, D), BF),
            pltpu.VMEM((4, TOK, D), BF),
            pltpu.VMEM((2, TOK, D), BF),
            pltpu.VMEM((TOK, D), BF),
            pltpu.VMEM((2 * TOK, D), BF),
        ]
        + [DMA((10,))] * 2
        + [DMA((7,))] * 2
        + [DMA((5,)), DMA((3,)), DMA((4,)), DMA((4,)), DMA((2,)), DMA(())],
        limit=63,
    )(m, t, y, z, g_all, wg, wu, wd)


KEPT = 8


def back_kernel(
    eg_in, mix_in, gm_in, gg1_in, gg2_in, tab_in, hid_in, m_in, cot_in, att_in, misc_in, rout_in, whole_in, wcol_in, x_in, lin_in,
    q_in, k_in, v_in, a_in, lse_in, cos_in, sin_in,
    out_o, ig_o, gq_o, gk_o, gv_o, go_o, pack_o, eg_o,
    gm, gg1, gg2, tab, hid, m_s, cot, att, misc, rout, wcol, x_s, lin, q_s, k_s, v_s, a_s, lse, cos_ref, sin_ref,
    gh, ga_s, go, q2_s, p_s, dk, dv, u_s, sums, st2, held, wb, wsum, wheld,
    dwt, dws, dheld, dsum, dw_o, vec, vheld, vtot, vheld2, swo, snd, pc1, rcv1, hop1, snd3, pc3, rcv3, hop3,
    s_1, r_1, s_2, r_2, s_3, r_3, s_go, r_go, s_st, r_st, s_w, r_w, s_d, r_d, s_e, r_e, s_v, r_v, s_v2, r_v2, lsem, l_1, l_3, esem, xsem,
    out_s, gq_s, gk_s, gv_s, go_s, pack_s, eg_s,
    za, zb, zc, zd, ze, zf, ya, yb, yc, yd, ye, yf, s_z, r_z, s_y, r_y, l_z, l_y,
):
    r = lax.axis_index("rep")
    e, x, c = place()
    others = ep_others(e)
    copies = rep_others(r)
    first = iota((TOK, 128), 1) < HEAD_DIM
    gain_a, gain_f, gain = misc.at[0:1], misc.at[1:2], misc.at[2:3, 0:256]
    lo, st = misc.at[8:16, 0:256], misc.at[16:32, 0:256]
    greet([{"ep": d} for d in others] + [{"rep": d} for d in copies])
    red1 = RingReduce(mix_in, TOK, pc1, snd, rcv1, hop1, (s_1, r_1), l_1)
    red2 = ChipReduce(TOK, swo, snd, pc1, rcv1, hop1, (s_2, r_2))
    red3 = RingReduce(wb, 128, pc3, snd3, rcv3, hop3, (s_3, r_3), l_3)
    by_z = GridReduce(True, eg_in, 0, za, zb, zc, zd, ze, zf, (s_z, r_z), l_z)
    by_y = GridReduce(False, eg_in, FF, ya, yb, yc, yd, ye, yf, (s_y, r_y), l_y)
    for copy in by_z.load + by_y.load:
        copy.start()
    red1.start()
    loads = [
        pltpu.make_async_copy(src, dst, lsem.at[k])
        for k, (src, dst) in enumerate(
            [
                (misc_in, misc), (gm_in, gm), (gg1_in, gg1), (gg2_in, gg2), (tab_in, tab), (hid_in, hid),
                (cot_in, cot), (rout_in, rout), (whole_in, wb.at[:, pl.ds(0, D)]), (q_in, q_s), (k_in, k_s), (lse_in, lse),
                (m_in, m_s), (att_in, att), (v_in, v_s), (a_in, a_s), (cos_in, cos_ref), (sin_in, sin_ref),
                (lin_in, lin), (wcol_in, wcol),
            ]
        )
    ]
    chips_order = [(x + 2) % 4, (x + 3) % 4, (x + 1) % 4, x]

    def x_load(k):
        return pltpu.make_async_copy(x_in.at[chip_tokens(chips_order[k])], x_s.at[k % 2], xsem.at[k % 2])

    for copy in loads + [x_load(0), x_load(1)]:
        copy.start()
    for copy in loads[:9]:
        copy.wait()

    def base(i):
        cut = jnp.minimum(i, 4)
        return cut * (cut + 1) // 2 + 5 * jnp.maximum(i - 4, 0)

    def spans(i, n):
        keys = pl.ds(pl.multiple_of((i - n + 1) * TOK, TOK), n * TOK)
        return keys, pl.ds(pl.multiple_of(base(i) * TOK, TOK), n * TOK)

    def probabilities(i, n):
        _, held_rows = spans(i, n)
        p_s[held_rows] = make_probabilities(i, n)

    def make_probabilities(i, n):
        keys, _ = spans(i, n)
        q2 = stack_heads(q_s[block_rows(i)].astype(F32) * HEAD_DIM ** (-0.5)).astype(BF)
        q2_s[i] = q2
        top = lse[i][0:1]
        low = jnp.concatenate([lo[pl.ds(i, 1)]] * 2, axis=1)
        key = (iota((n * TOK, 2 * TOK), 0) + (i - n + 1) * TOK).astype(F32)
        query = (iota((n * TOK, 2 * TOK), 1) % TOK + i * TOK).astype(F32)
        allowed = (key >= low) & (key <= query)
        return jnp.where(allowed, jnp.exp(dot_nt(k_s[keys], q2) - top), 0.0).astype(BF)

    def probabilities_later(i, carry):
        probabilities(i, 5)

        @pl.when(i == 4)
        def _():
            red1.push_opp()

        @pl.when(i == 5)
        def _():
            red1.push_near()

        return carry


    hidden = hid[...]
    weights = tab[EXPERTS:]
    grads = jnp.concatenate([ref[d][:PAIR] for d in range(EP) for ref in (gg1, gg2)], axis=0)
    mean = jnp.sum(weights * grads, axis=0, keepdims=True)
    grad_logits = weights * (grads - mean)
    grad_moe = gm[...] + dot_tn(grad_logits.astype(BF), rout[...])
    r2 = lax.rsqrt(jnp.mean(hidden * hidden, axis=1, keepdims=True) + EPSILON)
    n = hidden * r2
    u = grad_moe * gain_f[...]
    grad_hidden = cot[...].astype(F32) + r2 * (u - n * jnp.mean(u * n, axis=1, keepdims=True))
    gh[...] = grad_hidden
    branch = grad_hidden.astype(BF)
    ga_s[...] = dot_nt(branch, wb[:, :D]).astype(BF)

    def own_cols(ref, b):
        return ref.at[:, pl.ds(pl.multiple_of(b * 128, 128), 128)]

    heads = [
        remote(own_cols(ga_s, d), go.at[block_rows(e)], (s_go, r_go), k, {"ep": d}) for k, d in enumerate(others)
    ]
    for copy in heads:
        copy.start()
    by_z.push()
    by_y.push()
    go[block_rows(e)] = own_cols(ga_s, e)[...]
    for copy in loads[9:]:
        copy.wait()
    for i in range(4):
        probabilities(i, i + 1)
    lax.fori_loop(4, KEPT, probabilities_later, 0)
    for copy in heads:
        copy.wait_recv()
    ffn = jnp.sum(grad_moe * n, axis=0, keepdims=True)
    logit_rows = jnp.transpose(jnp.concatenate([grad_logits, jnp.zeros((96, TOK), F32)], axis=0)).astype(BF)
    router_rows = dot_tn(m_s[...], logit_rows)
    vec[...] = jnp.zeros((8, D), F32)
    vec[3:4] = ffn
    router_rows = router_rows.reshape(REP, EP, 8, 128)
    for d in range(EP):
        wb[d * 128 : (d + 1) * 128, D:] = router_rows[:, d].reshape(128, 128).astype(BF)
    for cols in range(0, D, 256):
        out_rows = dot_tn(att[...], branch[:, cols : cols + 256]).reshape(REP, EP, 8, 256)
        for d in range(EP):
            wb[d * 128 : (d + 1) * 128, cols : cols + 256] = out_rows[:, d].reshape(128, 256).astype(BF)
    red3.start()
    by_z.stage.relay()
    by_y.stage.relay()
    dk[...] = jnp.zeros((LENGTH, 128), F32)
    dv[...] = jnp.zeros((LENGTH, 128), F32)

    def part(ref, b, size):
        return ref.at[pl.ds(pl.multiple_of(b * size, 8), size)]

    spread_w = [remote(part(wsum, d, 8), wheld.at[r], (s_w, r_w), k, {"rep": d}) for k, d in enumerate(copies)]

    def attend_back(i, n):
        keys, held_rows = spans(i, n)
        rows = block_rows(i)
        grad = stack_heads(go[rows].astype(F32))
        do2 = grad.astype(BF)
        out = a_s[rows].astype(F32)
        settle = lane_row(grad * jnp.concatenate([out, out], axis=0))
        p = p_s[held_rows]
        ds = (p.astype(F32) * (dot_nt(v_s[keys], do2) - settle)).astype(BF)
        dv[keys] += dot(p, do2)
        dk[keys] += dot(ds, q2_s[i])
        dq = dot_tn(k_s[keys], ds)
        grad_q = merge_heads(jnp.transpose(dq)) * HEAD_DIM ** (-0.5)
        grad_q = turn(grad_q.astype(BF).astype(F32), cos_ref[rows], -sin_ref[rows])
        u_s[rows, :128] = grad_q
        cq = column(lax.rsqrt(st[pl.ds(2 * i, 1)] * (1.0 / D) + EPSILON))
        sums[pl.ds(2 * i, 1)] = lane_row(grad_q * gain[:, :128] * lin[rows, :128] * cq)

    def attend_back_later(i, carry):
        attend_back(i, 5)
        return carry

    for i in range(4):
        attend_back(i, i + 1)
    red3.push_opp()
    red3.push_near()
    lax.fori_loop(4, 6, attend_back_later, 0)
    red1.relay()
    red3.relay()
    lax.fori_loop(6, EP, attend_back_later, 0)

    def close(b, carry):
        rows = block_rows(b)
        grad_k, grad_v = dk[rows], dv[rows]
        grad_k = grad_k + pltpu.roll(grad_k, HEAD_DIM, 1)
        grad_v = grad_v + pltpu.roll(grad_v, HEAD_DIM, 1)
        both = jnp.where(first, grad_k, grad_v).astype(BF).astype(F32)
        both = jnp.where(first, turn(both, cos_ref[rows], -sin_ref[rows]), both)
        u_s[rows, 128:] = both
        ck = column(lax.rsqrt(st[pl.ds(2 * b + 1, 1)] * (1.0 / KV) + EPSILON))
        sums[pl.ds(2 * b + 1, 1)] = lane_row(jnp.where(first, both * gain[:, 128:] * lin[rows, 128:] * ck, 0.0))
        return carry

    lax.fori_loop(0, EP, close, 0)
    red1.finish(gm)
    stats = [remote(sums, held.at[e], (s_st, r_st), k, {"ep": d}) for k, d in enumerate(others)]
    for copy in stats:
        copy.start()
    held[e] = sums[...]
    out_s[...] = (hid[...] + gm[...]).astype(BF)
    ends = [pltpu.make_async_copy(out_s, out_o, esem.at[0])]
    ends[0].start()
    red3.finish(wsum)
    for copy in spread_w:
        copy.start()
    wheld[r] = part(wsum, r, 8)[...]
    by_z.turn()
    by_y.turn()
    dwt[...] = jnp.zeros((256, D), F32)
    for copy in stats:
        copy.wait_recv()
    total = held[0]
    for k in range(1, EP):
        total = total + held[k]
    st2[...] = total

    def project_back(b, slot):
        rows = block_rows(b)
        values = x_s[slot, pl.ds(pl.multiple_of(b % 2 * TOK, TOK), TOK)].astype(F32)
        r1 = lax.rsqrt(jnp.mean(values * values, axis=1, keepdims=True) + EPSILON)
        n1 = values * r1
        normed = (n1 * gain_a[...]).astype(BF)
        cq = column(lax.rsqrt(st[pl.ds(2 * b, 1)] * (1.0 / D) + EPSILON))
        ck = column(lax.rsqrt(st[pl.ds(2 * b + 1, 1)] * (1.0 / KV) + EPSILON))
        mq = column(st2[pl.ds(2 * b, 1)] * (1.0 / D))
        mk = column(st2[pl.ds(2 * b + 1, 1)] * (1.0 / KV))
        uq, uk = u_s[rows, :128], u_s[rows, 128:]
        nq = lin[rows, :128] * cq
        nk = lin[rows, 128:] * ck
        gq = cq * (uq * gain[:, :128] - nq * mq)
        gk = jnp.where(first, ck * (uk * gain[:, 128:] - nk * mk), uk)
        glin = jnp.concatenate([gq, gk], axis=1).astype(BF)
        vec[1:2, :128] += jnp.sum(uq * nq, axis=0, keepdims=True)
        vec[2:3, :128] += jnp.sum(uk * nk, axis=0, keepdims=True)
        gn = dot_nt(glin, wcol[...])
        vec[0:1] += jnp.sum(gn * n1, axis=0, keepdims=True)
        dwt[...] += dot_tn(glin, normed)
        return gn.astype(BF)

    def chips(k, carry):
        q = (x + 2 + k - (k // 2) * (2 * k - 1)) % 4
        for step in range(4):

            @pl.when(k == step)
            def _(step=step):
                x_load(step).wait()

        swo[k] = project_back(q * 2 + 1 - c, k % 2)
        red2.swap(k).start()
        snd[k] = project_back(q * 2 + c, k % 2)
        for step in range(2):

            @pl.when(k == step)
            def _(step=step):
                x_load(step + 2).start()

        @pl.when(k == 1)
        def _():
            red2.send_opp()

        @pl.when(k == 2)
        def _():
            red2.send_near()

        return carry

    lax.fori_loop(0, 4, chips, 0)
    red2.merge(3)
    red2.send_far()
    dws[...] = jnp.transpose(dwt[...]).astype(BF)
    spread_d = [remote(part(dws, d, 64), dheld.at[r], (s_d, r_d), k, {"rep": d}) for k, d in enumerate(copies)]
    for copy in spread_d:
        copy.start()
    by_z.last.relay()
    by_y.last.relay()
    dheld[r] = part(dws, r, 64)[...]
    gain_q, gain_k = vec[1:2, :128], vec[2:3, :128]
    low, spread = iota((1, 128), 1) < 32, iota((1, 128), 1) // 32 == 2
    gain_k = jnp.where(low, gain_k, jnp.where(spread, pltpu.roll(gain_k, 32, 1), 0.0))
    vec[1:3, :128] = jnp.zeros((2, 128), F32)
    vec[1:2, pl.ds(pl.multiple_of(e * 128, 128), 128)] = gain_q
    vec[2:3, pl.ds(pl.multiple_of(e * 128, 128), 128)] = gain_k
    spread_v = [remote(vec, vheld.at[e], (s_v, r_v), k, {"ep": d}) for k, d in enumerate(others)]
    for copy in spread_v:
        copy.start()
    vheld[e] = vec[...]
    for copy in spread_v:
        copy.wait_recv()
    total = vheld[0]
    for k in range(1, EP):
        total = total + vheld[k]
    vtot[...] = total
    def lanes_of(d):
        return vtot.at[:, pl.ds(pl.multiple_of(d // 2 * 128, 128), 128)]

    spread_v2 = [remote(lanes_of(d), vheld2.at[r], (s_v2, r_v2), k, {"rep": d}) for k, d in enumerate(copies)]
    for copy in spread_v2:
        copy.start()
    vheld2[r] = lanes_of(r)[...]
    for copy in spread_w:
        copy.wait_recv()
    total = wheld[0]
    for k in range(1, REP):
        total = total + wheld[k]
    go_s[...] = total[:, :D]
    pack_s[0:8] = total[:, D:]
    for copy in spread_d:
        copy.wait_recv()
    total = dheld[0].astype(F32)
    for k in range(1, REP):
        total = total + dheld[k].astype(F32)
    dsum[...] = total
    spread_e = [remote(part(dsum, d, 8), dw_o.at[e], (s_e, r_e), k, {"ep": d}) for k, d in enumerate(others)]
    for copy in spread_e:
        copy.start()
    dw_o[e] = part(dsum, e, 8)[...]
    for copy in spread_v2:
        copy.wait_recv()
    total = vheld2[0]
    for k in range(1, REP):
        total = total + vheld2[k]
    start = r % 2 * 64
    rows_d, lanes_d = iota((128, 128), 0), iota((128, 128), 1)
    eight = jnp.where((rows_d == start + e * 8 + lanes_d) & (lanes_d < 8), 1.0, 0.0)
    four = jnp.where((rows_d == start + e * 4 + lanes_d) & (lanes_d < 4), 1.0, 0.0)

    def pick(sel):
        return jnp.dot(total, sel, preferred_element_type=F32, precision=HIGH)

    eights, fours = pick(eight), pick(four)
    pack_s[8:16] = jnp.where(iota((8, 128), 0) == 2, fours, eights)
    by_z.finish(eg_s, 0)
    by_y.finish(eg_s, FF)
    red2.finish(gm)
    values = x_s[1, pl.ds(pl.multiple_of(c * TOK, TOK), TOK)].astype(F32)
    r1 = lax.rsqrt(jnp.mean(values * values, axis=1, keepdims=True) + EPSILON)
    n1 = values * r1
    z = gm[...] * gain_a[...]
    gh[...] = gh[...] + r1 * (z - n1 * jnp.mean(z * n1, axis=1, keepdims=True))
    for copy in spread_e:
        copy.wait_recv()
    low_lanes = iota((8, 128), 1) < HEAD_DIM
    for d in range(EP):
        gq_s[:, d * 128 : (d + 1) * 128] = dw_o[d][:, :128]
    for d in range(EP // 2):
        even, odd = dw_o[2 * d][:, 128:], dw_o[2 * d + 1][:, 128:]
        gk_s[:, d * 128 : (d + 1) * 128] = jnp.where(low_lanes, even, pltpu.roll(odd, HEAD_DIM, 1))
        gv_s[:, d * 128 : (d + 1) * 128] = jnp.where(low_lanes, pltpu.roll(even, HEAD_DIM, 1), odd)
    pairs = [(gh, ig_o), (gq_s, gq_o), (gk_s, gk_o), (gv_s, gv_o), (go_s, go_o), (pack_s, pack_o), (eg_s, eg_o)]
    for k, (src, dst) in enumerate(pairs):
        ends.append(pltpu.make_async_copy(src, dst, esem.at[1 + k]))
        ends[-1].start()
    for copy in ends:
        copy.wait()
    for copy in heads + stats + spread_w + spread_d + spread_e + spread_v + spread_v2:
        copy.wait_send()


W_OUT = 12
X_ALL = 14


def back(*args):
    def vm(dims, dtype=F32):
        return pltpu.VMEM(dims, dtype)

    held = [vm((2, 2 * TOK, D), BF) if k == X_ALL else vm(a.shape, a.dtype) for k, a in enumerate(args) if k > 1 and k != W_OUT]
    results = [((TOK, D), BF), ((TOK, D), F32), ((8, D), F32), ((8, KV), F32), ((8, KV), F32), ((8, D), F32), ((16, 128), F32)]
    results.append(((PAIR, BLOCK, D), BF))
    landing = [vm((4, TOK, D), BF), vm((2, TOK, D), BF), vm((TOK, D), BF)]
    return comm_call(
        back_kernel,
        "back",
        6,
        [shape(*result) for result in results],
        [ANY] * 23,
        [ANY] * 8,
        held
        + [
            vm((TOK, D)),
            vm((TOK, D), BF),
            vm((LENGTH, 128), BF),
            vm((EP, 2 * TOK, 128), BF),
            vm(((10 + 5 * (KEPT - 4)) * TOK, 2 * TOK), BF),
            vm((LENGTH, 128)),
            vm((LENGTH, 128)),
            vm((LENGTH, 256)),
            vm((16, 256)),
            vm((16, 256)),
            vm((EP, 16, 256)),
            vm((D, WB), BF),
            vm((128, WB)),
            vm((REP, 8, WB)),
            vm((256, D)),
            vm((D, 256), BF),
            vm((REP, 64, 256), BF),
            vm((64, 256)),
            vm((EP, 8, 256)),
            vm((8, D)),
            vm((EP, 8, D)),
            vm((8, D)),
            vm((REP, 8, 128)),
            vm((4, TOK, D), BF),
            vm((4, TOK, D), BF),
        ]
        + landing
        + [vm((4, 128, WB), BF), vm((4, 128, WB), BF), vm((2, 128, WB), BF), vm((128, WB), BF)]
        + [DMA((10,))] * 6
        + [DMA((7,))] * 4
        + [DMA((15,))] * 4
        + [DMA((7,))] * 4
        + [DMA((15,))] * 2
        + [DMA((20,)), DMA((4,)), DMA((4,)), DMA((8,)), DMA((2,))]
        + [vm(*result) for k, result in enumerate(results) if k != 1]
        + grid_scratch() * 2
        + [DMA((12,))] * 4
        + [DMA((4,))] * 2,
        limit=64,
    )(*args)


def finish_kernel(
    xa_in, xb_in, out_in, ig_in, gq_in, gk_in, gv_in, go_in, pack,
    out_o, ig_o, gq_o, gk_o, gv_o, go_o, gr_o, va_o, vq_o, vk_o, vf_o, gate_o, up_o, down_o,
    x_s, gate_s, up_s, down_s, out_s, ig_s, gq_s, gk_s, gv_s, go_s, sem,
):
    loads = [
        pltpu.make_async_copy(xa_in, x_s.at[pl.ds(0, PAIR)], sem.at[9]),
        pltpu.make_async_copy(xb_in, x_s.at[pl.ds(PAIR, PAIR)], sem.at[10]),
    ]
    for load in loads:
        load.start()
    stages = [out_s, ig_s, gq_s, gk_s, gv_s, go_s]
    fetch = [
        pltpu.make_async_copy(src, dst, sem.at[k])
        for k, (src, dst) in enumerate(zip([out_in, ig_in, gq_in, gk_in, gv_in, go_in], stages))
    ]
    copies = [
        pltpu.make_async_copy(src, dst, sem.at[k])
        for k, (src, dst) in enumerate(zip(stages, [out_o, ig_o, gq_o, gk_o, gv_o, go_o]))
    ]
    for copy in fetch:
        copy.start()
    gr_o[...] = pack[0:8, :EXPERTS]
    va_o[...] = pack[8:9, :8]
    vq_o[...] = pack[9:10, :8]
    vk_o[...] = pack[10:11, :4]
    vf_o[...] = pack[11:12, :8]
    for load, copy in zip(fetch, copies):
        load.wait()
        copy.start()
    for load in loads:
        load.wait()
    gate_s[...] = x_s[:, :64, :FF].astype(F32)
    up_s[...] = x_s[:, :64, FF:].astype(F32)
    down_s[...] = x_s[:, 64:].astype(F32)
    pairs = [(gate_s, gate_o), (up_s, up_o), (down_s, down_o)]
    for k, (src, dst) in enumerate(pairs):
        copies.append(pltpu.make_async_copy(src, dst, sem.at[6 + k]))
        copies[-1].start()
    for copy in copies:
        copy.wait()


def finish(xa, xb, out, ig, gq, gk, gv, go, pack):
    gate, down = shape((LOCAL, 64, FF)), shape((LOCAL, 32, D))
    return pl.pallas_call(
        finish_kernel,
        out_shape=[shape(a.shape, a.dtype) for a in (out, ig, gq, gk, gv, go)]
        + [shape((8, EXPERTS)), shape((1, 8)), shape((1, 8)), shape((1, 4)), shape((1, 8)), gate, gate, down],
        in_specs=[ANY] * 8 + [VM],
        out_specs=[ANY] * 6 + [VM] * 5 + [ANY] * 3,
        scratch_shapes=[
            pltpu.VMEM((LOCAL, BLOCK, D), BF),
            pltpu.VMEM(gate.shape, F32),
            pltpu.VMEM(gate.shape, F32),
            pltpu.VMEM(down.shape, F32),
        ]
        + [pltpu.VMEM(a.shape, a.dtype) for a in (out, ig, gq, gk, gv, go)]
        + [
            DMA((11,)),
        ],
        compiler_params=pltpu.CompilerParams(vmem_limit_bytes=62 * MIB),
        name="finish",
    )(xa, xb, out, ig, gq, gk, gv, go, pack)


def body(
    tokens,
    segments,
    routes,
    w_query,
    w_key,
    w_value,
    w_out,
    w_router,
    gain_attn,
    gain_query,
    gain_key,
    gain_ffn,
    w_gate,
    w_up,
    w_down,
    out_grad,
):
    gains = [gain.reshape(1, -1) for gain in (gain_attn, gain_query, gain_key, gain_ffn)]
    cosine, sine = turn_tables()
    (
        x_all, g_all, lin, q, k, v, att, lse, hidden, moe_in, tables, attended, misc, router, whole_out, w_cols,
    ) = front(
        tokens, out_grad, w_query, w_key, w_value, w_out, w_router, *gains, segments, routes.T, cosine, sine
    )
    def over_copies(grads):
        grads = grads.reshape(PAIR, REP * BLOCK, D)
        return lax.psum_scatter(grads, "rep", scatter_dimension=1, tiled=True)

    m_all, tabs, y, z, gg_first, grads = experts_first(moe_in, tables, g_all, w_gate, w_up, w_down)
    sums_first = over_copies(grads)
    grad_moe, mixture, gg_last, grads = experts_last(m_all, tabs, y, z, g_all, w_gate, w_up, w_down)
    *rows, sums_last = back(
        grads.reshape(PAIR, 4, 4, BLOCK, D), mixture, grad_moe, gg_first, gg_last, tables, hidden, moe_in, out_grad, attended, misc, router, whole_out,
        w_cols, x_all, lin, q, k, v, att, lse, cosine, sine,
    )
    out, ig, gq, gk, gv, go, gr, va, vq, vk, vf, gate, up, down = finish(sums_first, sums_last, *rows)
    return out, ig, gq, gk, gv, go, gr, va.reshape(8), vq.reshape(8), vk.reshape(4), vf.reshape(8), gate, up, down


def solution(mesh):
    both = P(("rep", "ep"), None)
    line = P(("rep", "ep"))
    owner = P("ep", None, None)
    kept = P("ep", "rep", None)
    return jax.shard_map(
        body,
        mesh=mesh,
        in_specs=(both, P("rep", None)) + (both,) * 6 + (line,) * 4 + (owner,) * 3 + (both,),
        out_specs=(both,) * 7 + (line,) * 4 + (kept,) * 3,
        check_vma=False,
    )
```

```python
import functools

import jax
import jax.numpy as jnp
import numpy as np
from jax import lax
from jax.experimental import pallas as pl
from jax.experimental.pallas import tpu as pltpu
from jax.sharding import PartitionSpec as P

BF = jnp.bfloat16
F32 = jnp.float32
MESH = pl.DeviceIdType.MESH
ANY = pl.BlockSpec(memory_space=pl.ANY)
VM = pl.BlockSpec(memory_space=pltpu.VMEM)
DMA = pltpu.SemaphoreType.DMA
MIB = 1 << 20

HEADS = 16
KV_HEADS = 8
HEAD_DIM = 64
TOP = 8
WINDOW = 1024
EPSILON = 1e-06
ROPE_BASE = 10000.0
MASKED = -1e30
EP = 8
REP = 16
TOK = 256
LENGTH = 2048
D = 1024
KV = 512
FF = 512
EXPERTS = 32
LOCAL = 4
CAP = 88
NT = (((1,), (1,)), ((), ()))
TN = (((0,), (0,)), ((), ()))
HIGH = lax.Precision.HIGHEST


def dot(a, b):
    return jnp.dot(a, b, preferred_element_type=F32)


def dot_nt(a, b, precision=None):
    return lax.dot_general(a, b, NT, preferred_element_type=F32, precision=precision)


def dot_tn(a, b):
    return lax.dot_general(a, b, TN, preferred_element_type=F32)


def iota(shape, dim):
    return lax.broadcasted_iota(jnp.int32, shape, dim)


def ep_device(x, c):
    return {"ep": x * 2 + c}


def greet(devices):
    barrier = pltpu.get_barrier_semaphore()
    for device in devices:
        pl.semaphore_signal(barrier, inc=1, device_id=device, device_id_type=MESH)
    pl.semaphore_wait(barrier, len(devices))


def remote(src, dst, sems, i, device):
    return pltpu.make_async_remote_copy(
        src_ref=src,
        dst_ref=dst,
        send_sem=sems[0].at[i],
        recv_sem=sems[1].at[i],
        device_id=device,
        device_id_type=MESH,
    )


def place():
    e = lax.axis_index("ep")
    return e, e // 2, e % 2


def ep_others(e):
    return [(e + k) % EP for k in range(1, EP)]


def rep_others(r):
    return [(r + k) % REP for k in range(1, REP)]


class RingGather:
    SEMS = 10

    def __init__(self, x_ref, o_ref, sems, lsem):
        e, x, c = place()
        self.n = n = x_ref.shape[0]
        h = n // 2
        self.o_ref = o_ref
        right, left = ep_device((x + 1) % 4, c), ep_device((x + 3) % 4, c)
        peer = ep_device(x, 1 - c)
        b_left, b_right, b_opp = (((x + 3) % 4) * 2 + c, ((x + 1) % 4) * 2 + c, ((x + 2) % 4) * 2 + c)

        def rows(b, off=0, size=n):
            return o_ref.at[pl.ds(pl.multiple_of(b * n + off, 16), size)]

        low, high = x_ref.at[pl.ds(0, h)], x_ref.at[pl.ds(h, h)]
        self.first = [
            remote(low, rows(e, 0, h), sems, 0, right),
            remote(high, rows(e, h, h), sems, 2, left),
            remote(high, rows(e, h, h), sems, 1, right),
            remote(low, rows(e, 0, h), sems, 3, left),
            remote(x_ref, rows(e), sems, 4, peer),
        ]
        self.fwd_right = remote(rows(b_left, 0, h), rows(b_left, 0, h), sems, 5, right)
        self.fwd_left = remote(rows(b_right, h, h), rows(b_right, h, h), sems, 6, left)
        self.to_peer = [
            remote(rows(b_left), rows(b_left), sems, 7, peer),
            remote(rows(b_right), rows(b_right), sems, 8, peer),
            remote(rows(b_opp), rows(b_opp), sems, 9, peer),
        ]
        self.own = pltpu.make_async_copy(x_ref, rows(e), lsem)

    def start(self):
        for copy in self.first:
            copy.start()
        self.own.start()

    def forward_half(self):
        self.first[0].wait_recv()
        self.fwd_right.start()
        self.first[1].wait_recv()
        self.fwd_left.start()

    def forward_rest(self):
        self.first[2].wait_recv()
        self.to_peer[0].start()
        self.first[3].wait_recv()
        self.to_peer[1].start()

    def finish(self):
        self.fwd_right.wait_recv()
        self.fwd_left.wait_recv()
        self.to_peer[2].start()
        self.first[4].wait_recv()
        for copy in self.to_peer:
            copy.wait_recv()
        self.own.wait()
        for copy in self.first + [self.fwd_right, self.fwd_left] + self.to_peer:
            copy.wait_send()


class RingReduce:
    SEMS = 10
    STEP = 64

    def __init__(self, p_ref, n, pc, snd, rcv, hop, sems, lsems):
        e, x, c = place()
        self.n, self.h = n, n // 2
        h = n // 2
        self.pc, self.snd, self.rcv, self.hop = pc, snd, rcv, hop
        right, left = ep_device((x + 1) % 4, c), ep_device((x + 3) % 4, c)
        peer = ep_device(x, 1 - c)

        def rows(b):
            return p_ref.at[pl.ds(pl.multiple_of(b * n, 16), n)]

        chips = [(x + 2) % 4, (x + 1) % 4, (x + 3) % 4, x]
        self.swap = [remote(rows(b * 2 + 1 - c), pc.at[k], sems, k, peer) for k, b in enumerate(chips)]
        self.load = [
            pltpu.make_async_copy(rows(b * 2 + c), snd.at[k], lsems.at[k]) for k, b in enumerate(chips)
        ]
        low, high = pl.ds(0, h), pl.ds(h, h)
        self.opp = [
            remote(snd.at[0, low], hop.at[low], sems, 4, right),
            remote(snd.at[0, high], hop.at[high], sems, 5, left),
        ]
        self.near = [
            remote(snd.at[1, high], rcv.at[0, high], sems, 6, right),
            remote(snd.at[2, low], rcv.at[1, low], sems, 7, left),
        ]
        self.far = [
            remote(snd.at[1, low], rcv.at[0, low], sems, 8, right),
            remote(snd.at[2, high], rcv.at[1, high], sems, 9, left),
        ]

    def rows_loop(self, low, count, body):
        step = self.STEP

        def loop(i, carry):
            body(pl.ds(pl.multiple_of(low + i * step, 16), step))
            return carry

        lax.fori_loop(0, count // step, loop, 0)

    def merge(self, k):
        def body(s):
            self.snd[k, s] = (self.snd[k, s].astype(F32) + self.pc[k, s].astype(F32)).astype(BF)

        self.load[k].wait()
        self.swap[k].wait_recv()
        self.rows_loop(0, self.n, body)

    def merge_hop(self, k, low):
        def body(s):
            self.snd[k, s] = (self.snd[k, s].astype(F32) + self.hop[s].astype(F32)).astype(BF)

        self.rows_loop(low, self.h, body)

    def start(self):
        for copy in self.swap + self.load:
            copy.start()

    def push_opp(self):
        self.merge(0)
        for copy in self.opp:
            copy.start()

    def push_near(self):
        self.merge(1)
        self.near[0].start()
        self.merge(2)
        self.near[1].start()
        self.merge(3)

    def relay(self):
        self.opp[0].wait_recv()
        self.merge_hop(1, 0)
        self.far[0].start()
        self.opp[1].wait_recv()
        self.merge_hop(2, self.h)
        self.far[1].start()

    def finish(self, out_ref):
        for copy in self.near + self.far:
            copy.wait_recv()

        def body(s):
            out_ref[s] = self.snd[3, s].astype(F32) + (
                self.rcv[0, s].astype(F32) + self.rcv[1, s].astype(F32)
            )

        self.rows_loop(0, self.n, body)
        for copy in self.swap + self.opp + self.near + self.far:
            copy.wait_send()


class AxisReduce:
    def __init__(self, devices, snd, hop, rcv, sems, base):
        right, left = devices
        self.snd, self.hop, self.rcv = snd, hop, rcv
        self.opp = [
            remote(snd.at[0, 0], hop.at[0], sems, base, right),
            remote(snd.at[0, 1], hop.at[1], sems, base + 1, left),
        ]
        self.near = [
            remote(snd.at[2, 1], rcv.at[0, 1], sems, base + 2, right),
            remote(snd.at[1, 0], rcv.at[1, 0], sems, base + 3, left),
        ]
        self.far = [
            remote(snd.at[2, 0], rcv.at[0, 0], sems, base + 4, right),
            remote(snd.at[1, 1], rcv.at[1, 1], sems, base + 5, left),
        ]

    def push(self):
        for copy in self.opp + self.near:
            copy.start()

    def relay(self):
        for k, (slot, half) in enumerate(((2, 0), (1, 1))):
            self.opp[k].wait_recv()
            self.snd[slot, half] = (self.snd[slot, half].astype(F32) + self.hop[half].astype(F32)).astype(BF)
            self.far[k].start()

    def arrive(self):
        for copy in self.near + self.far:
            copy.wait_recv()

    def total(self, *index):
        return self.snd[(3,) + index].astype(F32) + (
            self.rcv[(0,) + index].astype(F32) + self.rcv[(1,) + index].astype(F32)
        )

    def leave(self):
        for copy in self.opp + self.near + self.far:
            copy.wait_send()


class GridReduce:
    def __init__(self, along_z, src, cols, snd, hop, rcv, snd2, hop2, rcv2, sems, lsems):
        r = lax.axis_index("rep")
        z, y = r // 4, r % 4
        along = (lambda k: {"rep": (z + k) % 4 * 4 + y}, lambda k: {"rep": z * 4 + (y + k) % 4})
        one, two = along if along_z else along[::-1]
        here, self.there = (z, y) if along_z else (y, z)
        offsets = (2, 3, 1, 0)
        cut = pl.ds(cols, FF)
        self.load = []
        for k, off in enumerate(offsets):
            b = (here + off) % 4
            block = src.at[:, b, :, :, cut] if along_z else src.at[:, :, b, :, cut]
            self.load.append(pltpu.make_async_copy(block, snd.at[k], lsems.at[k]))
        self.offsets, self.snd2 = offsets, snd2
        self.stage = AxisReduce((one(1), one(3)), snd, hop, rcv, sems, 0)
        self.last = AxisReduce((two(1), two(3)), snd2, hop2, rcv2, sems, 6)

    def push(self):
        for copy in self.load:
            copy.wait()
        self.stage.push()

    def turn(self):
        self.stage.arrive()
        for k, off in enumerate(self.offsets):
            b = (self.there + off) % 4
            for n in range(PAIR):
                self.snd2[k, n] = self.stage.total(n, b).astype(BF)
        self.last.push()

    def finish(self, out_ref, cols):
        self.last.arrive()
        for n in range(PAIR):
            out_ref[n, :, cols : cols + FF] = self.last.total(n).astype(BF)
        self.stage.leave()
        self.last.leave()


def grid_scratch():
    blocks = [(4, PAIR, 4, BLOCK, FF), (PAIR, 4, BLOCK, FF), (2, PAIR, 4, BLOCK, FF)]
    blocks += [(4, PAIR, BLOCK, FF), (PAIR, BLOCK, FF), (2, PAIR, BLOCK, FF)]
    return [pltpu.VMEM(dims, BF) for dims in blocks]


def comm_call(kernel, name, collective_id, out_shape, in_specs, out_specs, scratch, limit=48):
    return pl.pallas_call(
        kernel,
        out_shape=out_shape,
        in_specs=in_specs,
        out_specs=out_specs,
        scratch_shapes=scratch,
        compiler_params=pltpu.CompilerParams(
            collective_id=collective_id, has_side_effects=True, vmem_limit_bytes=limit * MIB
        ),
        name=name,
    )


def shape(dims, dtype=F32):
    return jax.ShapeDtypeStruct(dims, dtype)


WB = D + 128


def columns(*rows):
    pad = jnp.zeros((128 - len(rows), rows[0].shape[1]), F32)
    turned = jnp.transpose(jnp.concatenate(list(rows) + [pad], axis=0))
    return [turned[:, k : k + 1] for k in range(len(rows))]


def row_sums(values, bounds):
    width = values.shape[1]
    high = values.astype(BF)
    low = (values - high.astype(F32)).astype(BF)
    lane, row = iota((8, width), 1), iota((8, width), 0)
    chosen = jnp.zeros((8, width), F32)
    for k, (first, last) in enumerate(bounds):
        chosen = jnp.where((row == k) & (lane >= first) & (lane < last), 1.0, chosen)
    chosen = chosen.astype(BF)
    return dot_nt(jnp.concatenate([chosen, chosen], axis=1), jnp.concatenate([high, low], axis=1))


PARTS = ((0, 128), (128, 192))


def turn_tables():
    half = HEAD_DIM // 2
    freq = np.float32(ROPE_BASE) ** (-(np.arange(half, dtype=np.float32) * np.float32(2.0) / np.float32(HEAD_DIM)))
    angles = np.arange(LENGTH, dtype=np.float32)[:, None] * freq.astype(np.float32)[None, :]
    c, s = np.cos(angles), np.sin(angles)
    cosine = np.concatenate([c, c, c, c], axis=1)
    sine = np.concatenate([-s, s, -s, s], axis=1)
    return cosine.astype(np.float32), sine.astype(np.float32)


def turn(u, cosine, sine):
    early = iota(u.shape, 1) % HEAD_DIM < HEAD_DIM // 2
    partner = jnp.where(early, pltpu.roll(u, 96, 1), pltpu.roll(u, 32, 1))
    return u * cosine + partner * sine


def block_rows(b):
    return pl.ds(pl.multiple_of(b * TOK, TOK), TOK)


def stack_heads(values):
    first = iota(values.shape, 1) < HEAD_DIM
    return jnp.concatenate([jnp.where(first, values, 0.0), jnp.where(first, 0.0, values)], axis=0)


def merge_heads(values):
    first = iota((TOK, 128), 1) < HEAD_DIM
    return jnp.where(first, values[:TOK], values[TOK:])


def front_kernel(
    tok, cot, wq, wk, wv, wo_in, router_in, ga_in, gq_in, gk_in, gf_in, seg, rts_in, cos_in, sin_in,
    x_all, g_all, lin_h, q_h, k_h, v_h, a_h, lse_h, hid_h, m_h, tab_h, att_h, misc_h, rout_h, whole_h, wcol_h,
    lin, q_o, k_o, v_o, a_o, lse_o, hid_o, m_o, tab_o, att_o, misc, rout_o, whole, wcol, hsem,
    x_s, cot_s, tiny, tiny_b, smalls, wsl, wos, wg, wog, wog2, w32, gains_s, cos_ref, sin_ref, sums, held,
    s_tok, r_tok, s_cot, r_cot, s_w, r_w, s_o, r_o, s_st, r_st, s_t, r_t, s_a, r_a, lsem,
):
    r = lax.axis_index("rep")
    e, x, c = place()
    others = ep_others(e)
    copies = rep_others(r)
    first = iota((TOK, 128), 1) < HEAD_DIM
    gain_a, gain_f, gain = misc.at[0:1], misc.at[1:2], misc.at[2:3, 0:256]
    lo, st = misc.at[8:16, 0:256], misc.at[16:32, 0:256]
    greet([{"ep": d} for d in others] + [{"rep": d} for d in copies])
    leaving = []

    def leave(*pairs):
        for src, dst in pairs:
            leaving.append(pltpu.make_async_copy(src, dst, hsem.at[len(leaving)]))
            leaving[-1].start()

    misc[...] = jnp.zeros((32, D), F32)

    tiny[...] = jnp.zeros((16, 128), F32)
    tiny[0:8, 0:EXPERTS] = router_in[...].astype(F32)
    for lane, ref in ((0, ga_in), (8, gq_in), (16, gk_in), (20, gf_in)):
        tiny[8:9, lane : lane + ref.shape[1]] = ref[...].astype(F32)
    tiny_b[...] = tiny[...].astype(BF)
    low_lanes = iota((8, 128), 1) < HEAD_DIM
    for d in range(EP):
        k_t = wk[:, (d // 2) * 128 : (d // 2 + 1) * 128].astype(F32)
        v_t = wv[:, (d // 2) * 128 : (d // 2 + 1) * 128].astype(F32)
        if d % 2:
            k_t = pltpu.roll(k_t, HEAD_DIM, 1)
        else:
            v_t = pltpu.roll(v_t, HEAD_DIM, 1)
        q_t = wq[:, d * 128 : (d + 1) * 128].astype(F32)
        wsl[d] = jnp.concatenate([q_t, jnp.where(low_lanes, k_t, v_t)], axis=0).astype(BF)
    for half in range(2):
        wos[half] = jnp.concatenate(
            [wo_in[:, j * 128 : (j + 1) * 128].astype(F32) for j in range(half * 4, half * 4 + 4)], axis=0
        ).astype(BF)

    def cols_of(b):
        return wg.at[r, pl.ds(pl.multiple_of(b * 16, 16), 16)]

    stage_w = [remote(wsl.at[d], cols_of(e), (s_w, r_w), k, {"ep": d}) for k, d in enumerate(others)]
    stage_t = [remote(tiny_b, smalls.at[e], (s_t, r_t), k, {"ep": d}) for k, d in enumerate(others)]
    stage_o = [remote(wos.at[d % 2], wog.at[r, e], (s_o, r_o), k, {"ep": d}) for k, d in enumerate(others)]
    spread_w = [remote(wg.at[r], wg.at[r], (s_w, r_w), 7 + k, {"rep": d}) for k, d in enumerate(copies)]
    spread_o = [remote(wog.at[r], wog.at[r], (s_o, r_o), 7 + k, {"rep": d}) for k, d in enumerate(copies)]
    other_half = remote(wog, wog2, (s_o, r_o), 22, ep_device(x, 1 - c))
    tokens = RingGather(tok, x_s, (s_tok, r_tok), lsem.at[0])
    grads = RingGather(cot_s, g_all, (s_cot, r_cot), lsem.at[1])
    for copy in stage_w + stage_t:
        copy.start()
    tokens.start()
    for copy in stage_o:
        copy.start()
    tables = [
        pltpu.make_async_copy(cos_in, cos_ref, lsem.at[2]),
        pltpu.make_async_copy(sin_in, sin_ref, lsem.at[3]),
        pltpu.make_async_copy(cot, cot_s, lsem.at[5]),
    ]
    for copy in tables:
        copy.start()
    cols_of(e)[...] = wsl[e]
    smalls[e] = tiny_b[...]
    wog[r, e] = wos[c]
    for copy in stage_w + stage_t:
        copy.wait_recv()
    router_tiles = [
        sum(pltpu.roll(smalls[4 * a + b][:8].astype(F32), 32 * b, 1) if b else smalls[4 * a][:8].astype(F32) for b in range(4))
        for a in range(2)
    ]
    gain_rows = [smalls[d][8:9].astype(F32) for d in range(EP)]
    wg[r, 128:160] = jnp.concatenate(router_tiles + gain_rows + [jnp.zeros((8, 128), F32)], axis=0).astype(BF)
    for copy in spread_w:
        copy.start()
    tokens.forward_half()
    tables[2].wait()
    grads.start()
    tokens.forward_rest()

    routed = rts_in[...]
    hit = jnp.zeros((EXPERTS, TOK), F32)
    for k in range(TOP):
        hit = jnp.where(iota((EXPERTS, TOK), 0) == routed[k : k + 1], 1.0, hit)
    before = jnp.where(iota((TOK, TOK), 0) < iota((TOK, TOK), 1), 1.0, 0.0).astype(BF)
    slots = jnp.where(hit > 0.0, dot(hit.astype(BF), before), -1.0)
    segs = jnp.concatenate([seg[:, b * TOK : (b + 1) * TOK] for b in range(EP)], axis=0)
    opening = jnp.zeros((EP, TOK), F32)
    for value in range(2):
        count = jnp.sum(jnp.where(segs == value, 1.0, 0.0), axis=1, keepdims=True)
        opening = opening + jnp.where(segs > value, jnp.sum(count, axis=0, keepdims=True), 0.0)
    places = (iota((EP, TOK), 0) * TOK + iota((EP, TOK), 1)).astype(F32)
    lo[...] = jnp.maximum(opening, places - (WINDOW - 1))

    for copy in spread_w:
        copy.wait_recv()
    for copy in stage_o:
        copy.wait_recv()
    for copy in spread_o:
        copy.start()

    def unpack(b, carry):
        for d in range(EP):
            tile = wg[b, d * 16 : d * 16 + 16].astype(F32)
            rows = pl.ds(pl.multiple_of(b * 64 + d * 8, 8), 8)
            w32[rows, 0:128] = tile[0:8]
            w32[rows, 128:256] = tile[8:16]
        extra = wg[b, 128:160].astype(F32)
        for d in range(EP):
            tile = extra[d // 4 * 8 : d // 4 * 8 + 8]
            if d % 4:
                tile = pltpu.roll(tile, 128 - 32 * (d % 4), 1)
            w32[pl.ds(pl.multiple_of(b * 64 + d * 8, 8), 8), 256:384] = tile
        gains_s[pl.ds(pl.multiple_of(b * 8, 8), 8)] = extra[16:24]
        return carry

    lax.fori_loop(0, REP, unpack, 0)
    wcol[...] = w32[:, :256].astype(BF)
    rout_o[...] = jnp.transpose(w32[:, 256:384])[:EXPERTS].astype(BF)
    packed = gains_s[...].astype(BF)

    def spread_gain(width, group, base, shift):
        lane = base + iota((128, width), 1) % group
        picked = dot(packed, jnp.where(iota((128, width), 0) == lane, 1.0, 0.0).astype(BF))
        mine = iota((128, width), 0) == shift + iota((128, width), 1) // group
        return jnp.sum(jnp.where(mine, picked, 0.0), axis=0, keepdims=True)

    gain_a[...] = spread_gain(D, 8, 0, 0)
    gain_f[...] = spread_gain(D, 8, 20, 0)
    key_part = spread_gain(128, 4, 16, e * 16)
    gain[:, :128] = spread_gain(128, 8, 8, e * 16)
    gain[:, 128:] = jnp.where(iota((1, 128), 1) < HEAD_DIM, key_part, 1.0)

    leave((wcol, wcol_h), (rout_o, rout_h))
    tokens.first[4].wait_recv()
    tokens.own.wait()

    def project(k, carry):
        @pl.when(k == 2)
        def _():
            tokens.fwd_right.wait_recv()
            tokens.fwd_left.wait_recv()
            tokens.to_peer[2].start()
            tokens.to_peer[1].wait_recv()

        @pl.when(k == 4)
        def _():
            tokens.to_peer[0].wait_recv()

        @pl.when(k == 6)
        def _():
            tokens.to_peer[2].wait_recv()

        g = k // 2
        b = (2 * (x + g + g // 2 - 2 * (g // 3)) + k % 2) % EP
        rows = block_rows(b)
        values = x_s[rows].astype(F32)
        r1 = lax.rsqrt(jnp.mean(values * values, axis=1, keepdims=True) + EPSILON)
        normed = (values * r1 * gain_a[...]).astype(BF)
        out = dot(normed, wcol[...])
        lin[rows] = out
        both = row_sums(out * out, PARTS)
        sums[pl.ds(2 * b, 1)] = both[0:1]
        sums[pl.ds(2 * b + 1, 1)] = both[1:2]
        return carry

    lax.fori_loop(0, EP, project, 0)
    stats = [remote(sums, held.at[e], (s_st, r_st), k, {"ep": d}) for k, d in enumerate(others)]
    for copy in stats:
        copy.start()
    held[e] = sums[...]
    keep = pltpu.make_async_copy(x_s, x_all, lsem.at[4])
    keep.start()
    for copy in tables[:2]:
        copy.wait()
    for copy in stats:
        copy.wait_recv()
    total = held[0]
    for k in range(1, EP):
        total = total + held[k]
    st[...] = total
    grads.forward_half()
    leave((lin, lin_h), (misc, misc_h))

    def prepare(b, carry):
        rows = block_rows(b)
        cq, ck = columns(
            lax.rsqrt(st[pl.ds(2 * b, 1)] * (1.0 / D) + EPSILON),
            lax.rsqrt(st[pl.ds(2 * b + 1, 1)] * (1.0 / KV) + EPSILON),
        )
        cosine, sine = cos_ref[rows], sin_ref[rows]
        q_o[rows] = turn(lin[rows, :128] * cq * gain[:, :128], cosine, sine).astype(BF)
        kv = lin[rows, 128:]
        kv = jnp.where(first, turn(kv * ck * gain[:, 128:], cosine, sine), kv)
        other = pltpu.roll(kv, HEAD_DIM, 1)
        k_o[rows] = jnp.where(first, kv, other).astype(BF)
        v_o[rows] = jnp.where(first, other, kv).astype(BF)
        return carry

    lax.fori_loop(0, EP, prepare, 0, unroll=2)
    leave((q_o, q_h), (k_o, k_h), (v_o, v_h))

    def heads(i, source):
        cols = pl.ds(pl.multiple_of(source * 128, 128), 128)
        return pltpu.make_async_remote_copy(
            src_ref=a_o.at[block_rows(i)],
            dst_ref=att_o.at[:, cols],
            send_sem=s_a.at[i],
            recv_sem=r_a.at[source],
            device_id={"ep": i},
            device_id_type=MESH,
        )

    def attend_block(i, n):
        rows = block_rows(i)
        past = (n - 1) * TOK
        q2 = stack_heads(q_o[rows].astype(F32) * HEAD_DIM ** (-0.5)).astype(BF)
        (lo_col,) = columns(lo[pl.ds(i, 1)])
        low = jnp.concatenate([lo_col, lo_col], axis=0)
        own_key = (iota((2 * TOK, TOK), 1) + i * TOK).astype(F32)
        query = (iota((2 * TOK, TOK), 0) % TOK + i * TOK).astype(F32)
        s_own = jnp.where((own_key >= low) & (own_key <= query), dot_nt(q2, k_o[rows]), MASKED)
        m = jnp.max(s_own, axis=1, keepdims=True)
        if past:
            early = pl.ds(pl.multiple_of((i - n + 1) * TOK, TOK), past)
            key = (iota((2 * TOK, past), 1) + (i - n + 1) * TOK).astype(F32)
            s = jnp.where(key >= low, dot_nt(q2, k_o[early]), MASKED)
            m = jnp.maximum(m, jnp.max(s, axis=1, keepdims=True))
        p_own = jnp.exp(s_own - m)
        total = jnp.sum(p_own, axis=1, keepdims=True)
        out = dot(p_own.astype(BF), v_o[rows])
        if past:
            p = jnp.exp(s - m)
            total = total + jnp.sum(p, axis=1, keepdims=True)
            out = out + dot(p.astype(BF), v_o[early])
        a_o[rows] = merge_heads(out / total).astype(BF)
        lse = jnp.broadcast_to(m + jnp.log(total), (2 * TOK, 128))
        lse_o[i] = jnp.transpose(lse)[:8]

        @pl.when(i != e)
        def _():
            heads(i, e).start()

        @pl.when(i == e)
        def _():
            att_o[:, pl.ds(pl.multiple_of(e * 128, 128), 128)] = a_o[rows]

    def later(i, carry):
        attend_block(i, 5)

        @pl.when(i == 5)
        def _():
            grads.fwd_right.wait_recv()
            grads.fwd_left.wait_recv()
            grads.to_peer[2].start()

        return carry

    for i in range(4):
        attend_block(i, i + 1)
    grads.forward_rest()
    for copy in spread_o:
        copy.wait_recv()
    other_half.start()
    lax.fori_loop(4, EP, later, 0)

    leave((a_o, a_h), (lse_o, lse_h))
    other_half.wait_recv()

    def unpack_out(b, carry):
        for d in range(EP):
            rows = pl.ds(pl.multiple_of(b * 64 + d * 8, 8), 8)
            for half, held_half in ((c, wog), (1 - c, wog2)):
                tile = held_half[b, d].astype(F32)
                for j in range(4):
                    w32[rows, pl.ds(pl.multiple_of(half * 512 + j * 128, 128), 128)] = tile[j * 8 : (j + 1) * 8]
        return carry

    lax.fori_loop(0, REP, unpack_out, 0)
    whole[...] = w32[...].astype(BF)
    leave((whole, whole_h))
    for d in others:
        heads(d, d).wait_recv()
    leave((att_o, att_h))

    hidden = x_s[block_rows(e)].astype(F32) + dot(att_o[...], whole[...])
    hid_o[...] = hidden
    r2 = lax.rsqrt(jnp.mean(hidden * hidden, axis=1, keepdims=True) + EPSILON)
    moe_in = (hidden * r2 * gain_f[...]).astype(BF)
    m_o[...] = moe_in
    leave((hid_o, hid_h), (m_o, m_h))
    logits = dot_nt(rout_o[...], moe_in)
    chosen = hit > 0.0
    logits = jnp.where(chosen, logits, MASKED)
    raised = jnp.where(chosen, jnp.exp(logits - jnp.max(logits, axis=0, keepdims=True)), 0.0)
    gates = raised / jnp.sum(raised, axis=0, keepdims=True)
    for d in range(EP):
        part = slice(d * LOCAL, (d + 1) * LOCAL)
        tab_o[d] = jnp.concatenate([slots[part], gates[part]], axis=0)
    leave((tab_o, tab_h))

    grads.first[4].wait_recv()
    for copy in grads.to_peer:
        copy.wait_recv()
    grads.own.wait()
    keep.wait()
    for copy in leaving:
        copy.wait()
    for d in others:
        heads(d, d).wait_send()
    for ring in (tokens, grads):
        for copy in ring.first + [ring.fwd_right, ring.fwd_left] + ring.to_peer:
            copy.wait_send()
    for copy in stage_w + stage_t + stage_o + spread_w + spread_o + stats + [other_half]:
        copy.wait_send()


def front(*args):
    results = [
        shape((LENGTH, D), BF),
        shape((LENGTH, D), BF),
        shape((LENGTH, 256)),
        shape((LENGTH, 128), BF),
        shape((LENGTH, 128), BF),
        shape((LENGTH, 128), BF),
        shape((LENGTH, 128), BF),
        shape((EP, 8, 2 * TOK)),
        shape((TOK, D)),
        shape((TOK, D), BF),
        shape((EP, 2 * LOCAL, TOK)),
        shape((TOK, D), BF),
        shape((32, D)),
        shape((EXPERTS, D), BF),
        shape((D, D), BF),
        shape((D, 256), BF),
    ]
    return comm_call(
        front_kernel,
        "front",
        1,
        results,
        [ANY, ANY] + [VM] * 11 + [ANY, ANY],
        [ANY] * len(results),
        [pltpu.VMEM(a.shape, a.dtype) for a in results[2:]]
        + [
            DMA((14,)),
            pltpu.VMEM((LENGTH, D), BF),
            pltpu.VMEM((TOK, D), BF),
            pltpu.VMEM((16, 128), F32),
            pltpu.VMEM((16, 128), BF),
            pltpu.VMEM((EP, 16, 128), BF),
            pltpu.VMEM((EP, 16, 128), BF),
            pltpu.VMEM((2, 32, 128), BF),
            pltpu.VMEM((REP, 160, 128), BF),
            pltpu.VMEM((REP, EP, 32, 128), BF),
            pltpu.VMEM((REP, EP, 32, 128), BF),
            pltpu.VMEM((D, D), F32),
            pltpu.VMEM((128, 128), F32),
            pltpu.VMEM((LENGTH, 128), F32),
            pltpu.VMEM((LENGTH, 128), F32),
            pltpu.VMEM((16, 256), F32),
            pltpu.VMEM((EP, 16, 256), F32),
        ]
        + [DMA((10,))] * 4
        + [DMA((23,))] * 4
        + [DMA((7,))] * 4
        + [DMA((8,))] * 2
        + [DMA((6,))],
        limit=60,
    )(*args)


class ChipReduce:
    SEMS = 10
    STEP = 64

    def __init__(self, n, swo, snd, pc, rcv, hop, sems):
        e, x, c = place()
        self.n, self.h = n, n // 2
        h = n // 2
        self.snd, self.pc, self.rcv, self.hop = snd, pc, rcv, hop
        right, left = ep_device((x + 1) % 4, c), ep_device((x + 3) % 4, c)
        peer = ep_device(x, 1 - c)
        self.swap = lambda k: remote(swo.at[k], pc.at[k], sems, k, peer)
        low, high = pl.ds(0, h), pl.ds(h, h)
        self.opp = [
            remote(snd.at[0, low], hop.at[low], sems, 4, right),
            remote(snd.at[0, high], hop.at[high], sems, 5, left),
        ]
        self.near = [
            remote(snd.at[2, high], rcv.at[0, high], sems, 6, right),
            remote(snd.at[1, low], rcv.at[1, low], sems, 7, left),
        ]
        self.far = [
            remote(snd.at[2, low], rcv.at[0, low], sems, 8, right),
            remote(snd.at[1, high], rcv.at[1, high], sems, 9, left),
        ]

    def rows_loop(self, low, count, body):
        step = self.STEP

        def loop(i, carry):
            body(pl.ds(pl.multiple_of(low + i * step, 16), step))
            return carry

        lax.fori_loop(0, count // step, loop, 0)

    def merge(self, k):
        def body(s):
            self.snd[k, s] = (self.snd[k, s].astype(F32) + self.pc[k, s].astype(F32)).astype(BF)

        self.swap(k).wait_recv()
        self.rows_loop(0, self.n, body)

    def merge_hop(self, k, low):
        def body(s):
            self.snd[k, s] = (self.snd[k, s].astype(F32) + self.hop[s].astype(F32)).astype(BF)

        self.rows_loop(low, self.h, body)

    def send_opp(self):
        self.merge(0)
        for copy in self.opp:
            copy.start()

    def near_right(self):
        self.merge(2)
        self.near[0].start()

    def near_left(self):
        self.merge(1)
        self.near[1].start()

    def send_near(self):
        self.near_right()
        self.near_left()

    def send_far(self):
        self.opp[0].wait_recv()
        self.merge_hop(2, 0)
        self.far[0].start()
        self.opp[1].wait_recv()
        self.merge_hop(1, self.h)
        self.far[1].start()

    def finish(self, out_ref):
        for copy in self.near + self.far:
            copy.wait_recv()

        def body(s):
            out_ref[s] = self.snd[3, s].astype(F32) + (
                self.rcv[0, s].astype(F32) + self.rcv[1, s].astype(F32)
            )

        self.rows_loop(0, self.n, body)
        for copy in [self.swap(k) for k in range(4)] + self.opp + self.near + self.far:
            copy.wait_send()


PAIR = 2
ROWS = EP * CAP
CHIP = 2 * CAP
BLOCK = 96


def chip_rows(q):
    return pl.ds(pl.multiple_of(q * CHIP, 16), CHIP)


def chip_tokens(q):
    return pl.ds(pl.multiple_of(q * 2 * TOK, 2 * TOK), 2 * TOK)


def expert_hits(tab, e, n, q):
    row = slice(n, n + 1)
    second = tab[2 * q + 1, row]
    slots = jnp.concatenate([tab[2 * q, row], jnp.where(second >= 0.0, second + CAP, -1.0)], axis=1)
    return iota((CHIP, 2 * TOK), 0).astype(F32) == slots


def one_hot(hit):
    return jnp.where(hit, 1.0, 0.0).astype(BF)


def expert_chip(q, e, start, tab, m_ref, g_ref, wgu, wd, a_s, act_s, gp_s, dgu_s, y_s, z_s, ggt):
    hits = [expert_hits(tab, e, start + n, q) for n in range(PAIR)]
    chosen = jnp.concatenate([one_hot(hit) for hit in hits], axis=0)
    rows = chip_rows(q)
    a_both = dot(chosen, m_ref[chip_tokens(q)]).astype(BF)
    c_both = dot(chosen, g_ref[chip_tokens(q)]).astype(BF)
    for n in range(PAIR):
        part = slice(n * CHIP, (n + 1) * CHIP)
        row = slice(LOCAL + start + n, LOCAL + start + n + 1)
        gates = jnp.concatenate([tab[2 * q, row], tab[2 * q + 1, row]], axis=1)
        weight = jnp.sum(jnp.where(hits[n], gates, 0.0), axis=1, keepdims=True)
        a, cot = a_both[part], c_both[part]
        lin = dot(a, wgu[n])
        back = dot_nt(cot, wd[n])
        gate_lin, up_lin = lin[:, :FF], lin[:, FF:]
        sig = jax.nn.sigmoid(gate_lin)
        silu = gate_lin * sig
        act = silu * up_lin
        act_low = act.astype(BF)
        produced = dot(act_low, wd[n]).astype(BF).astype(F32)
        gg = jnp.sum(act * back, axis=1, keepdims=True)
        back = back * weight
        dgate = (back * up_lin * sig * (1.0 + gate_lin * (1.0 - sig))).astype(BF)
        dup = (back * silu).astype(BF)
        dgu = jnp.concatenate([dgate, dup], axis=1)
        a_s[n, rows] = a
        act_s[n, rows] = act_low
        gp_s[n, rows] = (weight * cot.astype(F32)).astype(BF)
        dgu_s[n, rows] = dgu
        y_s[n, rows] = (weight * produced).astype(BF)
        z_s[n, rows] = dot_nt(dgu, wgu[n]).astype(BF)
        gg_row = jnp.sum(jnp.where(hits[n], gg, 0.0), axis=0, keepdims=True)
        ggt[2 * q, n : n + 1] = gg_row[:, :TOK]
        ggt[2 * q + 1, n : n + 1] = gg_row[:, TOK:]


def expert_grads(n, a_s, act_s, gp_s, dgu_s, eg):
    eg[n, :, :64] = dot_tn(a_s[n], dgu_s[n]).astype(BF).reshape(REP, 64, D)
    eg[n, :, 64:] = dot_tn(act_s[n], gp_s[n]).astype(BF).reshape(REP, 32, D)


def load_weights(start, wg_in, wu_in, wd_in, wgu, wd, sems):
    some = pl.ds(start, PAIR)
    return [
        pltpu.make_async_copy(wg_in.at[some], wgu.at[:, :, pl.ds(0, FF)], sems.at[0]),
        pltpu.make_async_copy(wu_in.at[some], wgu.at[:, :, pl.ds(FF, FF)], sems.at[1]),
        pltpu.make_async_copy(wd_in.at[some], wd, sems.at[2]),
    ]


def send_gates(ggt, gg_o, e, sems, lsem):
    copies = [remote(ggt.at[d], gg_o.at[e], sems, k, {"ep": d}) for k, d in enumerate(ep_others(e))]
    return copies, pltpu.make_async_copy(ggt.at[e], gg_o.at[e], lsem)


def experts_first_kernel(
    m_in, t_in, g_in, wg_in, wu_in, wd_in, m_o, tab_o, y_o, z_o, gg_o, eg_o,
    m_ref, tab, g_ref, wgu, wd, a_s, act_s, gp_s, dgu_s, y_s, z_s, ggt, eg,
    s_m, r_m, s_t, r_t, s_g, r_g, lsem, wsem, gsem, esem,
):
    e, x, c = place()
    others = ep_others(e)
    greet([{"ep": d} for d in others])
    ring = RingGather(m_in, m_ref, (s_m, r_m), lsem.at[0])
    tables = [remote(t_in.at[d], tab.at[e], (s_t, r_t), k, {"ep": d}) for k, d in enumerate(others)]
    for copy in tables:
        copy.start()
    ring.start()
    own = pltpu.make_async_copy(t_in.at[e], tab.at[e], lsem.at[1])
    loads = load_weights(0, wg_in, wu_in, wd_in, wgu, wd, wsem)
    cots = [
        pltpu.make_async_copy(g_in.at[chip_tokens(q)], g_ref.at[chip_tokens(q)], gsem.at[k])
        for k, q in enumerate([x, (x + 1) % 4, (x + 3) % 4, (x + 2) % 4])
    ]
    for copy in [own] + loads + cots:
        copy.start()
    ggt[...] = jnp.zeros((EP, 8, TOK), F32)
    kept = pltpu.make_async_copy(m_ref, m_o, lsem.at[2])

    def chips(k, carry):
        @pl.when(k == 0)
        def _():
            ring.first[0].wait_recv()
            ring.fwd_right.start()
            ring.first[1].wait_recv()
            ring.fwd_left.start()
            ring.first[4].wait_recv()
            ring.own.wait()
            own.wait()
            for copy in tables:
                copy.wait_recv()
            for copy in loads:
                copy.wait()
            cots[0].wait()

        @pl.when(k == 1)
        def _():
            ring.first[3].wait_recv()
            ring.to_peer[1].start()
            ring.first[2].wait_recv()
            ring.to_peer[0].start()
            ring.to_peer[1].wait_recv()
            cots[1].wait()

        @pl.when(k == 2)
        def _():
            ring.fwd_right.wait_recv()
            ring.fwd_left.wait_recv()
            ring.to_peer[2].start()
            ring.to_peer[0].wait_recv()
            cots[2].wait()

        @pl.when(k == 3)
        def _():
            ring.to_peer[2].wait_recv()
            cots[3].wait()
            kept.start()

        q = (x + k + k // 2 - 2 * (k // 3)) % 4
        expert_chip(q, e, 0, tab, m_ref, g_ref, wgu, wd, a_s, act_s, gp_s, dgu_s, y_s, z_s, ggt)
        return carry

    lax.fori_loop(0, 4, chips, 0)
    gates, own_gates = send_gates(ggt, gg_o, e, (s_g, r_g), lsem.at[3])
    states = [
        pltpu.make_async_copy(tab, tab_o, lsem.at[4]),
        pltpu.make_async_copy(y_s, y_o, lsem.at[5]),
        pltpu.make_async_copy(z_s, z_o, lsem.at[6]),
    ]
    for copy in gates + [own_gates] + states:
        copy.start()
    for n in range(PAIR):
        expert_grads(n, a_s, act_s, gp_s, dgu_s, eg)
        states.append(pltpu.make_async_copy(eg.at[n], eg_o.at[n], esem.at[n]))
        states[-1].start()
    for copy in states + [kept, own_gates]:
        copy.wait()
    for copy in gates:
        copy.wait_recv()
    for copy in ring.first + [ring.fwd_right, ring.fwd_left] + ring.to_peer + tables + gates:
        copy.wait_send()


def pair_scratch():
    return [
        pltpu.VMEM((LENGTH, D), BF),
        pltpu.VMEM((EP, 2 * LOCAL, TOK), F32),
        pltpu.VMEM((LENGTH, D), BF),
        pltpu.VMEM((PAIR, D, 2 * FF), BF),
        pltpu.VMEM((PAIR, FF, D), BF),
        pltpu.VMEM((PAIR, ROWS, D), BF),
        pltpu.VMEM((PAIR, ROWS, FF), BF),
        pltpu.VMEM((PAIR, ROWS, D), BF),
        pltpu.VMEM((PAIR, ROWS, D), BF),
        pltpu.VMEM((PAIR, ROWS, D), BF),
        pltpu.VMEM((PAIR, ROWS, D), BF),
        pltpu.VMEM((EP, 8, TOK), F32),
        pltpu.VMEM((PAIR, REP, BLOCK, D), BF),
    ]


def experts_first(m, t, g_all, wg, wu, wd):
    return comm_call(
        experts_first_kernel,
        "experts_first",
        2,
        [
            shape((LENGTH, D), BF),
            shape((EP, 2 * LOCAL, TOK)),
            shape((PAIR, ROWS, D), BF),
            shape((PAIR, ROWS, D), BF),
            shape((EP, 8, TOK)),
            shape((PAIR, REP, BLOCK, D), BF),
        ],
        [ANY] * 6,
        [ANY] * 6,
        pair_scratch()
        + [DMA((10,))] * 2
        + [DMA((7,))] * 4
        + [DMA((7,)), DMA((3,)), DMA((4,)), DMA((2,))],
        limit=60,
    )(m, t, g_all, wg, wu, wd)


def experts_last_kernel(
    m_in, t_in, y_in, z_in, g_in, wg_in, wu_in, wd_in, gm_o, mix_o, gg_o, eg_o,
    m_ref, tab, g_ref, wgu, wd, a_s, act_s, gp_s, dgu_s, y_s, z_s, ggt, eg,
    y_f, z_f, gm, swo, snd, pc, rcv, hop, mix_z, mix_y,
    s_r, r_r, s_g, r_g, lsem, wsem, gsem, msem, esem, osem,
):
    e, x, c = place()
    order = [(x + 2) % 4, (x + 3) % 4, (x + 1) % 4, x]
    loads = [pltpu.make_async_copy(t_in, tab, lsem.at[0])] + load_weights(2, wg_in, wu_in, wd_in, wgu, wd, wsem)
    rows = [
        (
            pltpu.make_async_copy(m_in.at[chip_tokens(q)], m_ref.at[chip_tokens(q)], msem.at[k]),
            pltpu.make_async_copy(g_in.at[chip_tokens(q)], g_ref.at[chip_tokens(q)], gsem.at[k]),
        )
        for k, q in enumerate(order)
    ]
    firsts = [pltpu.make_async_copy(z_in, z_f, lsem.at[1]), pltpu.make_async_copy(y_in, y_f, lsem.at[2])]
    for copy in loads + list(rows[0]) + [firsts[0]] + list(rows[1] + rows[2] + rows[3]) + [firsts[1]]:
        copy.start()
    greet([{"ep": d} for d in ep_others(e)])
    red = ChipReduce(TOK, swo, snd, pc, rcv, hop, (s_r, r_r))
    ggt[...] = jnp.zeros((EP, 8, TOK), F32)

    def combine(q, early, late):
        chosen = jnp.concatenate([one_hot(expert_hits(tab, e, n, q)) for n in range(LOCAL)], axis=0)
        part = chip_rows(q)
        values = [ref[n, part] for ref in (early, late) for n in range(PAIR)]
        return dot_tn(chosen, jnp.concatenate(values, axis=0)).astype(BF)

    for copy in loads:
        copy.wait()

    def chips(k, carry):
        for step in range(4):

            @pl.when(k == step)
            def _(step=step):
                for copy in rows[step]:
                    copy.wait()
                if step == 0:
                    firsts[0].wait()

        q = (x + 2 + k - (k // 2) * (2 * k - 1)) % 4
        expert_chip(q, e, 2, tab, m_ref, g_ref, wgu, wd, a_s, act_s, gp_s, dgu_s, y_s, z_s, ggt)

        @pl.when(k == 2)
        def _():
            red.near_left()

        @pl.when(k == 3)
        def _():
            red.near_right()

        mix_z[...] = combine(q, z_f, z_s)
        swo[k] = mix_z[pl.ds(pl.multiple_of((1 - c) * TOK, TOK), TOK)]
        red.swap(k).start()
        snd[k] = mix_z[pl.ds(pl.multiple_of(c * TOK, TOK), TOK)]

        @pl.when(k == 0)
        def _():
            red.send_opp()

        return carry

    lax.fori_loop(0, 4, chips, 0)
    red.send_far()
    gates, own_gates = send_gates(ggt, gg_o, e, (s_g, r_g), lsem.at[3])
    for copy in gates + [own_gates]:
        copy.start()
    states = []

    def grads(n):
        expert_grads(n, a_s, act_s, gp_s, dgu_s, eg)
        states.append(pltpu.make_async_copy(eg.at[n], eg_o.at[n], esem.at[n]))
        states[-1].start()

    grads(0)
    grads(1)
    red.merge(3)
    firsts[1].wait()

    def mixture(q, carry):
        values = combine(q, y_f, y_s)

        @pl.when(q > 0)
        def _():
            pltpu.make_async_copy(mix_y, mix_o.at[chip_tokens(q)], osem).wait()

        mix_y[...] = values
        pltpu.make_async_copy(mix_y, mix_o.at[chip_tokens(q)], osem).start()
        return carry

    lax.fori_loop(0, 4, mixture, 0)
    red.finish(gm)
    last = pltpu.make_async_copy(gm, gm_o, lsem.at[4])
    last.start()
    pltpu.make_async_copy(mix_y, mix_o.at[chip_tokens(3)], osem).wait()
    for copy in states + [own_gates, last]:
        copy.wait()
    for copy in gates:
        copy.wait_recv()
    for copy in gates:
        copy.wait_send()


def experts_last(m, t, y, z, g_all, wg, wu, wd):
    return comm_call(
        experts_last_kernel,
        "experts_last",
        4,
        [
            shape((TOK, D)),
            shape((LENGTH, D), BF),
            shape((EP, 8, TOK)),
            shape((PAIR, REP, BLOCK, D), BF),
        ],
        [ANY] * 8,
        [ANY] * 4,
        pair_scratch()
        + [
            pltpu.VMEM((PAIR, ROWS, D), BF),
            pltpu.VMEM((PAIR, ROWS, D), BF),
            pltpu.VMEM((TOK, D), F32),
            pltpu.VMEM((4, TOK, D), BF),
            pltpu.VMEM((4, TOK, D), BF),
            pltpu.VMEM((4, TOK, D), BF),
            pltpu.VMEM((2, TOK, D), BF),
            pltpu.VMEM((TOK, D), BF),
            pltpu.VMEM((2 * TOK, D), BF),
            pltpu.VMEM((2 * TOK, D), BF),
        ]
        + [DMA((10,))] * 2
        + [DMA((7,))] * 2
        + [DMA((5,)), DMA((3,)), DMA((4,)), DMA((4,)), DMA((2,)), DMA(())],
        limit=63,
    )(m, t, y, z, g_all, wg, wu, wd)


KEPT = 8


def back_kernel(
    eg_in, mix_in, gm_in, gg1_in, gg2_in, tab_in, hid_in, m_in, cot_in, att_in, misc_in, rout_in, whole_in, wcol_in, x_in, lin_in,
    q_in, k_in, v_in, a_in, lse_in, cos_in, sin_in,
    out_o, ig_o, gq_o, gk_o, gv_o, go_o, pack_o, eg_o,
    gm, gg1, gg2, tab, hid, m_s, cot, att, misc, rout, wcol, x_s, lin, q_s, k_s, v_s, a_s, lse, cos_ref, sin_ref,
    gh, ga_s, go, q2_s, p_s, dk, dv, u_s, sums, st2, held, wb, wsum, wheld,
    dwt, dws, dheld, dsum, dw_o, vec, vheld, vtot, vheld2, swo, snd, pc1, rcv1, hop1, snd3, pc3, rcv3, hop3,
    s_1, r_1, s_2, r_2, s_3, r_3, s_go, r_go, s_st, r_st, s_w, r_w, s_d, r_d, s_e, r_e, s_v, r_v, s_v2, r_v2, lsem, l_1, l_3, esem, xsem,
    out_s, gq_s, gk_s, gv_s, go_s, pack_s, eg_s,
    za, zb, zc, zd, ze, zf, ya, yb, yc, yd, ye, yf, s_z, r_z, s_y, r_y, l_z, l_y,
):
    r = lax.axis_index("rep")
    e, x, c = place()
    others = ep_others(e)
    copies = rep_others(r)
    first = iota((TOK, 128), 1) < HEAD_DIM
    gain_a, gain_f, gain = misc.at[0:1], misc.at[1:2], misc.at[2:3, 0:256]
    lo, st = misc.at[8:16, 0:256], misc.at[16:32, 0:256]
    greet([{"ep": d} for d in others] + [{"rep": d} for d in copies])
    red1 = RingReduce(mix_in, TOK, pc1, snd, rcv1, hop1, (s_1, r_1), l_1)
    red2 = ChipReduce(TOK, swo, snd, pc1, rcv1, hop1, (s_2, r_2))
    red3 = RingReduce(wb, 128, pc3, snd3, rcv3, hop3, (s_3, r_3), l_3)
    by_z = GridReduce(True, eg_in, 0, za, zb, zc, zd, ze, zf, (s_z, r_z), l_z)
    by_y = GridReduce(False, eg_in, FF, ya, yb, yc, yd, ye, yf, (s_y, r_y), l_y)
    loads = [
        pltpu.make_async_copy(src, dst, lsem.at[k])
        for k, (src, dst) in enumerate(
            [
                (misc_in, misc), (gm_in, gm), (gg1_in, gg1), (gg2_in, gg2), (tab_in, tab), (hid_in, hid),
                (cot_in, cot), (rout_in, rout), (whole_in, wb.at[:, pl.ds(0, D)]), (q_in, q_s), (k_in, k_s), (lse_in, lse),
                (m_in, m_s), (att_in, att), (v_in, v_s), (a_in, a_s), (cos_in, cos_ref), (sin_in, sin_ref),
                (lin_in, lin), (wcol_in, wcol),
            ]
        )
    ]
    chips_order = [(x + 2) % 4, (x + 3) % 4, (x + 1) % 4, x]

    def x_load(k):
        return pltpu.make_async_copy(x_in.at[chip_tokens(chips_order[k])], x_s.at[k % 2], xsem.at[k % 2])

    for copy in loads + [x_load(0), x_load(1)] + by_z.load + by_y.load:
        copy.start()
    red1.start()
    for copy in loads[:9]:
        copy.wait()

    def base(i):
        cut = jnp.minimum(i, 4)
        return cut * (cut + 1) // 2 + 5 * jnp.maximum(i - 4, 0)

    def spans(i, n):
        keys = pl.ds(pl.multiple_of((i - n + 1) * TOK, TOK), n * TOK)
        return keys, pl.ds(pl.multiple_of(base(i) * TOK, TOK), n * TOK)

    def probabilities(i, n):
        _, held_rows = spans(i, n)
        p_s[held_rows] = make_probabilities(i, n)

    def make_probabilities(i, n):
        keys, _ = spans(i, n)
        q2 = stack_heads(q_s[block_rows(i)].astype(F32) * HEAD_DIM ** (-0.5)).astype(BF)
        q2_s[i] = q2
        top = lse[i][0:1]
        low = jnp.concatenate([lo[pl.ds(i, 1)]] * 2, axis=1)
        key = (iota((n * TOK, 2 * TOK), 0) + (i - n + 1) * TOK).astype(F32)
        query = (iota((n * TOK, 2 * TOK), 1) % TOK + i * TOK).astype(F32)
        allowed = (key >= low) & (key <= query)
        return jnp.where(allowed, jnp.exp(dot_nt(k_s[keys], q2) - top), 0.0).astype(BF)

    def probabilities_later(i, carry):
        probabilities(i, 5)

        @pl.when(i == 4)
        def _():
            red1.push_opp()

        @pl.when(i == 5)
        def _():
            red1.push_near()

        return carry


    hidden = hid[...]
    weights = jnp.concatenate([tab[d][LOCAL:] for d in range(EP)], axis=0)
    grads = jnp.concatenate([ref[d][:PAIR] for d in range(EP) for ref in (gg1, gg2)], axis=0)
    mean = jnp.sum(weights * grads, axis=0, keepdims=True)
    grad_logits = weights * (grads - mean)
    grad_moe = gm[...] + dot_tn(grad_logits.astype(BF), rout[...])
    r2 = lax.rsqrt(jnp.mean(hidden * hidden, axis=1, keepdims=True) + EPSILON)
    n = hidden * r2
    u = grad_moe * gain_f[...]
    grad_hidden = cot[...].astype(F32) + r2 * (u - n * jnp.mean(u * n, axis=1, keepdims=True))
    gh[...] = grad_hidden
    branch = grad_hidden.astype(BF)
    ga_s[...] = dot_nt(branch, wb[:, :D]).astype(BF)

    def own_cols(ref, b):
        return ref.at[:, pl.ds(pl.multiple_of(b * 128, 128), 128)]

    heads = [
        remote(own_cols(ga_s, d), go.at[block_rows(e)], (s_go, r_go), k, {"ep": d}) for k, d in enumerate(others)
    ]
    for copy in heads:
        copy.start()
    by_z.push()
    by_y.push()
    go[block_rows(e)] = own_cols(ga_s, e)[...]
    for copy in loads[9:12]:
        copy.wait()
    for i in range(4):
        probabilities(i, i + 1)
    lax.fori_loop(4, KEPT, probabilities_later, 0)
    for copy in loads[12:]:
        copy.wait()
    for copy in heads:
        copy.wait_recv()
    ffn = jnp.sum(grad_moe * n, axis=0, keepdims=True)
    logit_rows = jnp.transpose(jnp.concatenate([grad_logits, jnp.zeros((96, TOK), F32)], axis=0)).astype(BF)
    router_rows = dot_tn(m_s[...], logit_rows)
    vec[...] = jnp.zeros((8, D), F32)
    vec[3:4] = ffn
    router_rows = router_rows.reshape(REP, EP, 8, 128)
    for d in range(EP):
        wb[d * 128 : (d + 1) * 128, D:] = router_rows[:, d].reshape(128, 128).astype(BF)
    for cols in range(0, D, 256):
        out_rows = dot_tn(att[...], branch[:, cols : cols + 256]).reshape(REP, EP, 8, 256)
        for d in range(EP):
            wb[d * 128 : (d + 1) * 128, cols : cols + 256] = out_rows[:, d].reshape(128, 256).astype(BF)
    red3.start()
    by_z.stage.relay()
    by_y.stage.relay()
    dk[...] = jnp.zeros((LENGTH, 128), F32)
    dv[...] = jnp.zeros((LENGTH, 128), F32)

    def part(ref, b, size):
        return ref.at[pl.ds(pl.multiple_of(b * size, 8), size)]

    spread_w = [remote(part(wsum, d, 8), wheld.at[r], (s_w, r_w), k, {"rep": d}) for k, d in enumerate(copies)]

    def attend_back(i, n):
        keys, held_rows = spans(i, n)
        rows = block_rows(i)
        grad = stack_heads(go[rows].astype(F32))
        do2 = grad.astype(BF)
        out = a_s[rows].astype(F32)
        settle = row_sums(grad * jnp.concatenate([out, out], axis=0), ((0, 128),))[0:1]
        p = p_s[held_rows]
        ds = (p.astype(F32) * (dot_nt(v_s[keys], do2) - settle)).astype(BF)
        dv[keys] += dot(p, do2)
        dk[keys] += dot(ds, q2_s[i])
        dq = dot_tn(k_s[keys], ds)
        u_s[rows, :128] = merge_heads(jnp.transpose(dq)) * HEAD_DIM ** (-0.5)

    def attend_back_later(i, carry):
        attend_back(i, 5)
        return carry

    for i in range(4):
        attend_back(i, i + 1)
    red3.push_opp()
    red3.push_near()
    lax.fori_loop(4, 6, attend_back_later, 0, unroll=True)
    red1.relay()
    red3.relay()
    lax.fori_loop(6, EP, attend_back_later, 0, unroll=True)

    def close(b, carry):
        rows = block_rows(b)
        grad_k, grad_v = dk[rows], dv[rows]
        grad_k = grad_k + pltpu.roll(grad_k, HEAD_DIM, 1)
        grad_v = grad_v + pltpu.roll(grad_v, HEAD_DIM, 1)
        both = jnp.where(first, grad_k, grad_v).astype(BF).astype(F32)
        cosine, sine = cos_ref[rows], -sin_ref[rows]
        both = jnp.where(first, turn(both, cosine, sine), both)
        grad_q = turn(u_s[rows, :128].astype(BF).astype(F32), cosine, sine)
        u_s[rows, :128] = grad_q
        u_s[rows, 128:] = both
        cq, ck = columns(
            lax.rsqrt(st[pl.ds(2 * b, 1)] * (1.0 / D) + EPSILON),
            lax.rsqrt(st[pl.ds(2 * b + 1, 1)] * (1.0 / KV) + EPSILON),
        )
        products = jnp.concatenate([grad_q * cq, both * ck], axis=1) * gain[...] * lin[rows]
        pair = row_sums(products, PARTS)
        sums[pl.ds(2 * b, 1)] = pair[0:1]
        sums[pl.ds(2 * b + 1, 1)] = pair[1:2]
        return carry

    lax.fori_loop(0, EP, close, 0, unroll=2)
    red1.finish(gm)
    stats = [remote(sums, held.at[e], (s_st, r_st), k, {"ep": d}) for k, d in enumerate(others)]
    for copy in stats:
        copy.start()
    held[e] = sums[...]
    out_s[...] = (hid[...] + gm[...]).astype(BF)
    ends = [pltpu.make_async_copy(out_s, out_o, esem.at[0])]
    ends[0].start()
    red3.finish(wsum)
    for copy in spread_w:
        copy.start()
    wheld[r] = part(wsum, r, 8)[...]
    by_z.turn()
    by_y.turn()
    dwt[...] = jnp.zeros((256, D), F32)
    for copy in stats:
        copy.wait_recv()
    total = held[0]
    for k in range(1, EP):
        total = total + held[k]
    st2[...] = total

    def project_back(b, slot):
        rows = block_rows(b)
        values = x_s[slot, pl.ds(pl.multiple_of(b % 2 * TOK, TOK), TOK)].astype(F32)
        r1 = lax.rsqrt(jnp.mean(values * values, axis=1, keepdims=True) + EPSILON)
        n1 = values * r1
        normed = (n1 * gain_a[...]).astype(BF)
        cq, ck, mq, mk = columns(
            lax.rsqrt(st[pl.ds(2 * b, 1)] * (1.0 / D) + EPSILON),
            lax.rsqrt(st[pl.ds(2 * b + 1, 1)] * (1.0 / KV) + EPSILON),
            st2[pl.ds(2 * b, 1)] * (1.0 / D),
            st2[pl.ds(2 * b + 1, 1)] * (1.0 / KV),
        )
        uq, uk = u_s[rows, :128], u_s[rows, 128:]
        nq = lin[rows, :128] * cq
        nk = lin[rows, 128:] * ck
        gq = cq * (uq * gain[:, :128] - nq * mq)
        gk = jnp.where(first, ck * (uk * gain[:, 128:] - nk * mk), uk)
        glin = jnp.concatenate([gq, gk], axis=1).astype(BF)
        vec[1:2, :128] += jnp.sum(uq * nq, axis=0, keepdims=True)
        vec[2:3, :128] += jnp.sum(uk * nk, axis=0, keepdims=True)
        gn = dot_nt(glin, wcol[...])
        vec[0:1] += jnp.sum(gn * n1, axis=0, keepdims=True)
        dwt[...] += dot_tn(glin, normed)
        return gn.astype(BF)

    def chips(k, carry):
        q = (x + 2 + k - (k // 2) * (2 * k - 1)) % 4
        for step in range(4):

            @pl.when(k == step)
            def _(step=step):
                x_load(step).wait()

        swo[k] = project_back(q * 2 + 1 - c, k % 2)
        red2.swap(k).start()

        @pl.when(k == 1)
        def _():
            red2.send_opp()

        @pl.when(k == 2)
        def _():
            red2.near_left()

        @pl.when(k == 3)
        def _():
            red2.near_right()

        snd[k] = project_back(q * 2 + c, k % 2)
        for step in range(2):

            @pl.when(k == step)
            def _(step=step):
                x_load(step + 2).start()

        return carry

    lax.fori_loop(0, 4, chips, 0)
    dws[...] = jnp.transpose(dwt[...]).astype(BF)
    spread_d = [remote(part(dws, d, 64), dheld.at[r], (s_d, r_d), k, {"rep": d}) for k, d in enumerate(copies)]
    for copy in spread_d:
        copy.start()
    dheld[r] = part(dws, r, 64)[...]
    gain_q, gain_k = vec[1:2, :128], vec[2:3, :128]
    low, spread = iota((1, 128), 1) < 32, iota((1, 128), 1) // 32 == 2
    gain_k = jnp.where(low, gain_k, jnp.where(spread, pltpu.roll(gain_k, 32, 1), 0.0))
    vec[1:3, :128] = jnp.zeros((2, 128), F32)
    vec[1:2, pl.ds(pl.multiple_of(e * 128, 128), 128)] = gain_q
    vec[2:3, pl.ds(pl.multiple_of(e * 128, 128), 128)] = gain_k
    spread_v = [remote(vec, vheld.at[e], (s_v, r_v), k, {"ep": d}) for k, d in enumerate(others)]
    for copy in spread_v:
        copy.start()
    vheld[e] = vec[...]
    red2.merge(3)
    red2.send_far()
    by_z.last.relay()
    by_y.last.relay()
    for copy in spread_v:
        copy.wait_recv()
    total = vheld[0]
    for k in range(1, EP):
        total = total + vheld[k]
    vtot[...] = total
    def lanes_of(d):
        return vtot.at[:, pl.ds(pl.multiple_of(d // 2 * 128, 128), 128)]

    spread_v2 = [remote(lanes_of(d), vheld2.at[r], (s_v2, r_v2), k, {"rep": d}) for k, d in enumerate(copies)]
    for copy in spread_v2:
        copy.start()
    vheld2[r] = lanes_of(r)[...]
    for copy in spread_w:
        copy.wait_recv()
    total = wheld[0]
    for k in range(1, REP):
        total = total + wheld[k]
    go_s[...] = total[:, :D]
    pack_s[0:8] = total[:, D:]
    for copy in spread_d:
        copy.wait_recv()
    total = dheld[0].astype(F32)
    for k in range(1, REP):
        total = total + dheld[k].astype(F32)
    dsum[...] = total
    spread_e = [remote(part(dsum, d, 8), dw_o.at[e], (s_e, r_e), k, {"ep": d}) for k, d in enumerate(others)]
    for copy in spread_e:
        copy.start()
    dw_o[e] = part(dsum, e, 8)[...]
    for copy in spread_v2:
        copy.wait_recv()
    total = vheld2[0]
    for k in range(1, REP):
        total = total + vheld2[k]
    start = r % 2 * 64
    rows_d, lanes_d = iota((128, 128), 0), iota((128, 128), 1)
    eight = jnp.where((rows_d == start + e * 8 + lanes_d) & (lanes_d < 8), 1.0, 0.0)
    four = jnp.where((rows_d == start + e * 4 + lanes_d) & (lanes_d < 4), 1.0, 0.0)

    def pick(sel):
        return jnp.dot(total, sel, preferred_element_type=F32, precision=HIGH)

    eights, fours = pick(eight), pick(four)
    pack_s[8:16] = jnp.where(iota((8, 128), 0) == 2, fours, eights)
    by_z.finish(eg_s, 0)
    by_y.finish(eg_s, FF)
    red2.finish(gm)
    values = x_s[1, pl.ds(pl.multiple_of(c * TOK, TOK), TOK)].astype(F32)
    r1 = lax.rsqrt(jnp.mean(values * values, axis=1, keepdims=True) + EPSILON)
    n1 = values * r1
    z = gm[...] * gain_a[...]
    gh[...] = gh[...] + r1 * (z - n1 * jnp.mean(z * n1, axis=1, keepdims=True))
    for copy in spread_e:
        copy.wait_recv()
    low_lanes = iota((8, 128), 1) < HEAD_DIM
    for d in range(EP):
        gq_s[:, d * 128 : (d + 1) * 128] = dw_o[d][:, :128]
    for d in range(EP // 2):
        even, odd = dw_o[2 * d][:, 128:], dw_o[2 * d + 1][:, 128:]
        gk_s[:, d * 128 : (d + 1) * 128] = jnp.where(low_lanes, even, pltpu.roll(odd, HEAD_DIM, 1))
        gv_s[:, d * 128 : (d + 1) * 128] = jnp.where(low_lanes, pltpu.roll(even, HEAD_DIM, 1), odd)
    pairs = [(gh, ig_o), (gq_s, gq_o), (gk_s, gk_o), (gv_s, gv_o), (go_s, go_o), (pack_s, pack_o), (eg_s, eg_o)]
    for k, (src, dst) in enumerate(pairs):
        ends.append(pltpu.make_async_copy(src, dst, esem.at[1 + k]))
        ends[-1].start()
    for copy in ends:
        copy.wait()
    for copy in heads + stats + spread_w + spread_d + spread_e + spread_v + spread_v2:
        copy.wait_send()


W_OUT = 12
X_ALL = 14


def back(*args):
    def vm(dims, dtype=F32):
        return pltpu.VMEM(dims, dtype)

    held = [vm((2, 2 * TOK, D), BF) if k == X_ALL else vm(a.shape, a.dtype) for k, a in enumerate(args) if k > 1 and k != W_OUT]
    results = [((TOK, D), BF), ((TOK, D), F32), ((8, D), F32), ((8, KV), F32), ((8, KV), F32), ((8, D), F32), ((16, 128), F32)]
    results.append(((PAIR, BLOCK, D), BF))
    landing = [vm((4, TOK, D), BF), vm((2, TOK, D), BF), vm((TOK, D), BF)]
    return comm_call(
        back_kernel,
        "back",
        6,
        [shape(*result) for result in results],
        [ANY] * 23,
        [ANY] * 8,
        held
        + [
            vm((TOK, D)),
            vm((TOK, D), BF),
            vm((LENGTH, 128), BF),
            vm((EP, 2 * TOK, 128), BF),
            vm(((10 + 5 * (KEPT - 4)) * TOK, 2 * TOK), BF),
            vm((LENGTH, 128)),
            vm((LENGTH, 128)),
            vm((LENGTH, 256)),
            vm((16, 256)),
            vm((16, 256)),
            vm((EP, 16, 256)),
            vm((D, WB), BF),
            vm((128, WB)),
            vm((REP, 8, WB)),
            vm((256, D)),
            vm((D, 256), BF),
            vm((REP, 64, 256), BF),
            vm((64, 256)),
            vm((EP, 8, 256)),
            vm((8, D)),
            vm((EP, 8, D)),
            vm((8, D)),
            vm((REP, 8, 128)),
            vm((4, TOK, D), BF),
            vm((4, TOK, D), BF),
        ]
        + landing
        + [vm((4, 128, WB), BF), vm((4, 128, WB), BF), vm((2, 128, WB), BF), vm((128, WB), BF)]
        + [DMA((10,))] * 6
        + [DMA((7,))] * 4
        + [DMA((15,))] * 4
        + [DMA((7,))] * 4
        + [DMA((15,))] * 2
        + [DMA((20,)), DMA((4,)), DMA((4,)), DMA((8,)), DMA((2,))]
        + [vm(*result) for k, result in enumerate(results) if k != 1]
        + grid_scratch() * 2
        + [DMA((12,))] * 4
        + [DMA((4,))] * 2,
        limit=64,
    )(*args)


def finish_kernel(
    xa_in, xb_in, out_in, ig_in, gq_in, gk_in, gv_in, go_in, pack,
    out_o, ig_o, gq_o, gk_o, gv_o, go_o, gr_o, va_o, vq_o, vk_o, vf_o, gate_o, up_o, down_o,
    x_s, gate_s, up_s, down_s, out_s, ig_s, gq_s, gk_s, gv_s, go_s, sem,
):
    loads = [
        pltpu.make_async_copy(xa_in, x_s.at[pl.ds(0, PAIR)], sem.at[9]),
        pltpu.make_async_copy(xb_in, x_s.at[pl.ds(PAIR, PAIR)], sem.at[10]),
    ]
    for load in loads:
        load.start()
    stages = [out_s, ig_s, gq_s, gk_s, gv_s, go_s]
    fetch = [
        pltpu.make_async_copy(src, dst, sem.at[k])
        for k, (src, dst) in enumerate(zip([out_in, ig_in, gq_in, gk_in, gv_in, go_in], stages))
    ]
    copies = [
        pltpu.make_async_copy(src, dst, sem.at[k])
        for k, (src, dst) in enumerate(zip(stages, [out_o, ig_o, gq_o, gk_o, gv_o, go_o]))
    ]
    for copy in fetch:
        copy.start()
    gr_o[...] = pack[0:8, :EXPERTS]
    va_o[...] = pack[8:9, :8]
    vq_o[...] = pack[9:10, :8]
    vk_o[...] = pack[10:11, :4]
    vf_o[...] = pack[11:12, :8]
    for load, copy in zip(fetch, copies):
        load.wait()
        copy.start()
    for load in loads:
        load.wait()
    gate_s[...] = x_s[:, :64, :FF].astype(F32)
    up_s[...] = x_s[:, :64, FF:].astype(F32)
    down_s[...] = x_s[:, 64:].astype(F32)
    pairs = [(gate_s, gate_o), (up_s, up_o), (down_s, down_o)]
    for k, (src, dst) in enumerate(pairs):
        copies.append(pltpu.make_async_copy(src, dst, sem.at[6 + k]))
        copies[-1].start()
    for copy in copies:
        copy.wait()


def finish(xa, xb, out, ig, gq, gk, gv, go, pack):
    gate, down = shape((LOCAL, 64, FF)), shape((LOCAL, 32, D))
    return pl.pallas_call(
        finish_kernel,
        out_shape=[shape(a.shape, a.dtype) for a in (out, ig, gq, gk, gv, go)]
        + [shape((8, EXPERTS)), shape((1, 8)), shape((1, 8)), shape((1, 4)), shape((1, 8)), gate, gate, down],
        in_specs=[ANY] * 8 + [VM],
        out_specs=[ANY] * 6 + [VM] * 5 + [ANY] * 3,
        scratch_shapes=[
            pltpu.VMEM((LOCAL, BLOCK, D), BF),
            pltpu.VMEM(gate.shape, F32),
            pltpu.VMEM(gate.shape, F32),
            pltpu.VMEM(down.shape, F32),
        ]
        + [pltpu.VMEM(a.shape, a.dtype) for a in (out, ig, gq, gk, gv, go)]
        + [
            DMA((11,)),
        ],
        compiler_params=pltpu.CompilerParams(vmem_limit_bytes=62 * MIB),
        name="finish",
    )(xa, xb, out, ig, gq, gk, gv, go, pack)


def body(
    tokens,
    segments,
    routes,
    w_query,
    w_key,
    w_value,
    w_out,
    w_router,
    gain_attn,
    gain_query,
    gain_key,
    gain_ffn,
    w_gate,
    w_up,
    w_down,
    out_grad,
):
    gains = [gain.reshape(1, -1) for gain in (gain_attn, gain_query, gain_key, gain_ffn)]
    cosine, sine = turn_tables()
    (
        x_all, g_all, lin, q, k, v, att, lse, hidden, moe_in, tables, attended, misc, router, whole_out, w_cols,
    ) = front(
        tokens, out_grad, w_query, w_key, w_value, w_out, w_router, *gains, segments, routes.T, cosine, sine
    )
    def over_copies(grads):
        grads = grads.reshape(PAIR, REP * BLOCK, D)
        return lax.psum_scatter(grads, "rep", scatter_dimension=1, tiled=True)

    m_all, tabs, y, z, gg_first, grads = experts_first(moe_in, tables, g_all, w_gate, w_up, w_down)
    sums_first = over_copies(grads)
    grad_moe, mixture, gg_last, grads = experts_last(m_all, tabs, y, z, g_all, w_gate, w_up, w_down)
    *rows, sums_last = back(
        grads.reshape(PAIR, 4, 4, BLOCK, D), mixture, grad_moe, gg_first, gg_last, tables, hidden, moe_in, out_grad, attended, misc, router, whole_out,
        w_cols, x_all, lin, q, k, v, att, lse, cosine, sine,
    )
    out, ig, gq, gk, gv, go, gr, va, vq, vk, vf, gate, up, down = finish(sums_first, sums_last, *rows)
    return out, ig, gq, gk, gv, go, gr, va.reshape(8), vq.reshape(8), vk.reshape(4), vf.reshape(8), gate, up, down


def solution(mesh):
    both = P(("rep", "ep"), None)
    line = P(("rep", "ep"))
    owner = P("ep", None, None)
    kept = P("ep", "rep", None)
    return jax.shard_map(
        body,
        mesh=mesh,
        in_specs=(both, P("rep", None)) + (both,) * 6 + (line,) * 4 + (owner,) * 3 + (both,),
        out_specs=(both,) * 7 + (line,) * 4 + (kept,) * 3,
        check_vma=False,
    )
```

```python
import functools

import jax
import jax.numpy as jnp
import numpy as np
from jax import lax
from jax.experimental import pallas as pl
from jax.experimental.pallas import tpu as pltpu
from jax.sharding import PartitionSpec as P

BF = jnp.bfloat16
F32 = jnp.float32
MESH = pl.DeviceIdType.MESH
ANY = pl.BlockSpec(memory_space=pl.ANY)
VM = pl.BlockSpec(memory_space=pltpu.VMEM)
DMA = pltpu.SemaphoreType.DMA
MIB = 1 << 20

HEADS = 16
KV_HEADS = 8
HEAD_DIM = 64
TOP = 8
WINDOW = 1024
EPSILON = 1e-06
ROPE_BASE = 10000.0
MASKED = -1e30
EP = 8
REP = 16
TOK = 256
LENGTH = 2048
D = 1024
KV = 512
FF = 512
EXPERTS = 32
LOCAL = 4
CAP = 88
NT = (((1,), (1,)), ((), ()))
TN = (((0,), (0,)), ((), ()))
HIGH = lax.Precision.HIGHEST


def dot(a, b):
    return jnp.dot(a, b, preferred_element_type=F32)


def dot_nt(a, b, precision=None):
    return lax.dot_general(a, b, NT, preferred_element_type=F32, precision=precision)


def dot_tn(a, b):
    return lax.dot_general(a, b, TN, preferred_element_type=F32)


def iota(shape, dim):
    return lax.broadcasted_iota(jnp.int32, shape, dim)


def ep_device(x, c):
    return {"ep": x * 2 + c}


def greet(devices, local_work=None):
    barrier = pltpu.get_barrier_semaphore()
    for device in devices:
        pl.semaphore_signal(barrier, inc=1, device_id=device, device_id_type=MESH)
    if local_work is not None:
        local_work()
    pl.semaphore_wait(barrier, len(devices))


def remote(src, dst, sems, i, device):
    return pltpu.make_async_remote_copy(
        src_ref=src,
        dst_ref=dst,
        send_sem=sems[0].at[i],
        recv_sem=sems[1].at[i],
        device_id=device,
        device_id_type=MESH,
    )


def place():
    e = lax.axis_index("ep")
    return e, e // 2, e % 2


def ep_others(e):
    return [(e + k) % EP for k in range(1, EP)]


def rep_others(r):
    return [(r + k) % REP for k in range(1, REP)]


class RingGather:
    SEMS = 10

    def __init__(self, x_ref, o_ref, sems, lsem):
        e, x, c = place()
        self.n = n = x_ref.shape[0]
        h = n // 2
        self.o_ref = o_ref
        right, left = ep_device((x + 1) % 4, c), ep_device((x + 3) % 4, c)
        peer = ep_device(x, 1 - c)
        b_left, b_right, b_opp = (((x + 3) % 4) * 2 + c, ((x + 1) % 4) * 2 + c, ((x + 2) % 4) * 2 + c)

        def rows(b, off=0, size=n):
            return o_ref.at[pl.ds(pl.multiple_of(b * n + off, 16), size)]

        low, high = x_ref.at[pl.ds(0, h)], x_ref.at[pl.ds(h, h)]
        self.first = [
            remote(low, rows(e, 0, h), sems, 0, right),
            remote(high, rows(e, h, h), sems, 2, left),
            remote(high, rows(e, h, h), sems, 1, right),
            remote(low, rows(e, 0, h), sems, 3, left),
            remote(x_ref, rows(e), sems, 4, peer),
        ]
        self.fwd_right = remote(rows(b_left, 0, h), rows(b_left, 0, h), sems, 5, right)
        self.fwd_left = remote(rows(b_right, h, h), rows(b_right, h, h), sems, 6, left)
        self.to_peer = [
            remote(rows(b_left), rows(b_left), sems, 7, peer),
            remote(rows(b_right), rows(b_right), sems, 8, peer),
            remote(rows(b_opp), rows(b_opp), sems, 9, peer),
        ]
        self.own = pltpu.make_async_copy(x_ref, rows(e), lsem)

    def start(self):
        for copy in self.first:
            copy.start()
        self.own.start()

    def forward_half(self):
        self.first[0].wait_recv()
        self.fwd_right.start()
        self.first[1].wait_recv()
        self.fwd_left.start()

    def forward_rest(self):
        self.first[2].wait_recv()
        self.to_peer[0].start()
        self.first[3].wait_recv()
        self.to_peer[1].start()

    def finish(self):
        self.fwd_right.wait_recv()
        self.fwd_left.wait_recv()
        self.to_peer[2].start()
        self.first[4].wait_recv()
        for copy in self.to_peer:
            copy.wait_recv()
        self.own.wait()
        for copy in self.first + [self.fwd_right, self.fwd_left] + self.to_peer:
            copy.wait_send()


class RingReduce:
    SEMS = 10
    STEP = 64

    def __init__(self, p_ref, n, pc, snd, rcv, hop, sems, lsems):
        e, x, c = place()
        self.n, self.h = n, n // 2
        h = n // 2
        self.pc, self.snd, self.rcv, self.hop = pc, snd, rcv, hop
        right, left = ep_device((x + 1) % 4, c), ep_device((x + 3) % 4, c)
        peer = ep_device(x, 1 - c)

        def rows(b):
            return p_ref.at[pl.ds(pl.multiple_of(b * n, 16), n)]

        chips = [(x + 2) % 4, (x + 1) % 4, (x + 3) % 4, x]
        self.swap = [remote(rows(b * 2 + 1 - c), pc.at[k], sems, k, peer) for k, b in enumerate(chips)]
        self.load = [
            pltpu.make_async_copy(rows(b * 2 + c), snd.at[k], lsems.at[k]) for k, b in enumerate(chips)
        ]
        low, high = pl.ds(0, h), pl.ds(h, h)
        self.opp = [
            remote(snd.at[0, low], hop.at[low], sems, 4, right),
            remote(snd.at[0, high], hop.at[high], sems, 5, left),
        ]
        self.near = [
            remote(snd.at[1, high], rcv.at[0, high], sems, 6, right),
            remote(snd.at[2, low], rcv.at[1, low], sems, 7, left),
        ]
        self.far = [
            remote(snd.at[1, low], rcv.at[0, low], sems, 8, right),
            remote(snd.at[2, high], rcv.at[1, high], sems, 9, left),
        ]

    def rows_loop(self, low, count, body):
        step = self.STEP

        def loop(i, carry):
            body(pl.ds(pl.multiple_of(low + i * step, 16), step))
            return carry

        lax.fori_loop(0, count // step, loop, 0)

    def merge(self, k):
        def body(s):
            self.snd[k, s] = (self.snd[k, s].astype(F32) + self.pc[k, s].astype(F32)).astype(BF)

        self.load[k].wait()
        self.swap[k].wait_recv()
        self.rows_loop(0, self.n, body)

    def merge_hop(self, k, low):
        def body(s):
            self.snd[k, s] = (self.snd[k, s].astype(F32) + self.hop[s].astype(F32)).astype(BF)

        self.rows_loop(low, self.h, body)

    def start(self):
        for copy in self.swap + self.load:
            copy.start()

    def push_opp(self):
        self.merge(0)
        for copy in self.opp:
            copy.start()

    def push_near(self):
        self.merge(1)
        self.near[0].start()
        self.merge(2)
        self.near[1].start()
        self.merge(3)

    def relay(self):
        self.opp[0].wait_recv()
        self.merge_hop(1, 0)
        self.far[0].start()
        self.opp[1].wait_recv()
        self.merge_hop(2, self.h)
        self.far[1].start()

    def finish(self, out_ref):
        for copy in self.near + self.far:
            copy.wait_recv()

        def body(s):
            out_ref[s] = self.snd[3, s].astype(F32) + (
                self.rcv[0, s].astype(F32) + self.rcv[1, s].astype(F32)
            )

        self.rows_loop(0, self.n, body)
        for copy in self.swap + self.opp + self.near + self.far:
            copy.wait_send()


class AxisReduce:
    def __init__(self, devices, snd, hop, rcv, sems, base):
        right, left = devices
        self.snd, self.hop, self.rcv = snd, hop, rcv
        self.opp = [
            remote(snd.at[0, 0], hop.at[0], sems, base, right),
            remote(snd.at[0, 1], hop.at[1], sems, base + 1, left),
        ]
        self.near = [
            remote(snd.at[2, 1], rcv.at[0, 1], sems, base + 2, right),
            remote(snd.at[1, 0], rcv.at[1, 0], sems, base + 3, left),
        ]
        self.far = [
            remote(snd.at[2, 0], rcv.at[0, 0], sems, base + 4, right),
            remote(snd.at[1, 1], rcv.at[1, 1], sems, base + 5, left),
        ]

    def push(self):
        for copy in self.opp + self.near:
            copy.start()

    def relay(self):
        for k, (slot, half) in enumerate(((2, 0), (1, 1))):
            self.opp[k].wait_recv()
            self.snd[slot, half] = (self.snd[slot, half].astype(F32) + self.hop[half].astype(F32)).astype(BF)
            self.far[k].start()

    def arrive(self):
        for copy in self.near + self.far:
            copy.wait_recv()

    def total(self, *index):
        return self.snd[(3,) + index].astype(F32) + (
            self.rcv[(0,) + index].astype(F32) + self.rcv[(1,) + index].astype(F32)
        )

    def leave(self):
        for copy in self.opp + self.near + self.far:
            copy.wait_send()


class GridReduce:
    def __init__(self, along_z, src, cols, snd, hop, rcv, snd2, hop2, rcv2, sems, lsems):
        r = lax.axis_index("rep")
        z, y = r // 4, r % 4
        along = (lambda k: {"rep": (z + k) % 4 * 4 + y}, lambda k: {"rep": z * 4 + (y + k) % 4})
        one, two = along if along_z else along[::-1]
        here, self.there = (z, y) if along_z else (y, z)
        offsets = (2, 3, 1, 0)
        cut = pl.ds(cols, FF)
        self.load = []
        for k, off in enumerate(offsets):
            b = (here + off) % 4
            block = src.at[:, b, :, :, cut] if along_z else src.at[:, :, b, :, cut]
            self.load.append(pltpu.make_async_copy(block, snd.at[k], lsems.at[k]))
        self.offsets, self.snd2 = offsets, snd2
        self.stage = AxisReduce((one(1), one(3)), snd, hop, rcv, sems, 0)
        self.last = AxisReduce((two(1), two(3)), snd2, hop2, rcv2, sems, 6)

    def push(self):
        for copy in self.load:
            copy.wait()
        self.stage.push()

    def turn(self):
        self.stage.arrive()
        for k, off in enumerate(self.offsets):
            b = (self.there + off) % 4
            for n in range(PAIR):
                self.snd2[k, n] = self.stage.total(n, b).astype(BF)
        self.last.push()

    def finish(self, out_ref, cols):
        self.last.arrive()
        for n in range(PAIR):
            out_ref[n, :, cols : cols + FF] = self.last.total(n).astype(BF)
        self.stage.leave()
        self.last.leave()


def grid_scratch():
    blocks = [(4, PAIR, 4, BLOCK, FF), (PAIR, 4, BLOCK, FF), (2, PAIR, 4, BLOCK, FF)]
    blocks += [(4, PAIR, BLOCK, FF), (PAIR, BLOCK, FF), (2, PAIR, BLOCK, FF)]
    return [pltpu.VMEM(dims, BF) for dims in blocks]


def comm_call(kernel, name, collective_id, out_shape, in_specs, out_specs, scratch, limit=48):
    return pl.pallas_call(
        kernel,
        out_shape=out_shape,
        in_specs=in_specs,
        out_specs=out_specs,
        scratch_shapes=scratch,
        compiler_params=pltpu.CompilerParams(
            collective_id=collective_id, has_side_effects=True, vmem_limit_bytes=limit * MIB
        ),
        name=name,
    )


def shape(dims, dtype=F32):
    return jax.ShapeDtypeStruct(dims, dtype)


WB = D + 128


def columns(*rows):
    pad = jnp.zeros((128 - len(rows), rows[0].shape[1]), F32)
    turned = jnp.transpose(jnp.concatenate(list(rows) + [pad], axis=0))
    return [turned[:, k : k + 1] for k in range(len(rows))]


def row_sums(values, bounds):
    width = values.shape[1]
    high = values.astype(BF)
    low = (values - high.astype(F32)).astype(BF)
    lane, row = iota((8, width), 1), iota((8, width), 0)
    chosen = jnp.zeros((8, width), F32)
    for k, (first, last) in enumerate(bounds):
        chosen = jnp.where((row == k) & (lane >= first) & (lane < last), 1.0, chosen)
    chosen = chosen.astype(BF)
    return dot_nt(jnp.concatenate([chosen, chosen], axis=1), jnp.concatenate([high, low], axis=1))


PARTS = ((0, 128), (128, 192))


def turn_tables():
    half = HEAD_DIM // 2
    freq = np.float32(ROPE_BASE) ** (-(np.arange(half, dtype=np.float32) * np.float32(2.0) / np.float32(HEAD_DIM)))
    angles = np.arange(LENGTH, dtype=np.float32)[:, None] * freq.astype(np.float32)[None, :]
    c, s = np.cos(angles), np.sin(angles)
    cosine = np.concatenate([c, c, c, c], axis=1)
    sine = np.concatenate([-s, s, -s, s], axis=1)
    return cosine.astype(np.float32), sine.astype(np.float32)


def turn(u, cosine, sine):
    early = iota(u.shape, 1) % HEAD_DIM < HEAD_DIM // 2
    partner = jnp.where(early, pltpu.roll(u, 96, 1), pltpu.roll(u, 32, 1))
    return u * cosine + partner * sine


def block_rows(b):
    return pl.ds(pl.multiple_of(b * TOK, TOK), TOK)


def stack_heads(values):
    first = iota(values.shape, 1) < HEAD_DIM
    return jnp.concatenate([jnp.where(first, values, 0.0), jnp.where(first, 0.0, values)], axis=0)


def merge_heads(values):
    first = iota((TOK, 128), 1) < HEAD_DIM
    return jnp.where(first, values[:TOK], values[TOK:])


def front_kernel(
    tok, cot, wq, wk, wv, wo_in, router_in, ga_in, gq_in, gk_in, gf_in, seg, rts_in, cos_in, sin_in,
    x_all, g_all, lin_h, q_h, k_h, v_h, a_h, lse_h, hid_h, m_h, tab_h, att_h, misc_h, rout_h, whole_h, wcol_h,
    lin, q_o, k_o, v_o, a_o, lse_o, hid_o, m_o, tab_o, att_o, misc, rout_o, whole, wcol, hsem,
    x_s, cot_s, tiny, tiny_b, smalls, wsl, wo_f, wo_r, wg, w32, gains_s, cos_ref, sin_ref, sums, held,
    s_tok, r_tok, s_cot, r_cot, s_w, r_w, s_o, r_o, s_st, r_st, s_t, r_t, s_a, r_a, lsem,
):
    r = lax.axis_index("rep")
    e, x, c = place()
    others = ep_others(e)
    copies = rep_others(r)
    first = iota((TOK, 128), 1) < HEAD_DIM
    gain_a, gain_f, gain = misc.at[0:1], misc.at[1:2], misc.at[2:3, 0:256]
    lo, st = misc.at[8:16, 0:256], misc.at[16:32, 0:256]
    leaving = []

    def leave(*pairs):
        for src, dst in pairs:
            leaving.append(pltpu.make_async_copy(src, dst, hsem.at[len(leaving)]))
            leaving[-1].start()

    tables = [
        pltpu.make_async_copy(cos_in, cos_ref, lsem.at[2]),
        pltpu.make_async_copy(sin_in, sin_ref, lsem.at[3]),
        pltpu.make_async_copy(cot, cot_s, lsem.at[5]),
    ]

    def prepare_tiles():
        misc[...] = jnp.zeros((32, D), F32)

        tiny[...] = jnp.zeros((16, 128), F32)
        tiny[0:8, 0:EXPERTS] = router_in[...].astype(F32)
        for lane, ref in ((0, ga_in), (8, gq_in), (16, gk_in), (20, gf_in)):
            tiny[8:9, lane : lane + ref.shape[1]] = ref[...].astype(F32)
        tiny_b[...] = tiny[...].astype(BF)
        low_lanes = iota((8, 128), 1) < HEAD_DIM
        for d in range(EP):
            k_t = wk[:, (d // 2) * 128 : (d // 2 + 1) * 128].astype(F32)
            v_t = wv[:, (d // 2) * 128 : (d // 2 + 1) * 128].astype(F32)
            if d % 2:
                k_t = pltpu.roll(k_t, HEAD_DIM, 1)
            else:
                v_t = pltpu.roll(v_t, HEAD_DIM, 1)
            q_t = wq[:, d * 128 : (d + 1) * 128].astype(F32)
            wsl[d] = jnp.concatenate([q_t, jnp.where(low_lanes, k_t, v_t)], axis=0).astype(BF)
        wo_f[...] = wo_in[...].astype(F32)
        for copy in tables:
            copy.start()

    greet([{"ep": d} for d in others] + [{"rep": d} for d in copies], prepare_tiles)
    half_cols = pl.ds(pl.multiple_of(c * 512, 512), 512)
    other_cols = pl.ds(pl.multiple_of((1 - c) * 512, 512), 512)
    peer = ep_device(x, 1 - c)

    def whole_rows(start, size):
        return whole.at[pl.ds(pl.multiple_of(start, 16), size), half_cols]

    pairing = remote(wo_f.at[:, other_cols], wo_r, (s_o, r_o), 19, peer)
    mine = whole_rows(r * 64 + x * 16, 16)
    stage_o = [remote(mine, mine, (s_o, r_o), k, ep_device((x + 1 + k) % 4, c)) for k in range(3)]
    mine = whole_rows(r * 64, 64)
    spread_o = [remote(mine, mine, (s_o, r_o), 3 + k, {"rep": d}) for k, d in enumerate(copies)]
    mine = whole_rows(0, D)
    other_half = remote(mine, mine, (s_o, r_o), 18, peer)

    def cols_of(b):
        return wg.at[r, pl.ds(pl.multiple_of(b * 16, 16), 16)]

    stage_w = [remote(wsl.at[d], cols_of(e), (s_w, r_w), k, {"ep": d}) for k, d in enumerate(others)]
    stage_t = [remote(tiny_b, smalls.at[e], (s_t, r_t), k, {"ep": d}) for k, d in enumerate(others)]
    spread_w = [remote(wg.at[r], wg.at[r], (s_w, r_w), 7 + k, {"rep": d}) for k, d in enumerate(copies)]
    tokens = RingGather(tok, x_s, (s_tok, r_tok), lsem.at[0])
    grads = RingGather(cot_s, g_all, (s_cot, r_cot), lsem.at[1])
    for copy in stage_w + stage_t + [pairing]:
        copy.start()
    tokens.start()
    cols_of(e)[...] = wsl[e]
    smalls[e] = tiny_b[...]
    for copy in stage_w + stage_t:
        copy.wait_recv()
    router_tiles = [
        sum(pltpu.roll(smalls[4 * a + b][:8].astype(F32), 32 * b, 1) if b else smalls[4 * a][:8].astype(F32) for b in range(4))
        for a in range(2)
    ]
    gain_rows = [smalls[d][8:9].astype(F32) for d in range(EP)]
    wg[r, 128:160] = jnp.concatenate(router_tiles + gain_rows + [jnp.zeros((8, 128), F32)], axis=0).astype(BF)
    for copy in spread_w:
        copy.start()
    pairing.wait_recv()
    own_half, peer_half = wo_f[:, half_cols], wo_r[...]
    upper, lower = jnp.where(c == 0, own_half, peer_half), jnp.where(c == 0, peer_half, own_half)
    whole[pl.ds(pl.multiple_of(r * 64 + x * 16, 16), 16), half_cols] = jnp.concatenate([upper, lower], axis=0).astype(BF)
    for copy in stage_o:
        copy.start()
    tokens.forward_half()
    tables[2].wait()
    grads.start()
    tokens.forward_rest()

    routed = rts_in[...]
    hit = jnp.zeros((EXPERTS, TOK), F32)
    for k in range(TOP):
        hit = jnp.where(iota((EXPERTS, TOK), 0) == routed[k : k + 1], 1.0, hit)
    before = jnp.where(iota((TOK, TOK), 0) < iota((TOK, TOK), 1), 1.0, 0.0).astype(BF)
    slots = jnp.where(hit > 0.0, dot(hit.astype(BF), before), -1.0)
    segs = jnp.concatenate([seg[:, b * TOK : (b + 1) * TOK] for b in range(EP)], axis=0)
    opening = jnp.zeros((EP, TOK), F32)
    for value in range(2):
        count = jnp.sum(jnp.where(segs == value, 1.0, 0.0), axis=1, keepdims=True)
        opening = opening + jnp.where(segs > value, jnp.sum(count, axis=0, keepdims=True), 0.0)
    places = (iota((EP, TOK), 0) * TOK + iota((EP, TOK), 1)).astype(F32)
    lo[...] = jnp.maximum(opening, places - (WINDOW - 1))

    for copy in spread_w:
        copy.wait_recv()
    for copy in stage_o:
        copy.wait_recv()
    for copy in spread_o:
        copy.start()

    def unpack(b, carry):
        for d in range(EP):
            tile = wg[b, d * 16 : d * 16 + 16].astype(F32)
            rows = pl.ds(pl.multiple_of(b * 64 + d * 8, 8), 8)
            w32[rows, 0:128] = tile[0:8]
            w32[rows, 128:256] = tile[8:16]
        extra = wg[b, 128:160].astype(F32)
        for d in range(EP):
            tile = extra[d // 4 * 8 : d // 4 * 8 + 8]
            if d % 4:
                tile = pltpu.roll(tile, 128 - 32 * (d % 4), 1)
            w32[pl.ds(pl.multiple_of(b * 64 + d * 8, 8), 8), 256:384] = tile
        gains_s[pl.ds(pl.multiple_of(b * 8, 8), 8)] = extra[16:24]
        return carry

    lax.fori_loop(0, REP, unpack, 0)
    wcol[...] = w32[:, :256].astype(BF)
    rout_o[...] = jnp.transpose(w32[:, 256:384])[:EXPERTS].astype(BF)
    packed = gains_s[...].astype(BF)

    def spread_gain(width, group, base, shift):
        lane = base + iota((128, width), 1) % group
        picked = dot(packed, jnp.where(iota((128, width), 0) == lane, 1.0, 0.0).astype(BF))
        mine = iota((128, width), 0) == shift + iota((128, width), 1) // group
        return jnp.sum(jnp.where(mine, picked, 0.0), axis=0, keepdims=True)

    gain_a[...] = spread_gain(D, 8, 0, 0)
    gain_f[...] = spread_gain(D, 8, 20, 0)
    key_part = spread_gain(128, 4, 16, e * 16)
    gain[:, :128] = spread_gain(128, 8, 8, e * 16)
    gain[:, 128:] = jnp.where(iota((1, 128), 1) < HEAD_DIM, key_part, 1.0)

    leave((wcol, wcol_h), (rout_o, rout_h))
    tokens.first[4].wait_recv()
    tokens.own.wait()

    def project(k, carry):
        @pl.when(k == 2)
        def _():
            tokens.fwd_right.wait_recv()
            tokens.fwd_left.wait_recv()
            tokens.to_peer[2].start()
            tokens.to_peer[1].wait_recv()

        @pl.when(k == 4)
        def _():
            tokens.to_peer[0].wait_recv()

        @pl.when(k == 6)
        def _():
            tokens.to_peer[2].wait_recv()

        g = k // 2
        b = (2 * (x + g + g // 2 - 2 * (g // 3)) + k % 2) % EP
        rows = block_rows(b)
        values = x_s[rows].astype(F32)
        r1 = lax.rsqrt(jnp.mean(values * values, axis=1, keepdims=True) + EPSILON)
        normed = (values * r1 * gain_a[...]).astype(BF)
        out = dot(normed, wcol[...])
        lin[rows] = out
        both = row_sums(out * out, PARTS)
        sums[pl.ds(2 * b, 1)] = both[0:1]
        sums[pl.ds(2 * b + 1, 1)] = both[1:2]
        return carry

    lax.fori_loop(0, EP, project, 0)
    stats = [remote(sums, held.at[e], (s_st, r_st), k, {"ep": d}) for k, d in enumerate(others)]
    for copy in stats:
        copy.start()
    held[e] = sums[...]
    keep = pltpu.make_async_copy(x_s, x_all, lsem.at[4])
    keep.start()
    for copy in tables[:2]:
        copy.wait()
    for copy in stats:
        copy.wait_recv()
    total = held[0]
    for k in range(1, EP):
        total = total + held[k]
    st[...] = total
    grads.forward_half()
    leave((lin, lin_h), (misc, misc_h))

    def prepare(b, carry):
        rows = block_rows(b)
        cq, ck = columns(
            lax.rsqrt(st[pl.ds(2 * b, 1)] * (1.0 / D) + EPSILON),
            lax.rsqrt(st[pl.ds(2 * b + 1, 1)] * (1.0 / KV) + EPSILON),
        )
        cosine, sine = cos_ref[rows], sin_ref[rows]
        q_o[rows] = turn(lin[rows, :128] * cq * gain[:, :128], cosine, sine).astype(BF)
        kv = lin[rows, 128:]
        kv = jnp.where(first, turn(kv * ck * gain[:, 128:], cosine, sine), kv)
        other = pltpu.roll(kv, HEAD_DIM, 1)
        k_o[rows] = jnp.where(first, kv, other).astype(BF)
        v_o[rows] = jnp.where(first, other, kv).astype(BF)
        return carry

    lax.fori_loop(0, EP, prepare, 0, unroll=2)
    leave((q_o, q_h), (k_o, k_h), (v_o, v_h))

    def heads(i, source):
        cols = pl.ds(pl.multiple_of(source * 128, 128), 128)
        return pltpu.make_async_remote_copy(
            src_ref=a_o.at[block_rows(i)],
            dst_ref=att_o.at[:, cols],
            send_sem=s_a.at[i],
            recv_sem=r_a.at[source],
            device_id={"ep": i},
            device_id_type=MESH,
        )

    def attend_block(i, n):
        rows = block_rows(i)
        past = (n - 1) * TOK
        q2 = stack_heads(q_o[rows].astype(F32) * HEAD_DIM ** (-0.5)).astype(BF)
        (lo_col,) = columns(lo[pl.ds(i, 1)])
        low = jnp.concatenate([lo_col, lo_col], axis=0)
        own_key = (iota((2 * TOK, TOK), 1) + i * TOK).astype(F32)
        query = (iota((2 * TOK, TOK), 0) % TOK + i * TOK).astype(F32)
        s_own = jnp.where((own_key >= low) & (own_key <= query), dot_nt(q2, k_o[rows]), MASKED)
        m = jnp.max(s_own, axis=1, keepdims=True)
        if past:
            early = pl.ds(pl.multiple_of((i - n + 1) * TOK, TOK), past)
            key = (iota((2 * TOK, past), 1) + (i - n + 1) * TOK).astype(F32)
            s = jnp.where(key >= low, dot_nt(q2, k_o[early]), MASKED)
            m = jnp.maximum(m, jnp.max(s, axis=1, keepdims=True))
        p_own = jnp.exp(s_own - m)
        total = jnp.sum(p_own, axis=1, keepdims=True)
        out = dot(p_own.astype(BF), v_o[rows])
        if past:
            p = jnp.exp(s - m)
            total = total + jnp.sum(p, axis=1, keepdims=True)
            out = out + dot(p.astype(BF), v_o[early])
        a_o[rows] = merge_heads(out / total).astype(BF)
        lse = jnp.broadcast_to(m + jnp.log(total), (2 * TOK, 128))
        lse_o[i] = jnp.transpose(lse)[:8]

        @pl.when(i != e)
        def _():
            heads(i, e).start()

        @pl.when(i == e)
        def _():
            att_o[:, pl.ds(pl.multiple_of(e * 128, 128), 128)] = a_o[rows]

    def later(i, carry):
        attend_block(i, 5)

        @pl.when(i == 5)
        def _():
            grads.fwd_right.wait_recv()
            grads.fwd_left.wait_recv()
            grads.to_peer[2].start()
            other_half.wait_recv()
            whole_out.start()

        return carry

    whole_out = pltpu.make_async_copy(whole, whole_h, hsem.at[len(leaving)])
    leaving.append(whole_out)

    for i in range(4):
        attend_block(i, i + 1)
    grads.forward_rest()
    for copy in spread_o:
        copy.wait_recv()
    other_half.start()
    lax.fori_loop(4, EP, later, 0)

    leave((a_o, a_h), (lse_o, lse_h))
    for d in others:
        heads(d, d).wait_recv()
    leave((att_o, att_h))

    hidden = x_s[block_rows(e)].astype(F32) + dot(att_o[...], whole[...])
    hid_o[...] = hidden
    r2 = lax.rsqrt(jnp.mean(hidden * hidden, axis=1, keepdims=True) + EPSILON)
    moe_in = (hidden * r2 * gain_f[...]).astype(BF)
    m_o[...] = moe_in
    leave((hid_o, hid_h), (m_o, m_h))
    logits = dot_nt(rout_o[...], moe_in)
    chosen = hit > 0.0
    logits = jnp.where(chosen, logits, MASKED)
    raised = jnp.where(chosen, jnp.exp(logits - jnp.max(logits, axis=0, keepdims=True)), 0.0)
    gates = raised / jnp.sum(raised, axis=0, keepdims=True)
    for d in range(EP):
        part = slice(d * LOCAL, (d + 1) * LOCAL)
        tab_o[d] = jnp.concatenate([slots[part], gates[part]], axis=0)
    leave((tab_o, tab_h))

    grads.first[4].wait_recv()
    for copy in grads.to_peer:
        copy.wait_recv()
    grads.own.wait()
    keep.wait()
    for copy in leaving:
        copy.wait()
    for d in others:
        heads(d, d).wait_send()
    for ring in (tokens, grads):
        for copy in ring.first + [ring.fwd_right, ring.fwd_left] + ring.to_peer:
            copy.wait_send()
    for copy in stage_w + stage_t + stage_o + spread_w + spread_o + stats + [other_half, pairing]:
        copy.wait_send()


def front(*args):
    results = [
        shape((LENGTH, D), BF),
        shape((LENGTH, D), BF),
        shape((LENGTH, 256)),
        shape((LENGTH, 128), BF),
        shape((LENGTH, 128), BF),
        shape((LENGTH, 128), BF),
        shape((LENGTH, 128), BF),
        shape((EP, 8, 2 * TOK)),
        shape((TOK, D)),
        shape((TOK, D), BF),
        shape((EP, 2 * LOCAL, TOK)),
        shape((TOK, D), BF),
        shape((32, D)),
        shape((EXPERTS, D), BF),
        shape((D, D), BF),
        shape((D, 256), BF),
    ]
    return comm_call(
        front_kernel,
        "front",
        1,
        results,
        [ANY, ANY] + [VM] * 11 + [ANY, ANY],
        [ANY] * len(results),
        [pltpu.VMEM(a.shape, a.dtype) for a in results[2:]]
        + [
            DMA((14,)),
            pltpu.VMEM((LENGTH, D), BF),
            pltpu.VMEM((TOK, D), BF),
            pltpu.VMEM((16, 128), F32),
            pltpu.VMEM((16, 128), BF),
            pltpu.VMEM((EP, 16, 128), BF),
            pltpu.VMEM((EP, 16, 128), BF),
            pltpu.VMEM((8, D), F32),
            pltpu.VMEM((8, 512), F32),
            pltpu.VMEM((REP, 160, 128), BF),
            pltpu.VMEM((D, 384), F32),
            pltpu.VMEM((128, 128), F32),
            pltpu.VMEM((LENGTH, 128), F32),
            pltpu.VMEM((LENGTH, 128), F32),
            pltpu.VMEM((16, 256), F32),
            pltpu.VMEM((EP, 16, 256), F32),
        ]
        + [DMA((10,))] * 4
        + [DMA((23,))] * 4
        + [DMA((7,))] * 4
        + [DMA((8,))] * 2
        + [DMA((6,))],
        limit=60,
    )(*args)


class ChipReduce:
    SEMS = 10
    STEP = 64

    def __init__(self, n, swo, snd, pc, rcv, hop, sems):
        e, x, c = place()
        self.n, self.h = n, n // 2
        h = n // 2
        self.snd, self.pc, self.rcv, self.hop = snd, pc, rcv, hop
        right, left = ep_device((x + 1) % 4, c), ep_device((x + 3) % 4, c)
        peer = ep_device(x, 1 - c)
        self.swap = lambda k: remote(swo.at[k], pc.at[k], sems, k, peer)
        low, high = pl.ds(0, h), pl.ds(h, h)
        self.opp = [
            remote(snd.at[0, low], hop.at[low], sems, 4, right),
            remote(snd.at[0, high], hop.at[high], sems, 5, left),
        ]
        self.near = [
            remote(snd.at[2, high], rcv.at[0, high], sems, 6, right),
            remote(snd.at[1, low], rcv.at[1, low], sems, 7, left),
        ]
        self.far = [
            remote(snd.at[2, low], rcv.at[0, low], sems, 8, right),
            remote(snd.at[1, high], rcv.at[1, high], sems, 9, left),
        ]

    def rows_loop(self, low, count, body):
        step = self.STEP

        def loop(i, carry):
            body(pl.ds(pl.multiple_of(low + i * step, 16), step))
            return carry

        lax.fori_loop(0, count // step, loop, 0)

    def merge(self, k):
        def body(s):
            self.snd[k, s] = (self.snd[k, s].astype(F32) + self.pc[k, s].astype(F32)).astype(BF)

        self.swap(k).wait_recv()
        self.rows_loop(0, self.n, body)

    def merge_hop(self, k, low):
        def body(s):
            self.snd[k, s] = (self.snd[k, s].astype(F32) + self.hop[s].astype(F32)).astype(BF)

        self.rows_loop(low, self.h, body)

    def send_opp(self):
        self.merge(0)
        for copy in self.opp:
            copy.start()

    def near_right(self):
        self.merge(2)
        self.near[0].start()

    def near_left(self):
        self.merge(1)
        self.near[1].start()

    def send_near(self):
        self.near_right()
        self.near_left()

    def send_far(self):
        self.opp[0].wait_recv()
        self.merge_hop(2, 0)
        self.far[0].start()
        self.opp[1].wait_recv()
        self.merge_hop(1, self.h)
        self.far[1].start()

    def finish(self, out_ref):
        for copy in self.near + self.far:
            copy.wait_recv()

        def body(s):
            out_ref[s] = self.snd[3, s].astype(F32) + (
                self.rcv[0, s].astype(F32) + self.rcv[1, s].astype(F32)
            )

        self.rows_loop(0, self.n, body)
        for copy in [self.swap(k) for k in range(4)] + self.opp + self.near + self.far:
            copy.wait_send()


PAIR = 2
ROWS = EP * CAP
CHIP = 2 * CAP
BLOCK = 96


def chip_rows(q):
    return pl.ds(pl.multiple_of(q * CHIP, 16), CHIP)


def chip_tokens(q):
    return pl.ds(pl.multiple_of(q * 2 * TOK, 2 * TOK), 2 * TOK)


def expert_hits(tab, e, n, q):
    row = slice(n, n + 1)
    second = tab[2 * q + 1, row]
    slots = jnp.concatenate([tab[2 * q, row], jnp.where(second >= 0.0, second + CAP, -1.0)], axis=1)
    return iota((CHIP, 2 * TOK), 0).astype(F32) == slots


def one_hot(hit):
    return jnp.where(hit, 1.0, 0.0).astype(BF)


def expert_chip(q, e, start, tab, m_ref, g_ref, wgu, wd, a_s, act_s, gp_s, dgu_s, y_s, z_s, ggt):
    hits = [expert_hits(tab, e, start + n, q) for n in range(PAIR)]
    chosen = jnp.concatenate([one_hot(hit) for hit in hits], axis=0)
    rows = chip_rows(q)
    a_both = dot(chosen, m_ref[chip_tokens(q)]).astype(BF)
    c_both = dot(chosen, g_ref[chip_tokens(q)]).astype(BF)
    for n in range(PAIR):
        part = slice(n * CHIP, (n + 1) * CHIP)
        row = slice(LOCAL + start + n, LOCAL + start + n + 1)
        gates = jnp.concatenate([tab[2 * q, row], tab[2 * q + 1, row]], axis=1)
        weight = jnp.sum(jnp.where(hits[n], gates, 0.0), axis=1, keepdims=True)
        a, cot = a_both[part], c_both[part]
        lin = dot(a, wgu[n])
        back = dot_nt(cot, wd[n])
        gate_lin, up_lin = lin[:, :FF], lin[:, FF:]
        sig = jax.nn.sigmoid(gate_lin)
        silu = gate_lin * sig
        act = silu * up_lin
        act_low = act.astype(BF)
        produced = dot(act_low, wd[n]).astype(BF).astype(F32)
        gg = jnp.sum(act * back, axis=1, keepdims=True)
        back = back * weight
        dgate = (back * up_lin * sig * (1.0 + gate_lin * (1.0 - sig))).astype(BF)
        dup = (back * silu).astype(BF)
        dgu = jnp.concatenate([dgate, dup], axis=1)
        a_s[n, rows] = a
        act_s[n, rows] = act_low
        gp_s[n, rows] = (weight * cot.astype(F32)).astype(BF)
        dgu_s[n, rows] = dgu
        y_s[n, rows] = (weight * produced).astype(BF)
        z_s[n, rows] = dot_nt(dgu, wgu[n]).astype(BF)
        gg_row = jnp.sum(jnp.where(hits[n], gg, 0.0), axis=0, keepdims=True)
        ggt[2 * q, n : n + 1] = gg_row[:, :TOK]
        ggt[2 * q + 1, n : n + 1] = gg_row[:, TOK:]


def expert_grads(n, a_s, act_s, gp_s, dgu_s, eg, eg_o, sems):
    copies = []
    for k, (first, size) in enumerate(((0, 64), (64, 32))):
        left, right = ((a_s, dgu_s), (act_s, gp_s))[k]
        eg[n, :, first : first + size] = dot_tn(left[n], right[n]).astype(BF).reshape(REP, size, D)
        some = pl.ds(first, size)
        copies.append(pltpu.make_async_copy(eg.at[n, :, some], eg_o.at[n, :, some], sems.at[2 * n + k]))
        copies[-1].start()
    return copies


def load_weights(start, wg_in, wu_in, wd_in, wgu, wd, sems):
    some = pl.ds(start, PAIR)
    return [
        pltpu.make_async_copy(wg_in.at[some], wgu.at[:, :, pl.ds(0, FF)], sems.at[0]),
        pltpu.make_async_copy(wu_in.at[some], wgu.at[:, :, pl.ds(FF, FF)], sems.at[1]),
        pltpu.make_async_copy(wd_in.at[some], wd, sems.at[2]),
    ]


def send_gates(ggt, gg_o, e, sems, lsem):
    copies = [remote(ggt.at[d], gg_o.at[e], sems, k, {"ep": d}) for k, d in enumerate(ep_others(e))]
    return copies, pltpu.make_async_copy(ggt.at[e], gg_o.at[e], lsem)


def experts_first_kernel(
    m_in, t_in, g_in, wg_in, wu_in, wd_in, m_o, tab_o, y_o, z_o, gg_o, eg_o,
    m_ref, tab, g_ref, wgu, wd, a_s, act_s, gp_s, dgu_s, y_s, z_s, ggt, eg,
    s_m, r_m, s_t, r_t, s_g, r_g, lsem, wsem, gsem, esem, ksem,
):
    e, x, c = place()
    others = ep_others(e)
    ring = RingGather(m_in, m_ref, (s_m, r_m), lsem.at[0])
    tables = [remote(t_in.at[d], tab.at[e], (s_t, r_t), k, {"ep": d}) for k, d in enumerate(others)]
    own = pltpu.make_async_copy(t_in.at[e], tab.at[e], lsem.at[1])
    loads = load_weights(0, wg_in, wu_in, wd_in, wgu, wd, wsem)
    cots = [
        pltpu.make_async_copy(g_in.at[chip_tokens(q)], g_ref.at[chip_tokens(q)], gsem.at[k])
        for k, q in enumerate([x, (x + 1) % 4, (x + 3) % 4, (x + 2) % 4])
    ]

    def fetch():
        for copy in [own] + loads + cots:
            copy.start()
        ggt[...] = jnp.zeros((EP, 8, TOK), F32)

    greet([{"ep": d} for d in others], fetch)
    for copy in tables:
        copy.start()
    ring.start()

    def keep(k, q):
        rows = chip_rows(q)
        return [
            pltpu.make_async_copy(m_ref.at[chip_tokens(q)], m_o.at[chip_tokens(q)], ksem.at[0, k]),
            pltpu.make_async_copy(y_s.at[:, rows], y_o.at[:, rows], ksem.at[1, k]),
            pltpu.make_async_copy(z_s.at[:, rows], z_o.at[:, rows], ksem.at[2, k]),
        ]

    def chips(k, carry):
        @pl.when(k == 0)
        def _():
            ring.first[0].wait_recv()
            ring.fwd_right.start()
            ring.first[1].wait_recv()
            ring.fwd_left.start()
            ring.first[4].wait_recv()
            ring.own.wait()
            own.wait()
            for copy in tables:
                copy.wait_recv()
            for copy in loads:
                copy.wait()
            cots[0].wait()

        @pl.when(k == 1)
        def _():
            ring.first[3].wait_recv()
            ring.to_peer[1].start()
            ring.first[2].wait_recv()
            ring.to_peer[0].start()
            ring.to_peer[1].wait_recv()
            cots[1].wait()

        @pl.when(k == 2)
        def _():
            ring.fwd_right.wait_recv()
            ring.fwd_left.wait_recv()
            ring.to_peer[2].start()
            ring.to_peer[0].wait_recv()
            cots[2].wait()

        @pl.when(k == 3)
        def _():
            ring.to_peer[2].wait_recv()
            cots[3].wait()

        q = (x + k + k // 2 - 2 * (k // 3)) % 4
        expert_chip(q, e, 0, tab, m_ref, g_ref, wgu, wd, a_s, act_s, gp_s, dgu_s, y_s, z_s, ggt)
        for copy in keep(k, q):
            copy.start()
        return carry

    lax.fori_loop(0, 4, chips, 0)
    gates, own_gates = send_gates(ggt, gg_o, e, (s_g, r_g), lsem.at[3])
    states = [pltpu.make_async_copy(tab, tab_o, lsem.at[2])]
    for copy in gates + [own_gates] + states:
        copy.start()
    for n in range(PAIR):
        states += expert_grads(n, a_s, act_s, gp_s, dgu_s, eg, eg_o, esem)
    for k, q in enumerate([x, (x + 1) % 4, (x + 3) % 4, (x + 2) % 4]):
        states += keep(k, q)
    for copy in states + [own_gates]:
        copy.wait()
    for copy in gates:
        copy.wait_recv()
    for copy in ring.first + [ring.fwd_right, ring.fwd_left] + ring.to_peer + tables + gates:
        copy.wait_send()


def pair_scratch():
    return [
        pltpu.VMEM((LENGTH, D), BF),
        pltpu.VMEM((EP, 2 * LOCAL, TOK), F32),
        pltpu.VMEM((LENGTH, D), BF),
        pltpu.VMEM((PAIR, D, 2 * FF), BF),
        pltpu.VMEM((PAIR, FF, D), BF),
        pltpu.VMEM((PAIR, ROWS, D), BF),
        pltpu.VMEM((PAIR, ROWS, FF), BF),
        pltpu.VMEM((PAIR, ROWS, D), BF),
        pltpu.VMEM((PAIR, ROWS, D), BF),
        pltpu.VMEM((PAIR, ROWS, D), BF),
        pltpu.VMEM((PAIR, ROWS, D), BF),
        pltpu.VMEM((EP, 8, TOK), F32),
        pltpu.VMEM((PAIR, REP, BLOCK, D), BF),
    ]


def experts_first(m, t, g_all, wg, wu, wd):
    return comm_call(
        experts_first_kernel,
        "experts_first",
        2,
        [
            shape((LENGTH, D), BF),
            shape((EP, 2 * LOCAL, TOK)),
            shape((PAIR, ROWS, D), BF),
            shape((PAIR, ROWS, D), BF),
            shape((EP, 8, TOK)),
            shape((PAIR, REP, BLOCK, D), BF),
        ],
        [ANY] * 6,
        [ANY] * 6,
        pair_scratch()
        + [DMA((10,))] * 2
        + [DMA((7,))] * 4
        + [DMA((4,)), DMA((3,)), DMA((4,)), DMA((4,)), DMA((3, 4))],
        limit=60,
    )(m, t, g_all, wg, wu, wd)


def experts_last_kernel(
    m_in, t_in, y_in, z_in, g_in, wg_in, wu_in, wd_in, gm_o, mix_o, gg_o, eg_o,
    m_ref, tab, g_ref, wgu, wd, a_s, act_s, gp_s, dgu_s, y_s, z_s, ggt, eg,
    y_f, z_f, gm, swo, snd, pc, rcv, hop, mix_z, mix_y,
    s_r, r_r, s_g, r_g, lsem, wsem, gsem, msem, esem, osem,
):
    e, x, c = place()
    order = [(x + 2) % 4, (x + 3) % 4, (x + 1) % 4, x]
    loads = [pltpu.make_async_copy(t_in, tab, lsem.at[0])] + load_weights(2, wg_in, wu_in, wd_in, wgu, wd, wsem)
    rows = [
        (
            pltpu.make_async_copy(m_in.at[chip_tokens(q)], m_ref.at[chip_tokens(q)], msem.at[k]),
            pltpu.make_async_copy(g_in.at[chip_tokens(q)], g_ref.at[chip_tokens(q)], gsem.at[k]),
        )
        for k, q in enumerate(order)
    ]
    firsts = [pltpu.make_async_copy(z_in, z_f, lsem.at[1]), pltpu.make_async_copy(y_in, y_f, lsem.at[2])]
    for copy in loads + list(rows[0]) + [firsts[0]] + list(rows[1] + rows[2] + rows[3]) + [firsts[1]]:
        copy.start()
    greet([{"ep": d} for d in ep_others(e)])
    red = ChipReduce(TOK, swo, snd, pc, rcv, hop, (s_r, r_r))
    ggt[...] = jnp.zeros((EP, 8, TOK), F32)

    def combine(q, early, late):
        chosen = jnp.concatenate([one_hot(expert_hits(tab, e, n, q)) for n in range(LOCAL)], axis=0)
        part = chip_rows(q)
        values = [ref[n, part] for ref in (early, late) for n in range(PAIR)]
        return dot_tn(chosen, jnp.concatenate(values, axis=0)).astype(BF)

    for copy in loads:
        copy.wait()

    def chips(k, carry):
        for step in range(4):

            @pl.when(k == step)
            def _(step=step):
                for copy in rows[step]:
                    copy.wait()

        q = (x + 2 + k - (k // 2) * (2 * k - 1)) % 4
        expert_chip(q, e, 2, tab, m_ref, g_ref, wgu, wd, a_s, act_s, gp_s, dgu_s, y_s, z_s, ggt)

        @pl.when(k == 2)
        def _():
            red.near_left()

        @pl.when(k == 3)
        def _():
            red.near_right()

        @pl.when(k == 0)
        def _():
            firsts[0].wait()

        mix_z[...] = combine(q, z_f, z_s)
        swo[k] = mix_z[pl.ds(pl.multiple_of((1 - c) * TOK, TOK), TOK)]
        red.swap(k).start()
        snd[k] = mix_z[pl.ds(pl.multiple_of(c * TOK, TOK), TOK)]

        @pl.when(k == 0)
        def _():
            red.send_opp()

        return carry

    lax.fori_loop(0, 4, chips, 0)
    red.send_far()
    gates, own_gates = send_gates(ggt, gg_o, e, (s_g, r_g), lsem.at[3])
    for copy in gates + [own_gates]:
        copy.start()
    states = []
    for n in range(PAIR):
        states += expert_grads(n, a_s, act_s, gp_s, dgu_s, eg, eg_o, esem)
    red.merge(3)
    firsts[1].wait()

    def mixture(q, carry):
        values = combine(q, y_f, y_s)

        @pl.when(q > 0)
        def _():
            pltpu.make_async_copy(mix_y, mix_o.at[chip_tokens(q)], osem).wait()

        mix_y[...] = values
        pltpu.make_async_copy(mix_y, mix_o.at[chip_tokens(q)], osem).start()
        return carry

    lax.fori_loop(0, 4, mixture, 0)
    red.finish(gm)
    last = pltpu.make_async_copy(gm, gm_o, lsem.at[4])
    last.start()
    pltpu.make_async_copy(mix_y, mix_o.at[chip_tokens(3)], osem).wait()
    for copy in states + [own_gates, last]:
        copy.wait()
    for copy in gates:
        copy.wait_recv()
    for copy in gates:
        copy.wait_send()


def experts_last(m, t, y, z, g_all, wg, wu, wd):
    return comm_call(
        experts_last_kernel,
        "experts_last",
        4,
        [
            shape((TOK, D)),
            shape((LENGTH, D), BF),
            shape((EP, 8, TOK)),
            shape((PAIR, REP, BLOCK, D), BF),
        ],
        [ANY] * 8,
        [ANY] * 4,
        pair_scratch()
        + [
            pltpu.VMEM((PAIR, ROWS, D), BF),
            pltpu.VMEM((PAIR, ROWS, D), BF),
            pltpu.VMEM((TOK, D), F32),
            pltpu.VMEM((4, TOK, D), BF),
            pltpu.VMEM((4, TOK, D), BF),
            pltpu.VMEM((4, TOK, D), BF),
            pltpu.VMEM((2, TOK, D), BF),
            pltpu.VMEM((TOK, D), BF),
            pltpu.VMEM((2 * TOK, D), BF),
            pltpu.VMEM((2 * TOK, D), BF),
        ]
        + [DMA((10,))] * 2
        + [DMA((7,))] * 2
        + [DMA((5,)), DMA((3,)), DMA((4,)), DMA((4,)), DMA((4,)), DMA(())],
        limit=63,
    )(m, t, y, z, g_all, wg, wu, wd)


KEPT = 8


def back_kernel(
    eg_in, mix_in, gm_in, gg1_in, gg2_in, tab_in, hid_in, m_in, cot_in, att_in, misc_in, rout_in, whole_in, wcol_in, x_in, lin_in,
    q_in, k_in, v_in, a_in, lse_in, cos_in, sin_in,
    out_o, ig_o, gq_o, gk_o, gv_o, go_o, pack_o, eg_o,
    gm, gg1, gg2, tab, hid, cot, misc, rout, wcol, x_s, lin, q_s, k_s, v_s, a_s, lse, cos_ref, sin_ref,
    gh, ga_s, go, q2_s, p_s, dk, dv, u_s, sums, st2, held, wb, wsum, wheld,
    dwt, dws, dheld, dsum, dw_o, vec, vheld, vtot, vheld2, swo, snd, pc1, rcv1, hop1, rcv2, snd3, pc3, rcv3, hop3,
    s_1, r_1, s_2, r_2, s_3, r_3, s_go, r_go, s_st, r_st, s_w, r_w, s_d, r_d, s_e, r_e, s_v, r_v, s_v2, r_v2, lsem, l_1, l_3, esem, xsem,
    out_s, gq_s, gk_s, gv_s, go_s, pack_s, eg_s,
    za, zb, zc, zd, ze, zf, ya, yb, yc, yd, ye, yf, s_z, r_z, s_y, r_y, l_z, l_y,
):
    r = lax.axis_index("rep")
    e, x, c = place()
    others = ep_others(e)
    copies = rep_others(r)
    first = iota((TOK, 128), 1) < HEAD_DIM
    gain_a, gain_f, gain = misc.at[0:1], misc.at[1:2], misc.at[2:3, 0:256]
    lo, st = misc.at[8:16, 0:256], misc.at[16:32, 0:256]
    red1 = RingReduce(mix_in, TOK, pc1, snd, rcv1, hop1, (s_1, r_1), l_1)
    red2 = ChipReduce(TOK, swo, snd, pc1, rcv2, hop1, (s_2, r_2))
    red3 = RingReduce(wb, 128, pc3, snd3, rcv3, hop3, (s_3, r_3), l_3)
    by_z = GridReduce(True, eg_in, 0, za, zb, zc, zd, ze, zf, (s_z, r_z), l_z)
    by_y = GridReduce(False, eg_in, FF, ya, yb, yc, yd, ye, yf, (s_y, r_y), l_y)
    loads = [
        pltpu.make_async_copy(src, dst, lsem.at[k])
        for k, (src, dst) in enumerate(
            [
                (misc_in, misc), (gm_in, gm), (gg1_in, gg1), (gg2_in, gg2), (tab_in, tab), (hid_in, hid),
                (cot_in, cot), (rout_in, rout), (whole_in, wb.at[:, pl.ds(0, D)]), (q_in, q_s), (k_in, k_s), (lse_in, lse),
                (m_in, rcv2.at[0]), (att_in, rcv2.at[1]), (v_in, v_s), (a_in, a_s), (cos_in, cos_ref), (sin_in, sin_ref),
                (lin_in, lin), (wcol_in, wcol),
            ]
        )
    ]
    chips_order = [(x + 2) % 4, (x + 3) % 4, (x + 1) % 4, x]

    def x_load(k):
        return pltpu.make_async_copy(x_in.at[chip_tokens(chips_order[k])], x_s.at[k % 2], xsem.at[k % 2])


    def fetch():
        for copy in loads + [x_load(0), x_load(1)] + by_z.load + by_y.load:
            copy.start()

    greet([{"ep": d} for d in others] + [{"rep": d} for d in copies], fetch)
    red1.start()
    for copy in loads[:9]:
        copy.wait()

    def base(i):
        cut = jnp.minimum(i, 4)
        return cut * (cut + 1) // 2 + 5 * jnp.maximum(i - 4, 0)

    def spans(i, n):
        keys = pl.ds(pl.multiple_of((i - n + 1) * TOK, TOK), n * TOK)
        return keys, pl.ds(pl.multiple_of(base(i) * TOK, TOK), n * TOK)

    def probabilities(i, n):
        _, held_rows = spans(i, n)
        p_s[held_rows] = make_probabilities(i, n)

    def make_probabilities(i, n):
        keys, _ = spans(i, n)
        q2 = stack_heads(q_s[block_rows(i)].astype(F32) * HEAD_DIM ** (-0.5)).astype(BF)
        q2_s[i] = q2
        top = lse[i][0:1]
        low = jnp.concatenate([lo[pl.ds(i, 1)]] * 2, axis=1)
        key = (iota((n * TOK, 2 * TOK), 0) + (i - n + 1) * TOK).astype(F32)
        query = (iota((n * TOK, 2 * TOK), 1) % TOK + i * TOK).astype(F32)
        allowed = (key >= low) & (key <= query)
        return jnp.where(allowed, jnp.exp(dot_nt(k_s[keys], q2) - top), 0.0).astype(BF)

    def probabilities_later(i, carry):
        probabilities(i, 5)

        @pl.when(i == 4)
        def _():
            red1.push_opp()

        @pl.when(i == 5)
        def _():
            red1.push_near()

        return carry


    hidden = hid[...]
    weights = jnp.concatenate([tab[d][LOCAL:] for d in range(EP)], axis=0)
    grads = jnp.concatenate([ref[d][:PAIR] for d in range(EP) for ref in (gg1, gg2)], axis=0)
    mean = jnp.sum(weights * grads, axis=0, keepdims=True)
    grad_logits = weights * (grads - mean)
    grad_moe = gm[...] + dot_tn(grad_logits.astype(BF), rout[...])
    r2 = lax.rsqrt(jnp.mean(hidden * hidden, axis=1, keepdims=True) + EPSILON)
    n = hidden * r2
    u = grad_moe * gain_f[...]
    grad_hidden = cot[...].astype(F32) + r2 * (u - n * jnp.mean(u * n, axis=1, keepdims=True))
    gh[...] = grad_hidden
    branch = grad_hidden.astype(BF)
    ga_s[...] = dot_nt(branch, wb[:, :D]).astype(BF)

    def own_cols(ref, b):
        return ref.at[:, pl.ds(pl.multiple_of(b * 128, 128), 128)]

    heads = [
        remote(own_cols(ga_s, d), go.at[block_rows(e)], (s_go, r_go), k, {"ep": d}) for k, d in enumerate(others)
    ]
    for copy in heads:
        copy.start()
    by_z.push()
    by_y.push()
    go[block_rows(e)] = own_cols(ga_s, e)[...]
    for copy in loads[9:12]:
        copy.wait()
    for i in range(4):
        probabilities(i, i + 1)
    lax.fori_loop(4, KEPT, probabilities_later, 0)
    for copy in loads[12:]:
        copy.wait()
    for copy in heads:
        copy.wait_recv()
    ffn = jnp.sum(grad_moe * n, axis=0, keepdims=True)
    logit_rows = jnp.transpose(jnp.concatenate([grad_logits, jnp.zeros((96, TOK), F32)], axis=0)).astype(BF)
    router_rows = dot_tn(rcv2[0], logit_rows)
    vec[...] = jnp.zeros((8, D), F32)
    vec[3:4] = ffn
    router_rows = router_rows.reshape(REP, EP, 8, 128)
    for d in range(EP):
        wb[d * 128 : (d + 1) * 128, D:] = router_rows[:, d].reshape(128, 128).astype(BF)
    for cols in range(0, D, 256):
        out_rows = dot_tn(rcv2[1], branch[:, cols : cols + 256]).reshape(REP, EP, 8, 256)
        for d in range(EP):
            wb[d * 128 : (d + 1) * 128, cols : cols + 256] = out_rows[:, d].reshape(128, 256).astype(BF)
    red3.start()
    by_z.stage.relay()
    by_y.stage.relay()
    dk[...] = jnp.zeros((LENGTH, 128), F32)
    dv[...] = jnp.zeros((LENGTH, 128), F32)

    def part(ref, b, size):
        return ref.at[pl.ds(pl.multiple_of(b * size, 8), size)]

    spread_w = [remote(part(wsum, d, 8), wheld.at[r], (s_w, r_w), k, {"rep": d}) for k, d in enumerate(copies)]

    def attend_back(i, n):
        keys, held_rows = spans(i, n)
        rows = block_rows(i)
        grad = stack_heads(go[rows].astype(F32))
        do2 = grad.astype(BF)
        out = a_s[rows].astype(F32)
        settle = row_sums(grad * jnp.concatenate([out, out], axis=0), ((0, 128),))[0:1]
        p = p_s[held_rows]
        ds = (p.astype(F32) * (dot_nt(v_s[keys], do2) - settle)).astype(BF)
        dv[keys] += dot(p, do2)
        dk[keys] += dot(ds, q2_s[i])
        dq = dot_tn(k_s[keys], ds)
        u_s[rows, :128] = merge_heads(jnp.transpose(dq)) * HEAD_DIM ** (-0.5)

    def attend_back_later(i, carry):
        attend_back(i, 5)
        return carry

    for i in range(4):
        attend_back(i, i + 1)
    red3.push_opp()
    red3.push_near()
    lax.fori_loop(4, 6, attend_back_later, 0, unroll=True)
    red1.relay()
    red3.relay()
    lax.fori_loop(6, EP, attend_back_later, 0, unroll=True)

    def close(b, carry):
        rows = block_rows(b)
        grad_k, grad_v = dk[rows], dv[rows]
        grad_k = grad_k + pltpu.roll(grad_k, HEAD_DIM, 1)
        grad_v = grad_v + pltpu.roll(grad_v, HEAD_DIM, 1)
        both = jnp.where(first, grad_k, grad_v).astype(BF).astype(F32)
        cosine, sine = cos_ref[rows], -sin_ref[rows]
        both = jnp.where(first, turn(both, cosine, sine), both)
        grad_q = turn(u_s[rows, :128].astype(BF).astype(F32), cosine, sine)
        u_s[rows, :128] = grad_q
        u_s[rows, 128:] = both
        cq, ck = columns(
            lax.rsqrt(st[pl.ds(2 * b, 1)] * (1.0 / D) + EPSILON),
            lax.rsqrt(st[pl.ds(2 * b + 1, 1)] * (1.0 / KV) + EPSILON),
        )
        products = jnp.concatenate([grad_q * cq, both * ck], axis=1) * gain[...] * lin[rows]
        pair = row_sums(products, PARTS)
        sums[pl.ds(2 * b, 1)] = pair[0:1]
        sums[pl.ds(2 * b + 1, 1)] = pair[1:2]
        return carry

    lax.fori_loop(0, EP, close, 0, unroll=2)
    stats = [remote(sums, held.at[e], (s_st, r_st), k, {"ep": d}) for k, d in enumerate(others)]
    for copy in stats:
        copy.start()
    held[e] = sums[...]
    red1.finish(gm)
    out_s[...] = (hid[...] + gm[...]).astype(BF)
    ends = [pltpu.make_async_copy(out_s, out_o, esem.at[0])]
    ends[0].start()
    red3.finish(wsum)
    for copy in spread_w:
        copy.start()
    wheld[r] = part(wsum, r, 8)[...]
    by_z.turn()
    by_y.turn()
    dwt[...] = jnp.zeros((256, D), F32)
    for copy in stats:
        copy.wait_recv()
    total = held[0]
    for k in range(1, EP):
        total = total + held[k]
    st2[...] = total

    def project_back(b, slot):
        rows = block_rows(b)
        values = x_s[slot, pl.ds(pl.multiple_of(b % 2 * TOK, TOK), TOK)].astype(F32)
        r1 = lax.rsqrt(jnp.mean(values * values, axis=1, keepdims=True) + EPSILON)
        n1 = values * r1
        normed = (n1 * gain_a[...]).astype(BF)
        cq, ck, mq, mk = columns(
            lax.rsqrt(st[pl.ds(2 * b, 1)] * (1.0 / D) + EPSILON),
            lax.rsqrt(st[pl.ds(2 * b + 1, 1)] * (1.0 / KV) + EPSILON),
            st2[pl.ds(2 * b, 1)] * (1.0 / D),
            st2[pl.ds(2 * b + 1, 1)] * (1.0 / KV),
        )
        uq, uk = u_s[rows, :128], u_s[rows, 128:]
        nq = lin[rows, :128] * cq
        nk = lin[rows, 128:] * ck
        gq = cq * (uq * gain[:, :128] - nq * mq)
        gk = jnp.where(first, ck * (uk * gain[:, 128:] - nk * mk), uk)
        glin = jnp.concatenate([gq, gk], axis=1).astype(BF)
        vec[1:2, :128] += jnp.sum(uq * nq, axis=0, keepdims=True)
        vec[2:3, :128] += jnp.sum(uk * nk, axis=0, keepdims=True)
        gn = dot_nt(glin, wcol[...])
        vec[0:1] += jnp.sum(gn * n1, axis=0, keepdims=True)
        dwt[...] += dot_tn(glin, normed)
        return gn.astype(BF)

    def chips(k, carry):
        q = (x + 2 + k - (k // 2) * (2 * k - 1)) % 4
        for step in range(4):

            @pl.when(k == step)
            def _(step=step):
                x_load(step).wait()

        swo[k] = project_back(q * 2 + 1 - c, k % 2)
        red2.swap(k).start()

        @pl.when(k == 1)
        def _():
            red2.send_opp()

        @pl.when(k == 2)
        def _():
            red2.near_left()

        @pl.when(k == 3)
        def _():
            red2.near_right()

        snd[k] = project_back(q * 2 + c, k % 2)
        for step in range(2):

            @pl.when(k == step)
            def _(step=step):
                x_load(step + 2).start()

        return carry

    lax.fori_loop(0, 4, chips, 0)
    dws[...] = jnp.transpose(dwt[...]).astype(BF)
    spread_d = [remote(part(dws, d, 64), dheld.at[r], (s_d, r_d), k, {"rep": d}) for k, d in enumerate(copies)]
    for copy in spread_d:
        copy.start()
    dheld[r] = part(dws, r, 64)[...]
    gain_q, gain_k = vec[1:2, :128], vec[2:3, :128]
    low, spread = iota((1, 128), 1) < 32, iota((1, 128), 1) // 32 == 2
    gain_k = jnp.where(low, gain_k, jnp.where(spread, pltpu.roll(gain_k, 32, 1), 0.0))
    vec[1:3, :128] = jnp.zeros((2, 128), F32)
    vec[1:2, pl.ds(pl.multiple_of(e * 128, 128), 128)] = gain_q
    vec[2:3, pl.ds(pl.multiple_of(e * 128, 128), 128)] = gain_k
    spread_v = [remote(vec, vheld.at[e], (s_v, r_v), k, {"ep": d}) for k, d in enumerate(others)]
    for copy in spread_v:
        copy.start()
    vheld[e] = vec[...]
    red2.merge(3)
    red2.send_far()
    by_z.last.relay()
    by_y.last.relay()
    for copy in spread_v:
        copy.wait_recv()
    total = vheld[0]
    for k in range(1, EP):
        total = total + vheld[k]
    vtot[...] = total
    def lanes_of(d):
        return vtot.at[:, pl.ds(pl.multiple_of(d // 2 * 128, 128), 128)]

    spread_v2 = [remote(lanes_of(d), vheld2.at[r], (s_v2, r_v2), k, {"rep": d}) for k, d in enumerate(copies)]
    for copy in spread_v2:
        copy.start()
    vheld2[r] = lanes_of(r)[...]
    for copy in spread_w:
        copy.wait_recv()
    total = wheld[0]
    for k in range(1, REP):
        total = total + wheld[k]
    go_s[...] = total[:, :D]
    pack_s[0:8] = total[:, D:]
    for copy in spread_d:
        copy.wait_recv()
    total = dheld[0].astype(F32)
    for k in range(1, REP):
        total = total + dheld[k].astype(F32)
    dsum[...] = total
    spread_e = [remote(part(dsum, d, 8), dw_o.at[e], (s_e, r_e), k, {"ep": d}) for k, d in enumerate(others)]
    for copy in spread_e:
        copy.start()
    dw_o[e] = part(dsum, e, 8)[...]
    for copy in spread_v2:
        copy.wait_recv()
    total = vheld2[0]
    for k in range(1, REP):
        total = total + vheld2[k]
    start = r % 2 * 64
    rows_d, lanes_d = iota((128, 128), 0), iota((128, 128), 1)
    eight = jnp.where((rows_d == start + e * 8 + lanes_d) & (lanes_d < 8), 1.0, 0.0)
    four = jnp.where((rows_d == start + e * 4 + lanes_d) & (lanes_d < 4), 1.0, 0.0)

    def pick(sel):
        return jnp.dot(total, sel, preferred_element_type=F32, precision=HIGH)

    eights, fours = pick(eight), pick(four)
    pack_s[8:16] = jnp.where(iota((8, 128), 0) == 2, fours, eights)
    by_z.finish(eg_s, 0)
    by_y.finish(eg_s, FF)
    for copy in spread_e:
        copy.wait_recv()
    low_lanes = iota((8, 128), 1) < HEAD_DIM
    for d in range(EP):
        gq_s[:, d * 128 : (d + 1) * 128] = dw_o[d][:, :128]
    for d in range(EP // 2):
        even, odd = dw_o[2 * d][:, 128:], dw_o[2 * d + 1][:, 128:]
        gk_s[:, d * 128 : (d + 1) * 128] = jnp.where(low_lanes, even, pltpu.roll(odd, HEAD_DIM, 1))
        gv_s[:, d * 128 : (d + 1) * 128] = jnp.where(low_lanes, pltpu.roll(even, HEAD_DIM, 1), odd)
    pairs = [(gq_s, gq_o), (gk_s, gk_o), (gv_s, gv_o), (go_s, go_o), (pack_s, pack_o), (eg_s, eg_o)]
    for k, (src, dst) in enumerate(pairs):
        ends.append(pltpu.make_async_copy(src, dst, esem.at[1 + k]))
        ends[-1].start()
    red2.finish(gm)
    values = x_s[1, pl.ds(pl.multiple_of(c * TOK, TOK), TOK)].astype(F32)
    r1 = lax.rsqrt(jnp.mean(values * values, axis=1, keepdims=True) + EPSILON)
    n1 = values * r1
    z = gm[...] * gain_a[...]
    gh[...] = gh[...] + r1 * (z - n1 * jnp.mean(z * n1, axis=1, keepdims=True))
    ends.append(pltpu.make_async_copy(gh, ig_o, esem.at[7]))
    ends[-1].start()
    for copy in ends:
        copy.wait()
    for copy in heads + stats + spread_w + spread_d + spread_e + spread_v + spread_v2:
        copy.wait_send()


ELSEWHERE = (7, 9, 12)
X_ALL = 14


def back(*args):
    def vm(dims, dtype=F32):
        return pltpu.VMEM(dims, dtype)

    held = [vm((2, 2 * TOK, D), BF) if k == X_ALL else vm(a.shape, a.dtype) for k, a in enumerate(args) if k > 1 and k not in ELSEWHERE]
    results = [((TOK, D), BF), ((TOK, D), F32), ((8, D), F32), ((8, KV), F32), ((8, KV), F32), ((8, D), F32), ((16, 128), F32)]
    results.append(((PAIR, BLOCK, D), BF))
    landing = [vm((4, TOK, D), BF), vm((2, TOK, D), BF), vm((TOK, D), BF)]
    return comm_call(
        back_kernel,
        "back",
        6,
        [shape(*result) for result in results],
        [ANY] * 23,
        [ANY] * 8,
        held
        + [
            vm((TOK, D)),
            vm((TOK, D), BF),
            vm((LENGTH, 128), BF),
            vm((EP, 2 * TOK, 128), BF),
            vm(((10 + 5 * (KEPT - 4)) * TOK, 2 * TOK), BF),
            vm((LENGTH, 128)),
            vm((LENGTH, 128)),
            vm((LENGTH, 256)),
            vm((16, 256)),
            vm((16, 256)),
            vm((EP, 16, 256)),
            vm((D, WB), BF),
            vm((128, WB)),
            vm((REP, 8, WB)),
            vm((256, D)),
            vm((D, 256), BF),
            vm((REP, 64, 256), BF),
            vm((64, 256)),
            vm((EP, 8, 256)),
            vm((8, D)),
            vm((EP, 8, D)),
            vm((8, D)),
            vm((REP, 8, 128)),
            vm((4, TOK, D), BF),
            vm((4, TOK, D), BF),
        ]
        + landing
        + [vm((2, TOK, D), BF)]
        + [vm((4, 128, WB), BF), vm((4, 128, WB), BF), vm((2, 128, WB), BF), vm((128, WB), BF)]
        + [DMA((10,))] * 6
        + [DMA((7,))] * 4
        + [DMA((15,))] * 4
        + [DMA((7,))] * 4
        + [DMA((15,))] * 2
        + [DMA((20,)), DMA((4,)), DMA((4,)), DMA((8,)), DMA((2,))]
        + [vm(*result) for k, result in enumerate(results) if k != 1]
        + grid_scratch() * 2
        + [DMA((12,))] * 4
        + [DMA((4,))] * 2,
        limit=64,
    )(*args)


def finish_kernel(
    xa_in, xb_in, out_in, ig_in, gq_in, gk_in, gv_in, go_in, pack_in,
    out_o, ig_o, gq_o, gk_o, gv_o, go_o, gr_o, va_o, vq_o, vk_o, vf_o, gate_o, up_o, down_o,
    x_s, gate_s, up_s, down_s, out_s, ig_s, gq_s, gk_s, gv_s, go_s, pack, gr_s, va_s, vq_s, vk_s, vf_s, sem,
):
    loads = [
        pltpu.make_async_copy(xa_in, x_s.at[pl.ds(0, PAIR)], sem.at[9]),
        pltpu.make_async_copy(xb_in, x_s.at[pl.ds(PAIR, PAIR)], sem.at[10]),
    ]
    for load in loads:
        load.start()
    stages = [out_s, ig_s, gq_s, gk_s, gv_s, go_s]
    fetch = [
        pltpu.make_async_copy(src, dst, sem.at[k])
        for k, (src, dst) in enumerate(zip([out_in, ig_in, gq_in, gk_in, gv_in, go_in], stages))
    ]
    copies = [
        pltpu.make_async_copy(src, dst, sem.at[k])
        for k, (src, dst) in enumerate(zip(stages, [out_o, ig_o, gq_o, gk_o, gv_o, go_o]))
    ]
    load_pack = pltpu.make_async_copy(pack_in, pack, sem.at[11])
    for copy in fetch + [load_pack]:
        copy.start()
    for load, copy in zip(fetch, copies):
        load.wait()
        copy.start()
    for load in loads:
        load.wait()
    gate_s[...] = x_s[:, :64, :FF].astype(F32)
    up_s[...] = x_s[:, :64, FF:].astype(F32)
    down_s[...] = x_s[:, 64:].astype(F32)
    load_pack.wait()
    gr_s[...] = pack[0:8, :EXPERTS]
    va_s[...] = pack[8:9, :8]
    vq_s[...] = pack[9:10, :8]
    vk_s[...] = pack[10:11, :4]
    vf_s[...] = pack[11:12, :8]
    pairs = [(gate_s, gate_o), (up_s, up_o), (down_s, down_o)]
    pairs += [(gr_s, gr_o), (va_s, va_o), (vq_s, vq_o), (vk_s, vk_o), (vf_s, vf_o)]
    for k, (src, dst) in enumerate(pairs):
        k = k if k < 5 else k + 1
        copies.append(pltpu.make_async_copy(src, dst, sem.at[6 + k]))
        copies[-1].start()
    for copy in copies:
        copy.wait()


def finish(xa, xb, out, ig, gq, gk, gv, go, pack):
    gate, down = shape((LOCAL, 64, FF)), shape((LOCAL, 32, D))
    return pl.pallas_call(
        finish_kernel,
        out_shape=[shape(a.shape, a.dtype) for a in (out, ig, gq, gk, gv, go)]
        + [shape((8, EXPERTS)), shape((1, 8)), shape((1, 8)), shape((1, 4)), shape((1, 8)), gate, gate, down],
        in_specs=[ANY] * 9,
        out_specs=[ANY] * 14,
        scratch_shapes=[
            pltpu.VMEM((LOCAL, BLOCK, D), BF),
            pltpu.VMEM(gate.shape, F32),
            pltpu.VMEM(gate.shape, F32),
            pltpu.VMEM(down.shape, F32),
        ]
        + [pltpu.VMEM(a.shape, a.dtype) for a in (out, ig, gq, gk, gv, go, pack)]
        + [pltpu.VMEM(dims, F32) for dims in ((8, EXPERTS), (1, 8), (1, 8), (1, 4), (1, 8))]
        + [
            DMA((16,)),
        ],
        compiler_params=pltpu.CompilerParams(vmem_limit_bytes=62 * MIB),
        name="finish",
    )(xa, xb, out, ig, gq, gk, gv, go, pack)


def body(
    tokens,
    segments,
    routes,
    w_query,
    w_key,
    w_value,
    w_out,
    w_router,
    gain_attn,
    gain_query,
    gain_key,
    gain_ffn,
    w_gate,
    w_up,
    w_down,
    out_grad,
):
    gains = [gain.reshape(1, -1) for gain in (gain_attn, gain_query, gain_key, gain_ffn)]
    cosine, sine = turn_tables()
    (
        x_all, g_all, lin, q, k, v, att, lse, hidden, moe_in, tables, attended, misc, router, whole_out, w_cols,
    ) = front(
        tokens, out_grad, w_query, w_key, w_value, w_out, w_router, *gains, segments, routes.T, cosine, sine
    )
    def over_copies(grads):
        grads = grads.reshape(PAIR, REP * BLOCK, D)
        return lax.psum_scatter(grads, "rep", scatter_dimension=1, tiled=True)

    m_all, tabs, y, z, gg_first, grads = experts_first(moe_in, tables, g_all, w_gate, w_up, w_down)
    sums_first = over_copies(grads)
    grad_moe, mixture, gg_last, grads = experts_last(m_all, tabs, y, z, g_all, w_gate, w_up, w_down)
    *rows, sums_last = back(
        grads.reshape(PAIR, 4, 4, BLOCK, D), mixture, grad_moe, gg_first, gg_last, tables, hidden, moe_in, out_grad, attended, misc, router, whole_out,
        w_cols, x_all, lin, q, k, v, att, lse, cosine, sine,
    )
    out, ig, gq, gk, gv, go, gr, va, vq, vk, vf, gate, up, down = finish(sums_first, sums_last, *rows)
    return out, ig, gq, gk, gv, go, gr, va.reshape(8), vq.reshape(8), vk.reshape(4), vf.reshape(8), gate, up, down


def solution(mesh):
    both = P(("rep", "ep"), None)
    line = P(("rep", "ep"))
    owner = P("ep", None, None)
    kept = P("ep", "rep", None)
    return jax.shard_map(
        body,
        mesh=mesh,
        in_specs=(both, P("rep", None)) + (both,) * 6 + (line,) * 4 + (owner,) * 3 + (both,),
        out_specs=(both,) * 7 + (line,) * 4 + (kept,) * 3,
        check_vma=False,
    )
```

```python
import functools

import jax
import jax.numpy as jnp
import numpy as np
from jax import lax
from jax.experimental import pallas as pl
from jax.experimental.pallas import tpu as pltpu
from jax.sharding import PartitionSpec as P

BF = jnp.bfloat16
F32 = jnp.float32
MESH = pl.DeviceIdType.MESH
ANY = pl.BlockSpec(memory_space=pl.ANY)
VM = pl.BlockSpec(memory_space=pltpu.VMEM)
DMA = pltpu.SemaphoreType.DMA
MIB = 1 << 20

HEADS = 16
KV_HEADS = 8
HEAD_DIM = 64
TOP = 8
WINDOW = 1024
EPSILON = 1e-06
ROPE_BASE = 10000.0
MASKED = -1e30
EP = 8
REP = 16
TOK = 256
LENGTH = 2048
D = 1024
KV = 512
FF = 512
EXPERTS = 32
LOCAL = 4
CAP = 88
NT = (((1,), (1,)), ((), ()))
TN = (((0,), (0,)), ((), ()))
HIGH = lax.Precision.HIGHEST


def dot(a, b):
    return jnp.dot(a, b, preferred_element_type=F32)


def dot_nt(a, b, precision=None):
    return lax.dot_general(a, b, NT, preferred_element_type=F32, precision=precision)


def dot_tn(a, b):
    return lax.dot_general(a, b, TN, preferred_element_type=F32)


def iota(shape, dim):
    return lax.broadcasted_iota(jnp.int32, shape, dim)


def ep_device(x, c):
    return {"ep": x * 2 + c}


def greet(devices, local_work=None):
    barrier = pltpu.get_barrier_semaphore()
    for device in devices:
        pl.semaphore_signal(barrier, inc=1, device_id=device, device_id_type=MESH)
    if local_work is not None:
        local_work()
    pl.semaphore_wait(barrier, len(devices))


def remote(src, dst, sems, i, device):
    return pltpu.make_async_remote_copy(
        src_ref=src,
        dst_ref=dst,
        send_sem=sems[0].at[i],
        recv_sem=sems[1].at[i],
        device_id=device,
        device_id_type=MESH,
    )


def place():
    e = lax.axis_index("ep")
    return e, e // 2, e % 2


def ep_others(e):
    return [(e + k) % EP for k in range(1, EP)]


def rep_others(r):
    return [(r + k) % REP for k in range(1, REP)]


class RingGather:
    SEMS = 10

    def __init__(self, x_ref, o_ref, sems, lsem):
        e, x, c = place()
        self.n = n = x_ref.shape[0]
        h = n // 2
        self.o_ref = o_ref
        right, left = ep_device((x + 1) % 4, c), ep_device((x + 3) % 4, c)
        peer = ep_device(x, 1 - c)
        b_left, b_right, b_opp = (((x + 3) % 4) * 2 + c, ((x + 1) % 4) * 2 + c, ((x + 2) % 4) * 2 + c)

        def rows(b, off=0, size=n):
            return o_ref.at[pl.ds(pl.multiple_of(b * n + off, 16), size)]

        low, high = x_ref.at[pl.ds(0, h)], x_ref.at[pl.ds(h, h)]
        self.first = [
            remote(low, rows(e, 0, h), sems, 0, right),
            remote(high, rows(e, h, h), sems, 2, left),
            remote(high, rows(e, h, h), sems, 1, right),
            remote(low, rows(e, 0, h), sems, 3, left),
            remote(x_ref, rows(e), sems, 4, peer),
        ]
        self.fwd_right = remote(rows(b_left, 0, h), rows(b_left, 0, h), sems, 5, right)
        self.fwd_left = remote(rows(b_right, h, h), rows(b_right, h, h), sems, 6, left)
        self.to_peer = [
            remote(rows(b_left), rows(b_left), sems, 7, peer),
            remote(rows(b_right), rows(b_right), sems, 8, peer),
            remote(rows(b_opp), rows(b_opp), sems, 9, peer),
        ]
        self.own = pltpu.make_async_copy(x_ref, rows(e), lsem)

    def start(self):
        for copy in self.first:
            copy.start()
        self.own.start()

    def forward_half(self):
        self.first[0].wait_recv()
        self.fwd_right.start()
        self.first[1].wait_recv()
        self.fwd_left.start()

    def forward_rest(self):
        self.first[2].wait_recv()
        self.to_peer[0].start()
        self.first[3].wait_recv()
        self.to_peer[1].start()

    def finish(self):
        self.fwd_right.wait_recv()
        self.fwd_left.wait_recv()
        self.to_peer[2].start()
        self.first[4].wait_recv()
        for copy in self.to_peer:
            copy.wait_recv()
        self.own.wait()
        for copy in self.first + [self.fwd_right, self.fwd_left] + self.to_peer:
            copy.wait_send()


class RingReduce:
    SEMS = 10
    STEP = 64

    def __init__(self, p_ref, n, pc, snd, rcv, hop, sems, lsems):
        e, x, c = place()
        self.n, self.h = n, n // 2
        h = n // 2
        self.pc, self.snd, self.rcv, self.hop = pc, snd, rcv, hop
        right, left = ep_device((x + 1) % 4, c), ep_device((x + 3) % 4, c)
        peer = ep_device(x, 1 - c)

        def rows(b):
            return p_ref.at[pl.ds(pl.multiple_of(b * n, 16), n)]

        chips = [(x + 2) % 4, (x + 1) % 4, (x + 3) % 4, x]
        self.swap = [remote(rows(b * 2 + 1 - c), pc.at[k], sems, k, peer) for k, b in enumerate(chips)]
        self.load = [
            pltpu.make_async_copy(rows(b * 2 + c), snd.at[k], lsems.at[k]) for k, b in enumerate(chips)
        ]
        low, high = pl.ds(0, h), pl.ds(h, h)
        self.opp = [
            remote(snd.at[0, low], hop.at[low], sems, 4, right),
            remote(snd.at[0, high], hop.at[high], sems, 5, left),
        ]
        self.near = [
            remote(snd.at[1, high], rcv.at[0, high], sems, 6, right),
            remote(snd.at[2, low], rcv.at[1, low], sems, 7, left),
        ]
        self.far = [
            remote(snd.at[1, low], rcv.at[0, low], sems, 8, right),
            remote(snd.at[2, high], rcv.at[1, high], sems, 9, left),
        ]

    def rows_loop(self, low, count, body):
        step = self.STEP

        def loop(i, carry):
            body(pl.ds(pl.multiple_of(low + i * step, 16), step))
            return carry

        lax.fori_loop(0, count // step, loop, 0)

    def merge(self, k):
        def body(s):
            self.snd[k, s] = (self.snd[k, s].astype(F32) + self.pc[k, s].astype(F32)).astype(BF)

        self.load[k].wait()
        self.swap[k].wait_recv()
        self.rows_loop(0, self.n, body)

    def merge_hop(self, k, low):
        def body(s):
            self.snd[k, s] = (self.snd[k, s].astype(F32) + self.hop[s].astype(F32)).astype(BF)

        self.rows_loop(low, self.h, body)

    def start(self):
        for copy in self.swap + self.load:
            copy.start()

    def push_opp(self):
        self.merge(0)
        for copy in self.opp:
            copy.start()

    def push_near(self):
        self.merge(1)
        self.near[0].start()
        self.merge(2)
        self.near[1].start()
        self.merge(3)

    def relay(self):
        self.opp[0].wait_recv()
        self.merge_hop(1, 0)
        self.far[0].start()
        self.opp[1].wait_recv()
        self.merge_hop(2, self.h)
        self.far[1].start()

    def finish(self, out_ref):
        for copy in self.near + self.far:
            copy.wait_recv()

        def body(s):
            out_ref[s] = self.snd[3, s].astype(F32) + (
                self.rcv[0, s].astype(F32) + self.rcv[1, s].astype(F32)
            )

        self.rows_loop(0, self.n, body)
        for copy in self.swap + self.opp + self.near + self.far:
            copy.wait_send()


class AxisReduce:
    def __init__(self, devices, snd, hop, rcv, sems, base):
        right, left = devices
        self.snd, self.hop, self.rcv = snd, hop, rcv
        self.opp = [
            remote(snd.at[0, 0], hop.at[0], sems, base, right),
            remote(snd.at[0, 1], hop.at[1], sems, base + 1, left),
        ]
        self.near = [
            remote(snd.at[2, 1], rcv.at[0, 1], sems, base + 2, right),
            remote(snd.at[1, 0], rcv.at[1, 0], sems, base + 3, left),
        ]
        self.far = [
            remote(snd.at[2, 0], rcv.at[0, 0], sems, base + 4, right),
            remote(snd.at[1, 1], rcv.at[1, 1], sems, base + 5, left),
        ]

    def push(self):
        for copy in self.opp + self.near:
            copy.start()

    def relay(self):
        for k, (slot, half) in enumerate(((2, 0), (1, 1))):
            self.opp[k].wait_recv()
            self.snd[slot, half] = (self.snd[slot, half].astype(F32) + self.hop[half].astype(F32)).astype(BF)
            self.far[k].start()

    def arrive(self):
        for copy in self.near + self.far:
            copy.wait_recv()

    def total(self, *index):
        return self.snd[(3,) + index].astype(F32) + (
            self.rcv[(0,) + index].astype(F32) + self.rcv[(1,) + index].astype(F32)
        )

    def leave(self):
        for copy in self.opp + self.near + self.far:
            copy.wait_send()


class GridReduce:
    def __init__(self, along_z, src, cols, snd, hop, rcv, snd2, hop2, rcv2, sems, lsems):
        r = lax.axis_index("rep")
        z, y = r // 4, r % 4
        along = (lambda k: {"rep": (z + k) % 4 * 4 + y}, lambda k: {"rep": z * 4 + (y + k) % 4})
        one, two = along if along_z else along[::-1]
        here, self.there = (z, y) if along_z else (y, z)
        offsets = (2, 3, 1, 0)
        cut = pl.ds(cols, FF)
        self.load = []
        for k, off in enumerate(offsets):
            b = (here + off) % 4
            block = src.at[:, b, :, :, cut] if along_z else src.at[:, :, b, :, cut]
            self.load.append(pltpu.make_async_copy(block, snd.at[k], lsems.at[k]))
        self.offsets, self.snd2 = offsets, snd2
        self.stage = AxisReduce((one(1), one(3)), snd, hop, rcv, sems, 0)
        self.last = AxisReduce((two(1), two(3)), snd2, hop2, rcv2, sems, 6)

    def push(self):
        for copy in self.load:
            copy.wait()
        self.stage.push()

    def turn(self):
        self.stage.arrive()
        for k, off in enumerate(self.offsets):
            b = (self.there + off) % 4
            for n in range(PAIR):
                self.snd2[k, n] = self.stage.total(n, b).astype(BF)
        self.last.push()

    def finish(self, out_ref, cols):
        self.last.arrive()
        for n in range(PAIR):
            out_ref[n, :, cols : cols + FF] = self.last.total(n).astype(BF)
        self.stage.leave()
        self.last.leave()


def grid_scratch():
    blocks = [(4, PAIR, 4, BLOCK, FF), (PAIR, 4, BLOCK, FF), (2, PAIR, 4, BLOCK, FF)]
    blocks += [(4, PAIR, BLOCK, FF), (PAIR, BLOCK, FF), (2, PAIR, BLOCK, FF)]
    return [pltpu.VMEM(dims, BF) for dims in blocks]


def comm_call(kernel, name, collective_id, out_shape, in_specs, out_specs, scratch, limit=48):
    return pl.pallas_call(
        kernel,
        out_shape=out_shape,
        in_specs=in_specs,
        out_specs=out_specs,
        scratch_shapes=scratch,
        compiler_params=pltpu.CompilerParams(
            collective_id=collective_id, has_side_effects=True, vmem_limit_bytes=limit * MIB
        ),
        name=name,
    )


def shape(dims, dtype=F32):
    return jax.ShapeDtypeStruct(dims, dtype)


WB = D + 128


def columns(*rows):
    pad = jnp.zeros((128 - len(rows), rows[0].shape[1]), F32)
    turned = jnp.transpose(jnp.concatenate(list(rows) + [pad], axis=0))
    return [turned[:, k : k + 1] for k in range(len(rows))]


def row_sums(values, bounds):
    width = values.shape[1]
    high = values.astype(BF)
    low = (values - high.astype(F32)).astype(BF)
    lane, row = iota((8, width), 1), iota((8, width), 0)
    chosen = jnp.zeros((8, width), F32)
    for k, (first, last) in enumerate(bounds):
        chosen = jnp.where((row == k) & (lane >= first) & (lane < last), 1.0, chosen)
    chosen = chosen.astype(BF)
    return dot_nt(jnp.concatenate([chosen, chosen], axis=1), jnp.concatenate([high, low], axis=1))


PARTS = ((0, 128), (128, 192))


def turn_tables():
    half = HEAD_DIM // 2
    freq = np.float32(ROPE_BASE) ** (-(np.arange(half, dtype=np.float32) * np.float32(2.0) / np.float32(HEAD_DIM)))
    angles = np.arange(LENGTH, dtype=np.float32)[:, None] * freq.astype(np.float32)[None, :]
    c, s = np.cos(angles), np.sin(angles)
    cosine = np.concatenate([c, c, c, c], axis=1)
    sine = np.concatenate([-s, s, -s, s], axis=1)
    return cosine.astype(np.float32), sine.astype(np.float32)


def turn(u, cosine, sine):
    early = iota(u.shape, 1) % HEAD_DIM < HEAD_DIM // 2
    partner = jnp.where(early, pltpu.roll(u, 96, 1), pltpu.roll(u, 32, 1))
    return u * cosine + partner * sine


def block_rows(b):
    return pl.ds(pl.multiple_of(b * TOK, TOK), TOK)


def stack_heads(values):
    first = iota(values.shape, 1) < HEAD_DIM
    return jnp.concatenate([jnp.where(first, values, 0.0), jnp.where(first, 0.0, values)], axis=0)


def merge_heads(values):
    first = iota((TOK, 128), 1) < HEAD_DIM
    return jnp.where(first, values[:TOK], values[TOK:])


def front_kernel(
    tok, cot, wq, wk, wv, wo_in, router_in, ga_in, gq_in, gk_in, gf_in, seg, rts_in, cos_in, sin_in,
    x_all, g_all, lin_h, q_h, k_h, v_h, a_h, lse_h, hid_h, m_h, tab_h, att_h, misc_h, rout_h, whole_h, wcol_h,
    lin, q_o, k_o, v_o, a_o, lse_o, hid_o, m_o, tab_o, att_o, misc, rout_o, whole, wcol, hsem,
    x_s, cot_s, tiny, tiny_b, smalls, wsl, wo_f, wo_r, wg, w32, gains_s, cos_ref, sin_ref, sums, held,
    s_tok, r_tok, s_cot, r_cot, s_w, r_w, s_o, r_o, s_st, r_st, s_t, r_t, s_a, r_a, lsem,
):
    r = lax.axis_index("rep")
    e, x, c = place()
    others = ep_others(e)
    copies = rep_others(r)
    first = iota((TOK, 128), 1) < HEAD_DIM
    gain_a, gain_f, gain = misc.at[0:1], misc.at[1:2], misc.at[2:3, 0:256]
    lo, st = misc.at[8:16, 0:256], misc.at[16:32, 0:256]
    leaving = []

    def leave(*pairs):
        for src, dst in pairs:
            leaving.append(pltpu.make_async_copy(src, dst, hsem.at[len(leaving)]))
            leaving[-1].start()

    tables = [
        pltpu.make_async_copy(cos_in, cos_ref, lsem.at[2]),
        pltpu.make_async_copy(sin_in, sin_ref, lsem.at[3]),
        pltpu.make_async_copy(cot, cot_s, lsem.at[5]),
    ]

    def prepare_tiles():
        misc[...] = jnp.zeros((32, D), F32)

        tiny[...] = jnp.zeros((16, 128), F32)
        tiny[0:8, 0:EXPERTS] = router_in[...].astype(F32)
        for lane, ref in ((0, ga_in), (8, gq_in), (16, gk_in), (20, gf_in)):
            tiny[8:9, lane : lane + ref.shape[1]] = ref[...].astype(F32)
        tiny_b[...] = tiny[...].astype(BF)
        low_lanes = iota((8, 128), 1) < HEAD_DIM
        for d in range(EP):
            k_t = wk[:, (d // 2) * 128 : (d // 2 + 1) * 128].astype(F32)
            v_t = wv[:, (d // 2) * 128 : (d // 2 + 1) * 128].astype(F32)
            if d % 2:
                k_t = pltpu.roll(k_t, HEAD_DIM, 1)
            else:
                v_t = pltpu.roll(v_t, HEAD_DIM, 1)
            q_t = wq[:, d * 128 : (d + 1) * 128].astype(F32)
            wsl[d] = jnp.concatenate([q_t, jnp.where(low_lanes, k_t, v_t)], axis=0).astype(BF)
        wo_f[...] = wo_in[...].astype(F32)
        for copy in tables:
            copy.start()

    greet([{"ep": d} for d in others] + [{"rep": d} for d in copies], prepare_tiles)
    half_cols = pl.ds(pl.multiple_of(c * 512, 512), 512)
    other_cols = pl.ds(pl.multiple_of((1 - c) * 512, 512), 512)
    peer = ep_device(x, 1 - c)

    def whole_rows(start, size):
        return whole.at[pl.ds(pl.multiple_of(start, 16), size), half_cols]

    pairing = remote(wo_f.at[:, other_cols], wo_r, (s_o, r_o), 19, peer)
    mine = whole_rows(r * 64 + x * 16, 16)
    stage_o = [remote(mine, mine, (s_o, r_o), k, ep_device((x + 1 + k) % 4, c)) for k in range(3)]
    mine = whole_rows(r * 64, 64)
    spread_o = [remote(mine, mine, (s_o, r_o), 3 + k, {"rep": d}) for k, d in enumerate(copies)]
    mine = whole_rows(0, D)
    other_half = remote(mine, mine, (s_o, r_o), 18, peer)

    def cols_of(b):
        return wg.at[r, pl.ds(pl.multiple_of(b * 16, 16), 16)]

    stage_w = [remote(wsl.at[d], cols_of(e), (s_w, r_w), k, {"ep": d}) for k, d in enumerate(others)]
    stage_t = [remote(tiny_b, smalls.at[e], (s_t, r_t), k, {"ep": d}) for k, d in enumerate(others)]
    spread_w = [remote(wg.at[r], wg.at[r], (s_w, r_w), 7 + k, {"rep": d}) for k, d in enumerate(copies)]
    tokens = RingGather(tok, x_s, (s_tok, r_tok), lsem.at[0])
    grads = RingGather(cot_s, g_all, (s_cot, r_cot), lsem.at[1])
    for copy in stage_w + stage_t + [pairing]:
        copy.start()
    tokens.start()
    cols_of(e)[...] = wsl[e]
    smalls[e] = tiny_b[...]
    for copy in stage_w + stage_t:
        copy.wait_recv()
    router_tiles = [
        sum(pltpu.roll(smalls[4 * a + b][:8].astype(F32), 32 * b, 1) if b else smalls[4 * a][:8].astype(F32) for b in range(4))
        for a in range(2)
    ]
    gain_rows = [smalls[d][8:9].astype(F32) for d in range(EP)]
    wg[r, 128:160] = jnp.concatenate(router_tiles + gain_rows + [jnp.zeros((8, 128), F32)], axis=0).astype(BF)
    for copy in spread_w:
        copy.start()
    pairing.wait_recv()
    own_half, peer_half = wo_f[:, half_cols], wo_r[...]
    upper, lower = jnp.where(c == 0, own_half, peer_half), jnp.where(c == 0, peer_half, own_half)
    whole[pl.ds(pl.multiple_of(r * 64 + x * 16, 16), 16), half_cols] = jnp.concatenate([upper, lower], axis=0).astype(BF)
    for copy in stage_o:
        copy.start()
    tokens.forward_half()
    tables[2].wait()
    grads.start()
    tokens.forward_rest()

    routed = rts_in[...]
    hit = jnp.zeros((EXPERTS, TOK), F32)
    for k in range(TOP):
        hit = jnp.where(iota((EXPERTS, TOK), 0) == routed[k : k + 1], 1.0, hit)
    before = jnp.where(iota((TOK, TOK), 0) < iota((TOK, TOK), 1), 1.0, 0.0).astype(BF)
    slots = jnp.where(hit > 0.0, dot(hit.astype(BF), before), -1.0)
    segs = jnp.concatenate([seg[:, b * TOK : (b + 1) * TOK] for b in range(EP)], axis=0)
    opening = jnp.zeros((EP, TOK), F32)
    for value in range(2):
        count = jnp.sum(jnp.where(segs == value, 1.0, 0.0), axis=1, keepdims=True)
        opening = opening + jnp.where(segs > value, jnp.sum(count, axis=0, keepdims=True), 0.0)
    places = (iota((EP, TOK), 0) * TOK + iota((EP, TOK), 1)).astype(F32)
    lo[...] = jnp.maximum(opening, places - (WINDOW - 1))

    for copy in spread_w:
        copy.wait_recv()
    for copy in stage_o:
        copy.wait_recv()
    for copy in spread_o:
        copy.start()

    def unpack(b, carry):
        for d in range(EP):
            tile = wg[b, d * 16 : d * 16 + 16].astype(F32)
            rows = pl.ds(pl.multiple_of(b * 64 + d * 8, 8), 8)
            w32[rows, 0:128] = tile[0:8]
            w32[rows, 128:256] = tile[8:16]
        extra = wg[b, 128:160].astype(F32)
        for d in range(EP):
            tile = extra[d // 4 * 8 : d // 4 * 8 + 8]
            if d % 4:
                tile = pltpu.roll(tile, 128 - 32 * (d % 4), 1)
            w32[pl.ds(pl.multiple_of(b * 64 + d * 8, 8), 8), 256:384] = tile
        gains_s[pl.ds(pl.multiple_of(b * 8, 8), 8)] = extra[16:24]
        return carry

    lax.fori_loop(0, REP, unpack, 0)
    wcol[...] = w32[:, :256].astype(BF)
    rout_o[...] = jnp.transpose(w32[:, 256:384])[:EXPERTS].astype(BF)
    packed = gains_s[...].astype(BF)

    def spread_gain(width, group, base, shift):
        lane = base + iota((128, width), 1) % group
        picked = dot(packed, jnp.where(iota((128, width), 0) == lane, 1.0, 0.0).astype(BF))
        mine = iota((128, width), 0) == shift + iota((128, width), 1) // group
        return jnp.sum(jnp.where(mine, picked, 0.0), axis=0, keepdims=True)

    gain_a[...] = spread_gain(D, 8, 0, 0)
    gain_f[...] = spread_gain(D, 8, 20, 0)
    key_part = spread_gain(128, 4, 16, e * 16)
    gain[:, :128] = spread_gain(128, 8, 8, e * 16)
    gain[:, 128:] = jnp.where(iota((1, 128), 1) < HEAD_DIM, key_part, 1.0)

    leave((wcol, wcol_h), (rout_o, rout_h))
    tokens.first[4].wait_recv()
    tokens.own.wait()

    def project(k, carry):
        @pl.when(k == 2)
        def _():
            tokens.fwd_right.wait_recv()
            tokens.fwd_left.wait_recv()
            tokens.to_peer[2].start()
            tokens.to_peer[1].wait_recv()

        @pl.when(k == 4)
        def _():
            tokens.to_peer[0].wait_recv()

        @pl.when(k == 6)
        def _():
            tokens.to_peer[2].wait_recv()

        g = k // 2
        b = (2 * (x + g + g // 2 - 2 * (g // 3)) + k % 2) % EP
        rows = block_rows(b)
        values = x_s[rows].astype(F32)
        r1 = lax.rsqrt(jnp.mean(values * values, axis=1, keepdims=True) + EPSILON)
        normed = (values * r1 * gain_a[...]).astype(BF)
        out = dot(normed, wcol[...])
        lin[rows] = out
        both = row_sums(out * out, PARTS)
        sums[pl.ds(2 * b, 1)] = both[0:1]
        sums[pl.ds(2 * b + 1, 1)] = both[1:2]
        return carry

    lax.fori_loop(0, EP, project, 0)
    stats = [remote(sums, held.at[e], (s_st, r_st), k, {"ep": d}) for k, d in enumerate(others)]
    for copy in stats:
        copy.start()
    held[e] = sums[...]
    keep = pltpu.make_async_copy(x_s, x_all, lsem.at[4])
    keep.start()
    for copy in tables[:2]:
        copy.wait()
    for copy in stats:
        copy.wait_recv()
    total = held[0]
    for k in range(1, EP):
        total = total + held[k]
    st[...] = total
    grads.forward_half()
    leave((lin, lin_h), (misc, misc_h))

    def prepare(b, carry):
        rows = block_rows(b)
        cq, ck = columns(
            lax.rsqrt(st[pl.ds(2 * b, 1)] * (1.0 / D) + EPSILON),
            lax.rsqrt(st[pl.ds(2 * b + 1, 1)] * (1.0 / KV) + EPSILON),
        )
        cosine, sine = cos_ref[rows], sin_ref[rows]
        q_o[rows] = turn(lin[rows, :128] * cq * gain[:, :128], cosine, sine).astype(BF)
        kv = lin[rows, 128:]
        kv = jnp.where(first, turn(kv * ck * gain[:, 128:], cosine, sine), kv)
        other = pltpu.roll(kv, HEAD_DIM, 1)
        k_o[rows] = jnp.where(first, kv, other).astype(BF)
        v_o[rows] = jnp.where(first, other, kv).astype(BF)
        return carry

    lax.fori_loop(0, EP, prepare, 0, unroll=2)
    leave((q_o, q_h), (k_o, k_h), (v_o, v_h))

    def heads(i, source):
        cols = pl.ds(pl.multiple_of(source * 128, 128), 128)
        return pltpu.make_async_remote_copy(
            src_ref=a_o.at[block_rows(i)],
            dst_ref=att_o.at[:, cols],
            send_sem=s_a.at[i],
            recv_sem=r_a.at[source],
            device_id={"ep": i},
            device_id_type=MESH,
        )

    def attend_block(i, n):
        rows = block_rows(i)
        past = (n - 1) * TOK
        q2 = stack_heads(q_o[rows].astype(F32) * HEAD_DIM ** (-0.5)).astype(BF)
        (lo_col,) = columns(lo[pl.ds(i, 1)])
        low = jnp.concatenate([lo_col, lo_col], axis=0)
        own_key = (iota((2 * TOK, TOK), 1) + i * TOK).astype(F32)
        query = (iota((2 * TOK, TOK), 0) % TOK + i * TOK).astype(F32)
        s_own = jnp.where((own_key >= low) & (own_key <= query), dot_nt(q2, k_o[rows]), MASKED)
        m = jnp.max(s_own, axis=1, keepdims=True)
        if past:
            early = pl.ds(pl.multiple_of((i - n + 1) * TOK, TOK), past)
            key = (iota((2 * TOK, past), 1) + (i - n + 1) * TOK).astype(F32)
            s = jnp.where(key >= low, dot_nt(q2, k_o[early]), MASKED)
            m = jnp.maximum(m, jnp.max(s, axis=1, keepdims=True))
        p_own = jnp.exp(s_own - m)
        total = jnp.sum(p_own, axis=1, keepdims=True)
        out = dot(p_own.astype(BF), v_o[rows])
        if past:
            p = jnp.exp(s - m)
            total = total + jnp.sum(p, axis=1, keepdims=True)
            out = out + dot(p.astype(BF), v_o[early])
        a_o[rows] = merge_heads(out / total).astype(BF)
        lse = jnp.broadcast_to(m + jnp.log(total), (2 * TOK, 128))
        lse_o[i] = jnp.transpose(lse)[:8]

        @pl.when(i != e)
        def _():
            heads(i, e).start()

        @pl.when(i == e)
        def _():
            att_o[:, pl.ds(pl.multiple_of(e * 128, 128), 128)] = a_o[rows]

    def later(i, carry):
        attend_block(i, 5)

        @pl.when(i == 5)
        def _():
            grads.fwd_right.wait_recv()
            grads.fwd_left.wait_recv()
            grads.to_peer[2].start()
            other_half.wait_recv()
            whole_out.start()

        return carry

    whole_out = pltpu.make_async_copy(whole, whole_h, hsem.at[len(leaving)])
    leaving.append(whole_out)

    for i in range(4):
        attend_block(i, i + 1)
    grads.forward_rest()
    for copy in spread_o:
        copy.wait_recv()
    other_half.start()
    lax.fori_loop(4, EP, later, 0)

    leave((a_o, a_h), (lse_o, lse_h))
    for d in others:
        heads(d, d).wait_recv()
    leave((att_o, att_h))

    hidden = x_s[block_rows(e)].astype(F32) + dot(att_o[...], whole[...])
    hid_o[...] = hidden
    r2 = lax.rsqrt(jnp.mean(hidden * hidden, axis=1, keepdims=True) + EPSILON)
    moe_in = (hidden * r2 * gain_f[...]).astype(BF)
    m_o[...] = moe_in
    leave((hid_o, hid_h), (m_o, m_h))
    logits = dot_nt(rout_o[...], moe_in)
    chosen = hit > 0.0
    logits = jnp.where(chosen, logits, MASKED)
    raised = jnp.where(chosen, jnp.exp(logits - jnp.max(logits, axis=0, keepdims=True)), 0.0)
    gates = raised / jnp.sum(raised, axis=0, keepdims=True)
    for d in range(EP):
        part = slice(d * LOCAL, (d + 1) * LOCAL)
        tab_o[d] = jnp.concatenate([slots[part], gates[part]], axis=0)
    leave((tab_o, tab_h))

    grads.first[4].wait_recv()
    for copy in grads.to_peer:
        copy.wait_recv()
    grads.own.wait()
    keep.wait()
    for copy in leaving:
        copy.wait()
    for d in others:
        heads(d, d).wait_send()
    for ring in (tokens, grads):
        for copy in ring.first + [ring.fwd_right, ring.fwd_left] + ring.to_peer:
            copy.wait_send()
    for copy in stage_w + stage_t + stage_o + spread_w + spread_o + stats + [other_half, pairing]:
        copy.wait_send()


def front(*args):
    results = [
        shape((LENGTH, D), BF),
        shape((LENGTH, D), BF),
        shape((LENGTH, 256)),
        shape((LENGTH, 128), BF),
        shape((LENGTH, 128), BF),
        shape((LENGTH, 128), BF),
        shape((LENGTH, 128), BF),
        shape((EP, 8, 2 * TOK)),
        shape((TOK, D)),
        shape((TOK, D), BF),
        shape((EP, 2 * LOCAL, TOK)),
        shape((TOK, D), BF),
        shape((32, D)),
        shape((EXPERTS, D), BF),
        shape((D, D), BF),
        shape((D, 256), BF),
    ]
    return comm_call(
        front_kernel,
        "front",
        1,
        results,
        [ANY, ANY] + [VM] * 11 + [ANY, ANY],
        [ANY] * len(results),
        [pltpu.VMEM(a.shape, a.dtype) for a in results[2:]]
        + [
            DMA((14,)),
            pltpu.VMEM((LENGTH, D), BF),
            pltpu.VMEM((TOK, D), BF),
            pltpu.VMEM((16, 128), F32),
            pltpu.VMEM((16, 128), BF),
            pltpu.VMEM((EP, 16, 128), BF),
            pltpu.VMEM((EP, 16, 128), BF),
            pltpu.VMEM((8, D), F32),
            pltpu.VMEM((8, 512), F32),
            pltpu.VMEM((REP, 160, 128), BF),
            pltpu.VMEM((D, 384), F32),
            pltpu.VMEM((128, 128), F32),
            pltpu.VMEM((LENGTH, 128), F32),
            pltpu.VMEM((LENGTH, 128), F32),
            pltpu.VMEM((16, 256), F32),
            pltpu.VMEM((EP, 16, 256), F32),
        ]
        + [DMA((10,))] * 4
        + [DMA((23,))] * 4
        + [DMA((7,))] * 4
        + [DMA((8,))] * 2
        + [DMA((6,))],
        limit=60,
    )(*args)


class ChipReduce:
    SEMS = 10
    STEP = 64

    def __init__(self, n, swo, snd, pc, rcv, hop, sems):
        e, x, c = place()
        self.n, self.h = n, n // 2
        h = n // 2
        self.snd, self.pc, self.rcv, self.hop = snd, pc, rcv, hop
        right, left = ep_device((x + 1) % 4, c), ep_device((x + 3) % 4, c)
        peer = ep_device(x, 1 - c)
        self.swap = lambda k: remote(swo.at[k], pc.at[k], sems, k, peer)
        low, high = pl.ds(0, h), pl.ds(h, h)
        self.opp = [
            remote(snd.at[0, low], hop.at[low], sems, 4, right),
            remote(snd.at[0, high], hop.at[high], sems, 5, left),
        ]
        self.near = [
            remote(snd.at[2, high], rcv.at[0, high], sems, 6, right),
            remote(snd.at[1, low], rcv.at[1, low], sems, 7, left),
        ]
        self.far = [
            remote(snd.at[2, low], rcv.at[0, low], sems, 8, right),
            remote(snd.at[1, high], rcv.at[1, high], sems, 9, left),
        ]

    def rows_loop(self, low, count, body):
        step = self.STEP

        def loop(i, carry):
            body(pl.ds(pl.multiple_of(low + i * step, 16), step))
            return carry

        lax.fori_loop(0, count // step, loop, 0)

    def merge(self, k):
        def body(s):
            self.snd[k, s] = (self.snd[k, s].astype(F32) + self.pc[k, s].astype(F32)).astype(BF)

        self.swap(k).wait_recv()
        self.rows_loop(0, self.n, body)

    def merge_hop(self, k, low):
        def body(s):
            self.snd[k, s] = (self.snd[k, s].astype(F32) + self.hop[s].astype(F32)).astype(BF)

        self.rows_loop(low, self.h, body)

    def send_opp(self):
        self.merge(0)
        for copy in self.opp:
            copy.start()

    def near_right(self):
        self.merge(2)
        self.near[0].start()

    def near_left(self):
        self.merge(1)
        self.near[1].start()

    def send_near(self):
        self.near_right()
        self.near_left()

    def far_right(self):
        self.opp[0].wait_recv()
        self.merge_hop(2, 0)
        self.far[0].start()

    def far_left(self):
        self.opp[1].wait_recv()
        self.merge_hop(1, self.h)
        self.far[1].start()

    def send_far(self):
        self.far_right()
        self.far_left()

    def finish(self, out_ref):
        for copy in self.near + self.far:
            copy.wait_recv()

        def body(s):
            out_ref[s] = self.snd[3, s].astype(F32) + (
                self.rcv[0, s].astype(F32) + self.rcv[1, s].astype(F32)
            )

        self.rows_loop(0, self.n, body)
        for copy in [self.swap(k) for k in range(4)] + self.opp + self.near + self.far:
            copy.wait_send()


PAIR = 2
ROWS = EP * CAP
CHIP = 2 * CAP
BLOCK = 96


def chip_rows(q):
    return pl.ds(pl.multiple_of(q * CHIP, 16), CHIP)


def chip_tokens(q):
    return pl.ds(pl.multiple_of(q * 2 * TOK, 2 * TOK), 2 * TOK)


def expert_hits(tab, e, n, q):
    row = slice(n, n + 1)
    second = tab[2 * q + 1, row]
    slots = jnp.concatenate([tab[2 * q, row], jnp.where(second >= 0.0, second + CAP, -1.0)], axis=1)
    return iota((CHIP, 2 * TOK), 0).astype(F32) == slots


def one_hot(hit):
    return jnp.where(hit, 1.0, 0.0).astype(BF)


def expert_chip(q, e, start, tab, m_ref, g_ref, wgu, wd, a_s, act_s, gp_s, dgu_s, y_s, z_s, ggt, between=None):
    hits = [expert_hits(tab, e, start + n, q) for n in range(PAIR)]
    chosen = jnp.concatenate([one_hot(hit) for hit in hits], axis=0)
    rows = chip_rows(q)
    a_both = dot(chosen, m_ref[chip_tokens(q)]).astype(BF)
    c_both = dot(chosen, g_ref[chip_tokens(q)]).astype(BF)
    for n in range(PAIR):
        part = slice(n * CHIP, (n + 1) * CHIP)
        row = slice(LOCAL + start + n, LOCAL + start + n + 1)
        gates = jnp.concatenate([tab[2 * q, row], tab[2 * q + 1, row]], axis=1)
        weight = jnp.sum(jnp.where(hits[n], gates, 0.0), axis=1, keepdims=True)
        a, cot = a_both[part], c_both[part]
        lin = dot(a, wgu[n])
        back = dot_nt(cot, wd[n])
        gate_lin, up_lin = lin[:, :FF], lin[:, FF:]
        sig = jax.nn.sigmoid(gate_lin)
        silu = gate_lin * sig
        act = silu * up_lin
        act_low = act.astype(BF)
        produced = dot(act_low, wd[n]).astype(BF).astype(F32)
        gg = jnp.sum(act * back, axis=1, keepdims=True)
        back = back * weight
        dgate = (back * up_lin * sig * (1.0 + gate_lin * (1.0 - sig))).astype(BF)
        dup = (back * silu).astype(BF)
        dgu = jnp.concatenate([dgate, dup], axis=1)
        a_s[n, rows] = a
        act_s[n, rows] = act_low
        gp_s[n, rows] = (weight * cot.astype(F32)).astype(BF)
        dgu_s[n, rows] = dgu
        y_s[n, rows] = (weight * produced).astype(BF)
        z_s[n, rows] = dot_nt(dgu, wgu[n]).astype(BF)
        gg_row = jnp.sum(jnp.where(hits[n], gg, 0.0), axis=0, keepdims=True)
        ggt[2 * q, n : n + 1] = gg_row[:, :TOK]
        ggt[2 * q + 1, n : n + 1] = gg_row[:, TOK:]
        if n == 0 and between is not None:
            between()


def expert_grads(n, a_s, act_s, gp_s, dgu_s, eg, eg_o, sems):
    copies = []
    for k, (first, size) in enumerate(((0, 64), (64, 32))):
        left, right = ((a_s, dgu_s), (act_s, gp_s))[k]
        eg[n, :, first : first + size] = dot_tn(left[n], right[n]).astype(BF).reshape(REP, size, D)
        some = pl.ds(first, size)
        copies.append(pltpu.make_async_copy(eg.at[n, :, some], eg_o.at[n, :, some], sems.at[2 * n + k]))
        copies[-1].start()
    return copies


def load_weights(start, wg_in, wu_in, wd_in, wgu, wd, sems):
    some = pl.ds(start, PAIR)
    return [
        pltpu.make_async_copy(wg_in.at[some], wgu.at[:, :, pl.ds(0, FF)], sems.at[0]),
        pltpu.make_async_copy(wu_in.at[some], wgu.at[:, :, pl.ds(FF, FF)], sems.at[1]),
        pltpu.make_async_copy(wd_in.at[some], wd, sems.at[2]),
    ]


def send_gates(ggt, gg_o, e, sems, lsem):
    copies = [remote(ggt.at[d], gg_o.at[e], sems, k, {"ep": d}) for k, d in enumerate(ep_others(e))]
    return copies, pltpu.make_async_copy(ggt.at[e], gg_o.at[e], lsem)


def experts_first_kernel(
    m_in, t_in, g_in, wg_in, wu_in, wd_in, m_o, tab_o, y_o, z_o, gg_o, eg_o,
    m_ref, tab, g_ref, wgu, wd, a_s, act_s, gp_s, dgu_s, y_s, z_s, ggt, eg,
    s_m, r_m, s_t, r_t, s_g, r_g, lsem, wsem, gsem, esem, ksem,
):
    e, x, c = place()
    others = ep_others(e)
    ring = RingGather(m_in, m_ref, (s_m, r_m), lsem.at[0])
    tables = [remote(t_in.at[d], tab.at[e], (s_t, r_t), k, {"ep": d}) for k, d in enumerate(others)]
    own = pltpu.make_async_copy(t_in.at[e], tab.at[e], lsem.at[1])
    loads = load_weights(0, wg_in, wu_in, wd_in, wgu, wd, wsem)
    cots = [
        pltpu.make_async_copy(g_in.at[chip_tokens(q)], g_ref.at[chip_tokens(q)], gsem.at[k])
        for k, q in enumerate([x, (x + 1) % 4, (x + 3) % 4, (x + 2) % 4])
    ]

    def fetch():
        for copy in [own] + loads + cots:
            copy.start()
        ggt[...] = jnp.zeros((EP, 8, TOK), F32)

    greet([{"ep": d} for d in others], fetch)
    for copy in tables:
        copy.start()
    ring.start()

    def keep(k, q):
        rows = chip_rows(q)
        return [
            pltpu.make_async_copy(m_ref.at[chip_tokens(q)], m_o.at[chip_tokens(q)], ksem.at[0, k]),
            pltpu.make_async_copy(y_s.at[:, rows], y_o.at[:, rows], ksem.at[1, k]),
            pltpu.make_async_copy(z_s.at[:, rows], z_o.at[:, rows], ksem.at[2, k]),
        ]

    def chips(k, carry):
        @pl.when(k == 0)
        def _():
            ring.first[0].wait_recv()
            ring.fwd_right.start()
            ring.first[1].wait_recv()
            ring.fwd_left.start()
            ring.first[4].wait_recv()
            ring.own.wait()
            own.wait()
            for copy in tables:
                copy.wait_recv()
            for copy in loads:
                copy.wait()
            cots[0].wait()

        @pl.when(k == 1)
        def _():
            ring.first[3].wait_recv()
            ring.to_peer[1].start()
            ring.first[2].wait_recv()
            ring.to_peer[0].start()
            ring.to_peer[1].wait_recv()
            cots[1].wait()

        @pl.when(k == 2)
        def _():
            ring.fwd_right.wait_recv()
            ring.fwd_left.wait_recv()
            ring.to_peer[2].start()
            ring.to_peer[0].wait_recv()
            cots[2].wait()

        @pl.when(k == 3)
        def _():
            ring.to_peer[2].wait_recv()
            cots[3].wait()

        q = (x + k + k // 2 - 2 * (k // 3)) % 4
        expert_chip(q, e, 0, tab, m_ref, g_ref, wgu, wd, a_s, act_s, gp_s, dgu_s, y_s, z_s, ggt)
        for copy in keep(k, q):
            copy.start()
        return carry

    lax.fori_loop(0, 4, chips, 0)
    gates, own_gates = send_gates(ggt, gg_o, e, (s_g, r_g), lsem.at[3])
    states = [pltpu.make_async_copy(tab, tab_o, lsem.at[2])]
    for copy in gates + [own_gates] + states:
        copy.start()
    for n in range(PAIR):
        states += expert_grads(n, a_s, act_s, gp_s, dgu_s, eg, eg_o, esem)
    for k, q in enumerate([x, (x + 1) % 4, (x + 3) % 4, (x + 2) % 4]):
        states += keep(k, q)
    for copy in states + [own_gates]:
        copy.wait()
    for copy in gates:
        copy.wait_recv()
    for copy in ring.first + [ring.fwd_right, ring.fwd_left] + ring.to_peer + tables + gates:
        copy.wait_send()


def pair_scratch():
    return [
        pltpu.VMEM((LENGTH, D), BF),
        pltpu.VMEM((EP, 2 * LOCAL, TOK), F32),
        pltpu.VMEM((LENGTH, D), BF),
        pltpu.VMEM((PAIR, D, 2 * FF), BF),
        pltpu.VMEM((PAIR, FF, D), BF),
        pltpu.VMEM((PAIR, ROWS, D), BF),
        pltpu.VMEM((PAIR, ROWS, FF), BF),
        pltpu.VMEM((PAIR, ROWS, D), BF),
        pltpu.VMEM((PAIR, ROWS, D), BF),
        pltpu.VMEM((PAIR, ROWS, D), BF),
        pltpu.VMEM((PAIR, ROWS, D), BF),
        pltpu.VMEM((EP, 8, TOK), F32),
        pltpu.VMEM((PAIR, REP, BLOCK, D), BF),
    ]


def experts_first(m, t, g_all, wg, wu, wd):
    return comm_call(
        experts_first_kernel,
        "experts_first",
        2,
        [
            shape((LENGTH, D), BF),
            shape((EP, 2 * LOCAL, TOK)),
            shape((PAIR, ROWS, D), BF),
            shape((PAIR, ROWS, D), BF),
            shape((EP, 8, TOK)),
            shape((PAIR, REP, BLOCK, D), BF),
        ],
        [ANY] * 6,
        [ANY] * 6,
        pair_scratch()
        + [DMA((10,))] * 2
        + [DMA((7,))] * 4
        + [DMA((4,)), DMA((3,)), DMA((4,)), DMA((4,)), DMA((3, 4))],
        limit=60,
    )(m, t, g_all, wg, wu, wd)


def experts_last_kernel(
    m_in, t_in, y_in, z_in, g_in, wg_in, wu_in, wd_in, gm_o, mix_o, gg_o, eg_o,
    m_ref, tab, g_ref, wgu, wd, a_s, act_s, gp_s, dgu_s, y_s, z_s, ggt, eg,
    y_f, z_f, gm, swo, snd, pc, rcv, hop, mix_z, mix_y,
    s_r, r_r, s_g, r_g, lsem, wsem, gsem, msem, esem, osem,
):
    e, x, c = place()
    order = [(x + 2) % 4, (x + 3) % 4, (x + 1) % 4, x]
    loads = [pltpu.make_async_copy(t_in, tab, lsem.at[0])] + load_weights(2, wg_in, wu_in, wd_in, wgu, wd, wsem)
    rows = [
        (
            pltpu.make_async_copy(m_in.at[chip_tokens(q)], m_ref.at[chip_tokens(q)], msem.at[k]),
            pltpu.make_async_copy(g_in.at[chip_tokens(q)], g_ref.at[chip_tokens(q)], gsem.at[k]),
        )
        for k, q in enumerate(order)
    ]
    firsts = [pltpu.make_async_copy(z_in, z_f, lsem.at[1]), pltpu.make_async_copy(y_in, y_f, lsem.at[2])]
    for copy in loads + list(rows[0]) + [firsts[0]] + list(rows[1] + rows[2] + rows[3]) + [firsts[1]]:
        copy.start()
    greet([{"ep": d} for d in ep_others(e)])
    red = ChipReduce(TOK, swo, snd, pc, rcv, hop, (s_r, r_r))
    ggt[...] = jnp.zeros((EP, 8, TOK), F32)

    def combine(q, early, late):
        chosen = jnp.concatenate([one_hot(expert_hits(tab, e, n, q)) for n in range(LOCAL)], axis=0)
        part = chip_rows(q)
        values = [ref[n, part] for ref in (early, late) for n in range(PAIR)]
        return dot_tn(chosen, jnp.concatenate(values, axis=0)).astype(BF)

    for copy in loads:
        copy.wait()

    def chips(k, carry):
        for step in range(4):

            @pl.when(k == step)
            def _(step=step):
                for copy in rows[step]:
                    copy.wait()

        q = (x + 2 + k - (k // 2) * (2 * k - 1)) % 4

        def send():
            @pl.when(k == 1)
            def _():
                red.send_opp()

            @pl.when(k == 2)
            def _():
                red.near_left()

            @pl.when(k == 3)
            def _():
                red.near_right()
                red.far_right()
                red.far_left()

        expert_chip(q, e, 2, tab, m_ref, g_ref, wgu, wd, a_s, act_s, gp_s, dgu_s, y_s, z_s, ggt, send)

        @pl.when(k == 0)
        def _():
            firsts[0].wait()

        mix_z[...] = combine(q, z_f, z_s)
        swo[k] = mix_z[pl.ds(pl.multiple_of((1 - c) * TOK, TOK), TOK)]
        red.swap(k).start()
        snd[k] = mix_z[pl.ds(pl.multiple_of(c * TOK, TOK), TOK)]
        return carry

    lax.fori_loop(0, 4, chips, 0)
    gates, own_gates = send_gates(ggt, gg_o, e, (s_g, r_g), lsem.at[3])
    for copy in gates + [own_gates]:
        copy.start()
    states = []
    for n in range(PAIR):
        states += expert_grads(n, a_s, act_s, gp_s, dgu_s, eg, eg_o, esem)
    red.merge(3)
    firsts[1].wait()

    def mixture(q, carry):
        values = combine(q, y_f, y_s)

        @pl.when(q > 0)
        def _():
            pltpu.make_async_copy(mix_y, mix_o.at[chip_tokens(q)], osem).wait()

        mix_y[...] = values
        pltpu.make_async_copy(mix_y, mix_o.at[chip_tokens(q)], osem).start()
        return carry

    lax.fori_loop(0, 4, mixture, 0)
    red.finish(gm)
    last = pltpu.make_async_copy(gm, gm_o, lsem.at[4])
    last.start()
    pltpu.make_async_copy(mix_y, mix_o.at[chip_tokens(3)], osem).wait()
    for copy in states + [own_gates, last]:
        copy.wait()
    for copy in gates:
        copy.wait_recv()
    for copy in gates:
        copy.wait_send()


def experts_last(m, t, y, z, g_all, wg, wu, wd):
    return comm_call(
        experts_last_kernel,
        "experts_last",
        4,
        [
            shape((TOK, D)),
            shape((LENGTH, D), BF),
            shape((EP, 8, TOK)),
            shape((PAIR, REP, BLOCK, D), BF),
        ],
        [ANY] * 8,
        [ANY] * 4,
        pair_scratch()
        + [
            pltpu.VMEM((PAIR, ROWS, D), BF),
            pltpu.VMEM((PAIR, ROWS, D), BF),
            pltpu.VMEM((TOK, D), F32),
            pltpu.VMEM((4, TOK, D), BF),
            pltpu.VMEM((4, TOK, D), BF),
            pltpu.VMEM((4, TOK, D), BF),
            pltpu.VMEM((2, TOK, D), BF),
            pltpu.VMEM((TOK, D), BF),
            pltpu.VMEM((2 * TOK, D), BF),
            pltpu.VMEM((2 * TOK, D), BF),
        ]
        + [DMA((10,))] * 2
        + [DMA((7,))] * 2
        + [DMA((5,)), DMA((3,)), DMA((4,)), DMA((4,)), DMA((4,)), DMA(())],
        limit=63,
    )(m, t, y, z, g_all, wg, wu, wd)


KEPT = 8


def back_kernel(
    eg_in, mix_in, gm_in, gg1_in, gg2_in, tab_in, hid_in, m_in, cot_in, att_in, misc_in, rout_in, whole_in, wcol_in, x_in, lin_in,
    q_in, k_in, v_in, a_in, lse_in, cos_in, sin_in,
    out_o, ig_o, gq_o, gk_o, gv_o, go_o, pack_o, eg_o,
    gm, gg1, gg2, tab, hid, cot, misc, rout, wcol, x_s, lin, q_s, k_s, v_s, a_s, lse, cos_ref, sin_ref,
    gh, ga_s, go, q2_s, p_s, dk, dv, u_s, sums, st2, held, wb, wsum, wheld,
    dwt, dws, dheld, dsum, dw_o, vec, vheld, vtot, vheld2, swo, snd, pc1, rcv1, hop1, rcv2, snd3, pc3, rcv3, hop3,
    s_1, r_1, s_2, r_2, s_3, r_3, s_go, r_go, s_st, r_st, s_w, r_w, s_d, r_d, s_e, r_e, s_v, r_v, s_v2, r_v2, lsem, l_1, l_3, esem, xsem,
    out_s, gq_s, gk_s, gv_s, go_s, pack_s, eg_s,
    za, zb, zc, zd, ze, zf, ya, yb, yc, yd, ye, yf, s_z, r_z, s_y, r_y, l_z, l_y,
):
    r = lax.axis_index("rep")
    e, x, c = place()
    others = ep_others(e)
    copies = rep_others(r)
    first = iota((TOK, 128), 1) < HEAD_DIM
    gain_a, gain_f, gain = misc.at[0:1], misc.at[1:2], misc.at[2:3, 0:256]
    lo, st = misc.at[8:16, 0:256], misc.at[16:32, 0:256]
    red1 = RingReduce(mix_in, TOK, pc1, snd, rcv1, hop1, (s_1, r_1), l_1)
    red2 = ChipReduce(TOK, swo, snd, pc1, rcv2, hop1, (s_2, r_2))
    red3 = RingReduce(wb, 128, pc3, snd3, rcv3, hop3, (s_3, r_3), l_3)
    by_z = GridReduce(True, eg_in, 0, za, zb, zc, zd, ze, zf, (s_z, r_z), l_z)
    by_y = GridReduce(False, eg_in, FF, ya, yb, yc, yd, ye, yf, (s_y, r_y), l_y)
    loads = [
        pltpu.make_async_copy(src, dst, lsem.at[k])
        for k, (src, dst) in enumerate(
            [
                (misc_in, misc), (gm_in, gm), (gg1_in, gg1), (gg2_in, gg2), (tab_in, tab), (hid_in, hid),
                (cot_in, cot), (rout_in, rout), (whole_in, wb.at[:, pl.ds(0, D)]), (q_in, q_s), (k_in, k_s), (lse_in, lse),
                (m_in, rcv2.at[0]), (att_in, rcv2.at[1]), (v_in, v_s), (a_in, a_s), (cos_in, cos_ref), (sin_in, sin_ref),
                (lin_in, lin), (wcol_in, wcol),
            ]
        )
    ]
    chips_order = [(x + 2) % 4, (x + 3) % 4, (x + 1) % 4, x]

    def x_load(k):
        return pltpu.make_async_copy(x_in.at[chip_tokens(chips_order[k])], x_s.at[k % 2], xsem.at[k % 2])


    def fetch():
        for copy in loads + [x_load(0), x_load(1)] + by_z.load + by_y.load:
            copy.start()

    greet([{"ep": d} for d in others] + [{"rep": d} for d in copies], fetch)
    red1.start()
    for copy in loads[:9]:
        copy.wait()

    def base(i):
        cut = jnp.minimum(i, 4)
        return cut * (cut + 1) // 2 + 5 * jnp.maximum(i - 4, 0)

    def spans(i, n):
        keys = pl.ds(pl.multiple_of((i - n + 1) * TOK, TOK), n * TOK)
        return keys, pl.ds(pl.multiple_of(base(i) * TOK, TOK), n * TOK)

    def probabilities(i, n):
        _, held_rows = spans(i, n)
        p_s[held_rows] = make_probabilities(i, n)

    def make_probabilities(i, n):
        keys, _ = spans(i, n)
        q2 = stack_heads(q_s[block_rows(i)].astype(F32) * HEAD_DIM ** (-0.5)).astype(BF)
        q2_s[i] = q2
        top = lse[i][0:1]
        low = jnp.concatenate([lo[pl.ds(i, 1)]] * 2, axis=1)
        key = (iota((n * TOK, 2 * TOK), 0) + (i - n + 1) * TOK).astype(F32)
        query = (iota((n * TOK, 2 * TOK), 1) % TOK + i * TOK).astype(F32)
        allowed = (key >= low) & (key <= query)
        return jnp.where(allowed, jnp.exp(dot_nt(k_s[keys], q2) - top), 0.0).astype(BF)

    def probabilities_later(i, carry):
        probabilities(i, 5)

        @pl.when(i == 4)
        def _():
            red1.push_opp()

        @pl.when(i == 5)
        def _():
            red1.push_near()

        return carry


    hidden = hid[...]
    weights = jnp.concatenate([tab[d][LOCAL:] for d in range(EP)], axis=0)
    grads = jnp.concatenate([ref[d][:PAIR] for d in range(EP) for ref in (gg1, gg2)], axis=0)
    mean = jnp.sum(weights * grads, axis=0, keepdims=True)
    grad_logits = weights * (grads - mean)
    grad_moe = gm[...] + dot_tn(grad_logits.astype(BF), rout[...])
    r2 = lax.rsqrt(jnp.mean(hidden * hidden, axis=1, keepdims=True) + EPSILON)
    n = hidden * r2
    u = grad_moe * gain_f[...]
    grad_hidden = cot[...].astype(F32) + r2 * (u - n * jnp.mean(u * n, axis=1, keepdims=True))
    gh[...] = grad_hidden
    branch = grad_hidden.astype(BF)
    ga_s[...] = dot_nt(branch, wb[:, :D]).astype(BF)

    def own_cols(ref, b):
        return ref.at[:, pl.ds(pl.multiple_of(b * 128, 128), 128)]

    heads = [
        remote(own_cols(ga_s, d), go.at[block_rows(e)], (s_go, r_go), k, {"ep": d}) for k, d in enumerate(others)
    ]
    for copy in heads:
        copy.start()
    by_z.push()
    by_y.push()
    go[block_rows(e)] = own_cols(ga_s, e)[...]
    for copy in loads[9:12]:
        copy.wait()
    for i in range(4):
        probabilities(i, i + 1)
    lax.fori_loop(4, KEPT, probabilities_later, 0)
    for copy in loads[12:]:
        copy.wait()
    for copy in heads:
        copy.wait_recv()
    ffn = jnp.sum(grad_moe * n, axis=0, keepdims=True)
    logit_rows = jnp.transpose(jnp.concatenate([grad_logits, jnp.zeros((96, TOK), F32)], axis=0)).astype(BF)
    router_rows = dot_tn(rcv2[0], logit_rows)
    vec[...] = jnp.zeros((8, D), F32)
    vec[3:4] = ffn
    router_rows = router_rows.reshape(REP, EP, 8, 128)
    for d in range(EP):
        wb[d * 128 : (d + 1) * 128, D:] = router_rows[:, d].reshape(128, 128).astype(BF)
    for cols in range(0, D, 256):
        out_rows = dot_tn(rcv2[1], branch[:, cols : cols + 256]).reshape(REP, EP, 8, 256)
        for d in range(EP):
            wb[d * 128 : (d + 1) * 128, cols : cols + 256] = out_rows[:, d].reshape(128, 256).astype(BF)
    red3.start()
    by_z.stage.relay()
    by_y.stage.relay()
    dk[...] = jnp.zeros((LENGTH, 128), F32)
    dv[...] = jnp.zeros((LENGTH, 128), F32)

    def part(ref, b, size):
        return ref.at[pl.ds(pl.multiple_of(b * size, 8), size)]

    spread_w = [remote(part(wsum, d, 8), wheld.at[r], (s_w, r_w), k, {"rep": d}) for k, d in enumerate(copies)]

    def attend_back(i, n):
        keys, held_rows = spans(i, n)
        rows = block_rows(i)
        grad = stack_heads(go[rows].astype(F32))
        do2 = grad.astype(BF)
        out = a_s[rows].astype(F32)
        settle = row_sums(grad * jnp.concatenate([out, out], axis=0), ((0, 128),))[0:1]
        p = p_s[held_rows]
        ds = (p.astype(F32) * (dot_nt(v_s[keys], do2) - settle)).astype(BF)
        dv[keys] += dot(p, do2)
        dk[keys] += dot(ds, q2_s[i])
        dq = dot_tn(k_s[keys], ds)
        u_s[rows, :128] = merge_heads(jnp.transpose(dq)) * HEAD_DIM ** (-0.5)

    def attend_back_later(i, carry):
        attend_back(i, 5)
        return carry

    for i in range(4):
        attend_back(i, i + 1)
    red3.push_opp()
    red3.push_near()
    lax.fori_loop(4, 6, attend_back_later, 0, unroll=True)
    red1.relay()
    red3.relay()
    lax.fori_loop(6, EP, attend_back_later, 0, unroll=True)

    def close(b, carry):
        rows = block_rows(b)
        grad_k, grad_v = dk[rows], dv[rows]
        grad_k = grad_k + pltpu.roll(grad_k, HEAD_DIM, 1)
        grad_v = grad_v + pltpu.roll(grad_v, HEAD_DIM, 1)
        both = jnp.where(first, grad_k, grad_v).astype(BF).astype(F32)
        cosine, sine = cos_ref[rows], -sin_ref[rows]
        both = jnp.where(first, turn(both, cosine, sine), both)
        grad_q = turn(u_s[rows, :128].astype(BF).astype(F32), cosine, sine)
        u_s[rows, :128] = grad_q
        u_s[rows, 128:] = both
        cq, ck = columns(
            lax.rsqrt(st[pl.ds(2 * b, 1)] * (1.0 / D) + EPSILON),
            lax.rsqrt(st[pl.ds(2 * b + 1, 1)] * (1.0 / KV) + EPSILON),
        )
        products = jnp.concatenate([grad_q * cq, both * ck], axis=1) * gain[...] * lin[rows]
        pair = row_sums(products, PARTS)
        sums[pl.ds(2 * b, 1)] = pair[0:1]
        sums[pl.ds(2 * b + 1, 1)] = pair[1:2]
        return carry

    lax.fori_loop(0, EP, close, 0, unroll=2)
    stats = [remote(sums, held.at[e], (s_st, r_st), k, {"ep": d}) for k, d in enumerate(others)]
    for copy in stats:
        copy.start()
    held[e] = sums[...]
    red1.finish(gm)
    out_s[...] = (hid[...] + gm[...]).astype(BF)
    ends = [pltpu.make_async_copy(out_s, out_o, esem.at[0])]
    ends[0].start()
    red3.finish(wsum)
    for copy in spread_w:
        copy.start()
    wheld[r] = part(wsum, r, 8)[...]
    by_z.turn()
    by_y.turn()
    dwt[...] = jnp.zeros((256, D), F32)
    for copy in stats:
        copy.wait_recv()
    total = held[0]
    for k in range(1, EP):
        total = total + held[k]
    st2[...] = total

    def project_back(b, slot):
        rows = block_rows(b)
        values = x_s[slot, pl.ds(pl.multiple_of(b % 2 * TOK, TOK), TOK)].astype(F32)
        r1 = lax.rsqrt(jnp.mean(values * values, axis=1, keepdims=True) + EPSILON)
        n1 = values * r1
        normed = (n1 * gain_a[...]).astype(BF)
        cq, ck, mq, mk = columns(
            lax.rsqrt(st[pl.ds(2 * b, 1)] * (1.0 / D) + EPSILON),
            lax.rsqrt(st[pl.ds(2 * b + 1, 1)] * (1.0 / KV) + EPSILON),
            st2[pl.ds(2 * b, 1)] * (1.0 / D),
            st2[pl.ds(2 * b + 1, 1)] * (1.0 / KV),
        )
        uq, uk = u_s[rows, :128], u_s[rows, 128:]
        nq = lin[rows, :128] * cq
        nk = lin[rows, 128:] * ck
        gq = cq * (uq * gain[:, :128] - nq * mq)
        gk = jnp.where(first, ck * (uk * gain[:, 128:] - nk * mk), uk)
        glin = jnp.concatenate([gq, gk], axis=1).astype(BF)
        vec[1:2, :128] += jnp.sum(uq * nq, axis=0, keepdims=True)
        vec[2:3, :128] += jnp.sum(uk * nk, axis=0, keepdims=True)
        gn = dot_nt(glin, wcol[...])
        vec[0:1] += jnp.sum(gn * n1, axis=0, keepdims=True)
        dwt[...] += dot_tn(glin, normed)
        return gn.astype(BF)

    def chips(k, carry):
        q = (x + 2 + k - (k // 2) * (2 * k - 1)) % 4
        for step in range(4):

            @pl.when(k == step)
            def _(step=step):
                x_load(step).wait()

        swo[k] = project_back(q * 2 + 1 - c, k % 2)
        red2.swap(k).start()

        @pl.when(k == 1)
        def _():
            red2.send_opp()

        @pl.when(k == 2)
        def _():
            red2.near_left()

        @pl.when(k == 3)
        def _():
            red2.near_right()

        snd[k] = project_back(q * 2 + c, k % 2)
        for step in range(2):

            @pl.when(k == step)
            def _(step=step):
                x_load(step + 2).start()

        return carry

    lax.fori_loop(0, 4, chips, 0)
    dws[...] = jnp.transpose(dwt[...]).astype(BF)
    spread_d = [remote(part(dws, d, 64), dheld.at[r], (s_d, r_d), k, {"rep": d}) for k, d in enumerate(copies)]
    for copy in spread_d:
        copy.start()
    dheld[r] = part(dws, r, 64)[...]
    gain_q, gain_k = vec[1:2, :128], vec[2:3, :128]
    low, spread = iota((1, 128), 1) < 32, iota((1, 128), 1) // 32 == 2
    gain_k = jnp.where(low, gain_k, jnp.where(spread, pltpu.roll(gain_k, 32, 1), 0.0))
    vec[1:3, :128] = jnp.zeros((2, 128), F32)
    vec[1:2, pl.ds(pl.multiple_of(e * 128, 128), 128)] = gain_q
    vec[2:3, pl.ds(pl.multiple_of(e * 128, 128), 128)] = gain_k
    spread_v = [remote(vec, vheld.at[e], (s_v, r_v), k, {"ep": d}) for k, d in enumerate(others)]
    for copy in spread_v:
        copy.start()
    vheld[e] = vec[...]
    red2.merge(3)
    red2.send_far()
    by_z.last.relay()
    by_y.last.relay()
    for copy in spread_v:
        copy.wait_recv()
    total = vheld[0]
    for k in range(1, EP):
        total = total + vheld[k]
    vtot[...] = total
    def lanes_of(d):
        return vtot.at[:, pl.ds(pl.multiple_of(d // 2 * 128, 128), 128)]

    spread_v2 = [remote(lanes_of(d), vheld2.at[r], (s_v2, r_v2), k, {"rep": d}) for k, d in enumerate(copies)]
    for copy in spread_v2:
        copy.start()
    vheld2[r] = lanes_of(r)[...]
    for copy in spread_w:
        copy.wait_recv()
    total = wheld[0]
    for k in range(1, REP):
        total = total + wheld[k]
    go_s[...] = total[:, :D]
    pack_s[0:8] = total[:, D:]
    for copy in spread_d:
        copy.wait_recv()
    total = dheld[0].astype(F32)
    for k in range(1, REP):
        total = total + dheld[k].astype(F32)
    dsum[...] = total
    spread_e = [remote(part(dsum, d, 8), dw_o.at[e], (s_e, r_e), k, {"ep": d}) for k, d in enumerate(others)]
    for copy in spread_e:
        copy.start()
    dw_o[e] = part(dsum, e, 8)[...]
    for copy in spread_v2:
        copy.wait_recv()
    total = vheld2[0]
    for k in range(1, REP):
        total = total + vheld2[k]
    start = r % 2 * 64
    rows_d, lanes_d = iota((128, 128), 0), iota((128, 128), 1)
    eight = jnp.where((rows_d == start + e * 8 + lanes_d) & (lanes_d < 8), 1.0, 0.0)
    four = jnp.where((rows_d == start + e * 4 + lanes_d) & (lanes_d < 4), 1.0, 0.0)

    def pick(sel):
        return jnp.dot(total, sel, preferred_element_type=F32, precision=HIGH)

    eights, fours = pick(eight), pick(four)
    pack_s[8:16] = jnp.where(iota((8, 128), 0) == 2, fours, eights)
    by_z.finish(eg_s, 0)
    by_y.finish(eg_s, FF)
    for copy in spread_e:
        copy.wait_recv()
    low_lanes = iota((8, 128), 1) < HEAD_DIM
    for d in range(EP):
        gq_s[:, d * 128 : (d + 1) * 128] = dw_o[d][:, :128]
    for d in range(EP // 2):
        even, odd = dw_o[2 * d][:, 128:], dw_o[2 * d + 1][:, 128:]
        gk_s[:, d * 128 : (d + 1) * 128] = jnp.where(low_lanes, even, pltpu.roll(odd, HEAD_DIM, 1))
        gv_s[:, d * 128 : (d + 1) * 128] = jnp.where(low_lanes, pltpu.roll(even, HEAD_DIM, 1), odd)
    pairs = [(gq_s, gq_o), (gk_s, gk_o), (gv_s, gv_o), (go_s, go_o), (pack_s, pack_o), (eg_s, eg_o)]
    for k, (src, dst) in enumerate(pairs):
        ends.append(pltpu.make_async_copy(src, dst, esem.at[1 + k]))
        ends[-1].start()
    red2.finish(gm)
    values = x_s[1, pl.ds(pl.multiple_of(c * TOK, TOK), TOK)].astype(F32)
    r1 = lax.rsqrt(jnp.mean(values * values, axis=1, keepdims=True) + EPSILON)
    n1 = values * r1
    z = gm[...] * gain_a[...]
    gh[...] = gh[...] + r1 * (z - n1 * jnp.mean(z * n1, axis=1, keepdims=True))
    ends.append(pltpu.make_async_copy(gh, ig_o, esem.at[7]))
    ends[-1].start()
    for copy in ends:
        copy.wait()
    for copy in heads + stats + spread_w + spread_d + spread_e + spread_v + spread_v2:
        copy.wait_send()


ELSEWHERE = (7, 9, 12)
X_ALL = 14


def back(*args):
    def vm(dims, dtype=F32):
        return pltpu.VMEM(dims, dtype)

    held = [vm((2, 2 * TOK, D), BF) if k == X_ALL else vm(a.shape, a.dtype) for k, a in enumerate(args) if k > 1 and k not in ELSEWHERE]
    results = [((TOK, D), BF), ((TOK, D), F32), ((8, D), F32), ((8, KV), F32), ((8, KV), F32), ((8, D), F32), ((16, 128), F32)]
    results.append(((PAIR, BLOCK, D), BF))
    landing = [vm((4, TOK, D), BF), vm((2, TOK, D), BF), vm((TOK, D), BF)]
    return comm_call(
        back_kernel,
        "back",
        6,
        [shape(*result) for result in results],
        [ANY] * 23,
        [ANY] * 8,
        held
        + [
            vm((TOK, D)),
            vm((TOK, D), BF),
            vm((LENGTH, 128), BF),
            vm((EP, 2 * TOK, 128), BF),
            vm(((10 + 5 * (KEPT - 4)) * TOK, 2 * TOK), BF),
            vm((LENGTH, 128)),
            vm((LENGTH, 128)),
            vm((LENGTH, 256)),
            vm((16, 256)),
            vm((16, 256)),
            vm((EP, 16, 256)),
            vm((D, WB), BF),
            vm((128, WB)),
            vm((REP, 8, WB)),
            vm((256, D)),
            vm((D, 256), BF),
            vm((REP, 64, 256), BF),
            vm((64, 256)),
            vm((EP, 8, 256)),
            vm((8, D)),
            vm((EP, 8, D)),
            vm((8, D)),
            vm((REP, 8, 128)),
            vm((4, TOK, D), BF),
            vm((4, TOK, D), BF),
        ]
        + landing
        + [vm((2, TOK, D), BF)]
        + [vm((4, 128, WB), BF), vm((4, 128, WB), BF), vm((2, 128, WB), BF), vm((128, WB), BF)]
        + [DMA((10,))] * 6
        + [DMA((7,))] * 4
        + [DMA((15,))] * 4
        + [DMA((7,))] * 4
        + [DMA((15,))] * 2
        + [DMA((20,)), DMA((4,)), DMA((4,)), DMA((8,)), DMA((2,))]
        + [vm(*result) for k, result in enumerate(results) if k != 1]
        + grid_scratch() * 2
        + [DMA((12,))] * 4
        + [DMA((4,))] * 2,
        limit=64,
    )(*args)


def finish_kernel(
    xa_in, xb_in, out_in, ig_in, gq_in, gk_in, gv_in, go_in, pack_in,
    out_o, ig_o, gq_o, gk_o, gv_o, go_o, gr_o, va_o, vq_o, vk_o, vf_o, gate_o, up_o, down_o,
    x_s, gate_s, up_s, down_s, out_s, ig_s, gq_s, gk_s, gv_s, go_s, pack, gr_s, va_s, vq_s, vk_s, vf_s, sem,
):
    loads = [
        pltpu.make_async_copy(xa_in, x_s.at[pl.ds(0, PAIR)], sem.at[9]),
        pltpu.make_async_copy(xb_in, x_s.at[pl.ds(PAIR, PAIR)], sem.at[10]),
    ]
    for load in loads:
        load.start()
    stages = [out_s, ig_s, gq_s, gk_s, gv_s, go_s]
    fetch = [
        pltpu.make_async_copy(src, dst, sem.at[k])
        for k, (src, dst) in enumerate(zip([out_in, ig_in, gq_in, gk_in, gv_in, go_in], stages))
    ]
    copies = [
        pltpu.make_async_copy(src, dst, sem.at[k])
        for k, (src, dst) in enumerate(zip(stages, [out_o, ig_o, gq_o, gk_o, gv_o, go_o]))
    ]
    load_pack = pltpu.make_async_copy(pack_in, pack, sem.at[11])
    for copy in fetch + [load_pack]:
        copy.start()
    for load, copy in zip(fetch, copies):
        load.wait()
        copy.start()
    for load in loads:
        load.wait()
    gate_s[...] = x_s[:, :64, :FF].astype(F32)
    up_s[...] = x_s[:, :64, FF:].astype(F32)
    down_s[...] = x_s[:, 64:].astype(F32)
    load_pack.wait()
    gr_s[...] = pack[0:8, :EXPERTS]
    va_s[...] = pack[8:9, :8]
    vq_s[...] = pack[9:10, :8]
    vk_s[...] = pack[10:11, :4]
    vf_s[...] = pack[11:12, :8]
    pairs = [(gate_s, gate_o), (up_s, up_o), (down_s, down_o)]
    pairs += [(gr_s, gr_o), (va_s, va_o), (vq_s, vq_o), (vk_s, vk_o), (vf_s, vf_o)]
    for k, (src, dst) in enumerate(pairs):
        k = k if k < 5 else k + 1
        copies.append(pltpu.make_async_copy(src, dst, sem.at[6 + k]))
        copies[-1].start()
    for copy in copies:
        copy.wait()


def finish(xa, xb, out, ig, gq, gk, gv, go, pack):
    gate, down = shape((LOCAL, 64, FF)), shape((LOCAL, 32, D))
    return pl.pallas_call(
        finish_kernel,
        out_shape=[shape(a.shape, a.dtype) for a in (out, ig, gq, gk, gv, go)]
        + [shape((8, EXPERTS)), shape((1, 8)), shape((1, 8)), shape((1, 4)), shape((1, 8)), gate, gate, down],
        in_specs=[ANY] * 9,
        out_specs=[ANY] * 14,
        scratch_shapes=[
            pltpu.VMEM((LOCAL, BLOCK, D), BF),
            pltpu.VMEM(gate.shape, F32),
            pltpu.VMEM(gate.shape, F32),
            pltpu.VMEM(down.shape, F32),
        ]
        + [pltpu.VMEM(a.shape, a.dtype) for a in (out, ig, gq, gk, gv, go, pack)]
        + [pltpu.VMEM(dims, F32) for dims in ((8, EXPERTS), (1, 8), (1, 8), (1, 4), (1, 8))]
        + [
            DMA((16,)),
        ],
        compiler_params=pltpu.CompilerParams(vmem_limit_bytes=62 * MIB),
        name="finish",
    )(xa, xb, out, ig, gq, gk, gv, go, pack)


def body(
    tokens,
    segments,
    routes,
    w_query,
    w_key,
    w_value,
    w_out,
    w_router,
    gain_attn,
    gain_query,
    gain_key,
    gain_ffn,
    w_gate,
    w_up,
    w_down,
    out_grad,
):
    gains = [gain.reshape(1, -1) for gain in (gain_attn, gain_query, gain_key, gain_ffn)]
    cosine, sine = turn_tables()
    (
        x_all, g_all, lin, q, k, v, att, lse, hidden, moe_in, tables, attended, misc, router, whole_out, w_cols,
    ) = front(
        tokens, out_grad, w_query, w_key, w_value, w_out, w_router, *gains, segments, routes.T, cosine, sine
    )
    def over_copies(grads):
        grads = grads.reshape(PAIR, REP * BLOCK, D)
        return lax.psum_scatter(grads, "rep", scatter_dimension=1, tiled=True)

    m_all, tabs, y, z, gg_first, grads = experts_first(moe_in, tables, g_all, w_gate, w_up, w_down)
    sums_first = over_copies(grads)
    grad_moe, mixture, gg_last, grads = experts_last(m_all, tabs, y, z, g_all, w_gate, w_up, w_down)
    *rows, sums_last = back(
        grads.reshape(PAIR, 4, 4, BLOCK, D), mixture, grad_moe, gg_first, gg_last, tables, hidden, moe_in, out_grad, attended, misc, router, whole_out,
        w_cols, x_all, lin, q, k, v, att, lse, cosine, sine,
    )
    out, ig, gq, gk, gv, go, gr, va, vq, vk, vf, gate, up, down = finish(sums_first, sums_last, *rows)
    return out, ig, gq, gk, gv, go, gr, va.reshape(8), vq.reshape(8), vk.reshape(4), vf.reshape(8), gate, up, down


def solution(mesh):
    both = P(("rep", "ep"), None)
    line = P(("rep", "ep"))
    owner = P("ep", None, None)
    kept = P("ep", "rep", None)
    return jax.shard_map(
        body,
        mesh=mesh,
        in_specs=(both, P("rep", None)) + (both,) * 6 + (line,) * 4 + (owner,) * 3 + (both,),
        out_specs=(both,) * 7 + (line,) * 4 + (kept,) * 3,
        check_vma=False,
    )
```

```python
import functools

import jax
import jax.numpy as jnp
import numpy as np
from jax import lax
from jax.experimental import pallas as pl
from jax.experimental.pallas import tpu as pltpu
from jax.sharding import PartitionSpec as P

BF = jnp.bfloat16
F32 = jnp.float32
MESH = pl.DeviceIdType.MESH
ANY = pl.BlockSpec(memory_space=pl.ANY)
VM = pl.BlockSpec(memory_space=pltpu.VMEM)
DMA = pltpu.SemaphoreType.DMA
MIB = 1 << 20

HEADS = 16
KV_HEADS = 8
HEAD_DIM = 64
TOP = 8
WINDOW = 1024
EPSILON = 1e-06
ROPE_BASE = 10000.0
MASKED = -1e30
EP = 8
REP = 16
TOK = 256
LENGTH = 2048
D = 1024
KV = 512
FF = 512
EXPERTS = 32
LOCAL = 4
CAP = 88
NT = (((1,), (1,)), ((), ()))
TN = (((0,), (0,)), ((), ()))
HIGH = lax.Precision.HIGHEST


def dot(a, b):
    return jnp.dot(a, b, preferred_element_type=F32)


def dot_nt(a, b, precision=None):
    return lax.dot_general(a, b, NT, preferred_element_type=F32, precision=precision)


def dot_tn(a, b):
    return lax.dot_general(a, b, TN, preferred_element_type=F32)


def iota(shape, dim):
    return lax.broadcasted_iota(jnp.int32, shape, dim)


def ep_device(x, c):
    return {"ep": x * 2 + c}


def greet(devices, local_work=None):
    barrier = pltpu.get_barrier_semaphore()
    for device in devices:
        pl.semaphore_signal(barrier, inc=1, device_id=device, device_id_type=MESH)
    if local_work is not None:
        local_work()
    pl.semaphore_wait(barrier, len(devices))


def remote(src, dst, sems, i, device):
    return pltpu.make_async_remote_copy(
        src_ref=src,
        dst_ref=dst,
        send_sem=sems[0].at[i],
        recv_sem=sems[1].at[i],
        device_id=device,
        device_id_type=MESH,
    )


def place():
    e = lax.axis_index("ep")
    return e, e // 2, e % 2


def ep_others(e):
    return [(e + k) % EP for k in range(1, EP)]


def rep_others(r):
    return [(r + k) % REP for k in range(1, REP)]


class RingGather:
    SEMS = 10

    def __init__(self, x_ref, o_ref, sems, lsem):
        e, x, c = place()
        self.n = n = x_ref.shape[0]
        h = n // 2
        self.o_ref = o_ref
        right, left = ep_device((x + 1) % 4, c), ep_device((x + 3) % 4, c)
        peer = ep_device(x, 1 - c)
        b_left, b_right, b_opp = (((x + 3) % 4) * 2 + c, ((x + 1) % 4) * 2 + c, ((x + 2) % 4) * 2 + c)

        def rows(b, off=0, size=n):
            return o_ref.at[pl.ds(pl.multiple_of(b * n + off, 16), size)]

        low, high = x_ref.at[pl.ds(0, h)], x_ref.at[pl.ds(h, h)]
        self.first = [
            remote(low, rows(e, 0, h), sems, 0, right),
            remote(high, rows(e, h, h), sems, 2, left),
            remote(high, rows(e, h, h), sems, 1, right),
            remote(low, rows(e, 0, h), sems, 3, left),
            remote(x_ref, rows(e), sems, 4, peer),
        ]
        self.fwd_right = remote(rows(b_left, 0, h), rows(b_left, 0, h), sems, 5, right)
        self.fwd_left = remote(rows(b_right, h, h), rows(b_right, h, h), sems, 6, left)
        self.to_peer = [
            remote(rows(b_left), rows(b_left), sems, 7, peer),
            remote(rows(b_right), rows(b_right), sems, 8, peer),
            remote(rows(b_opp), rows(b_opp), sems, 9, peer),
        ]
        self.own = pltpu.make_async_copy(x_ref, rows(e), lsem)

    def start(self):
        for copy in self.first:
            copy.start()
        self.own.start()

    def forward_half(self):
        self.first[0].wait_recv()
        self.fwd_right.start()
        self.first[1].wait_recv()
        self.fwd_left.start()

    def forward_rest(self):
        self.first[2].wait_recv()
        self.to_peer[0].start()
        self.first[3].wait_recv()
        self.to_peer[1].start()

    def finish(self):
        self.fwd_right.wait_recv()
        self.fwd_left.wait_recv()
        self.to_peer[2].start()
        self.first[4].wait_recv()
        for copy in self.to_peer:
            copy.wait_recv()
        self.own.wait()
        for copy in self.first + [self.fwd_right, self.fwd_left] + self.to_peer:
            copy.wait_send()


class RingReduce:
    SEMS = 10
    STEP = 64

    def __init__(self, p_ref, n, pc, snd, rcv, hop, sems, lsems):
        e, x, c = place()
        self.n, self.h = n, n // 2
        h = n // 2
        self.pc, self.snd, self.rcv, self.hop = pc, snd, rcv, hop
        right, left = ep_device((x + 1) % 4, c), ep_device((x + 3) % 4, c)
        peer = ep_device(x, 1 - c)

        def rows(b):
            return p_ref.at[pl.ds(pl.multiple_of(b * n, 16), n)]

        chips = [(x + 2) % 4, (x + 1) % 4, (x + 3) % 4, x]
        self.swap = [remote(rows(b * 2 + 1 - c), pc.at[k], sems, k, peer) for k, b in enumerate(chips)]
        self.load = [
            pltpu.make_async_copy(rows(b * 2 + c), snd.at[k], lsems.at[k]) for k, b in enumerate(chips)
        ]
        low, high = pl.ds(0, h), pl.ds(h, h)
        self.opp = [
            remote(snd.at[0, low], hop.at[low], sems, 4, right),
            remote(snd.at[0, high], hop.at[high], sems, 5, left),
        ]
        self.near = [
            remote(snd.at[1, high], rcv.at[0, high], sems, 6, right),
            remote(snd.at[2, low], rcv.at[1, low], sems, 7, left),
        ]
        self.far = [
            remote(snd.at[1, low], rcv.at[0, low], sems, 8, right),
            remote(snd.at[2, high], rcv.at[1, high], sems, 9, left),
        ]

    def rows_loop(self, low, count, body):
        step = self.STEP

        def loop(i, carry):
            body(pl.ds(pl.multiple_of(low + i * step, 16), step))
            return carry

        lax.fori_loop(0, count // step, loop, 0)

    def merge(self, k):
        def body(s):
            self.snd[k, s] = (self.snd[k, s].astype(F32) + self.pc[k, s].astype(F32)).astype(BF)

        self.load[k].wait()
        self.swap[k].wait_recv()
        self.rows_loop(0, self.n, body)

    def merge_hop(self, k, low):
        def body(s):
            self.snd[k, s] = (self.snd[k, s].astype(F32) + self.hop[s].astype(F32)).astype(BF)

        self.rows_loop(low, self.h, body)

    def start(self):
        for copy in self.swap + self.load:
            copy.start()

    def push_opp(self):
        self.merge(0)
        for copy in self.opp:
            copy.start()

    def push_near(self):
        self.merge(1)
        self.near[0].start()
        self.merge(2)
        self.near[1].start()
        self.merge(3)

    def relay(self):
        self.opp[0].wait_recv()
        self.merge_hop(1, 0)
        self.far[0].start()
        self.opp[1].wait_recv()
        self.merge_hop(2, self.h)
        self.far[1].start()

    def finish(self, out_ref):
        for copy in self.near + self.far:
            copy.wait_recv()

        def body(s):
            out_ref[s] = self.snd[3, s].astype(F32) + (
                self.rcv[0, s].astype(F32) + self.rcv[1, s].astype(F32)
            )

        self.rows_loop(0, self.n, body)
        for copy in self.swap + self.opp + self.near + self.far:
            copy.wait_send()


class AxisReduce:
    def __init__(self, devices, snd, hop, rcv, sems, base):
        right, left = devices
        self.snd, self.hop, self.rcv = snd, hop, rcv
        self.opp = [
            remote(snd.at[0, 0], hop.at[0], sems, base, right),
            remote(snd.at[0, 1], hop.at[1], sems, base + 1, left),
        ]
        self.near = [
            remote(snd.at[2, 1], rcv.at[0, 1], sems, base + 2, right),
            remote(snd.at[1, 0], rcv.at[1, 0], sems, base + 3, left),
        ]
        self.far = [
            remote(snd.at[2, 0], rcv.at[0, 0], sems, base + 4, right),
            remote(snd.at[1, 1], rcv.at[1, 1], sems, base + 5, left),
        ]

    def push(self):
        for copy in self.opp + self.near:
            copy.start()

    def relay(self):
        for k, (slot, half) in enumerate(((2, 0), (1, 1))):
            self.opp[k].wait_recv()
            self.snd[slot, half] = (self.snd[slot, half].astype(F32) + self.hop[half].astype(F32)).astype(BF)
            self.far[k].start()

    def arrive(self):
        for copy in self.near + self.far:
            copy.wait_recv()

    def total(self, *index):
        return self.snd[(3,) + index].astype(F32) + (
            self.rcv[(0,) + index].astype(F32) + self.rcv[(1,) + index].astype(F32)
        )

    def leave(self):
        for copy in self.opp + self.near + self.far:
            copy.wait_send()


class GridReduce:
    def __init__(self, along_z, src, cols, snd, hop, rcv, snd2, hop2, rcv2, sems, lsems):
        r = lax.axis_index("rep")
        z, y = r // 4, r % 4
        along = (lambda k: {"rep": (z + k) % 4 * 4 + y}, lambda k: {"rep": z * 4 + (y + k) % 4})
        one, two = along if along_z else along[::-1]
        here, self.there = (z, y) if along_z else (y, z)
        offsets = (2, 3, 1, 0)
        cut = pl.ds(cols, FF)
        self.load = []
        for k, off in enumerate(offsets):
            b = (here + off) % 4
            block = src.at[:, b, :, :, cut] if along_z else src.at[:, :, b, :, cut]
            self.load.append(pltpu.make_async_copy(block, snd.at[k], lsems.at[k]))
        self.offsets, self.snd2 = offsets, snd2
        self.stage = AxisReduce((one(1), one(3)), snd, hop, rcv, sems, 0)
        self.last = AxisReduce((two(1), two(3)), snd2, hop2, rcv2, sems, 6)

    def push(self):
        for copy in self.load:
            copy.wait()
        self.stage.push()

    def turn(self):
        self.stage.arrive()
        for k, off in enumerate(self.offsets):
            b = (self.there + off) % 4
            for n in range(PAIR):
                self.snd2[k, n] = self.stage.total(n, b).astype(BF)
        self.last.push()

    def finish(self, out_ref, cols):
        self.last.arrive()
        for n in range(PAIR):
            out_ref[n, :, cols : cols + FF] = self.last.total(n).astype(BF)
        self.stage.leave()
        self.last.leave()


def grid_scratch():
    blocks = [(4, PAIR, 4, BLOCK, FF), (PAIR, 4, BLOCK, FF), (2, PAIR, 4, BLOCK, FF)]
    blocks += [(4, PAIR, BLOCK, FF), (PAIR, BLOCK, FF), (2, PAIR, BLOCK, FF)]
    return [pltpu.VMEM(dims, BF) for dims in blocks]


def comm_call(kernel, name, collective_id, out_shape, in_specs, out_specs, scratch, limit=48):
    return pl.pallas_call(
        kernel,
        out_shape=out_shape,
        in_specs=in_specs,
        out_specs=out_specs,
        scratch_shapes=scratch,
        compiler_params=pltpu.CompilerParams(
            collective_id=collective_id, has_side_effects=True, vmem_limit_bytes=limit * MIB
        ),
        name=name,
    )


def shape(dims, dtype=F32):
    return jax.ShapeDtypeStruct(dims, dtype)


WB = D + 128


def columns(*rows):
    pad = jnp.zeros((128 - len(rows), rows[0].shape[1]), F32)
    turned = jnp.transpose(jnp.concatenate(list(rows) + [pad], axis=0))
    return [turned[:, k : k + 1] for k in range(len(rows))]


def row_sums(values, bounds):
    width = values.shape[1]
    high = values.astype(BF)
    low = (values - high.astype(F32)).astype(BF)
    lane, row = iota((8, width), 1), iota((8, width), 0)
    chosen = jnp.zeros((8, width), F32)
    for k, (first, last) in enumerate(bounds):
        chosen = jnp.where((row == k) & (lane >= first) & (lane < last), 1.0, chosen)
    chosen = chosen.astype(BF)
    return dot_nt(jnp.concatenate([chosen, chosen], axis=1), jnp.concatenate([high, low], axis=1))


PARTS = ((0, 128), (128, 192))


def turn_tables():
    half = HEAD_DIM // 2
    freq = np.float32(ROPE_BASE) ** (-(np.arange(half, dtype=np.float32) * np.float32(2.0) / np.float32(HEAD_DIM)))
    angles = np.arange(LENGTH, dtype=np.float32)[:, None] * freq.astype(np.float32)[None, :]
    c, s = np.cos(angles), np.sin(angles)
    cosine = np.concatenate([c, c, c, c], axis=1)
    sine = np.concatenate([-s, s, -s, s], axis=1)
    return cosine.astype(np.float32), sine.astype(np.float32)


def turn(u, cosine, sine):
    early = iota(u.shape, 1) % HEAD_DIM < HEAD_DIM // 2
    partner = jnp.where(early, pltpu.roll(u, 96, 1), pltpu.roll(u, 32, 1))
    return u * cosine + partner * sine


def block_rows(b):
    return pl.ds(pl.multiple_of(b * TOK, TOK), TOK)


def stack_heads(values):
    first = iota(values.shape, 1) < HEAD_DIM
    return jnp.concatenate([jnp.where(first, values, 0.0), jnp.where(first, 0.0, values)], axis=0)


def merge_heads(values):
    first = iota((TOK, 128), 1) < HEAD_DIM
    return jnp.where(first, values[:TOK], values[TOK:])


def front_kernel(
    tok, cot, wq, wk, wv, wo_in, router_in, ga_in, gq_in, gk_in, gf_in, seg, rts_in, cos_in, sin_in,
    x_all, g_all, lin_h, q_h, k_h, v_h, a_h, lse_h, hid_h, m_h, tab_h, att_h, misc_h, rout_h, whole_h, wcol_h,
    lin, q_o, k_o, v_o, a_o, lse_o, hid_o, m_o, tab_o, att_o, misc, rout_o, whole, wcol, hsem,
    x_s, cot_s, tiny, tiny_b, smalls, wsl, wo_f, wo_r, wg, w32, gains_s, cos_ref, sin_ref, sums, held,
    s_tok, r_tok, s_cot, r_cot, s_w, r_w, s_o, r_o, s_st, r_st, s_t, r_t, s_a, r_a, lsem,
):
    r = lax.axis_index("rep")
    e, x, c = place()
    others = ep_others(e)
    copies = rep_others(r)
    first = iota((TOK, 128), 1) < HEAD_DIM
    gain_a, gain_f, gain = misc.at[0:1], misc.at[1:2], misc.at[2:3, 0:256]
    lo, st = misc.at[8:16, 0:256], misc.at[16:32, 0:256]
    leaving = []

    def leave(*pairs):
        for src, dst in pairs:
            leaving.append(pltpu.make_async_copy(src, dst, hsem.at[len(leaving)]))
            leaving[-1].start()

    tables = [
        pltpu.make_async_copy(cos_in, cos_ref, lsem.at[2]),
        pltpu.make_async_copy(sin_in, sin_ref, lsem.at[3]),
        pltpu.make_async_copy(cot, cot_s, lsem.at[5]),
    ]

    def prepare_tiles():
        misc[...] = jnp.zeros((32, D), F32)

        tiny[...] = jnp.zeros((16, 128), F32)
        tiny[0:8, 0:EXPERTS] = router_in[...].astype(F32)
        for lane, ref in ((0, ga_in), (8, gq_in), (16, gk_in), (20, gf_in)):
            tiny[8:9, lane : lane + ref.shape[1]] = ref[...].astype(F32)
        tiny_b[...] = tiny[...].astype(BF)
        low_lanes = iota((8, 128), 1) < HEAD_DIM
        for d in range(EP):
            k_t = wk[:, (d // 2) * 128 : (d // 2 + 1) * 128].astype(F32)
            v_t = wv[:, (d // 2) * 128 : (d // 2 + 1) * 128].astype(F32)
            if d % 2:
                k_t = pltpu.roll(k_t, HEAD_DIM, 1)
            else:
                v_t = pltpu.roll(v_t, HEAD_DIM, 1)
            q_t = wq[:, d * 128 : (d + 1) * 128].astype(F32)
            wsl[d] = jnp.concatenate([q_t, jnp.where(low_lanes, k_t, v_t)], axis=0).astype(BF)
        wo_f[...] = wo_in[...].astype(F32)
        for copy in tables:
            copy.start()

    greet([{"ep": d} for d in others] + [{"rep": d} for d in copies], prepare_tiles)
    half_cols = pl.ds(pl.multiple_of(c * 512, 512), 512)
    other_cols = pl.ds(pl.multiple_of((1 - c) * 512, 512), 512)
    peer = ep_device(x, 1 - c)

    def whole_rows(start, size):
        return whole.at[pl.ds(pl.multiple_of(start, 16), size), half_cols]

    pairing = remote(wo_f.at[:, other_cols], wo_r, (s_o, r_o), 19, peer)
    mine = whole_rows(r * 64 + x * 16, 16)
    stage_o = [remote(mine, mine, (s_o, r_o), k, ep_device((x + 1 + k) % 4, c)) for k in range(3)]
    mine = whole_rows(r * 64, 64)
    spread_o = [remote(mine, mine, (s_o, r_o), 3 + k, {"rep": d}) for k, d in enumerate(copies)]
    mine = whole_rows(0, D)
    other_half = remote(mine, mine, (s_o, r_o), 18, peer)

    def cols_of(b):
        return wg.at[r, pl.ds(pl.multiple_of(b * 16, 16), 16)]

    stage_w = [remote(wsl.at[d], cols_of(e), (s_w, r_w), k, {"ep": d}) for k, d in enumerate(others)]
    stage_t = [remote(tiny_b, smalls.at[e], (s_t, r_t), k, {"ep": d}) for k, d in enumerate(others)]
    spread_w = [remote(wg.at[r], wg.at[r], (s_w, r_w), 7 + k, {"rep": d}) for k, d in enumerate(copies)]
    tokens = RingGather(tok, x_s, (s_tok, r_tok), lsem.at[0])
    grads = RingGather(cot_s, g_all, (s_cot, r_cot), lsem.at[1])
    for copy in stage_w + stage_t + [pairing]:
        copy.start()
    tokens.start()
    cols_of(e)[...] = wsl[e]
    smalls[e] = tiny_b[...]
    for copy in stage_w + stage_t:
        copy.wait_recv()
    router_tiles = [
        sum(pltpu.roll(smalls[4 * a + b][:8].astype(F32), 32 * b, 1) if b else smalls[4 * a][:8].astype(F32) for b in range(4))
        for a in range(2)
    ]
    gain_rows = [smalls[d][8:9].astype(F32) for d in range(EP)]
    wg[r, 128:160] = jnp.concatenate(router_tiles + gain_rows + [jnp.zeros((8, 128), F32)], axis=0).astype(BF)
    for copy in spread_w:
        copy.start()
    pairing.wait_recv()
    own_half, peer_half = wo_f[:, half_cols], wo_r[...]
    upper, lower = jnp.where(c == 0, own_half, peer_half), jnp.where(c == 0, peer_half, own_half)
    whole[pl.ds(pl.multiple_of(r * 64 + x * 16, 16), 16), half_cols] = jnp.concatenate([upper, lower], axis=0).astype(BF)
    for copy in stage_o:
        copy.start()
    tokens.forward_half()
    tables[2].wait()
    grads.start()
    tokens.forward_rest()

    routed = rts_in[...]
    hit = jnp.zeros((EXPERTS, TOK), F32)
    for k in range(TOP):
        hit = jnp.where(iota((EXPERTS, TOK), 0) == routed[k : k + 1], 1.0, hit)
    before = jnp.where(iota((TOK, TOK), 0) < iota((TOK, TOK), 1), 1.0, 0.0).astype(BF)
    slots = jnp.where(hit > 0.0, dot(hit.astype(BF), before), -1.0)
    segs = jnp.concatenate([seg[:, b * TOK : (b + 1) * TOK] for b in range(EP)], axis=0)
    opening = jnp.zeros((EP, TOK), F32)
    for value in range(2):
        count = jnp.sum(jnp.where(segs == value, 1.0, 0.0), axis=1, keepdims=True)
        opening = opening + jnp.where(segs > value, jnp.sum(count, axis=0, keepdims=True), 0.0)
    places = (iota((EP, TOK), 0) * TOK + iota((EP, TOK), 1)).astype(F32)
    lo[...] = jnp.maximum(opening, places - (WINDOW - 1))

    for copy in spread_w:
        copy.wait_recv()
    for copy in stage_o:
        copy.wait_recv()
    for copy in spread_o:
        copy.start()

    def unpack(b, carry):
        for d in range(EP):
            tile = wg[b, d * 16 : d * 16 + 16].astype(F32)
            rows = pl.ds(pl.multiple_of(b * 64 + d * 8, 8), 8)
            w32[rows, 0:128] = tile[0:8]
            w32[rows, 128:256] = tile[8:16]
        extra = wg[b, 128:160].astype(F32)
        for d in range(EP):
            tile = extra[d // 4 * 8 : d // 4 * 8 + 8]
            if d % 4:
                tile = pltpu.roll(tile, 128 - 32 * (d % 4), 1)
            w32[pl.ds(pl.multiple_of(b * 64 + d * 8, 8), 8), 256:384] = tile
        gains_s[pl.ds(pl.multiple_of(b * 8, 8), 8)] = extra[16:24]
        return carry

    lax.fori_loop(0, REP, unpack, 0)
    wcol[...] = w32[:, :256].astype(BF)
    rout_o[...] = jnp.transpose(w32[:, 256:384])[:EXPERTS].astype(BF)
    packed = gains_s[...].astype(BF)

    def spread_gain(width, group, base, shift):
        lane = base + iota((128, width), 1) % group
        picked = dot(packed, jnp.where(iota((128, width), 0) == lane, 1.0, 0.0).astype(BF))
        mine = iota((128, width), 0) == shift + iota((128, width), 1) // group
        return jnp.sum(jnp.where(mine, picked, 0.0), axis=0, keepdims=True)

    gain_a[...] = spread_gain(D, 8, 0, 0)
    gain_f[...] = spread_gain(D, 8, 20, 0)
    key_part = spread_gain(128, 4, 16, e * 16)
    gain[:, :128] = spread_gain(128, 8, 8, e * 16)
    gain[:, 128:] = jnp.where(iota((1, 128), 1) < HEAD_DIM, key_part, 1.0)

    leave((wcol, wcol_h), (rout_o, rout_h))
    tokens.first[4].wait_recv()
    tokens.own.wait()

    def project(k, carry):
        @pl.when(k == 2)
        def _():
            tokens.fwd_right.wait_recv()
            tokens.fwd_left.wait_recv()
            tokens.to_peer[2].start()
            tokens.to_peer[1].wait_recv()

        @pl.when(k == 4)
        def _():
            tokens.to_peer[0].wait_recv()

        @pl.when(k == 6)
        def _():
            tokens.to_peer[2].wait_recv()

        g = k // 2
        b = (2 * (x + g + g // 2 - 2 * (g // 3)) + k % 2) % EP
        rows = block_rows(b)
        values = x_s[rows].astype(F32)
        r1 = lax.rsqrt(jnp.mean(values * values, axis=1, keepdims=True) + EPSILON)
        normed = (values * r1 * gain_a[...]).astype(BF)
        out = dot(normed, wcol[...])
        lin[rows] = out
        both = row_sums(out * out, PARTS)
        sums[pl.ds(2 * b, 1)] = both[0:1]
        sums[pl.ds(2 * b + 1, 1)] = both[1:2]
        return carry

    lax.fori_loop(0, EP, project, 0)
    stats = [remote(sums, held.at[e], (s_st, r_st), k, {"ep": d}) for k, d in enumerate(others)]
    for copy in stats:
        copy.start()
    held[e] = sums[...]
    keep = pltpu.make_async_copy(x_s, x_all, lsem.at[4])
    keep.start()
    for copy in tables[:2]:
        copy.wait()
    for copy in stats:
        copy.wait_recv()
    total = held[0]
    for k in range(1, EP):
        total = total + held[k]
    st[...] = total
    grads.forward_half()
    leave((lin, lin_h), (misc, misc_h))

    def prepare(b, carry):
        rows = block_rows(b)
        cq, ck = columns(
            lax.rsqrt(st[pl.ds(2 * b, 1)] * (1.0 / D) + EPSILON),
            lax.rsqrt(st[pl.ds(2 * b + 1, 1)] * (1.0 / KV) + EPSILON),
        )
        cosine, sine = cos_ref[rows], sin_ref[rows]
        q_o[rows] = turn(lin[rows, :128] * cq * gain[:, :128], cosine, sine).astype(BF)
        kv = lin[rows, 128:]
        kv = jnp.where(first, turn(kv * ck * gain[:, 128:], cosine, sine), kv)
        other = pltpu.roll(kv, HEAD_DIM, 1)
        k_o[rows] = jnp.where(first, kv, other).astype(BF)
        v_o[rows] = jnp.where(first, other, kv).astype(BF)
        return carry

    lax.fori_loop(0, EP, prepare, 0, unroll=2)
    leave((q_o, q_h), (k_o, k_h), (v_o, v_h))

    def heads(i, source):
        cols = pl.ds(pl.multiple_of(source * 128, 128), 128)
        return pltpu.make_async_remote_copy(
            src_ref=a_o.at[block_rows(i)],
            dst_ref=att_o.at[:, cols],
            send_sem=s_a.at[i],
            recv_sem=r_a.at[source],
            device_id={"ep": i},
            device_id_type=MESH,
        )

    def attend_block(i, n):
        rows = block_rows(i)
        past = (n - 1) * TOK
        q2 = stack_heads(q_o[rows].astype(F32) * HEAD_DIM ** (-0.5)).astype(BF)
        (lo_col,) = columns(lo[pl.ds(i, 1)])
        low = jnp.concatenate([lo_col, lo_col], axis=0)
        own_key = (iota((2 * TOK, TOK), 1) + i * TOK).astype(F32)
        query = (iota((2 * TOK, TOK), 0) % TOK + i * TOK).astype(F32)
        s_own = jnp.where((own_key >= low) & (own_key <= query), dot_nt(q2, k_o[rows]), MASKED)
        m = jnp.max(s_own, axis=1, keepdims=True)
        if past:
            early = pl.ds(pl.multiple_of((i - n + 1) * TOK, TOK), past)
            key = (iota((2 * TOK, past), 1) + (i - n + 1) * TOK).astype(F32)
            s = jnp.where(key >= low, dot_nt(q2, k_o[early]), MASKED)
            m = jnp.maximum(m, jnp.max(s, axis=1, keepdims=True))
        p_own = jnp.exp(s_own - m)
        total = jnp.sum(p_own, axis=1, keepdims=True)
        out = dot(p_own.astype(BF), v_o[rows])
        if past:
            p = jnp.exp(s - m)
            total = total + jnp.sum(p, axis=1, keepdims=True)
            out = out + dot(p.astype(BF), v_o[early])
        a_o[rows] = merge_heads(out / total).astype(BF)
        lse = jnp.broadcast_to(m + jnp.log(total), (2 * TOK, 128))
        lse_o[i] = jnp.transpose(lse)[:8]

        @pl.when(i != e)
        def _():
            heads(i, e).start()

        @pl.when(i == e)
        def _():
            att_o[:, pl.ds(pl.multiple_of(e * 128, 128), 128)] = a_o[rows]

    def later(i, carry):
        attend_block(i, 5)

        @pl.when(i == 5)
        def _():
            grads.fwd_right.wait_recv()
            grads.fwd_left.wait_recv()
            grads.to_peer[2].start()
            other_half.wait_recv()
            whole_out.start()

        return carry

    whole_out = pltpu.make_async_copy(whole, whole_h, hsem.at[len(leaving)])
    leaving.append(whole_out)

    for i in range(4):
        attend_block(i, i + 1)
    grads.forward_rest()
    for copy in spread_o:
        copy.wait_recv()
    other_half.start()
    lax.fori_loop(4, EP, later, 0, unroll=2)

    leave((a_o, a_h), (lse_o, lse_h))
    for d in others:
        heads(d, d).wait_recv()
    leave((att_o, att_h))

    hidden = x_s[block_rows(e)].astype(F32) + dot(att_o[...], whole[...])
    hid_o[...] = hidden
    r2 = lax.rsqrt(jnp.mean(hidden * hidden, axis=1, keepdims=True) + EPSILON)
    moe_in = (hidden * r2 * gain_f[...]).astype(BF)
    m_o[...] = moe_in
    leave((hid_o, hid_h), (m_o, m_h))
    logits = dot_nt(rout_o[...], moe_in)
    chosen = hit > 0.0
    logits = jnp.where(chosen, logits, MASKED)
    raised = jnp.where(chosen, jnp.exp(logits - jnp.max(logits, axis=0, keepdims=True)), 0.0)
    gates = raised / jnp.sum(raised, axis=0, keepdims=True)
    for d in range(EP):
        part = slice(d * LOCAL, (d + 1) * LOCAL)
        tab_o[d] = jnp.concatenate([slots[part], gates[part]], axis=0)
    leave((tab_o, tab_h))

    grads.first[4].wait_recv()
    for copy in grads.to_peer:
        copy.wait_recv()
    grads.own.wait()
    keep.wait()
    for copy in leaving:
        copy.wait()
    for d in others:
        heads(d, d).wait_send()
    for ring in (tokens, grads):
        for copy in ring.first + [ring.fwd_right, ring.fwd_left] + ring.to_peer:
            copy.wait_send()
    for copy in stage_w + stage_t + stage_o + spread_w + spread_o + stats + [other_half, pairing]:
        copy.wait_send()


def front(*args):
    results = [
        shape((LENGTH, D), BF),
        shape((LENGTH, D), BF),
        shape((LENGTH, 256)),
        shape((LENGTH, 128), BF),
        shape((LENGTH, 128), BF),
        shape((LENGTH, 128), BF),
        shape((LENGTH, 128), BF),
        shape((EP, 8, 2 * TOK)),
        shape((TOK, D)),
        shape((TOK, D), BF),
        shape((EP, 2 * LOCAL, TOK)),
        shape((TOK, D), BF),
        shape((32, D)),
        shape((EXPERTS, D), BF),
        shape((D, D), BF),
        shape((D, 256), BF),
    ]
    return comm_call(
        front_kernel,
        "front",
        1,
        results,
        [ANY, ANY] + [VM] * 11 + [ANY, ANY],
        [ANY] * len(results),
        [pltpu.VMEM(a.shape, a.dtype) for a in results[2:]]
        + [
            DMA((14,)),
            pltpu.VMEM((LENGTH, D), BF),
            pltpu.VMEM((TOK, D), BF),
            pltpu.VMEM((16, 128), F32),
            pltpu.VMEM((16, 128), BF),
            pltpu.VMEM((EP, 16, 128), BF),
            pltpu.VMEM((EP, 16, 128), BF),
            pltpu.VMEM((8, D), F32),
            pltpu.VMEM((8, 512), F32),
            pltpu.VMEM((REP, 160, 128), BF),
            pltpu.VMEM((D, 384), F32),
            pltpu.VMEM((128, 128), F32),
            pltpu.VMEM((LENGTH, 128), F32),
            pltpu.VMEM((LENGTH, 128), F32),
            pltpu.VMEM((16, 256), F32),
            pltpu.VMEM((EP, 16, 256), F32),
        ]
        + [DMA((10,))] * 4
        + [DMA((23,))] * 4
        + [DMA((7,))] * 4
        + [DMA((8,))] * 2
        + [DMA((6,))],
        limit=60,
    )(*args)


class ChipReduce:
    SEMS = 10
    STEP = 64

    def __init__(self, n, swo, snd, pc, rcv, hop, sems):
        e, x, c = place()
        self.n, self.h = n, n // 2
        h = n // 2
        self.snd, self.pc, self.rcv, self.hop = snd, pc, rcv, hop
        right, left = ep_device((x + 1) % 4, c), ep_device((x + 3) % 4, c)
        peer = ep_device(x, 1 - c)
        self.swap = lambda k: remote(swo.at[k], pc.at[k], sems, k, peer)
        low, high = pl.ds(0, h), pl.ds(h, h)
        self.opp = [
            remote(snd.at[0, low], hop.at[low], sems, 4, right),
            remote(snd.at[0, high], hop.at[high], sems, 5, left),
        ]
        self.near = [
            remote(snd.at[2, high], rcv.at[0, high], sems, 6, right),
            remote(snd.at[1, low], rcv.at[1, low], sems, 7, left),
        ]
        self.far = [
            remote(snd.at[2, low], rcv.at[0, low], sems, 8, right),
            remote(snd.at[1, high], rcv.at[1, high], sems, 9, left),
        ]

    def rows_loop(self, low, count, body):
        step = self.STEP

        def loop(i, carry):
            body(pl.ds(pl.multiple_of(low + i * step, 16), step))
            return carry

        lax.fori_loop(0, count // step, loop, 0)

    def merge(self, k):
        def body(s):
            self.snd[k, s] = (self.snd[k, s].astype(F32) + self.pc[k, s].astype(F32)).astype(BF)

        self.swap(k).wait_recv()
        self.rows_loop(0, self.n, body)

    def merge_hop(self, k, low):
        def body(s):
            self.snd[k, s] = (self.snd[k, s].astype(F32) + self.hop[s].astype(F32)).astype(BF)

        self.rows_loop(low, self.h, body)

    def send_opp(self):
        self.merge(0)
        for copy in self.opp:
            copy.start()

    def near_right(self):
        self.merge(2)
        self.near[0].start()

    def near_left(self):
        self.merge(1)
        self.near[1].start()

    def send_near(self):
        self.near_right()
        self.near_left()

    def far_right(self):
        self.opp[0].wait_recv()
        self.merge_hop(2, 0)
        self.far[0].start()

    def far_left(self):
        self.opp[1].wait_recv()
        self.merge_hop(1, self.h)
        self.far[1].start()

    def send_far(self):
        self.far_right()
        self.far_left()

    def finish(self, out_ref):
        for copy in self.near + self.far:
            copy.wait_recv()

        def body(s):
            out_ref[s] = self.snd[3, s].astype(F32) + (
                self.rcv[0, s].astype(F32) + self.rcv[1, s].astype(F32)
            )

        self.rows_loop(0, self.n, body)
        for copy in [self.swap(k) for k in range(4)] + self.opp + self.near + self.far:
            copy.wait_send()


PAIR = 2
ROWS = EP * CAP
CHIP = 2 * CAP
BLOCK = 96


def chip_rows(q):
    return pl.ds(pl.multiple_of(q * CHIP, 16), CHIP)


def chip_tokens(q):
    return pl.ds(pl.multiple_of(q * 2 * TOK, 2 * TOK), 2 * TOK)


def expert_hits(tab, e, n, q):
    row = slice(n, n + 1)
    second = tab[2 * q + 1, row]
    slots = jnp.concatenate([tab[2 * q, row], jnp.where(second >= 0.0, second + CAP, -1.0)], axis=1)
    return iota((CHIP, 2 * TOK), 0).astype(F32) == slots


def one_hot(hit):
    return jnp.where(hit, 1.0, 0.0).astype(BF)


def expert_chip(q, e, start, tab, m_ref, g_ref, wgu, wd, a_s, act_s, gp_s, dgu_s, y_s, z_s, ggt, between=None):
    hits = [expert_hits(tab, e, start + n, q) for n in range(PAIR)]
    chosen = jnp.concatenate([one_hot(hit) for hit in hits], axis=0)
    rows = chip_rows(q)
    a_both = dot(chosen, m_ref[chip_tokens(q)]).astype(BF)
    c_both = dot(chosen, g_ref[chip_tokens(q)]).astype(BF)
    for n in range(PAIR):
        part = slice(n * CHIP, (n + 1) * CHIP)
        row = slice(LOCAL + start + n, LOCAL + start + n + 1)
        gates = jnp.concatenate([tab[2 * q, row], tab[2 * q + 1, row]], axis=1)
        weight = jnp.sum(jnp.where(hits[n], gates, 0.0), axis=1, keepdims=True)
        a, cot = a_both[part], c_both[part]
        lin = dot(a, wgu[n])
        back = dot_nt(cot, wd[n])
        gate_lin, up_lin = lin[:, :FF], lin[:, FF:]
        sig = jax.nn.sigmoid(gate_lin)
        silu = gate_lin * sig
        act = silu * up_lin
        act_low = act.astype(BF)
        produced = dot(act_low, wd[n]).astype(BF).astype(F32)
        gg = jnp.sum(act * back, axis=1, keepdims=True)
        back = back * weight
        dgate = (back * up_lin * sig * (1.0 + gate_lin * (1.0 - sig))).astype(BF)
        dup = (back * silu).astype(BF)
        dgu = jnp.concatenate([dgate, dup], axis=1)
        a_s[n, rows] = a
        act_s[n, rows] = act_low
        gp_s[n, rows] = (weight * cot.astype(F32)).astype(BF)
        dgu_s[n, rows] = dgu
        y_s[n, rows] = (weight * produced).astype(BF)
        z_s[n, rows] = dot_nt(dgu, wgu[n]).astype(BF)
        gg_row = jnp.sum(jnp.where(hits[n], gg, 0.0), axis=0, keepdims=True)
        ggt[2 * q, n : n + 1] = gg_row[:, :TOK]
        ggt[2 * q + 1, n : n + 1] = gg_row[:, TOK:]
        if n == 0 and between is not None:
            between()


def expert_grads(n, a_s, act_s, gp_s, dgu_s, eg, eg_o, sems):
    copies = []
    for k, (first, size) in enumerate(((0, 64), (64, 32))):
        left, right = ((a_s, dgu_s), (act_s, gp_s))[k]
        eg[n, :, first : first + size] = dot_tn(left[n], right[n]).astype(BF).reshape(REP, size, D)
        some = pl.ds(first, size)
        copies.append(pltpu.make_async_copy(eg.at[n, :, some], eg_o.at[n, :, some], sems.at[2 * n + k]))
        copies[-1].start()
    return copies


def load_weights(start, wg_in, wu_in, wd_in, wgu, wd, sems):
    some = pl.ds(start, PAIR)
    return [
        pltpu.make_async_copy(wg_in.at[some], wgu.at[:, :, pl.ds(0, FF)], sems.at[0]),
        pltpu.make_async_copy(wu_in.at[some], wgu.at[:, :, pl.ds(FF, FF)], sems.at[1]),
        pltpu.make_async_copy(wd_in.at[some], wd, sems.at[2]),
    ]


def send_gates(ggt, gg_o, e, sems, lsem):
    copies = [remote(ggt.at[d], gg_o.at[e], sems, k, {"ep": d}) for k, d in enumerate(ep_others(e))]
    return copies, pltpu.make_async_copy(ggt.at[e], gg_o.at[e], lsem)


def experts_first_kernel(
    m_in, t_in, g_in, wg_in, wu_in, wd_in, m_o, tab_o, y_o, z_o, gg_o, eg_o,
    m_ref, tab, g_ref, wgu, wd, a_s, act_s, gp_s, dgu_s, y_s, z_s, ggt, eg,
    s_m, r_m, s_t, r_t, s_g, r_g, lsem, wsem, gsem, esem, ksem,
):
    e, x, c = place()
    others = ep_others(e)
    ring = RingGather(m_in, m_ref, (s_m, r_m), lsem.at[0])
    tables = [remote(t_in.at[d], tab.at[e], (s_t, r_t), k, {"ep": d}) for k, d in enumerate(others)]
    own = pltpu.make_async_copy(t_in.at[e], tab.at[e], lsem.at[1])
    loads = load_weights(0, wg_in, wu_in, wd_in, wgu, wd, wsem)
    cots = [
        pltpu.make_async_copy(g_in.at[chip_tokens(q)], g_ref.at[chip_tokens(q)], gsem.at[k])
        for k, q in enumerate([x, (x + 1) % 4, (x + 3) % 4, (x + 2) % 4])
    ]

    def fetch():
        for copy in [own] + loads + cots:
            copy.start()
        ggt[...] = jnp.zeros((EP, 8, TOK), F32)

    greet([{"ep": d} for d in others], fetch)
    for copy in tables:
        copy.start()
    ring.start()

    def keep(k, q):
        rows = chip_rows(q)
        return [
            pltpu.make_async_copy(m_ref.at[chip_tokens(q)], m_o.at[chip_tokens(q)], ksem.at[0, k]),
            pltpu.make_async_copy(y_s.at[:, rows], y_o.at[:, rows], ksem.at[1, k]),
            pltpu.make_async_copy(z_s.at[:, rows], z_o.at[:, rows], ksem.at[2, k]),
        ]

    def chips(k, carry):
        @pl.when(k == 0)
        def _():
            ring.first[0].wait_recv()
            ring.fwd_right.start()
            ring.first[1].wait_recv()
            ring.fwd_left.start()
            ring.first[4].wait_recv()
            ring.own.wait()
            own.wait()
            for copy in tables:
                copy.wait_recv()
            for copy in loads:
                copy.wait()
            cots[0].wait()

        @pl.when(k == 1)
        def _():
            ring.first[3].wait_recv()
            ring.to_peer[1].start()
            ring.first[2].wait_recv()
            ring.to_peer[0].start()
            ring.to_peer[1].wait_recv()
            cots[1].wait()

        @pl.when(k == 2)
        def _():
            ring.fwd_right.wait_recv()
            ring.fwd_left.wait_recv()
            ring.to_peer[2].start()
            ring.to_peer[0].wait_recv()
            cots[2].wait()

        @pl.when(k == 3)
        def _():
            ring.to_peer[2].wait_recv()
            cots[3].wait()

        q = (x + k + k // 2 - 2 * (k // 3)) % 4
        expert_chip(q, e, 0, tab, m_ref, g_ref, wgu, wd, a_s, act_s, gp_s, dgu_s, y_s, z_s, ggt)
        for copy in keep(k, q):
            copy.start()
        return carry

    lax.fori_loop(0, 4, chips, 0)
    gates, own_gates = send_gates(ggt, gg_o, e, (s_g, r_g), lsem.at[3])
    states = [pltpu.make_async_copy(tab, tab_o, lsem.at[2])]
    for copy in gates + [own_gates] + states:
        copy.start()
    for n in range(PAIR):
        states += expert_grads(n, a_s, act_s, gp_s, dgu_s, eg, eg_o, esem)
    for k, q in enumerate([x, (x + 1) % 4, (x + 3) % 4, (x + 2) % 4]):
        states += keep(k, q)
    for copy in states + [own_gates]:
        copy.wait()
    for copy in gates:
        copy.wait_recv()
    for copy in ring.first + [ring.fwd_right, ring.fwd_left] + ring.to_peer + tables + gates:
        copy.wait_send()


def pair_scratch():
    return [
        pltpu.VMEM((LENGTH, D), BF),
        pltpu.VMEM((EP, 2 * LOCAL, TOK), F32),
        pltpu.VMEM((LENGTH, D), BF),
        pltpu.VMEM((PAIR, D, 2 * FF), BF),
        pltpu.VMEM((PAIR, FF, D), BF),
        pltpu.VMEM((PAIR, ROWS, D), BF),
        pltpu.VMEM((PAIR, ROWS, FF), BF),
        pltpu.VMEM((PAIR, ROWS, D), BF),
        pltpu.VMEM((PAIR, ROWS, D), BF),
        pltpu.VMEM((PAIR, ROWS, D), BF),
        pltpu.VMEM((PAIR, ROWS, D), BF),
        pltpu.VMEM((EP, 8, TOK), F32),
        pltpu.VMEM((PAIR, REP, BLOCK, D), BF),
    ]


def experts_first(m, t, g_all, wg, wu, wd):
    return comm_call(
        experts_first_kernel,
        "experts_first",
        2,
        [
            shape((LENGTH, D), BF),
            shape((EP, 2 * LOCAL, TOK)),
            shape((PAIR, ROWS, D), BF),
            shape((PAIR, ROWS, D), BF),
            shape((EP, 8, TOK)),
            shape((PAIR, REP, BLOCK, D), BF),
        ],
        [ANY] * 6,
        [ANY] * 6,
        pair_scratch()
        + [DMA((10,))] * 2
        + [DMA((7,))] * 4
        + [DMA((4,)), DMA((3,)), DMA((4,)), DMA((4,)), DMA((3, 4))],
        limit=60,
    )(m, t, g_all, wg, wu, wd)


def experts_last_kernel(
    m_in, t_in, y_in, z_in, g_in, wg_in, wu_in, wd_in, gm_o, mix_o, gg_o, eg_o,
    m_ref, tab, g_ref, wgu, wd, a_s, act_s, gp_s, dgu_s, y_s, z_s, ggt, eg,
    y_f, z_f, gm, swo, snd, pc, rcv, hop, mix_z, mix_y,
    s_r, r_r, s_g, r_g, lsem, wsem, gsem, msem, esem, osem,
):
    e, x, c = place()
    order = [(x + 2) % 4, (x + 3) % 4, (x + 1) % 4, x]
    loads = [pltpu.make_async_copy(t_in, tab, lsem.at[0])] + load_weights(2, wg_in, wu_in, wd_in, wgu, wd, wsem)
    rows = [
        (
            pltpu.make_async_copy(m_in.at[chip_tokens(q)], m_ref.at[chip_tokens(q)], msem.at[k]),
            pltpu.make_async_copy(g_in.at[chip_tokens(q)], g_ref.at[chip_tokens(q)], gsem.at[k]),
        )
        for k, q in enumerate(order)
    ]
    firsts = [pltpu.make_async_copy(z_in, z_f, lsem.at[1]), pltpu.make_async_copy(y_in, y_f, lsem.at[2])]
    for copy in loads + list(rows[0]) + [firsts[0]] + list(rows[1] + rows[2] + rows[3]) + [firsts[1]]:
        copy.start()
    greet([{"ep": d} for d in ep_others(e)])
    red = ChipReduce(TOK, swo, snd, pc, rcv, hop, (s_r, r_r))
    ggt[...] = jnp.zeros((EP, 8, TOK), F32)

    def combine(q, early, late):
        chosen = jnp.concatenate([one_hot(expert_hits(tab, e, n, q)) for n in range(LOCAL)], axis=0)
        part = chip_rows(q)
        values = [ref[n, part] for ref in (early, late) for n in range(PAIR)]
        return dot_tn(chosen, jnp.concatenate(values, axis=0)).astype(BF)

    for copy in loads:
        copy.wait()

    def chips(k, carry):
        for step in range(4):

            @pl.when(k == step)
            def _(step=step):
                for copy in rows[step]:
                    copy.wait()

        q = (x + 2 + k - (k // 2) * (2 * k - 1)) % 4

        def send():
            @pl.when(k == 1)
            def _():
                red.send_opp()

            @pl.when(k == 2)
            def _():
                red.near_left()

            @pl.when(k == 3)
            def _():
                red.near_right()
                red.far_right()
                red.far_left()

        expert_chip(q, e, 2, tab, m_ref, g_ref, wgu, wd, a_s, act_s, gp_s, dgu_s, y_s, z_s, ggt, send)

        @pl.when(k == 0)
        def _():
            firsts[0].wait()

        mix_z[...] = combine(q, z_f, z_s)
        swo[k] = mix_z[pl.ds(pl.multiple_of((1 - c) * TOK, TOK), TOK)]
        red.swap(k).start()
        snd[k] = mix_z[pl.ds(pl.multiple_of(c * TOK, TOK), TOK)]
        return carry

    lax.fori_loop(0, 4, chips, 0)
    gates, own_gates = send_gates(ggt, gg_o, e, (s_g, r_g), lsem.at[3])
    for copy in gates + [own_gates]:
        copy.start()
    states = []
    for n in range(PAIR):
        states += expert_grads(n, a_s, act_s, gp_s, dgu_s, eg, eg_o, esem)
    red.merge(3)
    firsts[1].wait()

    def mixture(q, carry):
        values = combine(q, y_f, y_s)

        @pl.when(q > 0)
        def _():
            pltpu.make_async_copy(mix_y, mix_o.at[chip_tokens(q)], osem).wait()

        mix_y[...] = values
        pltpu.make_async_copy(mix_y, mix_o.at[chip_tokens(q)], osem).start()
        return carry

    lax.fori_loop(0, 4, mixture, 0)
    red.finish(gm)
    last = pltpu.make_async_copy(gm, gm_o, lsem.at[4])
    last.start()
    pltpu.make_async_copy(mix_y, mix_o.at[chip_tokens(3)], osem).wait()
    for copy in states + [own_gates, last]:
        copy.wait()
    for copy in gates:
        copy.wait_recv()
    for copy in gates:
        copy.wait_send()


def experts_last(m, t, y, z, g_all, wg, wu, wd):
    return comm_call(
        experts_last_kernel,
        "experts_last",
        4,
        [
            shape((TOK, D)),
            shape((LENGTH, D), BF),
            shape((EP, 8, TOK)),
            shape((PAIR, REP, BLOCK, D), BF),
        ],
        [ANY] * 8,
        [ANY] * 4,
        pair_scratch()
        + [
            pltpu.VMEM((PAIR, ROWS, D), BF),
            pltpu.VMEM((PAIR, ROWS, D), BF),
            pltpu.VMEM((TOK, D), F32),
            pltpu.VMEM((4, TOK, D), BF),
            pltpu.VMEM((4, TOK, D), BF),
            pltpu.VMEM((4, TOK, D), BF),
            pltpu.VMEM((2, TOK, D), BF),
            pltpu.VMEM((TOK, D), BF),
            pltpu.VMEM((2 * TOK, D), BF),
            pltpu.VMEM((2 * TOK, D), BF),
        ]
        + [DMA((10,))] * 2
        + [DMA((7,))] * 2
        + [DMA((5,)), DMA((3,)), DMA((4,)), DMA((4,)), DMA((4,)), DMA(())],
        limit=63,
    )(m, t, y, z, g_all, wg, wu, wd)


KEPT = 8


def back_kernel(
    eg_in, mix_in, gm_in, gg1_in, gg2_in, tab_in, hid_in, m_in, cot_in, att_in, misc_in, rout_in, whole_in, wcol_in, x_in, lin_in,
    q_in, k_in, v_in, a_in, lse_in, cos_in, sin_in,
    out_o, ig_o, gq_o, gk_o, gv_o, go_o, pack_o, eg_o,
    gm, gg1, gg2, tab, hid, cot, misc, rout, wcol, x_s, lin, q_s, k_s, v_s, a_s, lse, cos_ref, sin_ref,
    gh, ga_s, go, q2_s, p_s, dk, dv, u_s, sums, st2, held, wb, wsum, wheld,
    dwt, dws, dheld, dsum, dw_o, vec, vheld, vtot, vheld2, swo, snd, pc1, rcv1, hop1, rcv2, snd3, pc3, rcv3, hop3,
    s_1, r_1, s_2, r_2, s_3, r_3, s_go, r_go, s_st, r_st, s_w, r_w, s_d, r_d, s_e, r_e, s_v, r_v, s_v2, r_v2, lsem, l_1, l_3, esem, xsem,
    out_s, gq_s, gk_s, gv_s, go_s, pack_s, eg_s,
    za, zb, zc, zd, ze, zf, ya, yb, yc, yd, ye, yf, s_z, r_z, s_y, r_y, l_z, l_y,
):
    r = lax.axis_index("rep")
    e, x, c = place()
    others = ep_others(e)
    copies = rep_others(r)
    first = iota((TOK, 128), 1) < HEAD_DIM
    gain_a, gain_f, gain = misc.at[0:1], misc.at[1:2], misc.at[2:3, 0:256]
    lo, st = misc.at[8:16, 0:256], misc.at[16:32, 0:256]
    red1 = RingReduce(mix_in, TOK, pc1, snd, rcv1, hop1, (s_1, r_1), l_1)
    red2 = ChipReduce(TOK, swo, snd, pc1, rcv2, hop1, (s_2, r_2))
    red3 = RingReduce(wb, 128, pc3, snd3, rcv3, hop3, (s_3, r_3), l_3)
    by_z = GridReduce(True, eg_in, 0, za, zb, zc, zd, ze, zf, (s_z, r_z), l_z)
    by_y = GridReduce(False, eg_in, FF, ya, yb, yc, yd, ye, yf, (s_y, r_y), l_y)
    loads = [
        pltpu.make_async_copy(src, dst, lsem.at[k])
        for k, (src, dst) in enumerate(
            [
                (misc_in, misc), (gm_in, gm), (gg1_in, gg1), (gg2_in, gg2), (tab_in, tab), (hid_in, hid),
                (cot_in, cot), (rout_in, rout), (whole_in, wb.at[:, pl.ds(0, D)]), (q_in, q_s), (k_in, k_s), (lse_in, lse),
                (m_in, rcv2.at[0]), (att_in, rcv2.at[1]), (v_in, v_s), (a_in, a_s), (cos_in, cos_ref), (sin_in, sin_ref),
                (lin_in, lin), (wcol_in, wcol),
            ]
        )
    ]
    chips_order = [(x + 2) % 4, (x + 3) % 4, (x + 1) % 4, x]

    def x_load(k):
        return pltpu.make_async_copy(x_in.at[chip_tokens(chips_order[k])], x_s.at[k % 2], xsem.at[k % 2])


    def fetch():
        for copy in loads + [x_load(0), x_load(1)] + by_z.load + by_y.load:
            copy.start()

    greet([{"ep": d} for d in others] + [{"rep": d} for d in copies], fetch)
    red1.start()
    for copy in loads[:9]:
        copy.wait()

    def base(i):
        cut = jnp.minimum(i, 4)
        return cut * (cut + 1) // 2 + 5 * jnp.maximum(i - 4, 0)

    def spans(i, n):
        keys = pl.ds(pl.multiple_of((i - n + 1) * TOK, TOK), n * TOK)
        return keys, pl.ds(pl.multiple_of(base(i) * TOK, TOK), n * TOK)

    def probabilities(i, n):
        _, held_rows = spans(i, n)
        p_s[held_rows] = make_probabilities(i, n)

    def make_probabilities(i, n):
        keys, _ = spans(i, n)
        q2 = stack_heads(q_s[block_rows(i)].astype(F32) * HEAD_DIM ** (-0.5)).astype(BF)
        q2_s[i] = q2
        top = lse[i][0:1]
        low = jnp.concatenate([lo[pl.ds(i, 1)]] * 2, axis=1)
        key = (iota((n * TOK, 2 * TOK), 0) + (i - n + 1) * TOK).astype(F32)
        query = (iota((n * TOK, 2 * TOK), 1) % TOK + i * TOK).astype(F32)
        allowed = (key >= low) & (key <= query)
        return jnp.where(allowed, jnp.exp(dot_nt(k_s[keys], q2) - top), 0.0).astype(BF)

    def probabilities_later(i, carry):
        probabilities(i, 5)

        @pl.when(i == 4)
        def _():
            red1.push_opp()

        @pl.when(i == 5)
        def _():
            red1.push_near()

        return carry


    hidden = hid[...]
    weights = jnp.concatenate([tab[d][LOCAL:] for d in range(EP)], axis=0)
    grads = jnp.concatenate([ref[d][:PAIR] for d in range(EP) for ref in (gg1, gg2)], axis=0)
    mean = jnp.sum(weights * grads, axis=0, keepdims=True)
    grad_logits = weights * (grads - mean)
    grad_moe = gm[...] + dot_tn(grad_logits.astype(BF), rout[...])
    r2 = lax.rsqrt(jnp.mean(hidden * hidden, axis=1, keepdims=True) + EPSILON)
    n = hidden * r2
    u = grad_moe * gain_f[...]
    grad_hidden = cot[...].astype(F32) + r2 * (u - n * jnp.mean(u * n, axis=1, keepdims=True))
    gh[...] = grad_hidden
    branch = grad_hidden.astype(BF)
    ga_s[...] = dot_nt(branch, wb[:, :D]).astype(BF)

    def own_cols(ref, b):
        return ref.at[:, pl.ds(pl.multiple_of(b * 128, 128), 128)]

    heads = [
        remote(own_cols(ga_s, d), go.at[block_rows(e)], (s_go, r_go), k, {"ep": d}) for k, d in enumerate(others)
    ]
    for copy in heads:
        copy.start()
    by_z.push()
    by_y.push()
    go[block_rows(e)] = own_cols(ga_s, e)[...]
    for copy in loads[9:12]:
        copy.wait()
    for i in range(4):
        probabilities(i, i + 1)
    lax.fori_loop(4, KEPT, probabilities_later, 0)
    for copy in loads[12:]:
        copy.wait()
    for copy in heads:
        copy.wait_recv()
    ffn = jnp.sum(grad_moe * n, axis=0, keepdims=True)
    logit_rows = jnp.transpose(jnp.concatenate([grad_logits, jnp.zeros((96, TOK), F32)], axis=0)).astype(BF)
    router_rows = dot_tn(rcv2[0], logit_rows)
    vec[...] = jnp.zeros((8, D), F32)
    vec[3:4] = ffn
    router_rows = router_rows.reshape(REP, EP, 8, 128)
    for d in range(EP):
        wb[d * 128 : (d + 1) * 128, D:] = router_rows[:, d].reshape(128, 128).astype(BF)
    for cols in range(0, D, 256):
        out_rows = dot_tn(rcv2[1], branch[:, cols : cols + 256]).reshape(REP, EP, 8, 256)
        for d in range(EP):
            wb[d * 128 : (d + 1) * 128, cols : cols + 256] = out_rows[:, d].reshape(128, 256).astype(BF)
    red3.start()
    by_z.stage.relay()
    by_y.stage.relay()
    dk[...] = jnp.zeros((LENGTH, 128), F32)
    dv[...] = jnp.zeros((LENGTH, 128), F32)

    def part(ref, b, size):
        return ref.at[pl.ds(pl.multiple_of(b * size, 8), size)]

    spread_w = [remote(part(wsum, d, 8), wheld.at[r], (s_w, r_w), k, {"rep": d}) for k, d in enumerate(copies)]

    def attend_back(i, n):
        keys, held_rows = spans(i, n)
        rows = block_rows(i)
        grad = stack_heads(go[rows].astype(F32))
        do2 = grad.astype(BF)
        out = a_s[rows].astype(F32)
        settle = row_sums(grad * jnp.concatenate([out, out], axis=0), ((0, 128),))[0:1]
        p = p_s[held_rows]
        ds = (p.astype(F32) * (dot_nt(v_s[keys], do2) - settle)).astype(BF)
        dv[keys] += dot(p, do2)
        dk[keys] += dot(ds, q2_s[i])
        dq = dot_tn(k_s[keys], ds)
        u_s[rows, :128] = merge_heads(jnp.transpose(dq)) * HEAD_DIM ** (-0.5)

    def attend_back_later(i, carry):
        attend_back(i, 5)
        return carry

    for i in range(4):
        attend_back(i, i + 1)
    red3.push_opp()
    red3.push_near()
    lax.fori_loop(4, 6, attend_back_later, 0, unroll=True)
    red1.relay()
    red3.relay()
    lax.fori_loop(6, EP, attend_back_later, 0, unroll=True)

    def close(b, carry):
        rows = block_rows(b)
        grad_k, grad_v = dk[rows], dv[rows]
        grad_k = grad_k + pltpu.roll(grad_k, HEAD_DIM, 1)
        grad_v = grad_v + pltpu.roll(grad_v, HEAD_DIM, 1)
        both = jnp.where(first, grad_k, grad_v).astype(BF).astype(F32)
        cosine, sine = cos_ref[rows], -sin_ref[rows]
        both = jnp.where(first, turn(both, cosine, sine), both)
        grad_q = turn(u_s[rows, :128].astype(BF).astype(F32), cosine, sine)
        u_s[rows, :128] = grad_q
        u_s[rows, 128:] = both
        cq, ck = columns(
            lax.rsqrt(st[pl.ds(2 * b, 1)] * (1.0 / D) + EPSILON),
            lax.rsqrt(st[pl.ds(2 * b + 1, 1)] * (1.0 / KV) + EPSILON),
        )
        products = jnp.concatenate([grad_q * cq, both * ck], axis=1) * gain[...] * lin[rows]
        pair = row_sums(products, PARTS)
        sums[pl.ds(2 * b, 1)] = pair[0:1]
        sums[pl.ds(2 * b + 1, 1)] = pair[1:2]
        return carry

    lax.fori_loop(0, EP, close, 0, unroll=2)
    stats = [remote(sums, held.at[e], (s_st, r_st), k, {"ep": d}) for k, d in enumerate(others)]
    for copy in stats:
        copy.start()
    held[e] = sums[...]
    red1.finish(gm)
    out_s[...] = (hid[...] + gm[...]).astype(BF)
    ends = [pltpu.make_async_copy(out_s, out_o, esem.at[0])]
    ends[0].start()
    red3.finish(wsum)
    for copy in spread_w:
        copy.start()
    wheld[r] = part(wsum, r, 8)[...]
    by_z.turn()
    by_y.turn()
    dwt[...] = jnp.zeros((256, D), F32)
    for copy in stats:
        copy.wait_recv()
    total = held[0]
    for k in range(1, EP):
        total = total + held[k]
    st2[...] = total

    def project_back(b, slot):
        rows = block_rows(b)
        values = x_s[slot, pl.ds(pl.multiple_of(b % 2 * TOK, TOK), TOK)].astype(F32)
        r1 = lax.rsqrt(jnp.mean(values * values, axis=1, keepdims=True) + EPSILON)
        n1 = values * r1
        normed = (n1 * gain_a[...]).astype(BF)
        cq, ck, mq, mk = columns(
            lax.rsqrt(st[pl.ds(2 * b, 1)] * (1.0 / D) + EPSILON),
            lax.rsqrt(st[pl.ds(2 * b + 1, 1)] * (1.0 / KV) + EPSILON),
            st2[pl.ds(2 * b, 1)] * (1.0 / D),
            st2[pl.ds(2 * b + 1, 1)] * (1.0 / KV),
        )
        uq, uk = u_s[rows, :128], u_s[rows, 128:]
        nq = lin[rows, :128] * cq
        nk = lin[rows, 128:] * ck
        gq = cq * (uq * gain[:, :128] - nq * mq)
        gk = jnp.where(first, ck * (uk * gain[:, 128:] - nk * mk), uk)
        glin = jnp.concatenate([gq, gk], axis=1).astype(BF)
        vec[1:2, :128] += jnp.sum(uq * nq, axis=0, keepdims=True)
        vec[2:3, :128] += jnp.sum(uk * nk, axis=0, keepdims=True)
        gn = dot_nt(glin, wcol[...])
        vec[0:1] += jnp.sum(gn * n1, axis=0, keepdims=True)
        dwt[...] += dot_tn(glin, normed)
        return gn.astype(BF)

    def chips(k, carry):
        q = (x + 2 + k - (k // 2) * (2 * k - 1)) % 4
        for step in range(4):

            @pl.when(k == step)
            def _(step=step):
                x_load(step).wait()

        swo[k] = project_back(q * 2 + 1 - c, k % 2)
        red2.swap(k).start()

        @pl.when(k == 1)
        def _():
            red2.send_opp()

        @pl.when(k == 2)
        def _():
            red2.near_left()

        @pl.when(k == 3)
        def _():
            red2.near_right()

        snd[k] = project_back(q * 2 + c, k % 2)
        for step in range(2):

            @pl.when(k == step)
            def _(step=step):
                x_load(step + 2).start()

        return carry

    lax.fori_loop(0, 4, chips, 0)
    dws[...] = jnp.transpose(dwt[...]).astype(BF)
    spread_d = [remote(part(dws, d, 64), dheld.at[r], (s_d, r_d), k, {"rep": d}) for k, d in enumerate(copies)]
    for copy in spread_d:
        copy.start()
    dheld[r] = part(dws, r, 64)[...]
    gain_q, gain_k = vec[1:2, :128], vec[2:3, :128]
    low, spread = iota((1, 128), 1) < 32, iota((1, 128), 1) // 32 == 2
    gain_k = jnp.where(low, gain_k, jnp.where(spread, pltpu.roll(gain_k, 32, 1), 0.0))
    vec[1:3, :128] = jnp.zeros((2, 128), F32)
    vec[1:2, pl.ds(pl.multiple_of(e * 128, 128), 128)] = gain_q
    vec[2:3, pl.ds(pl.multiple_of(e * 128, 128), 128)] = gain_k
    spread_v = [remote(vec, vheld.at[e], (s_v, r_v), k, {"ep": d}) for k, d in enumerate(others)]
    for copy in spread_v:
        copy.start()
    vheld[e] = vec[...]
    red2.merge(3)
    red2.send_far()
    by_z.last.relay()
    by_y.last.relay()
    for copy in spread_v:
        copy.wait_recv()
    total = vheld[0]
    for k in range(1, EP):
        total = total + vheld[k]
    vtot[...] = total
    def lanes_of(d):
        return vtot.at[:, pl.ds(pl.multiple_of(d // 2 * 128, 128), 128)]

    spread_v2 = [remote(lanes_of(d), vheld2.at[r], (s_v2, r_v2), k, {"rep": d}) for k, d in enumerate(copies)]
    for copy in spread_v2:
        copy.start()
    vheld2[r] = lanes_of(r)[...]
    for copy in spread_w:
        copy.wait_recv()
    total = wheld[0]
    for k in range(1, REP):
        total = total + wheld[k]
    go_s[...] = total[:, :D]
    pack_s[0:8] = total[:, D:]
    for copy in spread_d:
        copy.wait_recv()
    total = dheld[0].astype(F32)
    for k in range(1, REP):
        total = total + dheld[k].astype(F32)
    dsum[...] = total
    spread_e = [remote(part(dsum, d, 8), dw_o.at[e], (s_e, r_e), k, {"ep": d}) for k, d in enumerate(others)]
    for copy in spread_e:
        copy.start()
    dw_o[e] = part(dsum, e, 8)[...]
    for copy in spread_v2:
        copy.wait_recv()
    total = vheld2[0]
    for k in range(1, REP):
        total = total + vheld2[k]
    start = r % 2 * 64
    rows_d, lanes_d = iota((128, 128), 0), iota((128, 128), 1)
    eight = jnp.where((rows_d == start + e * 8 + lanes_d) & (lanes_d < 8), 1.0, 0.0)
    four = jnp.where((rows_d == start + e * 4 + lanes_d) & (lanes_d < 4), 1.0, 0.0)

    def pick(sel):
        return jnp.dot(total, sel, preferred_element_type=F32, precision=HIGH)

    eights, fours = pick(eight), pick(four)
    pack_s[8:16] = jnp.where(iota((8, 128), 0) == 2, fours, eights)
    by_z.finish(eg_s, 0)
    by_y.finish(eg_s, FF)
    for copy in spread_e:
        copy.wait_recv()
    low_lanes = iota((8, 128), 1) < HEAD_DIM
    for d in range(EP):
        gq_s[:, d * 128 : (d + 1) * 128] = dw_o[d][:, :128]
    for d in range(EP // 2):
        even, odd = dw_o[2 * d][:, 128:], dw_o[2 * d + 1][:, 128:]
        gk_s[:, d * 128 : (d + 1) * 128] = jnp.where(low_lanes, even, pltpu.roll(odd, HEAD_DIM, 1))
        gv_s[:, d * 128 : (d + 1) * 128] = jnp.where(low_lanes, pltpu.roll(even, HEAD_DIM, 1), odd)
    pairs = [(gq_s, gq_o), (gk_s, gk_o), (gv_s, gv_o), (go_s, go_o), (pack_s, pack_o), (eg_s, eg_o)]
    for k, (src, dst) in enumerate(pairs):
        ends.append(pltpu.make_async_copy(src, dst, esem.at[1 + k]))
        ends[-1].start()
    red2.finish(gm)
    values = x_s[1, pl.ds(pl.multiple_of(c * TOK, TOK), TOK)].astype(F32)
    r1 = lax.rsqrt(jnp.mean(values * values, axis=1, keepdims=True) + EPSILON)
    n1 = values * r1
    z = gm[...] * gain_a[...]
    gh[...] = gh[...] + r1 * (z - n1 * jnp.mean(z * n1, axis=1, keepdims=True))
    ends.append(pltpu.make_async_copy(gh, ig_o, esem.at[7]))
    ends[-1].start()
    for copy in ends:
        copy.wait()
    for copy in heads + stats + spread_w + spread_d + spread_e + spread_v + spread_v2:
        copy.wait_send()


ELSEWHERE = (7, 9, 12)
X_ALL = 14


def back(*args):
    def vm(dims, dtype=F32):
        return pltpu.VMEM(dims, dtype)

    held = [vm((2, 2 * TOK, D), BF) if k == X_ALL else vm(a.shape, a.dtype) for k, a in enumerate(args) if k > 1 and k not in ELSEWHERE]
    results = [((TOK, D), BF), ((TOK, D), F32), ((8, D), F32), ((8, KV), F32), ((8, KV), F32), ((8, D), F32), ((16, 128), F32)]
    results.append(((PAIR, BLOCK, D), BF))
    landing = [vm((4, TOK, D), BF), vm((2, TOK, D), BF), vm((TOK, D), BF)]
    return comm_call(
        back_kernel,
        "back",
        6,
        [shape(*result) for result in results],
        [ANY] * 23,
        [ANY] * 8,
        held
        + [
            vm((TOK, D)),
            vm((TOK, D), BF),
            vm((LENGTH, 128), BF),
            vm((EP, 2 * TOK, 128), BF),
            vm(((10 + 5 * (KEPT - 4)) * TOK, 2 * TOK), BF),
            vm((LENGTH, 128)),
            vm((LENGTH, 128)),
            vm((LENGTH, 256)),
            vm((16, 256)),
            vm((16, 256)),
            vm((EP, 16, 256)),
            vm((D, WB), BF),
            vm((128, WB)),
            vm((REP, 8, WB)),
            vm((256, D)),
            vm((D, 256), BF),
            vm((REP, 64, 256), BF),
            vm((64, 256)),
            vm((EP, 8, 256)),
            vm((8, D)),
            vm((EP, 8, D)),
            vm((8, D)),
            vm((REP, 8, 128)),
            vm((4, TOK, D), BF),
            vm((4, TOK, D), BF),
        ]
        + landing
        + [vm((2, TOK, D), BF)]
        + [vm((4, 128, WB), BF), vm((4, 128, WB), BF), vm((2, 128, WB), BF), vm((128, WB), BF)]
        + [DMA((10,))] * 6
        + [DMA((7,))] * 4
        + [DMA((15,))] * 4
        + [DMA((7,))] * 4
        + [DMA((15,))] * 2
        + [DMA((20,)), DMA((4,)), DMA((4,)), DMA((8,)), DMA((2,))]
        + [vm(*result) for k, result in enumerate(results) if k != 1]
        + grid_scratch() * 2
        + [DMA((12,))] * 4
        + [DMA((4,))] * 2,
        limit=64,
    )(*args)


def finish_kernel(
    xa_in, xb_in, out_in, ig_in, gq_in, gk_in, gv_in, go_in, pack_in,
    out_o, ig_o, gq_o, gk_o, gv_o, go_o, gr_o, va_o, vq_o, vk_o, vf_o, gate_o, up_o, down_o,
    x_s, gate_s, up_s, down_s, out_s, ig_s, gq_s, gk_s, gv_s, go_s, pack, gr_s, va_s, vq_s, vk_s, vf_s, sem,
):
    loads = [
        pltpu.make_async_copy(xa_in, x_s.at[pl.ds(0, PAIR)], sem.at[9]),
        pltpu.make_async_copy(xb_in, x_s.at[pl.ds(PAIR, PAIR)], sem.at[10]),
    ]
    for load in loads:
        load.start()
    stages = [out_s, ig_s, gq_s, gk_s, gv_s, go_s]
    fetch = [
        pltpu.make_async_copy(src, dst, sem.at[k])
        for k, (src, dst) in enumerate(zip([out_in, ig_in, gq_in, gk_in, gv_in, go_in], stages))
    ]
    copies = [
        pltpu.make_async_copy(src, dst, sem.at[k])
        for k, (src, dst) in enumerate(zip(stages, [out_o, ig_o, gq_o, gk_o, gv_o, go_o]))
    ]
    load_pack = pltpu.make_async_copy(pack_in, pack, sem.at[11])
    for copy in fetch + [load_pack]:
        copy.start()
    for load, copy in zip(fetch, copies):
        load.wait()
        copy.start()
    for load in loads:
        load.wait()
    gate_s[...] = x_s[:, :64, :FF].astype(F32)
    up_s[...] = x_s[:, :64, FF:].astype(F32)
    down_s[...] = x_s[:, 64:].astype(F32)
    load_pack.wait()
    gr_s[...] = pack[0:8, :EXPERTS]
    va_s[...] = pack[8:9, :8]
    vq_s[...] = pack[9:10, :8]
    vk_s[...] = pack[10:11, :4]
    vf_s[...] = pack[11:12, :8]
    pairs = [(gate_s, gate_o), (up_s, up_o), (down_s, down_o)]
    pairs += [(gr_s, gr_o), (va_s, va_o), (vq_s, vq_o), (vk_s, vk_o), (vf_s, vf_o)]
    for k, (src, dst) in enumerate(pairs):
        k = k if k < 5 else k + 1
        copies.append(pltpu.make_async_copy(src, dst, sem.at[6 + k]))
        copies[-1].start()
    for copy in copies:
        copy.wait()


def finish(xa, xb, out, ig, gq, gk, gv, go, pack):
    gate, down = shape((LOCAL, 64, FF)), shape((LOCAL, 32, D))
    return pl.pallas_call(
        finish_kernel,
        out_shape=[shape(a.shape, a.dtype) for a in (out, ig, gq, gk, gv, go)]
        + [shape((8, EXPERTS)), shape((1, 8)), shape((1, 8)), shape((1, 4)), shape((1, 8)), gate, gate, down],
        in_specs=[ANY] * 9,
        out_specs=[ANY] * 14,
        scratch_shapes=[
            pltpu.VMEM((LOCAL, BLOCK, D), BF),
            pltpu.VMEM(gate.shape, F32),
            pltpu.VMEM(gate.shape, F32),
            pltpu.VMEM(down.shape, F32),
        ]
        + [pltpu.VMEM(a.shape, a.dtype) for a in (out, ig, gq, gk, gv, go, pack)]
        + [pltpu.VMEM(dims, F32) for dims in ((8, EXPERTS), (1, 8), (1, 8), (1, 4), (1, 8))]
        + [
            DMA((16,)),
        ],
        compiler_params=pltpu.CompilerParams(vmem_limit_bytes=62 * MIB),
        name="finish",
    )(xa, xb, out, ig, gq, gk, gv, go, pack)


def body(
    tokens,
    segments,
    routes,
    w_query,
    w_key,
    w_value,
    w_out,
    w_router,
    gain_attn,
    gain_query,
    gain_key,
    gain_ffn,
    w_gate,
    w_up,
    w_down,
    out_grad,
):
    gains = [gain.reshape(1, -1) for gain in (gain_attn, gain_query, gain_key, gain_ffn)]
    cosine, sine = turn_tables()
    (
        x_all, g_all, lin, q, k, v, att, lse, hidden, moe_in, tables, attended, misc, router, whole_out, w_cols,
    ) = front(
        tokens, out_grad, w_query, w_key, w_value, w_out, w_router, *gains, segments, routes.T, cosine, sine
    )
    def over_copies(grads):
        grads = grads.reshape(PAIR, REP * BLOCK, D)
        return lax.psum_scatter(grads, "rep", scatter_dimension=1, tiled=True)

    m_all, tabs, y, z, gg_first, grads = experts_first(moe_in, tables, g_all, w_gate, w_up, w_down)
    sums_first = over_copies(grads)
    grad_moe, mixture, gg_last, grads = experts_last(m_all, tabs, y, z, g_all, w_gate, w_up, w_down)
    *rows, sums_last = back(
        grads.reshape(PAIR, 4, 4, BLOCK, D), mixture, grad_moe, gg_first, gg_last, tables, hidden, moe_in, out_grad, attended, misc, router, whole_out,
        w_cols, x_all, lin, q, k, v, att, lse, cosine, sine,
    )
    out, ig, gq, gk, gv, go, gr, va, vq, vk, vf, gate, up, down = finish(sums_first, sums_last, *rows)
    return out, ig, gq, gk, gv, go, gr, va.reshape(8), vq.reshape(8), vk.reshape(4), vf.reshape(8), gate, up, down


def solution(mesh):
    both = P(("rep", "ep"), None)
    line = P(("rep", "ep"))
    owner = P("ep", None, None)
    kept = P("ep", "rep", None)
    return jax.shard_map(
        body,
        mesh=mesh,
        in_specs=(both, P("rep", None)) + (both,) * 6 + (line,) * 4 + (owner,) * 3 + (both,),
        out_specs=(both,) * 7 + (line,) * 4 + (kept,) * 3,
        check_vma=False,
    )
```
